32 devices in a mesh: groups: 2 (over x), gx: 8 (over z, y), gy: 2 (over core).
Axes of the slice: x: 2, y: 2, z: 4, core: 2. Of those that a mesh axis runs over, the one named last changes fastest.
Arguments:
- activations: bfloat16 [128, 18432], P(('groups', 'gx'), 'gy'), parts along dimension 0, may hold values from -300 to 300
- norm_gain: bfloat16 [18432], P('gy'), may hold values from 0.099609375 to 1.8984375
- query_weight: bfloat16 [12288, 18432], P('gx', 'gy'), may hold values from -0.046875 to 0.046875
- keyval_weight: bfloat16 [512, 18432], P('gx', 'gy'), may hold values from -0.046875 to 0.046875
- output_weight: bfloat16 [12288, 18432], P('gy', 'gx'), may hold values from -0.3125 to 0.3125
- cache_keys: bfloat16 [128, 2048, 256], P(('groups', 'gx', 'gy')), parts along dimension 0, may hold values from -1000 to 1000
- cache_values: bfloat16 [128, 2048, 256], P(('groups', 'gx', 'gy')), parts along dimension 0, may hold values from -6 to 6
- cache_lengths: int32 [128], P(('groups', 'gx', 'gy')), parts along dimension 0, may hold values from 2 to 2048, as said below
Outputs:
- attention_out: bfloat16 [128, 18432], P(('groups', 'gy'), 'gx'), parts along dimension 0
The draws below stay inside these ranges and needn't reach their ends.
There are 2 independent parts, one for each index of `groups`. The reference program is written for one: setup_inputs(seed, part) draws one part's arguments, and reference() takes and returns one part's arrays. A program takes and returns all parts, laid end to end along the dimension named above; an argument that names none is the same for every part. Nothing has to cross between parts.
Inputs may be any that keep to these rules, and one draw needn't show every extreme that they name: `cache_lengths`: the largest of a part's values is exactly 2048.
All inputs are finite; a program needn't handle non-finite values.
Results may differ from the reference program's by a relative error of at most 0.007.
The reference program's roundings to bfloat16 on the way count: a program that leaves them out, or rounds other values in their place, can miss the bound.
Values may be sent and summed in bfloat16 or wider, within the bound.
No kernel may reach another device: no remote copies, remote signals or barrier semaphores. Data moves between devices by JAX's collectives and lax.ppermute only.
A program may use at most 192 MiB of HBM per device.

```python
import math
import jax
import jax.numpy as jnp
from jax import lax

D = 18432
HEADS = 48
DH = 256
CACHE = 2048
HQ = 12288
ROWS = 64


def draw_activations(key, part):
    key = jax.random.fold_in(key, 11)
    row_key, column_key, base_key = jax.random.split(key, 3)
    row_scale = jnp.exp(jax.random.uniform(row_key, (ROWS, 1), jnp.float32, 0.0, math.log(10.0)))
    ramp = jnp.arange(D, dtype=jnp.float32) / D
    column_scale = jnp.exp(jax.random.uniform(column_key, (1, D), jnp.float32, 0.0, math.log(10.0)) + math.log(3.0) * ramp[None, :])
    values = jnp.clip(jax.random.normal(base_key, (ROWS, D), jnp.float32), -4.0, 4.0)
    return (values * row_scale * column_scale / 5.0).astype(jnp.bfloat16)


def draw_cache_keys(key, part):
    key = jax.random.fold_in(key, 23)
    entries = jnp.clip(jax.random.normal(key, (ROWS, CACHE, DH), jnp.float32), -6.0, 6.0)
    return entries.astype(jnp.bfloat16)


def draw_cache_lengths(key, part):
    key = jax.random.fold_in(key, 37)
    pick_key, short_key, long_key, top_key = jax.random.split(key, 4)
    shorter = jax.random.randint(short_key, (ROWS,), 2, CACHE // 4 + 1)
    longer = jax.random.randint(long_key, (ROWS,), 2, CACHE + 1)
    picked = jax.random.randint(pick_key, (ROWS,), 0, 4)
    lengths = jnp.where(picked > 0, longer, shorter)
    top_row = jax.random.randint(top_key, (), 0, ROWS)
    lengths = jnp.where(jnp.arange(ROWS) == top_row, CACHE, lengths)
    return lengths.astype(jnp.int32)


def level_of(stream_key, shape, cuts, low, largest):
    def one(axis_at, parts):
        heights = jax.random.uniform(jax.random.fold_in(jax.random.fold_in(stream_key, 6), axis_at), (parts,), jnp.float32, low / len(cuts), largest / len(cuts))
        return jnp.repeat(jnp.exp(heights), shape[axis_at] // parts).reshape((-1,) + (1,) * (len(shape) - axis_at - 1))

    level = one(*cuts[0])
    for cut in cuts[1:]:
        level = level * one(*cut)
    return level


def bell_draw(rng, shape, width, bound, cuts=(), kind=jnp.bfloat16):
    result = jax.random.normal(rng, shape, jnp.float32) * width
    if len(cuts) > 0:
        result = level_of(rng, shape, cuts, -0.22, 0.18) * result
    return jnp.clip(result, min=-bound, max=bound).astype(kind)


def setup_inputs(seed: int = 0, part: int = 0) -> dict:
    streams_of = jax.random.split(jax.random.key(seed), 9)
    part_keys = jax.random.split(jax.random.fold_in(streams_of[8], part), 9)
    return {
        "activations": draw_activations(jax.random.fold_in(jax.random.fold_in(streams_of[8], part), 71), part),
        "norm_gain": jnp.clip(1.0 + 0.18 * jax.random.normal(streams_of[1], (D,), jnp.float32), 0.099609375, 1.8984375).astype(jnp.bfloat16),
        "query_weight": bell_draw(streams_of[2], (HQ, D), D ** -0.5, 0.046875, ((0, 8), (1, 2))),
        "keyval_weight": bell_draw(streams_of[3], (2 * DH, D), D ** -0.5, 0.046875, ((0, 8), (1, 2))),
        "output_weight": bell_draw(streams_of[4], (HQ, D), (HQ // 32) ** -0.5, 0.3125, ((0, 2), (1, 8))),
        "cache_keys": draw_cache_keys(jax.random.fold_in(jax.random.fold_in(streams_of[8], part), 71), part),
        "cache_values": bell_draw(part_keys[6], (ROWS, CACHE, DH), 1.0, 6.0, ((0, 16),)),
        "cache_lengths": draw_cache_lengths(jax.random.fold_in(jax.random.fold_in(streams_of[8], part), 71), part),
    }


epsilon = 1e-06
contract = (((1,), (1,)), ((), ()))

def rotate(vectors, places):
    half_width = vectors.shape[-1] // 2
    indices = jnp.arange(half_width, dtype=jnp.float32)
    frequency = jnp.exp(-math.log(10000.0) * indices / half_width)
    angles = places * frequency
    cosine = jnp.cos(angles)
    sine = jnp.sin(angles)
    first_half = vectors[..., :half_width]
    second_half = vectors[..., half_width:]
    return jnp.concatenate([first_half * cosine - second_half * sine, second_half * cosine + first_half * sine], axis=-1)

def reference(activations, norm_gain, query_weight, keyval_weight, output_weight, cache_keys, cache_values, cache_lengths):
    inputs = activations.astype(jnp.float32)
    row_mean = lax.optimization_barrier(jnp.sum(inputs, axis=1, keepdims=True)) / D
    row_square = lax.optimization_barrier(jnp.sum(inputs * inputs, axis=1, keepdims=True)) / D
    variance = row_square - row_mean * row_mean
    normed = ((inputs - row_mean) * lax.rsqrt(variance + epsilon) * norm_gain.astype(jnp.float32)).astype(jnp.bfloat16)
    projected_query = lax.dot_general(normed, query_weight, contract, preferred_element_type=jnp.float32).astype(jnp.bfloat16)
    projected_keyval = lax.dot_general(normed, keyval_weight, contract, preferred_element_type=jnp.float32).astype(jnp.bfloat16)
    score_scale = 1.0 / math.sqrt(DH)

    def one_row(operands):
        query_row, keyval_row, row_keys, row_values, length = operands
        places = length.astype(jnp.float32)
        queries = rotate(query_row.astype(jnp.float32).reshape(HEADS, DH), places).astype(jnp.bfloat16)
        new_key = rotate(keyval_row[:DH].astype(jnp.float32), places).astype(jnp.bfloat16)
        new_value = keyval_row[DH:].astype(jnp.float32)
        scores = jnp.dot(queries, row_keys.T, preferred_element_type=jnp.float32) * score_scale
        visible = jnp.arange(CACHE) < length
        scores = jnp.where(visible[None, :], scores, -1e+30)
        own_score = jnp.dot(queries, new_key, preferred_element_type=jnp.float32) * score_scale
        highest = jnp.maximum(lax.optimization_barrier(jnp.max(scores, axis=1)), own_score)
        weights = jnp.exp(scores - highest[:, None])
        own_weight = jnp.exp(own_score - highest)
        totals = lax.optimization_barrier(jnp.sum(weights, axis=1)) + own_weight
        blended = jnp.dot(weights.astype(jnp.bfloat16), row_values, preferred_element_type=jnp.float32)
        blended = blended + own_weight[:, None] * new_value[None, :]
        return (blended / totals[:, None]).astype(jnp.bfloat16).reshape(HEADS * DH)
    attended = lax.map(one_row, (projected_query, projected_keyval, cache_keys, cache_values, cache_lengths))
    return jnp.dot(attended, output_weight, preferred_element_type=jnp.float32).astype(jnp.bfloat16)
```

```python
import math

import jax
import jax.numpy as jnp
from jax import lax
from jax.sharding import PartitionSpec as P

D = 18432
HEADS = 48
DH = 256


epsilon = 1e-06
contract = (((1,), (1,)), ((), ()))


def rotate(vectors, places):
    half_width = vectors.shape[-1] // 2
    indices = jnp.arange(half_width, dtype=jnp.float32)
    frequency = jnp.exp(-math.log(10000.0) * indices / half_width)
    angles = places * frequency
    cosine = jnp.cos(angles)
    sine = jnp.sin(angles)
    first_half = vectors[..., :half_width]
    second_half = vectors[..., half_width:]
    return jnp.concatenate(
        [first_half * cosine - second_half * sine, second_half * cosine + first_half * sine],
        axis=-1,
    )


def ring_order(n):
    return list(range(0, n, 2)) + list(range(n - 1, 0, -2))


def swap_pair(x):
    return lax.ppermute(x, "gy", [(0, 1), (1, 0)])


def ring_gather(shard, n):
    order = ring_order(n)
    onward = [(order[p], order[(p + 1) % n]) for p in range(n)]
    back = [(order[p], order[(p - 1) % n]) for p in range(n)]
    place = jnp.array([order.index(i) for i in range(n)], jnp.int32)[lax.axis_index("gx")]
    owner = jnp.array(order, jnp.int32)
    rows, cols = shard.shape
    half = cols // 2
    pieces = [(0, shard)]
    left = right = shard
    for step in range(1, n // 2):
        left = lax.ppermute(left, "gx", onward)
        right = lax.ppermute(right, "gx", back)
        pieces += [(-step, left), (step, right)]
    far_left = lax.ppermute(left[:, :half], "gx", onward)
    far_right = lax.ppermute(right[:, half:], "gx", back)
    pieces.append((n // 2, jnp.concatenate([far_left, far_right], axis=1)))
    whole = jnp.zeros((n * rows, cols), shard.dtype)
    for offset, piece in pieces:
        source = owner[(place + offset) % n]
        whole = lax.dynamic_update_slice(whole, piece, (source * rows, 0))
    return whole


def spread_rows(stats, n):
    if n > 8:
        return lax.all_gather(stats, "gx", axis=0, tiled=True)
    me = lax.axis_index("gx")
    rows = stats.shape[0]
    whole = jnp.zeros((n * rows,) + stats.shape[1:], stats.dtype)
    whole = lax.dynamic_update_slice(whole, stats, (me * rows, 0))
    for shift in range(1, n):
        got = lax.ppermute(stats, "gx", [(i, (i + shift) % n) for i in range(n)])
        whole = lax.dynamic_update_slice(whole, got, (((me - shift) % n) * rows, 0))
    return whole


def on_device(
    activations,
    norm_gain,
    query_weight,
    keyval_weight,
    output_weight,
    cache_keys,
    cache_values,
    cache_lengths,
):
    n = lax.axis_size("gx")
    side = lax.axis_index("gy")
    everyone = ring_gather(activations, n).astype(jnp.float32)
    inputs = activations.astype(jnp.float32)
    sums = jnp.stack([jnp.sum(inputs, axis=1), jnp.sum(inputs * inputs, axis=1)], axis=1)
    sums = sums + swap_pair(sums)
    sums = spread_rows(sums, n)
    row_mean = sums[:, :1] / D
    row_square = sums[:, 1:] / D
    variance = row_square - row_mean * row_mean
    shard_rows = (
        (everyone - row_mean) * lax.rsqrt(variance + epsilon) * norm_gain.astype(jnp.float32)
    ).astype(jnp.bfloat16)
    query_part = lax.dot_general(
        shard_rows, query_weight, contract, preferred_element_type=jnp.float32
    )
    keyval_part = lax.dot_general(
        shard_rows, keyval_weight, contract, preferred_element_type=jnp.float32
    )
    partial_sums = jnp.concatenate([query_part, keyval_part], axis=1)
    local_rows = cache_lengths.shape[0]
    stripe = partial_sums.shape[1]
    by_side = partial_sums.reshape(n, 2, local_rows, stripe)
    keep = lax.dynamic_index_in_dim(by_side, side, axis=1, keepdims=False)
    give = lax.dynamic_index_in_dim(by_side, 1 - side, axis=1, keepdims=False)
    projected = (keep + swap_pair(give)).astype(jnp.bfloat16)
    gathered = lax.all_to_all(projected, "gx", split_axis=0, concat_axis=0, tiled=True)
    gathered = jnp.swapaxes(gathered, 0, 1)
    query_cols = query_weight.shape[0]
    queries = gathered[:, :, :query_cols].reshape(local_rows, HEADS, DH)
    keyvals = gathered[:, :, query_cols:].reshape(local_rows, 2 * DH)
    places = cache_lengths.astype(jnp.float32)
    queries = rotate(queries.astype(jnp.float32), places[:, None, None]).astype(jnp.bfloat16)
    new_keys = rotate(keyvals[:, :DH].astype(jnp.float32), places[:, None]).astype(jnp.bfloat16)
    new_values = keyvals[:, DH:].astype(jnp.float32)
    score_scale = 1.0 / math.sqrt(DH)
    scores = (
        jnp.einsum("rhd,rtd->rht", queries, cache_keys, preferred_element_type=jnp.float32)
        * score_scale
    )
    visible = jnp.arange(cache_keys.shape[1])[None, :] < cache_lengths[:, None]
    scores = jnp.where(visible[:, None, :], scores, -1e30)
    own_score = (
        jnp.einsum("rhd,rd->rh", queries, new_keys, preferred_element_type=jnp.float32)
        * score_scale
    )
    highest = jnp.maximum(jnp.max(scores, axis=2), own_score)
    weights = jnp.exp(scores - highest[:, :, None])
    own_weight = jnp.exp(own_score - highest)
    totals = jnp.sum(weights, axis=2) + own_weight
    blended = jnp.einsum(
        "rht,rtd->rhd",
        weights.astype(jnp.bfloat16),
        cache_values,
        preferred_element_type=jnp.float32,
    )
    blended = blended + own_weight[:, :, None] * new_values[:, None, :]
    attended = (blended / totals[:, :, None]).astype(jnp.bfloat16).reshape(local_rows, 2, -1)
    mine = lax.dynamic_index_in_dim(attended, side, axis=1, keepdims=False)
    other = lax.dynamic_index_in_dim(attended, 1 - side, axis=1, keepdims=False)
    other = swap_pair(other)
    first = jnp.where(side == 0, mine, other)
    second = jnp.where(side == 0, other, mine)
    swapped = jnp.concatenate([first, second], axis=0)
    partial_out = jnp.dot(
        ring_gather(swapped, n),
        output_weight,
        preferred_element_type=jnp.float32,
    )
    by_side = partial_out.reshape(2, -1, partial_out.shape[1])
    keep = lax.dynamic_index_in_dim(by_side, side, axis=0, keepdims=False)
    give = lax.dynamic_index_in_dim(by_side, 1 - side, axis=0, keepdims=False)
    return (keep + swap_pair(give)).astype(jnp.bfloat16)


def solution(mesh):
    return jax.shard_map(
        on_device,
        mesh=mesh,
        in_specs=(
            P(("groups", "gx"), "gy"),
            P("gy"),
            P("gx", "gy"),
            P("gx", "gy"),
            P("gy", "gx"),
            P(("groups", "gx", "gy"), None, None),
            P(("groups", "gx", "gy"), None, None),
            P(("groups", "gx", "gy")),
        ),
        out_specs=P(("groups", "gy"), "gx"),
        check_vma=False,
    )
```

```python
import math

import jax
import jax.numpy as jnp
from jax import lax
from jax.experimental import pallas as pl
from jax.experimental.pallas import tpu as pltpu
from jax.sharding import PartitionSpec as P

D = 18432
HEADS = 48
DH = 256


epsilon = 1e-06
contract = (((1,), (1,)), ((), ()))
MIB = 1 << 20
ANY = pl.BlockSpec(memory_space=pl.ANY)
IN_VMEM = pl.BlockSpec(memory_space=pltpu.VMEM)
IN_SMEM = pl.BlockSpec(memory_space=pltpu.SMEM)


def rotate(vectors, places):
    half_width = vectors.shape[-1] // 2
    indices = jnp.arange(half_width, dtype=jnp.float32)
    frequency = jnp.exp(-math.log(10000.0) * indices / half_width)
    angles = places * frequency
    cosine = jnp.cos(angles)
    sine = jnp.sin(angles)
    first_half = vectors[..., :half_width]
    second_half = vectors[..., half_width:]
    return jnp.concatenate(
        [first_half * cosine - second_half * sine, second_half * cosine + first_half * sine],
        axis=-1,
    )


def ring_order(n):
    return list(range(0, n, 2)) + list(range(n - 1, 0, -2))


def swap_pair(x):
    return lax.ppermute(x, "gy", [(0, 1), (1, 0)])


class Ring:
    def __init__(self, n):
        self.n = n
        order = ring_order(n)
        self.onward = [(order[p], order[(p + 1) % n]) for p in range(n)]
        self.back = [(order[p], order[(p - 1) % n]) for p in range(n)]
        self.across = [(order[p], order[(p + n // 2) % n]) for p in range(n)]
        self.offsets = [0]
        for step in range(1, n // 2):
            self.offsets += [-step, step]
        self.offsets.append(n // 2)

    def owners(self):
        n = self.n
        me = lax.axis_index("gx")
        place = jnp.where(me % 2 == 0, me // 2, n - 1 - me // 2)
        at = (place + jnp.array(self.offsets, jnp.int32) + n) % n
        owner = jnp.where(at < n // 2, 2 * at, 2 * (n - 1 - at) + 1)
        return jnp.concatenate([owner, lax.axis_index("gy")[None]]).astype(jnp.int32)

    def step(self, left, right):
        return lax.ppermute(left, "gx", self.onward), lax.ppermute(right, "gx", self.back)


def load_kernel(count, *refs):
    sources, targets, sems = refs[:count], refs[-count - 1 : -1], refs[-1]
    copies = [
        pltpu.make_async_copy(source, target, sems.at[i])
        for i, (source, target) in enumerate(zip(sources, targets))
    ]
    for copy in copies:
        copy.start()
    for copy in copies:
        copy.wait()


def load(arrays, after=()):
    return pl.pallas_call(
        lambda *refs: load_kernel(len(arrays), *refs),
        out_shape=[pltpu.VMEM(a.shape, a.dtype) for a in arrays],
        in_specs=[ANY] * (len(arrays) + len(after)),
        out_specs=[IN_VMEM] * len(arrays),
        scratch_shapes=[pltpu.SemaphoreType.DMA((len(arrays),))],
        compiler_params=pltpu.CompilerParams(vmem_limit_bytes=4 * MIB),
        name="load",
    )(*arrays, *after)


def load_rows_kernel(start, size, *refs):
    source, target, sem = refs[0], refs[-2], refs[-1]
    copy = pltpu.make_async_copy(source.at[pl.ds(start, size)], target, sem)
    copy.start()
    copy.wait()


def load_rows(array, start, size, after=()):
    return pl.pallas_call(
        lambda *refs: load_rows_kernel(start, size, *refs),
        out_shape=pltpu.VMEM((size,) + array.shape[1:], array.dtype),
        in_specs=[ANY] * (1 + len(after)),
        out_specs=IN_VMEM,
        scratch_shapes=[pltpu.SemaphoreType.DMA],
        compiler_params=pltpu.CompilerParams(vmem_limit_bytes=4 * MIB),
        name="load_rows",
    )(array, *after)


def sums_kernel(*refs):
    out = refs[-1]
    rows = refs[0].shape[0]
    lane = lax.broadcasted_iota(jnp.int32, (rows, 128), 1)
    for i, ref in enumerate(refs[:-1]):
        x = ref[...].astype(jnp.float32)
        total = jnp.sum(x, axis=1, keepdims=True)
        square = jnp.sum(x * x, axis=1, keepdims=True)
        both = jnp.where(lane == 0, total, jnp.where(lane == 1, square, 0.0))
        out[i * rows : (i + 1) * rows, :] = both


def row_sums(shards):
    rows = shards[0].shape[0]
    return pl.pallas_call(
        sums_kernel,
        out_shape=jax.ShapeDtypeStruct((len(shards) * rows, 128), jnp.float32),
        in_specs=[IN_VMEM] * len(shards),
        out_specs=IN_VMEM,
        compiler_params=pltpu.CompilerParams(vmem_limit_bytes=16 * MIB),
        name="row_sums",
    )(*shards)


def project_kernel(n, parts, *refs):
    owners, sums_a, sums_b, gain = refs[:4]
    near = refs[4 : 4 + n - 1]
    far = refs[4 + n - 1 : 4 + n + 1]
    weights = refs[4 + n + 1 : 4 + n + 1 + parts]
    keep, give, normed, total = refs[4 + n + 1 + parts :]
    rows = near[0].shape[0]
    half = far[0].shape[1]
    sums = sums_a[...] + sums_b[...]
    row_mean = sums[:, :1] / D
    row_square = sums[:, 1:2] / D
    scale = lax.rsqrt(row_square - row_mean * row_mean + epsilon)
    for part in range(2):
        cols = slice(part * half, (part + 1) * half)
        for i in range(n):
            at = slice(i * rows, (i + 1) * rows)
            x = near[i][:, cols] if i < n - 1 else far[part][...]
            x = (x.astype(jnp.float32) - row_mean[at]) * scale[at] * gain[:, cols]
            normed[at, cols] = x
        x = normed[:, cols].astype(jnp.bfloat16)
        start = 0
        for weight in weights:
            width = weight.shape[0]
            term = lax.dot_general(
                x, weight[:, cols], contract, preferred_element_type=jnp.float32
            )
            if part == 0:
                total[:, start : start + width] = term
            else:
                total[:, start : start + width] += term
            start += width
    side = owners[n]
    local = rows // 2
    for i in range(n):
        block = total[i * rows : (i + 1) * rows, :]
        low, high = block[:local], block[local:]
        keep[owners[i]] = jnp.where(side == 0, low, high)
        give[owners[i]] = jnp.where(side == 0, high, low)


def project(n, owners, sums, gain, near, far, weights):
    rows, width = near[0].shape
    stripe = sum(w.shape[0] for w in weights)
    shape = jax.ShapeDtypeStruct((n, rows // 2, stripe), jnp.float32)
    return pl.pallas_call(
        lambda *refs: project_kernel(n, len(weights), *refs),
        out_shape=[shape, shape],
        in_specs=[IN_SMEM] + [IN_VMEM] * (3 + n + 1 + len(weights)),
        out_specs=[IN_VMEM, IN_VMEM],
        scratch_shapes=[
            pltpu.VMEM((n * rows, width), jnp.float32),
            pltpu.VMEM((n * rows, stripe), jnp.float32),
        ],
        compiler_params=pltpu.CompilerParams(vmem_limit_bytes=(24 if n <= 8 else 48) * MIB),
        name="project",
    )(owners, *sums, gain, *near, *far, *weights)


def output_kernel(n, parts, *refs):
    owners = refs[0]
    near = refs[1:n]
    far = refs[n : n + 2]
    weights = refs[n + 2 : n + 2 + parts]
    keep, give, total, placed = refs[n + 2 + parts :]
    rows = near[0].shape[0]
    half = far[0].shape[1]
    depth = weights[0].shape[0]
    for part, weight in enumerate(weights):
        start = part * depth
        cols = slice(start, start + depth)
        pieces = [ref[:, cols] for ref in near]
        for i, ref in enumerate(far):
            low, high = max(start, i * half), min(start + depth, (i + 1) * half)
            if low < high:
                last = ref[:, low - i * half : high - i * half]
                pieces.append(last)
        if len(pieces) > n:
            pieces[n - 1 :] = [jnp.concatenate(pieces[n - 1 :], axis=1)]
        x = jnp.concatenate([p.astype(jnp.float32) for p in pieces], axis=0)
        term = jnp.dot(
            x.astype(jnp.bfloat16), weight[...], preferred_element_type=jnp.float32
        )
        if part == 0:
            total[...] = term
        else:
            total[...] += term
    for i in range(n):
        placed[owners[i]] = total[i * rows : (i + 1) * rows, :]
    side = owners[n]
    keep[...] = placed[pl.ds(side * (n // 2), n // 2)]
    give[...] = placed[pl.ds((1 - side) * (n // 2), n // 2)]


def output_project(n, owners, near, far, weights):
    rows = near[0].shape[0]
    cols = weights[0].shape[1]
    shape = jax.ShapeDtypeStruct((n // 2, rows, cols), jnp.float32)
    return pl.pallas_call(
        lambda *refs: output_kernel(n, len(weights), *refs),
        out_shape=[shape, shape],
        in_specs=[IN_SMEM] + [IN_VMEM] * (n + 1 + len(weights)),
        out_specs=[IN_VMEM, IN_VMEM],
        scratch_shapes=[
            pltpu.VMEM((n * rows, cols), jnp.float32),
            pltpu.VMEM((n, rows, cols), jnp.float32),
        ],
        compiler_params=pltpu.CompilerParams(vmem_limit_bytes=(24 if n <= 8 else 48) * MIB),
        name="output_project",
    )(owners, *near, *far, *weights)


def on_device(
    activations,
    norm_gain,
    query_weight,
    keyval_weight,
    output_weight,
    cache_keys,
    cache_values,
    cache_lengths,
):
    n = lax.axis_size("gx")
    ring = Ring(n)
    owners = ring.owners()
    query_cols = query_weight.shape[0]
    pieces = 3 if query_cols % (3 * 256) == 0 else 1
    piece = query_cols // pieces
    weights = []

    left = right = activations
    near = [activations]
    own_sums = row_sums([activations])
    far_sums = lax.ppermute(own_sums, "gx", ring.across)
    sums = [own_sums]
    for step in range(1, n // 2):
        if step <= pieces:
            after = [] if step == 1 else [left, right]
            weights.append(load_rows(query_weight, (step - 1) * piece, piece, after))
        left, right = ring.step(left, right)
        near += [left, right]
        sums.append(row_sums([left, right]))
    weights += load([keyval_weight], [left, right])
    half = activations.shape[1] // 2
    far = ring.step(left[:, :half], right[:, half:])
    sums = jnp.concatenate(sums + [far_sums], axis=0)
    sums = (sums, swap_pair(sums))
    gain = norm_gain.astype(jnp.float32)[None, :]
    keep, give = project(n, owners, sums, gain, near, far, weights)
    projected = (keep + swap_pair(give)).astype(jnp.bfloat16)
    local_rows = cache_lengths.shape[0]
    gathered = lax.all_to_all(projected, "gx", split_axis=0, concat_axis=0, tiled=True)
    gathered = jnp.swapaxes(gathered, 0, 1)
    queries = gathered[:, :, :query_cols].reshape(local_rows, HEADS, DH)
    keyvals = gathered[:, :, query_cols:].reshape(local_rows, 2 * DH)
    places = cache_lengths.astype(jnp.float32)
    queries = rotate(queries.astype(jnp.float32), places[:, None, None]).astype(jnp.bfloat16)
    new_keys = rotate(keyvals[:, :DH].astype(jnp.float32), places[:, None]).astype(jnp.bfloat16)
    new_values = keyvals[:, DH:].astype(jnp.float32)
    score_scale = 1.0 / math.sqrt(DH)
    scores = (
        jnp.einsum("rhd,rtd->rht", queries, cache_keys, preferred_element_type=jnp.float32)
        * score_scale
    )
    visible = jnp.arange(cache_keys.shape[1])[None, :] < cache_lengths[:, None]
    scores = jnp.where(visible[:, None, :], scores, -1e30)
    own_score = (
        jnp.einsum("rhd,rd->rh", queries, new_keys, preferred_element_type=jnp.float32)
        * score_scale
    )
    highest = jnp.maximum(jnp.max(scores, axis=2), own_score)
    weights = jnp.exp(scores - highest[:, :, None])
    own_weight = jnp.exp(own_score - highest)
    totals = jnp.sum(weights, axis=2) + own_weight
    blended = jnp.einsum(
        "rht,rtd->rhd",
        weights.astype(jnp.bfloat16),
        cache_values,
        preferred_element_type=jnp.float32,
    )
    blended = blended + own_weight[:, :, None] * new_values[:, None, :]
    attended = (blended / totals[:, :, None]).astype(jnp.bfloat16).reshape(local_rows, 2, -1)
    side = owners[n]
    mine = lax.dynamic_index_in_dim(attended, side, axis=1, keepdims=False)
    other = lax.dynamic_index_in_dim(attended, 1 - side, axis=1, keepdims=False)
    other = swap_pair(other)
    first = jnp.where(side == 0, mine, other)
    second = jnp.where(side == 0, other, mine)
    swapped = jnp.concatenate([first, second], axis=0)

    depth = output_weight.shape[0] // 4
    out_weights = [load_rows(output_weight, 0, depth, [projected])]
    left = right = swapped
    near = [swapped]
    for step in range(1, n // 2):
        if step <= 3:
            out_weights.append(load_rows(output_weight, step * depth, depth, [left, right]))
        left, right = ring.step(left, right)
        near += [left, right]
    half = swapped.shape[1] // 2
    far = ring.step(left[:, :half], right[:, half:])
    keep, give = output_project(n, owners, near, far, out_weights)
    out = (keep + swap_pair(give)).astype(jnp.bfloat16)
    return out.reshape(-1, out.shape[-1])


def solution(mesh):
    return jax.shard_map(
        on_device,
        mesh=mesh,
        in_specs=(
            P(("groups", "gx"), "gy"),
            P("gy"),
            P("gx", "gy"),
            P("gx", "gy"),
            P("gy", "gx"),
            P(("groups", "gx", "gy"), None, None),
            P(("groups", "gx", "gy"), None, None),
            P(("groups", "gx", "gy")),
        ),
        out_specs=P(("groups", "gy"), "gx"),
        check_vma=False,
    )
```

```python
import math

import jax
import jax.numpy as jnp
from jax import lax
from jax.experimental import pallas as pl
from jax.experimental.pallas import tpu as pltpu
from jax.sharding import PartitionSpec as P

D = 18432
HEADS = 48
DH = 256


epsilon = 1e-06
contract = (((1,), (1,)), ((), ()))
MIB = 1 << 20
ANY = pl.BlockSpec(memory_space=pl.ANY)
IN_HBM = pl.BlockSpec(memory_space=pltpu.HBM)
IN_VMEM = pl.BlockSpec(memory_space=pltpu.VMEM)
IN_SMEM = pl.BlockSpec(memory_space=pltpu.SMEM)


def rotate(vectors, places):
    half_width = vectors.shape[-1] // 2
    indices = jnp.arange(half_width, dtype=jnp.float32)
    frequency = jnp.exp(-math.log(10000.0) * indices / half_width)
    angles = places * frequency
    cosine = jnp.cos(angles)
    sine = jnp.sin(angles)
    first_half = vectors[..., :half_width]
    second_half = vectors[..., half_width:]
    return jnp.concatenate(
        [first_half * cosine - second_half * sine, second_half * cosine + first_half * sine],
        axis=-1,
    )


def ring_order(n):
    return list(range(0, n, 2)) + list(range(n - 1, 0, -2))


def swap_pair(x):
    return lax.ppermute(x, "gy", [(0, 1), (1, 0)])


class Ring:
    def __init__(self, n):
        self.n = n
        order = ring_order(n)
        self.onward = [(order[p], order[(p + 1) % n]) for p in range(n)]
        self.back = [(order[p], order[(p - 1) % n]) for p in range(n)]
        self.across = [(order[p], order[(p + n // 2) % n]) for p in range(n)]
        self.offsets = [0]
        for step in range(1, n // 2):
            self.offsets += [-step, step]
        self.offsets.append(n // 2)

    def owners(self):
        n = self.n
        me = lax.axis_index("gx")
        place = jnp.where(me % 2 == 0, me // 2, n - 1 - me // 2)
        at = (place + jnp.array(self.offsets, jnp.int32) + n) % n
        owner = jnp.where(at < n // 2, 2 * at, 2 * (n - 1 - at) + 1)
        return jnp.concatenate([owner, lax.axis_index("gy")[None]]).astype(jnp.int32)

    def step(self, left, right):
        return lax.ppermute(left, "gx", self.onward), lax.ppermute(right, "gx", self.back)


def load_kernel(start, *refs):
    source, target, sem = refs[0], refs[-2], refs[-1]
    copy = pltpu.make_async_copy(source.at[pl.ds(start, target.shape[0])], target, sem)
    copy.start()
    copy.wait()


def load(array, start, size, after=()):
    return pl.pallas_call(
        lambda *refs: load_kernel(start, *refs),
        out_shape=pltpu.VMEM((size,) + array.shape[1:], array.dtype),
        in_specs=[IN_HBM] + [ANY] * len(after),
        out_specs=IN_VMEM,
        scratch_shapes=[pltpu.SemaphoreType.DMA],
        compiler_params=pltpu.CompilerParams(vmem_limit_bytes=MIB),
        name="load",
    )(pltpu.with_memory_space_constraint(array, pltpu.HBM), *after)


def in_vmem(array):
    return pltpu.with_memory_space_constraint(array, pltpu.VMEM)


def before(done, *rest):
    held = lax.optimization_barrier((done,) + rest)
    return held[0], held[1:]


def sums_kernel(*refs):
    out = refs[-1]
    rows = refs[0].shape[0]
    lane = lax.broadcasted_iota(jnp.int32, (rows, 128), 1)
    for i, ref in enumerate(refs[:-1]):
        x = ref[...].astype(jnp.float32)
        total = jnp.sum(x, axis=1, keepdims=True)
        square = jnp.sum(x * x, axis=1, keepdims=True)
        both = jnp.where(lane == 0, total, jnp.where(lane == 1, square, 0.0))
        out[i * rows : (i + 1) * rows, :] = both


def row_sums(shards):
    rows = shards[0].shape[0]
    return pl.pallas_call(
        sums_kernel,
        out_shape=jax.ShapeDtypeStruct((len(shards) * rows, 128), jnp.float32),
        in_specs=[IN_VMEM] * len(shards),
        out_specs=IN_VMEM,
        compiler_params=pltpu.CompilerParams(vmem_limit_bytes=16 * MIB),
        name="row_sums",
    )(*shards)


def project_kernel(n, parts, *refs):
    owners, sums_a, sums_b, gain = refs[:4]
    near = refs[4 : 4 + n - 1]
    far = refs[4 + n - 1 : 4 + n + 1]
    weights = refs[4 + n + 1 : 4 + n + 1 + parts]
    keep, give, normed, total = refs[4 + n + 1 + parts :]
    rows = near[0].shape[0]
    half = far[0].shape[1]
    sums = sums_a[...] + sums_b[...]
    row_mean = sums[:, :1] / D
    row_square = sums[:, 1:2] / D
    scale = lax.rsqrt(row_square - row_mean * row_mean + epsilon)
    for part in range(2):
        cols = slice(part * half, (part + 1) * half)
        for i in range(n):
            at = slice(i * rows, (i + 1) * rows)
            x = near[i][:, cols] if i < n - 1 else far[part][...]
            x = (x.astype(jnp.float32) - row_mean[at]) * scale[at] * gain[:, cols]
            normed[at, cols] = x
        x = normed[:, cols].astype(jnp.bfloat16)
        start = 0
        for weight in weights:
            width = weight.shape[0]
            term = lax.dot_general(
                x, weight[:, cols], contract, preferred_element_type=jnp.float32
            )
            if part == 0:
                total[:, start : start + width] = term
            else:
                total[:, start : start + width] += term
            start += width
    side = owners[n]
    local = rows // 2
    for i in range(n):
        block = total[i * rows : (i + 1) * rows, :]
        low, high = block[:local], block[local:]
        keep[owners[i]] = jnp.where(side == 0, low, high)
        give[owners[i]] = jnp.where(side == 0, high, low)


def project(n, owners, sums, gain, near, far, weights):
    rows, width = near[0].shape
    stripe = sum(w.shape[0] for w in weights)
    shape = jax.ShapeDtypeStruct((n, rows // 2, stripe), jnp.float32)
    return pl.pallas_call(
        lambda *refs: project_kernel(n, len(weights), *refs),
        out_shape=[shape, shape],
        in_specs=[IN_SMEM] + [IN_VMEM] * (3 + n + 1 + len(weights)),
        out_specs=[IN_VMEM, IN_VMEM],
        scratch_shapes=[
            pltpu.VMEM((n * rows, width), jnp.float32),
            pltpu.VMEM((n * rows, stripe), jnp.float32),
        ],
        compiler_params=pltpu.CompilerParams(vmem_limit_bytes=(10 if n <= 8 else 48) * MIB),
        name="project",
    )(owners, *sums, gain, *near, *far, *[in_vmem(w) for w in weights])


def output_kernel(n, parts, *refs):
    owners = refs[0]
    near = refs[1:n]
    far = refs[n : n + 2]
    weights = refs[n + 2 : n + 2 + parts]
    keep, give, total, placed = refs[n + 2 + parts :]
    rows = near[0].shape[0]
    half = far[0].shape[1]
    depth = weights[0].shape[0]
    for part, weight in enumerate(weights):
        start = part * depth
        cols = slice(start, start + depth)
        pieces = [ref[:, cols] for ref in near]
        for i, ref in enumerate(far):
            low, high = max(start, i * half), min(start + depth, (i + 1) * half)
            if low < high:
                last = ref[:, low - i * half : high - i * half]
                pieces.append(last)
        if len(pieces) > n:
            pieces[n - 1 :] = [jnp.concatenate(pieces[n - 1 :], axis=1)]
        x = jnp.concatenate([p.astype(jnp.float32) for p in pieces], axis=0)
        term = jnp.dot(
            x.astype(jnp.bfloat16), weight[...], preferred_element_type=jnp.float32
        )
        if part == 0:
            total[...] = term
        else:
            total[...] += term
    for i in range(n):
        placed[owners[i]] = total[i * rows : (i + 1) * rows, :]
    side = owners[n]
    keep[...] = placed[pl.ds(side * (n // 2), n // 2)]
    give[...] = placed[pl.ds((1 - side) * (n // 2), n // 2)]


def output_project(n, owners, near, far, weights):
    rows = near[0].shape[0]
    cols = weights[0].shape[1]
    shape = jax.ShapeDtypeStruct((n // 2, rows, cols), jnp.float32)
    return pl.pallas_call(
        lambda *refs: output_kernel(n, len(weights), *refs),
        out_shape=[shape, shape],
        in_specs=[IN_SMEM] + [IN_VMEM] * (n + 1 + len(weights)),
        out_specs=[IN_VMEM, IN_VMEM],
        scratch_shapes=[
            pltpu.VMEM((n * rows, cols), jnp.float32),
            pltpu.VMEM((n, rows, cols), jnp.float32),
        ],
        compiler_params=pltpu.CompilerParams(vmem_limit_bytes=(10 if n <= 8 else 48) * MIB),
        name="output_project",
    )(owners, *near, *far, *[in_vmem(w) for w in weights])


def on_device(
    activations,
    norm_gain,
    query_weight,
    keyval_weight,
    output_weight,
    cache_keys,
    cache_values,
    cache_lengths,
):
    n = lax.axis_size("gx")
    ring = Ring(n)
    owners = ring.owners()
    query_cols = query_weight.shape[0]
    pieces = 3 if query_cols % (3 * 256) == 0 else 1
    piece = query_cols // pieces
    weights = []

    left = right = activations
    near = [activations]
    own_sums = row_sums([activations])
    far_sums = lax.ppermute(own_sums, "gx", ring.across)
    sums = [own_sums]
    for step in range(1, n // 2):
        after = [] if step == 1 else [left, right]
        left, right = ring.step(left, right)
        near += [left, right]
        if step <= pieces:
            loaded = load(query_weight, (step - 1) * piece, piece, after)
            loaded, (left, right) = before(loaded, left, right)
            weights.append(loaded)
        sums.append(row_sums([left, right]))
    weights.append(load(keyval_weight, 0, keyval_weight.shape[0], [left, right]))
    half = activations.shape[1] // 2
    far = ring.step(left[:, :half], right[:, half:])
    sums = jnp.concatenate(sums + [far_sums], axis=0)
    sums = (sums, swap_pair(sums))
    gain = norm_gain.astype(jnp.float32)[None, :]
    keep, give = project(n, owners, sums, gain, near, far, weights)
    projected = (keep + swap_pair(give)).astype(jnp.bfloat16)
    local_rows = cache_lengths.shape[0]
    depth = output_weight.shape[0] // 4
    out_weights = [load(output_weight, 0, depth, [projected])]
    gathered = lax.all_to_all(projected, "gx", split_axis=0, concat_axis=0, tiled=True)
    out_weights[0], (gathered,) = before(out_weights[0], gathered)
    gathered = jnp.swapaxes(gathered, 0, 1)
    queries = gathered[:, :, :query_cols].reshape(local_rows, HEADS, DH)
    keyvals = gathered[:, :, query_cols:].reshape(local_rows, 2 * DH)
    places = cache_lengths.astype(jnp.float32)
    queries = rotate(queries.astype(jnp.float32), places[:, None, None]).astype(jnp.bfloat16)
    new_keys = rotate(keyvals[:, :DH].astype(jnp.float32), places[:, None]).astype(jnp.bfloat16)
    new_values = keyvals[:, DH:].astype(jnp.float32)
    score_scale = 1.0 / math.sqrt(DH)
    scores = (
        jnp.einsum("rhd,rtd->rht", queries, cache_keys, preferred_element_type=jnp.float32)
        * score_scale
    )
    visible = jnp.arange(cache_keys.shape[1])[None, :] < cache_lengths[:, None]
    scores = jnp.where(visible[:, None, :], scores, -1e30)
    own_score = (
        jnp.einsum("rhd,rd->rh", queries, new_keys, preferred_element_type=jnp.float32)
        * score_scale
    )
    highest = jnp.maximum(jnp.max(scores, axis=2), own_score)
    weights = jnp.exp(scores - highest[:, :, None])
    own_weight = jnp.exp(own_score - highest)
    totals = jnp.sum(weights, axis=2) + own_weight
    blended = jnp.einsum(
        "rht,rtd->rhd",
        weights.astype(jnp.bfloat16),
        cache_values,
        preferred_element_type=jnp.float32,
    )
    blended = blended + own_weight[:, :, None] * new_values[:, None, :]
    attended = (blended / totals[:, :, None]).astype(jnp.bfloat16).reshape(local_rows, 2, -1)
    side = owners[n]
    mine = lax.dynamic_index_in_dim(attended, side, axis=1, keepdims=False)
    other = lax.dynamic_index_in_dim(attended, 1 - side, axis=1, keepdims=False)
    other = swap_pair(other)
    first = jnp.where(side == 0, mine, other)
    second = jnp.where(side == 0, other, mine)
    swapped = jnp.concatenate([first, second], axis=0)

    left = right = swapped
    near = [swapped]
    for step in range(1, n // 2):
        after = [left, right]
        left, right = ring.step(left, right)
        near += [left, right]
        if step <= 3:
            loaded = load(output_weight, step * depth, depth, after)
            loaded, (left, right) = before(loaded, left, right)
            out_weights.append(loaded)
    half = swapped.shape[1] // 2
    far = ring.step(left[:, :half], right[:, half:])
    keep, give = output_project(n, owners, near, far, out_weights)
    out = (keep + swap_pair(give)).astype(jnp.bfloat16)
    return out.reshape(-1, out.shape[-1])


def solution(mesh):
    return jax.shard_map(
        on_device,
        mesh=mesh,
        in_specs=(
            P(("groups", "gx"), "gy"),
            P("gy"),
            P("gx", "gy"),
            P("gx", "gy"),
            P("gy", "gx"),
            P(("groups", "gx", "gy"), None, None),
            P(("groups", "gx", "gy"), None, None),
            P(("groups", "gx", "gy")),
        ),
        out_specs=P(("groups", "gy"), "gx"),
        check_vma=False,
    )
```

```python
import math

import jax
import jax.numpy as jnp
from jax import lax
from jax.experimental import pallas as pl
from jax.experimental.pallas import tpu as pltpu
from jax.sharding import PartitionSpec as P

D = 18432
HEADS = 48
DH = 256


epsilon = 1e-06
contract = (((1,), (1,)), ((), ()))
MIB = 1 << 20
ANY = pl.BlockSpec(memory_space=pl.ANY)
IN_HBM = pl.BlockSpec(memory_space=pltpu.HBM)
IN_VMEM = pl.BlockSpec(memory_space=pltpu.VMEM)
IN_SMEM = pl.BlockSpec(memory_space=pltpu.SMEM)


def rotate(vectors, places):
    half_width = vectors.shape[-1] // 2
    indices = jnp.arange(half_width, dtype=jnp.float32)
    frequency = jnp.exp(-math.log(10000.0) * indices / half_width)
    angles = places * frequency
    cosine = jnp.cos(angles)
    sine = jnp.sin(angles)
    first_half = vectors[..., :half_width]
    second_half = vectors[..., half_width:]
    return jnp.concatenate(
        [first_half * cosine - second_half * sine, second_half * cosine + first_half * sine],
        axis=-1,
    )


def ring_order(n):
    return list(range(0, n, 2)) + list(range(n - 1, 0, -2))


def swap_pair(x):
    return lax.ppermute(x, "gy", [(0, 1), (1, 0)])


class Ring:
    def __init__(self, n):
        self.n = n
        order = ring_order(n)
        self.onward = [(order[p], order[(p + 1) % n]) for p in range(n)]
        self.back = [(order[p], order[(p - 1) % n]) for p in range(n)]
        self.across = [(order[p], order[(p + n // 2) % n]) for p in range(n)]
        self.offsets = [0]
        for step in range(1, n // 2):
            self.offsets += [-step, step]
        self.offsets.append(n // 2)

    def owners(self):
        n = self.n
        me = lax.axis_index("gx")
        place = jnp.where(me % 2 == 0, me // 2, n - 1 - me // 2)
        at = (place + jnp.array(self.offsets, jnp.int32) + n) % n
        owner = jnp.where(at < n // 2, 2 * at, 2 * (n - 1 - at) + 1)
        return jnp.concatenate([owner, lax.axis_index("gy")[None]]).astype(jnp.int32)

    def step(self, left, right):
        return lax.ppermute(left, "gx", self.onward), lax.ppermute(right, "gx", self.back)


def start_copies(source, target, sems, count):
    rows = source.shape[0]
    size = -(-rows // (16 * count)) * 16
    copies = []
    for i, first in enumerate(range(0, rows, size)):
        at = pl.ds(first, min(size, rows - first))
        copy = pltpu.make_async_copy(source.at[at], target.at[at], sems.at[i])
        copy.start()
        copies.append(copy)
    return copies


def load_kernel(jobs, *refs):
    sources, buffer, sems = refs[: len(jobs)], refs[-2], refs[-1]
    copies = []
    for i, (source, (first, size, at)) in enumerate(zip(sources, jobs)):
        part = source.at[pl.ds(first, size)]
        copies += start_copies(part, buffer.at[pl.ds(at, size)], sems.at[i], 4)
    for copy in copies:
        copy.wait()


def load(buffer, jobs, after=()):
    new = isinstance(buffer, tuple)
    shape = buffer if new else buffer.shape
    arrays = [in_hbm(job[0]) for job in jobs]
    held = [] if new else [in_vmem(buffer)]
    return pl.pallas_call(
        lambda *refs: load_kernel([job[1:] for job in jobs], *refs),
        out_shape=pltpu.VMEM(shape, jnp.bfloat16),
        in_specs=[IN_HBM] * len(jobs) + [IN_VMEM] * len(held) + [ANY] * len(after),
        out_specs=IN_VMEM,
        input_output_aliases={} if new else {len(jobs): 0},
        scratch_shapes=[pltpu.SemaphoreType.DMA((len(jobs), 4))],
        compiler_params=pltpu.CompilerParams(vmem_limit_bytes=MIB),
        name="load",
    )(*arrays, *held, *after)


def in_hbm(array):
    return pltpu.with_memory_space_constraint(array, pltpu.HBM)


def in_vmem(array):
    return pltpu.with_memory_space_constraint(array, pltpu.VMEM)


def before(done, *rest):
    held = lax.optimization_barrier((done,) + rest)
    return held[0], held[1:]


def sums_kernel(*refs):
    out = refs[-1]
    rows = refs[0].shape[0]
    lane = lax.broadcasted_iota(jnp.int32, (rows, 128), 1)
    for i, ref in enumerate(refs[:-1]):
        x = ref[...].astype(jnp.float32)
        total = jnp.sum(x, axis=1, keepdims=True)
        square = jnp.sum(x * x, axis=1, keepdims=True)
        both = jnp.where(lane == 0, total, jnp.where(lane == 1, square, 0.0))
        out[i * rows : (i + 1) * rows, :] = both


def row_sums(shards):
    rows = shards[0].shape[0]
    return pl.pallas_call(
        sums_kernel,
        out_shape=jax.ShapeDtypeStruct((len(shards) * rows, 128), jnp.float32),
        in_specs=[IN_VMEM] * len(shards),
        out_specs=IN_VMEM,
        compiler_params=pltpu.CompilerParams(vmem_limit_bytes=16 * MIB),
        name="row_sums",
    )(*shards)


def project_kernel(n, turned, *refs):
    owners, sums_a, sums_b, gain = refs[:4]
    near = refs[4 : 4 + n - 1]
    far = refs[4 + n - 1 : 4 + n + 1]
    early, query_weight, keyval_weight, keep, give = refs[4 + n + 1 : 4 + n + 6]
    normed, late, keyval, total, sems = refs[4 + n + 6 :]
    at = pl.ds(early.shape[0], late.shape[0])
    copies = start_copies(query_weight.at[at], late, sems.at[0], 4)
    copies += start_copies(keyval_weight, keyval, sems.at[1], 1)
    rows = near[0].shape[0]
    half = far[0].shape[1]
    sums = sums_a[...] + sums_b[...]
    row_mean = sums[:, :1] / D
    row_square = sums[:, 1:2] / D
    scale = lax.rsqrt(row_square - row_mean * row_mean + epsilon)
    blocks = []

    def multiply(weight, part, start):
        cols = slice(part * half, (part + 1) * half)
        pair = (weight[:, cols], blocks[part])
        pair = pair if turned else pair[::-1]
        term = lax.dot_general(*pair, contract, preferred_element_type=jnp.float32)
        stripe = slice(start, start + weight.shape[0])
        where = (stripe, slice(None)) if turned else (slice(None), stripe)
        if part == 0:
            total[where] = term
        else:
            total[where] += term

    for part in range(2):
        cols = slice(part * half, (part + 1) * half)
        for i in range(n):
            at = slice(i * rows, (i + 1) * rows)
            x = near[i][:, cols] if i < n - 1 else far[part][...]
            x = (x.astype(jnp.float32) - row_mean[at]) * scale[at] * gain[:, cols]
            normed[at, cols] = x
        blocks.append(normed[:, cols].astype(jnp.bfloat16))
        multiply(early, part, 0)
    for copy in copies:
        copy.wait()
    for part in range(2):
        multiply(late, part, early.shape[0])
        multiply(keyval, part, early.shape[0] + late.shape[0])
    side = owners[n]
    local = rows // 2
    width = 128 if turned else total.shape[1]
    height = total.shape[0] if turned else total.shape[1]
    for start in range(0, height, width):
        size = min(width, height - start)
        cols = slice(start, start + size)
        stripe = total[cols, :].T if turned else total[...]
        for i in range(n):
            block = stripe[i * rows : (i + 1) * rows]
            low, high = block[:local], block[local:]
            keep[owners[i], :, cols] = jnp.where(side == 0, low, high)
            give[owners[i], :, cols] = jnp.where(side == 0, high, low)


def project(n, owners, sums, gain, near, far, early, query_weight, keyval_weight):
    rows, width = near[0].shape
    late = (query_weight.shape[0] - early.shape[0], width)
    stripe = query_weight.shape[0] + keyval_weight.shape[0]
    shape = jax.ShapeDtypeStruct((n, rows // 2, stripe), jnp.float32)
    turned = n <= 8
    sums_shape = (stripe, n * rows) if turned else (n * rows, stripe)
    return pl.pallas_call(
        lambda *refs: project_kernel(n, turned, *refs),
        out_shape=[shape, shape],
        in_specs=[IN_SMEM] + [IN_VMEM] * (3 + n + 2) + [IN_HBM] * 2,
        out_specs=[IN_VMEM] * 2,
        scratch_shapes=[
            pltpu.VMEM((n * rows, width), jnp.float32),
            pltpu.VMEM(late, jnp.bfloat16),
            pltpu.VMEM(keyval_weight.shape, jnp.bfloat16),
            pltpu.VMEM(sums_shape, jnp.float32),
            pltpu.SemaphoreType.DMA((2, 4)),
        ],
        compiler_params=pltpu.CompilerParams(vmem_limit_bytes=(18 if n <= 8 else 44) * MIB),
        name="project",
    )(owners, *sums, gain, *near, *far, in_vmem(early), in_hbm(query_weight), in_hbm(keyval_weight))


def attend_kernel(scalars, queries, new_keys, new_values, cache_keys, cache_values, mine, other, keys, values, sems):
    rows, heads, _ = queries.shape
    side = scalars[rows]
    score_scale = 1.0 / math.sqrt(DH)
    copies = []
    for r in range(rows):
        for i, (source, target) in enumerate([(cache_keys, keys), (cache_values, values)]):
            copies.append(pltpu.make_async_copy(source.at[r], target.at[r], sems.at[i, r]))
            copies[-1].start()
    for r in range(rows):
        q = queries[r]
        copies[2 * r].wait()
        scores = lax.dot_general(q, keys[r], contract, preferred_element_type=jnp.float32)
        scores = scores * score_scale
        place = lax.broadcasted_iota(jnp.int32, scores.shape, 1)
        scores = jnp.where(place < scalars[r], scores, -1e30)
        new_key = new_keys[r : r + 1, :].astype(jnp.float32)
        own_score = jnp.sum(q.astype(jnp.float32) * new_key, axis=1, keepdims=True) * score_scale
        highest = jnp.maximum(jnp.max(scores, axis=1, keepdims=True), own_score)
        weights = jnp.exp(scores - highest)
        own_weight = jnp.exp(own_score - highest)
        totals = jnp.sum(weights, axis=1, keepdims=True) + own_weight
        copies[2 * r + 1].wait()
        blended = jnp.dot(
            weights.astype(jnp.bfloat16), values[r], preferred_element_type=jnp.float32
        )
        blended = (blended + own_weight * new_values[r : r + 1, :]) / totals
        low, high = blended[: heads // 2], blended[heads // 2 :]
        mine[r] = jnp.where(side == 0, low, high).astype(jnp.bfloat16)
        other[r] = jnp.where(side == 0, high, low).astype(jnp.bfloat16)


def attend(scalars, queries, new_keys, new_values, keys, values):
    rows, heads, _ = queries.shape
    shape = jax.ShapeDtypeStruct((rows, heads // 2, DH), jnp.bfloat16)
    return pl.pallas_call(
        attend_kernel,
        out_shape=[shape, shape],
        in_specs=[IN_SMEM] + [IN_VMEM] * 3 + [IN_HBM] * 2,
        out_specs=[IN_VMEM] * 2,
        scratch_shapes=[
            pltpu.VMEM(keys.shape, jnp.bfloat16),
            pltpu.VMEM(values.shape, jnp.bfloat16),
            pltpu.SemaphoreType.DMA((2, rows)),
        ],
        compiler_params=pltpu.CompilerParams(vmem_limit_bytes=14 * MIB),
        name="attend",
    )(scalars, queries, new_keys, new_values, in_hbm(keys), in_hbm(values))


def output_kernel(n, *refs):
    owners = refs[0]
    near = refs[1:n]
    far = refs[n : n + 2]
    early, weight, keep, give, late, total, placed, sems = refs[n + 2 :]
    first = early.shape[0]
    copies = start_copies(weight.at[pl.ds(first, late.shape[0])], late, sems, 4)
    rows = near[0].shape[0]
    half = far[0].shape[1]
    x = [ref[...].astype(jnp.float32) for ref in near]
    x.append(jnp.concatenate([ref[...].astype(jnp.float32) for ref in far], axis=1))
    x = jnp.concatenate(x, axis=0).astype(jnp.bfloat16)
    total[...] = jnp.dot(x[:, :first], early[...], preferred_element_type=jnp.float32)
    for copy in copies:
        copy.wait()
    total[...] += jnp.dot(x[:, first:], late[...], preferred_element_type=jnp.float32)
    for i in range(n):
        placed[owners[i]] = total[i * rows : (i + 1) * rows, :]
    side = owners[n]
    keep[...] = placed[pl.ds(side * (n // 2), n // 2)]
    give[...] = placed[pl.ds((1 - side) * (n // 2), n // 2)]


def output_project(n, owners, near, far, early, weight):
    rows = near[0].shape[0]
    depth, cols = weight.shape
    shape = jax.ShapeDtypeStruct((n // 2, rows, cols), jnp.float32)
    return pl.pallas_call(
        lambda *refs: output_kernel(n, *refs),
        out_shape=[shape, shape],
        in_specs=[IN_SMEM] + [IN_VMEM] * (n + 2) + [IN_HBM],
        out_specs=[IN_VMEM] * 2,
        scratch_shapes=[
            pltpu.VMEM((depth - early.shape[0], cols), jnp.bfloat16),
            pltpu.VMEM((n * rows, cols), jnp.float32),
            pltpu.VMEM((n, rows, cols), jnp.float32),
            pltpu.SemaphoreType.DMA((4,)),
        ],
        compiler_params=pltpu.CompilerParams(vmem_limit_bytes=(18 if n <= 8 else 44) * MIB),
        name="output_project",
    )(owners, *near, *far, in_vmem(early), in_hbm(weight))


def on_device(
    activations,
    norm_gain,
    query_weight,
    keyval_weight,
    output_weight,
    cache_keys,
    cache_values,
    cache_lengths,
):
    n = lax.axis_size("gx")
    ring = Ring(n)
    owners = ring.owners()
    query_cols, width = query_weight.shape
    piece = query_cols // 64 * 16
    weight = (3 * piece, width)

    left = right = activations
    near = [activations]
    own_sums = row_sums([activations])
    far_sums = lax.ppermute(own_sums, "gx", ring.across)
    sums = [own_sums]
    for step in range(1, n // 2):
        after = [] if step == 1 else [left, right]
        left, right = ring.step(left, right)
        near += [left, right]
        if step <= 3:
            start = (step - 1) * piece
            weight = load(weight, [(query_weight, start, piece, start)], after)
            weight, (left, right) = before(weight, left, right)
        sums.append(row_sums([left, right]))
    half = activations.shape[1] // 2
    far = ring.step(left[:, :half], right[:, half:])
    sums = jnp.concatenate(sums + [far_sums], axis=0)
    sums = (sums, swap_pair(sums))
    gain = norm_gain.astype(jnp.float32)[None, :]
    keep, give = project(
        n, owners, sums, gain, near, far, weight, query_weight, keyval_weight
    )
    projected = (keep + swap_pair(give)).astype(jnp.bfloat16)
    local_rows = cache_lengths.shape[0]
    depth, out_cols = output_weight.shape
    early = depth // 48 * 32
    out_weight = load((early, out_cols), [(output_weight, 0, early, 0)], [projected])
    gathered = lax.all_to_all(projected, "gx", split_axis=0, concat_axis=0, tiled=True)
    out_weight, (gathered,) = before(out_weight, gathered)
    gathered = jnp.swapaxes(gathered, 0, 1)
    queries = gathered[:, :, :query_cols].reshape(local_rows, HEADS, DH)
    keyvals = gathered[:, :, query_cols:].reshape(local_rows, 2 * DH)
    places = cache_lengths.astype(jnp.float32)
    queries = rotate(queries.astype(jnp.float32), places[:, None, None]).astype(jnp.bfloat16)
    new_keys = rotate(keyvals[:, :DH].astype(jnp.float32), places[:, None]).astype(jnp.bfloat16)
    new_values = keyvals[:, DH:].astype(jnp.float32)
    side = lax.axis_index("gy")
    scalars = jnp.concatenate([cache_lengths, side[None].astype(jnp.int32)])
    mine, other = attend(
        scalars, queries, new_keys, new_values, cache_keys, cache_values
    )
    mine = mine.reshape(local_rows, -1)
    other = swap_pair(other.reshape(local_rows, -1))
    first = jnp.where(side == 0, mine, other)
    second = jnp.where(side == 0, other, mine)
    swapped = jnp.concatenate([first, second], axis=0)

    left = right = swapped
    near = [swapped]
    for step in range(1, n // 2):
        left, right = ring.step(left, right)
        near += [left, right]
    half = swapped.shape[1] // 2
    far = ring.step(left[:, :half], right[:, half:])
    keep, give = output_project(n, owners, near, far, out_weight, output_weight)
    out = (keep + swap_pair(give)).astype(jnp.bfloat16)
    return out.reshape(-1, out.shape[-1])


def solution(mesh):
    return jax.shard_map(
        on_device,
        mesh=mesh,
        in_specs=(
            P(("groups", "gx"), "gy"),
            P("gy"),
            P("gx", "gy"),
            P("gx", "gy"),
            P("gy", "gx"),
            P(("groups", "gx", "gy"), None, None),
            P(("groups", "gx", "gy"), None, None),
            P(("groups", "gx", "gy")),
        ),
        out_specs=P(("groups", "gy"), "gx"),
        check_vma=False,
    )
```

```python
import math

import jax
import jax.numpy as jnp
from jax import lax
from jax.experimental import pallas as pl
from jax.experimental.pallas import tpu as pltpu
from jax.sharding import PartitionSpec as P

D = 18432
HEADS = 48
DH = 256


epsilon = 1e-06
contract = (((1,), (1,)), ((), ()))
MIB = 1 << 20
ANY = pl.BlockSpec(memory_space=pl.ANY)
IN_HBM = pl.BlockSpec(memory_space=pltpu.HBM)
IN_VMEM = pl.BlockSpec(memory_space=pltpu.VMEM)
IN_SMEM = pl.BlockSpec(memory_space=pltpu.SMEM)


def rotate(vectors, places):
    half_width = vectors.shape[-1] // 2
    indices = jnp.arange(half_width, dtype=jnp.float32)
    frequency = jnp.exp(-math.log(10000.0) * indices / half_width)
    angles = places * frequency
    cosine = jnp.cos(angles)
    sine = jnp.sin(angles)
    first_half = vectors[..., :half_width]
    second_half = vectors[..., half_width:]
    return jnp.concatenate(
        [first_half * cosine - second_half * sine, second_half * cosine + first_half * sine],
        axis=-1,
    )


def ring_order(n):
    return list(range(0, n, 2)) + list(range(n - 1, 0, -2))


def swap_pair(x):
    return lax.ppermute(x, "gy", [(0, 1), (1, 0)])


class Ring:
    def __init__(self, n):
        self.n = n
        order = ring_order(n)
        self.onward = [(order[p], order[(p + 1) % n]) for p in range(n)]
        self.back = [(order[p], order[(p - 1) % n]) for p in range(n)]
        self.across = [(order[p], order[(p + n // 2) % n]) for p in range(n)]
        self.offsets = [0]
        for step in range(1, n // 2):
            self.offsets += [-step, step]
        self.offsets.append(n // 2)

    def owners(self):
        n = self.n
        me = lax.axis_index("gx")
        place = jnp.where(me % 2 == 0, me // 2, n - 1 - me // 2)
        at = (place + jnp.array(self.offsets, jnp.int32) + n) % n
        owner = jnp.where(at < n // 2, 2 * at, 2 * (n - 1 - at) + 1)
        return jnp.concatenate([owner, lax.axis_index("gy")[None]]).astype(jnp.int32)

    def step(self, left, right):
        return lax.ppermute(left, "gx", self.onward), lax.ppermute(right, "gx", self.back)


def start_copies(source, target, sems, count):
    rows = source.shape[0]
    size = -(-rows // (16 * count)) * 16
    copies = []
    for i, first in enumerate(range(0, rows, size)):
        at = pl.ds(first, min(size, rows - first))
        copy = pltpu.make_async_copy(source.at[at], target.at[at], sems.at[i])
        copy.start()
        copies.append(copy)
    return copies


def load_kernel(jobs, *refs):
    sources, targets, sems = refs[: len(jobs)], refs[-1 - len(jobs) : -1], refs[-1]
    copies = []
    for i, (first, size) in enumerate(jobs):
        part = sources[i].at[pl.ds(first, size)]
        if len(part.shape) == 3:
            for row in range(size):
                copies.append(pltpu.make_async_copy(part.at[row], targets[i].at[row], sems.at[i, row]))
                copies[-1].start()
        else:
            copies += start_copies(part, targets[i], sems.at[i], 4)
    for copy in copies:
        copy.wait()


def load(jobs, after=()):
    return pl.pallas_call(
        lambda *refs: load_kernel([job[1:] for job in jobs], *refs),
        out_shape=[pltpu.VMEM((size,) + array.shape[1:], array.dtype) for array, _, size in jobs],
        in_specs=[IN_HBM] * len(jobs) + [ANY] * len(after),
        out_specs=[IN_VMEM] * len(jobs),
        scratch_shapes=[pltpu.SemaphoreType.DMA((len(jobs), 4))],
        compiler_params=pltpu.CompilerParams(vmem_limit_bytes=MIB),
        name="load",
    )(*[in_hbm(job[0]) for job in jobs], *after)


def in_hbm(array):
    return pltpu.with_memory_space_constraint(array, pltpu.HBM)


def in_vmem(array):
    return pltpu.with_memory_space_constraint(array, pltpu.VMEM)


def before(done, *rest):
    held = lax.optimization_barrier((done,) + rest)
    return held[0], held[1:]


def sums_kernel(ready, count, *refs):
    out = refs[-1]
    start = 0
    for ref in refs[:ready]:
        out[start : start + ref.shape[0], :] = ref[...]
        start += ref.shape[0]
    rows = refs[ready].shape[0]
    lane = lax.broadcasted_iota(jnp.int32, (rows, 128), 1)
    for ref in refs[ready : ready + count]:
        x = ref[...].astype(jnp.float32)
        total = jnp.sum(x, axis=1, keepdims=True)
        square = jnp.sum(x * x, axis=1, keepdims=True)
        both = jnp.where(lane == 0, total, jnp.where(lane == 1, square, 0.0))
        out[start : start + rows, :] = both
        start += rows


def row_sums(shards, ready=(), after=()):
    rows = shards[0].shape[0] * len(shards) + sum(r.shape[0] for r in ready)
    return pl.pallas_call(
        lambda *refs: sums_kernel(len(ready), len(shards), *refs),
        out_shape=jax.ShapeDtypeStruct((rows, 128), jnp.float32),
        in_specs=[IN_VMEM] * (len(ready) + len(shards)) + [ANY] * len(after),
        out_specs=IN_VMEM,
        compiler_params=pltpu.CompilerParams(vmem_limit_bytes=8 * MIB),
        name="row_sums",
    )(*ready, *shards, *after)


def project_kernel(n, parts, *refs):
    owners, sums_a, sums_b, gain = refs[:4]
    near = refs[4 : 4 + n - 1]
    far = refs[4 + n - 1 : 4 + n + 1]
    early = refs[4 + n + 1 : 4 + n + 1 + parts]
    query_weight, keyval_weight, keep, give = refs[4 + n + 1 + parts : 4 + n + 5 + parts]
    normed, late, keyval, total, sems = refs[4 + n + 5 + parts :]
    at = pl.ds(sum(w.shape[0] for w in early), late.shape[0])
    copies = start_copies(query_weight.at[at], late, sems.at[0], 4)
    copies += start_copies(keyval_weight, keyval, sems.at[1], 1)
    rows = near[0].shape[0]
    half = far[0].shape[1]
    sums = sums_a[...] + sums_b[...]
    row_mean = sums[:, :1] / D
    row_square = sums[:, 1:2] / D
    scale = lax.rsqrt(row_square - row_mean * row_mean + epsilon)
    blocks = []

    def multiply(weights, part, start):
        cols = slice(part * half, (part + 1) * half)
        for weight in weights:
            term = lax.dot_general(
                blocks[part], weight[:, cols], contract, preferred_element_type=jnp.float32
            )
            stripe = slice(start, start + weight.shape[0])
            if part == 0:
                total[:, stripe] = term
            else:
                total[:, stripe] += term
            start = stripe.stop
        return start

    for part in range(2):
        cols = slice(part * half, (part + 1) * half)
        for i in range(n):
            at = slice(i * rows, (i + 1) * rows)
            x = near[i][:, cols] if i < n - 1 else far[part][...]
            x = (x.astype(jnp.float32) - row_mean[at]) * scale[at] * gain[:, cols]
            normed[at, cols] = x
        blocks.append(normed[:, cols].astype(jnp.bfloat16))
        done = multiply(early, part, 0)
    for copy in copies:
        copy.wait()
    for part in range(2):
        multiply([late, keyval], part, done)
    side = owners[n]
    local = rows // 2
    for i in range(n):
        block = total[i * rows : (i + 1) * rows, :]
        low, high = block[:local], block[local:]
        keep[owners[i]] = jnp.where(side == 0, low, high)
        give[owners[i]] = jnp.where(side == 0, high, low)


def project(n, owners, sums, gain, near, far, early, query_weight, keyval_weight):
    rows, width = near[0].shape
    late = (query_weight.shape[0] - sum(w.shape[0] for w in early), width)
    stripe = query_weight.shape[0] + keyval_weight.shape[0]
    shape = jax.ShapeDtypeStruct((n, rows // 2, stripe), jnp.float32)
    return pl.pallas_call(
        lambda *refs: project_kernel(n, len(early), *refs),
        out_shape=[shape, shape],
        in_specs=[IN_SMEM] + [IN_VMEM] * (3 + n + 1 + len(early)) + [IN_HBM] * 2,
        out_specs=[IN_VMEM] * 2,
        scratch_shapes=[
            pltpu.VMEM((n * rows, width), jnp.float32),
            pltpu.VMEM(late, jnp.bfloat16),
            pltpu.VMEM(keyval_weight.shape, jnp.bfloat16),
            pltpu.VMEM((n * rows, stripe), jnp.float32),
            pltpu.SemaphoreType.DMA((2, 4)),
        ],
        compiler_params=pltpu.CompilerParams(vmem_limit_bytes=(20 if n <= 8 else 44) * MIB),
        name="project",
    )(
        owners,
        *sums,
        gain,
        *near,
        *far,
        *[in_vmem(w) for w in early],
        in_hbm(query_weight),
        in_hbm(keyval_weight),
    )


def attend_kernel(scalars, queries, new_keys, new_values, keys, values, mine, other):
    rows, heads, _ = queries.shape
    side = scalars[rows]
    score_scale = 1.0 / math.sqrt(DH)
    for r in range(rows):
        q = queries[r]
        scores = lax.dot_general(q, keys[r], contract, preferred_element_type=jnp.float32)
        scores = scores * score_scale
        place = lax.broadcasted_iota(jnp.int32, scores.shape, 1)
        scores = jnp.where(place < scalars[r], scores, -1e30)
        new_key = new_keys[r : r + 1, :].astype(jnp.float32)
        own_score = jnp.sum(q.astype(jnp.float32) * new_key, axis=1, keepdims=True) * score_scale
        highest = jnp.maximum(jnp.max(scores, axis=1, keepdims=True), own_score)
        weights = jnp.exp(scores - highest)
        own_weight = jnp.exp(own_score - highest)
        totals = jnp.sum(weights, axis=1, keepdims=True) + own_weight
        blended = jnp.dot(
            weights.astype(jnp.bfloat16), values[r], preferred_element_type=jnp.float32
        )
        blended = (blended + own_weight * new_values[r : r + 1, :]) / totals
        low, high = blended[: heads // 2], blended[heads // 2 :]
        mine[r] = jnp.where(side == 0, low, high).astype(jnp.bfloat16)
        other[r] = jnp.where(side == 0, high, low).astype(jnp.bfloat16)


def attend(scalars, queries, new_keys, new_values, keys, values):
    rows, heads, _ = queries.shape
    shape = jax.ShapeDtypeStruct((rows, heads // 2, DH), jnp.bfloat16)
    return pl.pallas_call(
        attend_kernel,
        out_shape=[shape, shape],
        in_specs=[IN_SMEM] + [IN_VMEM] * 5,
        out_specs=[IN_VMEM] * 2,
        compiler_params=pltpu.CompilerParams(vmem_limit_bytes=6 * MIB),
        name="attend",
    )(scalars, queries, new_keys, new_values, in_vmem(keys), in_vmem(values))


def output_kernel(n, parts, *refs):
    owners = refs[0]
    near = refs[1:n]
    far = refs[n : n + 2]
    early = refs[n + 2 : n + 2 + parts]
    weight, keep, give, late, total, placed, sems = refs[n + 2 + parts :]
    first = sum(w.shape[0] for w in early)
    copies = start_copies(weight.at[pl.ds(first, late.shape[0])], late, sems, 4)
    rows = near[0].shape[0]
    x = [ref[...].astype(jnp.float32) for ref in near]
    x.append(jnp.concatenate([ref[...].astype(jnp.float32) for ref in far], axis=1))
    x = jnp.concatenate(x, axis=0).astype(jnp.bfloat16)
    start = 0
    for ref in early:
        stop = start + ref.shape[0]
        term = jnp.dot(x[:, start:stop], ref[...], preferred_element_type=jnp.float32)
        if start == 0:
            total[...] = term
        else:
            total[...] += term
        start = stop
    for copy in copies:
        copy.wait()
    total[...] += jnp.dot(x[:, first:], late[...], preferred_element_type=jnp.float32)
    for i in range(n):
        placed[owners[i]] = total[i * rows : (i + 1) * rows, :]
    side = owners[n]
    keep[...] = placed[pl.ds(side * (n // 2), n // 2)]
    give[...] = placed[pl.ds((1 - side) * (n // 2), n // 2)]


def output_project(n, owners, near, far, early, weight):
    rows = near[0].shape[0]
    depth, cols = weight.shape
    late = (depth - sum(w.shape[0] for w in early), cols)
    shape = jax.ShapeDtypeStruct((n // 2, rows, cols), jnp.float32)
    return pl.pallas_call(
        lambda *refs: output_kernel(n, len(early), *refs),
        out_shape=[shape, shape],
        in_specs=[IN_SMEM] + [IN_VMEM] * (n + 1 + len(early)) + [IN_HBM],
        out_specs=[IN_VMEM] * 2,
        scratch_shapes=[
            pltpu.VMEM(late, jnp.bfloat16),
            pltpu.VMEM((n * rows, cols), jnp.float32),
            pltpu.VMEM((n, rows, cols), jnp.float32),
            pltpu.SemaphoreType.DMA((4,)),
        ],
        compiler_params=pltpu.CompilerParams(vmem_limit_bytes=(18 if n <= 8 else 44) * MIB),
        name="output_project",
    )(owners, *near, *far, *[in_vmem(w) for w in early], in_hbm(weight))


def on_device(
    activations,
    norm_gain,
    query_weight,
    keyval_weight,
    output_weight,
    cache_keys,
    cache_values,
    cache_lengths,
):
    n = lax.axis_size("gx")
    ring = Ring(n)
    owners = ring.owners()
    query_cols = query_weight.shape[0]
    unit = query_cols // 96 * 16
    early = []

    left = right = activations
    near = [activations]
    for step in range(1, n // 2):
        after = near[1:][-2:]
        arrived = near[-2:] if step > 1 else None
        left, right = ring.step(left, right)
        near += [left, right]
        if step == 2:
            sums = row_sums([activations, *arrived])
            far_sums = lax.ppermute(sums[: activations.shape[0]], "gx", ring.across)
        elif step > 2:
            sums = row_sums(arrived, [sums])
        if step <= 3:
            first, size = [(0, 2), (2, 1), (3, 1)][step - 1]
            loaded = load([(query_weight, first * unit, size * unit)], after)
            loaded, (left, right) = before(loaded[0], left, right)
            near[-2:] = [left, right]
            early.append(loaded)
    half = activations.shape[1] // 2
    cut, (cut_right, left, right) = before(left[:, :half], right[:, half:], left, right)
    far = ring.step(cut, cut_right)
    sums = row_sums([left, right], [sums])
    sums = jnp.concatenate([sums, far_sums], axis=0)
    sums = (sums, swap_pair(sums))
    gain = norm_gain.astype(jnp.float32)[None, :]
    keep, give = project(
        n, owners, sums, gain, near, far, early, query_weight, keyval_weight
    )
    projected = (keep + swap_pair(give)).astype(jnp.bfloat16)
    local_rows = cache_lengths.shape[0]
    unit = output_weight.shape[0] // 96 * 16
    keys, values, loaded = load(
        [
            (cache_keys, 0, local_rows),
            (cache_values, 0, local_rows),
            (output_weight, 0, unit),
        ],
        [projected],
    )
    early = [loaded]
    gathered = lax.all_to_all(projected, "gx", split_axis=0, concat_axis=0, tiled=True)
    keys, (gathered,) = before(keys, gathered)
    gathered = jnp.swapaxes(gathered, 0, 1)
    queries = gathered[:, :, :query_cols].reshape(local_rows, HEADS, DH)
    keyvals = gathered[:, :, query_cols:].reshape(local_rows, 2 * DH)
    places = cache_lengths.astype(jnp.float32)
    queries = rotate(queries.astype(jnp.float32), places[:, None, None]).astype(jnp.bfloat16)
    new_keys = rotate(keyvals[:, :DH].astype(jnp.float32), places[:, None]).astype(jnp.bfloat16)
    new_values = keyvals[:, DH:].astype(jnp.float32)
    side = lax.axis_index("gy")
    scalars = jnp.concatenate([cache_lengths, side[None].astype(jnp.int32)])
    mine, other = attend(
        scalars, queries, new_keys, new_values, keys, values
    )
    mine = mine.reshape(local_rows, -1)
    other = swap_pair(other.reshape(local_rows, -1))
    first = jnp.where(side == 0, mine, other)
    second = jnp.where(side == 0, other, mine)
    swapped = jnp.concatenate([first, second], axis=0)

    left = right = swapped
    near = [swapped]
    for step in range(1, n // 2):
        after = near[-2:]
        left, right = ring.step(left, right)
        near += [left, right]
        if step <= 3:
            loaded = load([(output_weight, step * unit, unit)], after)
            loaded, (left, right) = before(loaded[0], left, right)
            near[-2:] = [left, right]
            early.append(loaded)
    half = swapped.shape[1] // 2
    far = ring.step(left[:, :half], right[:, half:])
    keep, give = output_project(n, owners, near, far, early, output_weight)
    out = (keep + swap_pair(give)).astype(jnp.bfloat16)
    return out.reshape(-1, out.shape[-1])


def solution(mesh):
    return jax.shard_map(
        on_device,
        mesh=mesh,
        in_specs=(
            P(("groups", "gx"), "gy"),
            P("gy"),
            P("gx", "gy"),
            P("gx", "gy"),
            P("gy", "gx"),
            P(("groups", "gx", "gy"), None, None),
            P(("groups", "gx", "gy"), None, None),
            P(("groups", "gx", "gy")),
        ),
        out_specs=P(("groups", "gy"), "gx"),
        check_vma=False,
    )
```

```python
import math

import jax
import jax.numpy as jnp
from jax import lax
from jax.experimental import pallas as pl
from jax.experimental.pallas import tpu as pltpu
from jax.sharding import PartitionSpec as P

D = 18432
HEADS = 48
DH = 256


epsilon = 1e-06
contract = (((1,), (1,)), ((), ()))
MIB = 1 << 20
ANY = pl.BlockSpec(memory_space=pl.ANY)
IN_HBM = pl.BlockSpec(memory_space=pltpu.HBM)
IN_VMEM = pl.BlockSpec(memory_space=pltpu.VMEM)
IN_SMEM = pl.BlockSpec(memory_space=pltpu.SMEM)


def rotate(vectors, places):
    half_width = vectors.shape[-1] // 2
    indices = jnp.arange(half_width, dtype=jnp.float32)
    frequency = jnp.exp(-math.log(10000.0) * indices / half_width)
    angles = places * frequency
    cosine = jnp.cos(angles)
    sine = jnp.sin(angles)
    first_half = vectors[..., :half_width]
    second_half = vectors[..., half_width:]
    return jnp.concatenate(
        [first_half * cosine - second_half * sine, second_half * cosine + first_half * sine],
        axis=-1,
    )


def ring_order(n):
    return list(range(0, n, 2)) + list(range(n - 1, 0, -2))


def swap_pair(x):
    return lax.ppermute(x, "gy", [(0, 1), (1, 0)])


class Ring:
    def __init__(self, n):
        order = ring_order(n)
        self.onward = [(order[p], order[(p + 1) % n]) for p in range(n)]
        self.back = [(order[p], order[(p - 1) % n]) for p in range(n)]
        self.across = [(order[p], order[(p + n // 2) % n]) for p in range(n)]

    def step(self, left, right):
        return lax.ppermute(left, "gx", self.onward), lax.ppermute(right, "gx", self.back)


def owners(n):
    offsets = [0]
    for step in range(1, n // 2):
        offsets += [-step, step]
    offsets.append(n // 2)
    me = lax.axis_index("gx")
    half = lax.div(me, 2)
    place = jnp.where(lax.rem(me, 2) == 0, half, n - 1 - half)
    result = []
    for offset in offsets:
        at = lax.rem(place + (offset + n), n)
        result.append(jnp.where(at < n // 2, 2 * at, 2 * (n - 1 - at) + 1))
    return result


def start_copies(source, target, sems, count):
    rows = source.shape[0]
    size = -(-rows // (16 * count)) * 16
    copies = []
    for i, first in enumerate(range(0, rows, size)):
        at = pl.ds(first, min(size, rows - first))
        copy = pltpu.make_async_copy(source.at[at], target.at[at], sems.at[i])
        copy.start()
        copies.append(copy)
    return copies


def load_kernel(jobs, *refs):
    sources, target, sems = refs[: len(jobs)], refs[-2], refs[-1]
    copies = []
    for i, (first, size, at) in enumerate(jobs):
        if at is None:
            at = target.shape[0] - 2 * size
            odd = lax.rem(lax.axis_index("gx"), 2)
            unused = pl.ds(pl.multiple_of(at + (1 - odd) * size, size), size)
            at = pl.multiple_of(at + odd * size, size)
            target[unused, :] = jnp.zeros((size, target.shape[1]), target.dtype)
        part = sources[i].at[pl.ds(first, size)]
        copies += start_copies(part, target.at[pl.ds(at, size)], sems.at[i], 4)
    for copy in copies:
        copy.wait()


def load(rows, jobs, after=()):
    array = jobs[0][0]
    return pl.pallas_call(
        lambda *refs: load_kernel([job[1:] for job in jobs], *refs),
        out_shape=pltpu.VMEM((rows, array.shape[1]), array.dtype),
        in_specs=[IN_HBM] * len(jobs) + [ANY] * len(after),
        out_specs=IN_VMEM,
        scratch_shapes=[pltpu.SemaphoreType.DMA((len(jobs), 4))],
        compiler_params=pltpu.CompilerParams(vmem_limit_bytes=MIB),
        name="load",
    )(*[in_hbm(job[0]) for job in jobs], *after)


def load_caches_kernel(*refs):
    sources, targets, sems = refs[:2], refs[-3:-1], refs[-1]
    copies = []
    for i, (source, target) in enumerate(zip(sources, targets)):
        for row in range(source.shape[0]):
            copies.append(pltpu.make_async_copy(source.at[row], target.at[row], sems.at[i, row]))
            copies[-1].start()
    for copy in copies:
        copy.wait()


def load_caches(keys, values, after):
    return pl.pallas_call(
        load_caches_kernel,
        out_shape=[pltpu.VMEM(a.shape, a.dtype) for a in (keys, values)],
        in_specs=[IN_HBM] * 2 + [ANY] * len(after),
        out_specs=[IN_VMEM] * 2,
        scratch_shapes=[pltpu.SemaphoreType.DMA((2, keys.shape[0]))],
        compiler_params=pltpu.CompilerParams(vmem_limit_bytes=MIB),
        name="load_caches",
    )(in_hbm(keys), in_hbm(values), *after)


def in_hbm(array):
    return pltpu.with_memory_space_constraint(array, pltpu.HBM)


def in_vmem(array):
    return pltpu.with_memory_space_constraint(array, pltpu.VMEM)


def before(done, *rest):
    held = lax.optimization_barrier((done,) + rest)
    return held[0], held[1:]


def sums_kernel(ready, count, *refs):
    out = refs[-1]
    start = 0
    for ref in refs[:ready]:
        out[start : start + ref.shape[0], :] = ref[...]
        start += ref.shape[0]
    rows = refs[ready].shape[0]
    lane = lax.broadcasted_iota(jnp.int32, (rows, 128), 1)
    for ref in refs[ready : ready + count]:
        x = ref[...].astype(jnp.float32)
        total = jnp.sum(x, axis=1, keepdims=True)
        square = jnp.sum(x * x, axis=1, keepdims=True)
        both = jnp.where(lane == 0, total, jnp.where(lane == 1, square, 0.0))
        out[start : start + rows, :] = both
        start += rows


def row_sums(shards, ready=(), after=()):
    rows = shards[0].shape[0] * len(shards) + sum(r.shape[0] for r in ready)
    return pl.pallas_call(
        lambda *refs: sums_kernel(len(ready), len(shards), *refs),
        out_shape=jax.ShapeDtypeStruct((rows, 128), jnp.float32),
        in_specs=[IN_VMEM] * (len(ready) + len(shards)) + [ANY] * len(after),
        out_specs=IN_VMEM,
        compiler_params=pltpu.CompilerParams(vmem_limit_bytes=8 * MIB),
        name="row_sums",
    )(*ready, *shards, *after)


def project_kernel(n, *refs):
    sums_a, sums_b, gain = refs[:3]
    near = refs[3 : 3 + n - 1]
    far = refs[3 + n - 1 : 3 + n + 1]
    weights = refs[3 + n + 1 : -4]
    keep, give, normed, total = refs[-4:]
    rows = near[0].shape[0]
    half = far[0].shape[1]
    sums = sums_a[...] + sums_b[...]
    row_mean = sums[:, :1] / D
    row_square = sums[:, 1:2] / D
    scale = lax.rsqrt(row_square - row_mean * row_mean + epsilon)
    for part in range(2):
        cols = slice(part * half, (part + 1) * half)
        for i in range(n):
            at = slice(i * rows, (i + 1) * rows)
            x = near[i][:, cols] if i < n - 1 else far[part][...]
            x = (x.astype(jnp.float32) - row_mean[at]) * scale[at] * gain[:, cols]
            normed[at, cols] = x
        x = normed[:, cols].astype(jnp.bfloat16)
        start = 0
        for weight in weights:
            term = lax.dot_general(
                x, weight[:, cols], contract, preferred_element_type=jnp.float32
            )
            stripe = slice(start, start + weight.shape[0])
            if part == 0:
                total[:, stripe] = term
            else:
                total[:, stripe] += term
            start = stripe.stop
    side = lax.axis_index("gy")
    local = rows // 2
    for i, owner in enumerate(owners(n)):
        block = total[i * rows : (i + 1) * rows, :]
        low, high = block[:local], block[local:]
        keep[owner] = jnp.where(side == 0, low, high)
        give[owner] = jnp.where(side == 0, high, low)


def project(n, sums, gain, near, far, weights):
    rows, width = near[0].shape
    stripe = sum(w.shape[0] for w in weights)
    shape = jax.ShapeDtypeStruct((n, rows // 2, stripe), jnp.float32)
    return pl.pallas_call(
        lambda *refs: project_kernel(n, *refs),
        out_shape=[shape, shape],
        in_specs=[IN_VMEM] * (3 + n + 1 + len(weights)),
        out_specs=[IN_VMEM] * 2,
        scratch_shapes=[
            pltpu.VMEM((n * rows, width), jnp.float32),
            pltpu.VMEM((n * rows, stripe), jnp.float32),
        ],
        compiler_params=pltpu.CompilerParams(vmem_limit_bytes=8 * MIB),
        name="project",
    )(*sums, gain, *near, *far, *[in_vmem(w) for w in weights])


def attend_kernel(lengths, arrived, cosine, sine, keys, values, mine, other, spread, held):
    n, rows, stripe = arrived.shape
    query_cols = stripe - 128
    side = lax.axis_index("gy")
    score_scale = 1.0 / math.sqrt(DH)
    for i in range(n):
        block = arrived[i].astype(jnp.float32)
        for r in range(rows):
            spread[r, i : i + 1, :] = block[r : r + 1, :]
    for r in range(rows):
        given = spread[r]
        cos, sin = cosine[r : r + 1, :], sine[r : r + 1, :]

        def turn(a, b):
            turned = jnp.concatenate([a * cos - b * sin, b * cos + a * sin], axis=1)
            return turned.astype(jnp.bfloat16)

        starts = range(0, query_cols, DH)
        q = turn(
            jnp.concatenate([given[:, c : c + DH // 2] for c in starts], axis=0),
            jnp.concatenate([given[:, c + DH // 2 : c + DH] for c in starts], axis=0),
        )
        new = [
            given[i : i + 1, query_cols:] + given[i + 1 : i + 2, query_cols:]
            for i in range(0, n, 2)
        ]
        new_key = turn(new[0], new[1]).astype(jnp.float32)
        new_value = jnp.concatenate(new[2:], axis=1)
        scores = lax.dot_general(q, keys[r], contract, preferred_element_type=jnp.float32)
        scores = scores * score_scale
        place = lax.broadcasted_iota(jnp.int32, scores.shape, 1)
        scores = jnp.where(place < lengths[r], scores, -1e30)
        own_score = jnp.sum(q.astype(jnp.float32) * new_key, axis=1, keepdims=True) * score_scale
        highest = jnp.maximum(jnp.max(scores, axis=1, keepdims=True), own_score)
        weights = jnp.exp(scores - highest)
        own_weight = jnp.exp(own_score - highest)
        totals = jnp.sum(weights, axis=1, keepdims=True) + own_weight
        blended = jnp.dot(
            weights.astype(jnp.bfloat16), values[r], preferred_element_type=jnp.float32
        )
        blended = (blended + own_weight * new_value) / totals
        for j in range(len(starts)):
            block = blended[j * n : (j + 1) * n]
            swapped = pltpu.roll(block, n // 2, 0)
            parts = [jnp.where(side == 0, block, swapped), jnp.where(side == 0, swapped, block)]
            for i in range(n // 2):
                at = (i * len(starts) + j) * DH
                for k, part in enumerate(parts):
                    held[k, r : r + 1, at : at + DH] = part[i : i + 1]
    mine[...] = held[0].astype(jnp.bfloat16)
    other[...] = held[1].astype(jnp.bfloat16)


def attend(lengths, arrived, cosine, sine, keys, values):
    n, rows, stripe = arrived.shape
    shape = jax.ShapeDtypeStruct((rows, HEADS * DH // 2), jnp.bfloat16)
    return pl.pallas_call(
        attend_kernel,
        out_shape=[shape, shape],
        in_specs=[IN_SMEM] + [IN_VMEM] * 5,
        out_specs=[IN_VMEM] * 2,
        scratch_shapes=[
            pltpu.VMEM((rows, n, stripe), jnp.float32),
            pltpu.VMEM((2, rows, HEADS * DH // 2), jnp.float32),
        ],
        compiler_params=pltpu.CompilerParams(vmem_limit_bytes=8 * MIB),
        name="attend",
    )(lengths, arrived, cosine, sine, in_vmem(keys), in_vmem(values))


def output_kernel(n, *refs):
    near = refs[: n - 1]
    far = refs[n - 1 : n + 1]
    weights = refs[n + 1 : -4]
    keep, give, total, placed = refs[-4:]
    rows = near[0].shape[0]
    half = far[0].shape[1]
    depth = weights[0].shape[0]
    for part, weight in enumerate(weights):
        start = part * depth
        cols = slice(start, start + depth)
        last = slice(start % half, start % half + depth)
        x = [ref[:, cols] for ref in near] + [far[start // half][:, last]]
        x = jnp.concatenate([piece.astype(jnp.float32) for piece in x], axis=0)
        term = jnp.dot(x.astype(jnp.bfloat16), weight[...], preferred_element_type=jnp.float32)
        if part == 0:
            total[...] = term
        else:
            total[...] += term
    side = lax.axis_index("gy")
    for i, owner in enumerate(owners(n)):
        block = total[i * rows : (i + 1) * rows, :]
        placed[owner] = jnp.where(side == 0, block, pltpu.roll(block, rows // 2, 0))
    keep[...] = placed[pl.ds(side * (n // 2), n // 2)]
    give[...] = placed[pl.ds((1 - side) * (n // 2), n // 2)]


def output_project(n, near, far, weights):
    rows = near[0].shape[0]
    cols = weights[0].shape[1]
    shape = jax.ShapeDtypeStruct((n // 2, rows, cols), jnp.float32)
    return pl.pallas_call(
        lambda *refs: output_kernel(n, *refs),
        out_shape=[shape, shape],
        in_specs=[IN_VMEM] * (n + 1 + len(weights)),
        out_specs=[IN_VMEM] * 2,
        scratch_shapes=[
            pltpu.VMEM((n * rows, cols), jnp.float32),
            pltpu.VMEM((n, rows, cols), jnp.float32),
        ],
        compiler_params=pltpu.CompilerParams(vmem_limit_bytes=8 * MIB),
        name="output_project",
    )(*near, *far, *[in_vmem(w) for w in weights])


def on_any_grid(
    activations,
    norm_gain,
    query_weight,
    keyval_weight,
    output_weight,
    cache_keys,
    cache_values,
    cache_lengths,
):
    inputs = activations.astype(jnp.float32)
    row_sums, square_sums = lax.psum(
        (jnp.sum(inputs, axis=1), jnp.sum(inputs * inputs, axis=1)), "gy"
    )
    row_mean = row_sums[:, None] / D
    row_square = square_sums[:, None] / D
    variance = row_square - row_mean * row_mean
    normed = (
        (inputs - row_mean) * lax.rsqrt(variance + epsilon) * norm_gain.astype(jnp.float32)
    ).astype(jnp.bfloat16)
    shard_rows = lax.all_gather(normed, "gx", axis=0, tiled=True)
    query_part = lax.dot_general(
        shard_rows, query_weight, contract, preferred_element_type=jnp.float32
    )
    keyval_part = lax.dot_general(
        shard_rows, keyval_weight, contract, preferred_element_type=jnp.float32
    )
    partial_sums = jnp.concatenate([query_part, keyval_part], axis=1)
    wide_count = lax.axis_size("gx")
    pair_count = lax.axis_size("gy")
    local_rows = cache_lengths.shape[0]
    stripe = partial_sums.shape[1]
    arrived = lax.all_to_all(partial_sums, ("gx", "gy"), split_axis=0, concat_axis=1, tiled=True)
    gathered = jnp.sum(arrived.reshape(local_rows, wide_count, pair_count, stripe), axis=2).astype(
        jnp.bfloat16
    )
    query_cols = query_weight.shape[0]
    queries = gathered[:, :, :query_cols].reshape(local_rows, HEADS, DH)
    keyvals = gathered[:, :, query_cols:].reshape(local_rows, 2 * DH)
    places = cache_lengths.astype(jnp.float32)
    queries = rotate(queries.astype(jnp.float32), places[:, None, None]).astype(jnp.bfloat16)
    new_keys = rotate(keyvals[:, :DH].astype(jnp.float32), places[:, None]).astype(jnp.bfloat16)
    new_values = keyvals[:, DH:].astype(jnp.float32)
    score_scale = 1.0 / math.sqrt(DH)
    scores = (
        jnp.einsum("rhd,rtd->rht", queries, cache_keys, preferred_element_type=jnp.float32)
        * score_scale
    )
    visible = jnp.arange(cache_keys.shape[1])[None, :] < cache_lengths[:, None]
    scores = jnp.where(visible[:, None, :], scores, -1e30)
    own_score = (
        jnp.einsum("rhd,rd->rh", queries, new_keys, preferred_element_type=jnp.float32)
        * score_scale
    )
    highest = jnp.maximum(jnp.max(scores, axis=2), own_score)
    weights = jnp.exp(scores - highest[:, :, None])
    own_weight = jnp.exp(own_score - highest)
    totals = jnp.sum(weights, axis=2) + own_weight
    blended = jnp.einsum(
        "rht,rtd->rhd",
        weights.astype(jnp.bfloat16),
        cache_values,
        preferred_element_type=jnp.float32,
    )
    blended = blended + own_weight[:, :, None] * new_values[:, None, :]
    attended = (blended / totals[:, :, None]).astype(jnp.bfloat16).reshape(local_rows, HEADS * DH)
    swapped = lax.all_to_all(attended, "gy", split_axis=1, concat_axis=0, tiled=True)
    partial_out = jnp.dot(
        lax.all_gather(swapped, "gx", axis=0, tiled=True),
        output_weight,
        preferred_element_type=jnp.float32,
    )
    return lax.psum_scatter(partial_out, "gy", scatter_dimension=0, tiled=True).astype(jnp.bfloat16)


def on_device(
    activations,
    norm_gain,
    query_weight,
    keyval_weight,
    output_weight,
    cache_keys,
    cache_values,
    cache_lengths,
):
    n = lax.axis_size("gx")
    ring = Ring(n)
    query_cols, width = query_weight.shape
    new_cols = keyval_weight.shape[0]
    piece = query_cols // 4
    weights = []

    indices = jnp.arange(DH // 2, dtype=jnp.float32)
    frequency = jnp.exp(-math.log(10000.0) * indices / (DH // 2))
    angles = cache_lengths.astype(jnp.float32)[:, None] * frequency
    cosine, sine = jnp.cos(angles), jnp.sin(angles)

    left = right = activations
    near = [activations]
    for step in range(1, n // 2):
        arrived = near[1:][-2:]
        left, right = ring.step(left, right)
        if step == 2:
            sums = row_sums([activations, *arrived])
            far_sums = lax.ppermute(sums[: activations.shape[0]], "gx", ring.across)
        elif step > 2:
            sums = row_sums(arrived, [sums])
        start = (step - 1) * piece
        weight = load(piece, [(query_weight, start, piece, 0)], arrived)
        weight, (left, right) = before(weight, left, right)
        weights.append(weight)
        near += [left, right]
    half = width // 2
    far = ring.step(left[:, :half], right[:, half:])
    sums = row_sums([left, right], [sums])
    jobs = [(query_weight, 3 * piece, piece, 0), (keyval_weight, 0, new_cols, None)]
    weight = load(piece + 2 * new_cols, jobs, [sums])
    sums = jnp.concatenate([sums, far_sums], axis=0)
    other_sums = swap_pair(sums)
    weight, (other_sums, *far) = before(weight, other_sums, *far)
    weights.append(weight)
    sums = (sums, other_sums)
    gain = norm_gain.astype(jnp.float32)[None, :]
    keep, give = project(n, sums, gain, near, far, weights)
    projected = (keep + swap_pair(give)).astype(jnp.bfloat16)

    piece = output_weight.shape[0] // 4
    arrived = lax.all_to_all(projected, "gx", split_axis=0, concat_axis=0, tiled=True)
    keys, values = load_caches(cache_keys, cache_values, [projected])
    weight = load(piece, [(output_weight, 0, piece, 0)], [projected])
    weight, (arrived,) = before(weight, arrived)
    weights = [weight]
    mine, other = attend(cache_lengths, arrived, cosine, sine, keys, values)
    shard = jnp.concatenate([mine, swap_pair(other)], axis=0)

    left = right = shard
    near = [shard]
    for step in range(1, n // 2):
        arrived = near[-2:]
        left, right = ring.step(left, right)
        start = step * piece
        weight = load(piece, [(output_weight, start, piece, 0)], arrived)
        weight, (left, right) = before(weight, left, right)
        weights.append(weight)
        near += [left, right]
    half = shard.shape[1] // 2
    far = ring.step(left[:, :half], right[:, half:])
    keep, give = output_project(n, near, far, weights)
    out = (keep + swap_pair(give)).astype(jnp.bfloat16)
    return out.reshape(-1, out.shape[-1])


def solution(mesh):
    return jax.shard_map(
        on_device if mesh.shape["gx"] == 8 else on_any_grid,
        mesh=mesh,
        in_specs=(
            P(("groups", "gx"), "gy"),
            P("gy"),
            P("gx", "gy"),
            P("gx", "gy"),
            P("gy", "gx"),
            P(("groups", "gx", "gy"), None, None),
            P(("groups", "gx", "gy"), None, None),
            P(("groups", "gx", "gy")),
        ),
        out_specs=P(("groups", "gy"), "gx"),
        check_vma=False,
    )
```

```python
import math

import jax
import jax.numpy as jnp
from jax import lax
from jax.experimental import pallas as pl
from jax.experimental.pallas import tpu as pltpu
from jax.sharding import PartitionSpec as P

D = 18432
HEADS = 48
DH = 256


epsilon = 1e-06
contract = (((1,), (1,)), ((), ()))
MIB = 1 << 20
ANY = pl.BlockSpec(memory_space=pl.ANY)
IN_HBM = pl.BlockSpec(memory_space=pltpu.HBM)
IN_VMEM = pl.BlockSpec(memory_space=pltpu.VMEM)
IN_SMEM = pl.BlockSpec(memory_space=pltpu.SMEM)


def rotate(vectors, places):
    half_width = vectors.shape[-1] // 2
    indices = jnp.arange(half_width, dtype=jnp.float32)
    frequency = jnp.exp(-math.log(10000.0) * indices / half_width)
    angles = places * frequency
    cosine = jnp.cos(angles)
    sine = jnp.sin(angles)
    first_half = vectors[..., :half_width]
    second_half = vectors[..., half_width:]
    return jnp.concatenate(
        [first_half * cosine - second_half * sine, second_half * cosine + first_half * sine],
        axis=-1,
    )


def ring_order(n):
    return list(range(0, n, 2)) + list(range(n - 1, 0, -2))


def swap_pair(x):
    return lax.ppermute(x, "gy", [(0, 1), (1, 0)])


class Ring:
    def __init__(self, n):
        order = ring_order(n)
        self.onward = [(order[p], order[(p + 1) % n]) for p in range(n)]
        self.back = [(order[p], order[(p - 1) % n]) for p in range(n)]
        self.across = [(order[p], order[(p + n // 2) % n]) for p in range(n)]

    def step(self, left, right):
        return lax.ppermute(left, "gx", self.onward), lax.ppermute(right, "gx", self.back)


def owners(n):
    offsets = [0]
    for step in range(1, n // 2):
        offsets += [-step, step]
    offsets.append(n // 2)
    me = lax.axis_index("gx")
    half = lax.div(me, 2)
    place = jnp.where(lax.rem(me, 2) == 0, half, n - 1 - half)
    result = []
    for offset in offsets:
        at = lax.rem(place + (offset + n), n)
        result.append(jnp.where(at < n // 2, 2 * at, 2 * (n - 1 - at) + 1))
    return result


def start_copies(source, target, sems, count):
    rows = source.shape[0]
    size = -(-rows // (16 * count)) * 16
    copies = []
    for i, first in enumerate(range(0, rows, size)):
        at = pl.ds(first, min(size, rows - first))
        copy = pltpu.make_async_copy(source.at[at], target.at[at], sems.at[i])
        copy.start()
        copies.append(copy)
    return copies


def load_kernel(jobs, *refs):
    sources, target, sems = refs[: len(jobs)], refs[-2], refs[-1]
    copies = []
    for i, (first, size, at) in enumerate(jobs):
        if at is None:
            at = target.shape[0] - 2 * size
            odd = lax.rem(lax.axis_index("gx"), 2)
            unused = pl.ds(pl.multiple_of(at + (1 - odd) * size, size), size)
            at = pl.multiple_of(at + odd * size, size)
            target[unused, :] = jnp.zeros((size, target.shape[1]), target.dtype)
        part = sources[i].at[pl.ds(first, size)]
        copies += start_copies(part, target.at[pl.ds(at, size)], sems.at[i], 4)
    for copy in copies:
        copy.wait()


def load(rows, jobs, after=()):
    array = jobs[0][0]
    return pl.pallas_call(
        lambda *refs: load_kernel([job[1:] for job in jobs], *refs),
        out_shape=pltpu.VMEM((rows, array.shape[1]), array.dtype),
        in_specs=[IN_HBM] * len(jobs) + [ANY] * len(after),
        out_specs=IN_VMEM,
        scratch_shapes=[pltpu.SemaphoreType.DMA((len(jobs), 4))],
        compiler_params=pltpu.CompilerParams(vmem_limit_bytes=MIB),
        name="load",
    )(*[in_hbm(job[0]) for job in jobs], *after)


def load_caches_kernel(*refs):
    sources, targets, sems = refs[:2], refs[-3:-1], refs[-1]
    copies = []
    for i, (source, target) in enumerate(zip(sources, targets)):
        for row in range(source.shape[0]):
            copies.append(pltpu.make_async_copy(source.at[row], target.at[row], sems.at[i, row]))
            copies[-1].start()
    for copy in copies:
        copy.wait()


def load_caches(keys, values, after):
    return pl.pallas_call(
        load_caches_kernel,
        out_shape=[pltpu.VMEM(a.shape, a.dtype) for a in (keys, values)],
        in_specs=[IN_HBM] * 2 + [ANY] * len(after),
        out_specs=[IN_VMEM] * 2,
        scratch_shapes=[pltpu.SemaphoreType.DMA((2, keys.shape[0]))],
        compiler_params=pltpu.CompilerParams(vmem_limit_bytes=MIB),
        name="load_caches",
    )(in_hbm(keys), in_hbm(values), *after)


def in_hbm(array):
    return pltpu.with_memory_space_constraint(array, pltpu.HBM)


def in_vmem(array):
    return pltpu.with_memory_space_constraint(array, pltpu.VMEM)


def before(done, *rest):
    held = lax.optimization_barrier((done,) + rest)
    return held[0], held[1:]


def sums_kernel(ready, count, *refs):
    out = refs[-1]
    start = 0
    for ref in refs[:ready]:
        out[start : start + ref.shape[0], :] = ref[...]
        start += ref.shape[0]
    rows = refs[ready].shape[0]
    lane = lax.broadcasted_iota(jnp.int32, (rows, 128), 1)
    for ref in refs[ready : ready + count]:
        x = ref[...].astype(jnp.float32)
        total = jnp.sum(x, axis=1, keepdims=True)
        square = jnp.sum(x * x, axis=1, keepdims=True)
        both = jnp.where(lane == 0, total, jnp.where(lane == 1, square, 0.0))
        out[start : start + rows, :] = both
        start += rows


def row_sums(shards, ready=(), after=()):
    rows = shards[0].shape[0] * len(shards) + sum(r.shape[0] for r in ready)
    return pl.pallas_call(
        lambda *refs: sums_kernel(len(ready), len(shards), *refs),
        out_shape=jax.ShapeDtypeStruct((rows, 128), jnp.float32),
        in_specs=[IN_VMEM] * (len(ready) + len(shards)) + [ANY] * len(after),
        out_specs=IN_VMEM,
        compiler_params=pltpu.CompilerParams(vmem_limit_bytes=8 * MIB),
        name="row_sums",
    )(*ready, *shards, *after)


def project_kernel(n, *refs):
    sums_a, sums_b, gain = refs[:3]
    near = refs[3 : 3 + n - 1]
    far = refs[3 + n - 1 : 3 + n + 1]
    weights = refs[3 + n + 1 : -4]
    keep, give, normed, total = refs[-4:]
    rows = near[0].shape[0]
    half = far[0].shape[1]
    sums = sums_a[...] + sums_b[...]
    row_mean = sums[:, :1] / D
    row_square = sums[:, 1:2] / D
    scale = lax.rsqrt(row_square - row_mean * row_mean + epsilon)
    for part in range(2):
        cols = slice(part * half, (part + 1) * half)
        for i in range(n):
            at = slice(i * rows, (i + 1) * rows)
            x = near[i][:, cols] if i < n - 1 else far[part][...]
            x = (x.astype(jnp.float32) - row_mean[at]) * scale[at] * gain[:, cols]
            normed[at, cols] = x
        x = normed[:, cols].astype(jnp.bfloat16)
        start = 0
        for weight in weights:
            term = lax.dot_general(
                x, weight[:, cols], contract, preferred_element_type=jnp.float32
            )
            stripe = slice(start, start + weight.shape[0])
            if part == 0:
                total[:, stripe] = term
            else:
                total[:, stripe] += term
            start = stripe.stop
    side = lax.axis_index("gy")
    local = rows // 2
    for i, owner in enumerate(owners(n)):
        block = total[i * rows : (i + 1) * rows, :]
        low, high = block[:local], block[local:]
        keep[owner] = jnp.where(side == 0, low, high)
        give[owner] = jnp.where(side == 0, high, low)


def project(n, sums, gain, near, far, weights):
    rows, width = near[0].shape
    stripe = sum(w.shape[0] for w in weights)
    shape = jax.ShapeDtypeStruct((n, rows // 2, stripe), jnp.float32)
    return pl.pallas_call(
        lambda *refs: project_kernel(n, *refs),
        out_shape=[shape, shape],
        in_specs=[IN_VMEM] * (3 + n + 1 + len(weights)),
        out_specs=[IN_VMEM] * 2,
        scratch_shapes=[
            pltpu.VMEM((n * rows, width), jnp.float32),
            pltpu.VMEM((n * rows, stripe), jnp.float32),
        ],
        compiler_params=pltpu.CompilerParams(vmem_limit_bytes=8 * MIB),
        name="project",
    )(*sums, gain, *near, *far, *[in_vmem(w) for w in weights])


def split_kernel(keep, got, *outs):
    me = lax.axis_index("gx")
    for d, out in enumerate(outs):
        at = jnp.bitwise_xor(me, d)
        out[...] = (keep[at] + got[at]).astype(jnp.bfloat16)


def split(keep, got):
    n = keep.shape[0]
    return pl.pallas_call(
        split_kernel,
        out_shape=[jax.ShapeDtypeStruct(keep.shape[1:], jnp.bfloat16)] * n,
        in_specs=[IN_VMEM] * 2,
        out_specs=[IN_VMEM] * n,
        compiler_params=pltpu.CompilerParams(vmem_limit_bytes=8 * MIB),
        name="split",
    )(keep, got)


def attend_kernel(n, lengths, *refs):
    arrived = refs[:n]
    cosine, sine, keys, values, mine, other, spread, held = refs[n:]
    rows, stripe = arrived[0].shape
    me = lax.axis_index("gx")
    query_cols = stripe - 128
    side = lax.axis_index("gy")
    score_scale = 1.0 / math.sqrt(DH)
    for d in range(n):
        block = arrived[d][...].astype(jnp.float32)
        for r in range(rows):
            spread[r, pl.ds(jnp.bitwise_xor(me, d), 1), :] = block[r : r + 1, :]
    for r in range(rows):
        given = spread[r]
        cos, sin = cosine[r : r + 1, :], sine[r : r + 1, :]

        def turn(a, b):
            turned = jnp.concatenate([a * cos - b * sin, b * cos + a * sin], axis=1)
            return turned.astype(jnp.bfloat16)

        starts = range(0, query_cols, DH)
        q = turn(
            jnp.concatenate([given[:, c : c + DH // 2] for c in starts], axis=0),
            jnp.concatenate([given[:, c + DH // 2 : c + DH] for c in starts], axis=0),
        )
        new = [
            given[i : i + 1, query_cols:] + given[i + 1 : i + 2, query_cols:]
            for i in range(0, n, 2)
        ]
        new_key = turn(new[0], new[1]).astype(jnp.float32)
        new_value = jnp.concatenate(new[2:], axis=1)
        scores = lax.dot_general(q, keys[r], contract, preferred_element_type=jnp.float32)
        scores = scores * score_scale
        place = lax.broadcasted_iota(jnp.int32, scores.shape, 1)
        scores = jnp.where(place < lengths[r], scores, -1e30)
        own_score = jnp.sum(q.astype(jnp.float32) * new_key, axis=1, keepdims=True) * score_scale
        highest = jnp.maximum(jnp.max(scores, axis=1, keepdims=True), own_score)
        weights = jnp.exp(scores - highest)
        own_weight = jnp.exp(own_score - highest)
        totals = jnp.sum(weights, axis=1, keepdims=True) + own_weight
        blended = jnp.dot(
            weights.astype(jnp.bfloat16), values[r], preferred_element_type=jnp.float32
        )
        blended = (blended + own_weight * new_value) / totals
        for j in range(len(starts)):
            block = blended[j * n : (j + 1) * n]
            swapped = pltpu.roll(block, n // 2, 0)
            parts = [jnp.where(side == 0, block, swapped), jnp.where(side == 0, swapped, block)]
            for i in range(n // 2):
                at = (i * len(starts) + j) * DH
                for k, part in enumerate(parts):
                    held[k, r : r + 1, at : at + DH] = part[i : i + 1]
    mine[...] = held[0].astype(jnp.bfloat16)
    other[...] = held[1].astype(jnp.bfloat16)


def attend(lengths, arrived, cosine, sine, keys, values):
    n = len(arrived)
    rows, stripe = arrived[0].shape
    shape = jax.ShapeDtypeStruct((rows, HEADS * DH // 2), jnp.bfloat16)
    return pl.pallas_call(
        lambda *refs: attend_kernel(n, *refs),
        out_shape=[shape, shape],
        in_specs=[IN_SMEM] + [IN_VMEM] * (n + 4),
        out_specs=[IN_VMEM] * 2,
        scratch_shapes=[
            pltpu.VMEM((rows, n, stripe), jnp.float32),
            pltpu.VMEM((2, rows, HEADS * DH // 2), jnp.float32),
        ],
        compiler_params=pltpu.CompilerParams(vmem_limit_bytes=8 * MIB),
        name="attend",
    )(lengths, *arrived, cosine, sine, in_vmem(keys), in_vmem(values))


def output_kernel(n, *refs):
    near = refs[: n - 1]
    far = refs[n - 1 : n + 1]
    weights = refs[n + 1 : -4]
    keep, give, total, placed = refs[-4:]
    rows = near[0].shape[0]
    half = far[0].shape[1]
    start = 0
    for weight in weights:
        cols = slice(start, start + weight.shape[0])
        last = slice(start % half, start % half + weight.shape[0])
        x = [ref[:, cols] for ref in near] + [far[start // half][:, last]]
        x = jnp.concatenate([piece.astype(jnp.float32) for piece in x], axis=0)
        term = jnp.dot(x.astype(jnp.bfloat16), weight[...], preferred_element_type=jnp.float32)
        if start == 0:
            total[...] = term
        else:
            total[...] += term
        start = cols.stop
    side = lax.axis_index("gy")
    for i, owner in enumerate(owners(n)):
        block = total[i * rows : (i + 1) * rows, :]
        placed[owner] = jnp.where(side == 0, block, pltpu.roll(block, rows // 2, 0))
    keep[...] = placed[pl.ds(side * (n // 2), n // 2)]
    give[...] = placed[pl.ds((1 - side) * (n // 2), n // 2)]


def output_project(n, near, far, weights):
    rows = near[0].shape[0]
    cols = weights[0].shape[1]
    shape = jax.ShapeDtypeStruct((n // 2, rows, cols), jnp.float32)
    return pl.pallas_call(
        lambda *refs: output_kernel(n, *refs),
        out_shape=[shape, shape],
        in_specs=[IN_VMEM] * (n + 1 + len(weights)),
        out_specs=[IN_VMEM] * 2,
        scratch_shapes=[
            pltpu.VMEM((n * rows, cols), jnp.float32),
            pltpu.VMEM((n, rows, cols), jnp.float32),
        ],
        compiler_params=pltpu.CompilerParams(vmem_limit_bytes=8 * MIB),
        name="output_project",
    )(*near, *far, *[in_vmem(w) for w in weights])


def on_any_grid(
    activations,
    norm_gain,
    query_weight,
    keyval_weight,
    output_weight,
    cache_keys,
    cache_values,
    cache_lengths,
):
    inputs = activations.astype(jnp.float32)
    row_sums, square_sums = lax.psum(
        (jnp.sum(inputs, axis=1), jnp.sum(inputs * inputs, axis=1)), "gy"
    )
    row_mean = row_sums[:, None] / D
    row_square = square_sums[:, None] / D
    variance = row_square - row_mean * row_mean
    normed = (
        (inputs - row_mean) * lax.rsqrt(variance + epsilon) * norm_gain.astype(jnp.float32)
    ).astype(jnp.bfloat16)
    shard_rows = lax.all_gather(normed, "gx", axis=0, tiled=True)
    query_part = lax.dot_general(
        shard_rows, query_weight, contract, preferred_element_type=jnp.float32
    )
    keyval_part = lax.dot_general(
        shard_rows, keyval_weight, contract, preferred_element_type=jnp.float32
    )
    partial_sums = jnp.concatenate([query_part, keyval_part], axis=1)
    wide_count = lax.axis_size("gx")
    pair_count = lax.axis_size("gy")
    local_rows = cache_lengths.shape[0]
    stripe = partial_sums.shape[1]
    arrived = lax.all_to_all(partial_sums, ("gx", "gy"), split_axis=0, concat_axis=1, tiled=True)
    gathered = jnp.sum(arrived.reshape(local_rows, wide_count, pair_count, stripe), axis=2).astype(
        jnp.bfloat16
    )
    query_cols = query_weight.shape[0]
    queries = gathered[:, :, :query_cols].reshape(local_rows, HEADS, DH)
    keyvals = gathered[:, :, query_cols:].reshape(local_rows, 2 * DH)
    places = cache_lengths.astype(jnp.float32)
    queries = rotate(queries.astype(jnp.float32), places[:, None, None]).astype(jnp.bfloat16)
    new_keys = rotate(keyvals[:, :DH].astype(jnp.float32), places[:, None]).astype(jnp.bfloat16)
    new_values = keyvals[:, DH:].astype(jnp.float32)
    score_scale = 1.0 / math.sqrt(DH)
    scores = (
        jnp.einsum("rhd,rtd->rht", queries, cache_keys, preferred_element_type=jnp.float32)
        * score_scale
    )
    visible = jnp.arange(cache_keys.shape[1])[None, :] < cache_lengths[:, None]
    scores = jnp.where(visible[:, None, :], scores, -1e30)
    own_score = (
        jnp.einsum("rhd,rd->rh", queries, new_keys, preferred_element_type=jnp.float32)
        * score_scale
    )
    highest = jnp.maximum(jnp.max(scores, axis=2), own_score)
    weights = jnp.exp(scores - highest[:, :, None])
    own_weight = jnp.exp(own_score - highest)
    totals = jnp.sum(weights, axis=2) + own_weight
    blended = jnp.einsum(
        "rht,rtd->rhd",
        weights.astype(jnp.bfloat16),
        cache_values,
        preferred_element_type=jnp.float32,
    )
    blended = blended + own_weight[:, :, None] * new_values[:, None, :]
    attended = (blended / totals[:, :, None]).astype(jnp.bfloat16).reshape(local_rows, HEADS * DH)
    swapped = lax.all_to_all(attended, "gy", split_axis=1, concat_axis=0, tiled=True)
    partial_out = jnp.dot(
        lax.all_gather(swapped, "gx", axis=0, tiled=True),
        output_weight,
        preferred_element_type=jnp.float32,
    )
    return lax.psum_scatter(partial_out, "gy", scatter_dimension=0, tiled=True).astype(jnp.bfloat16)


def on_device(
    activations,
    norm_gain,
    query_weight,
    keyval_weight,
    output_weight,
    cache_keys,
    cache_values,
    cache_lengths,
):
    n = lax.axis_size("gx")
    ring = Ring(n)
    query_cols, width = query_weight.shape
    new_cols = keyval_weight.shape[0]
    piece = query_cols // 4
    weights = []

    indices = jnp.arange(DH // 2, dtype=jnp.float32)
    frequency = jnp.exp(-math.log(10000.0) * indices / (DH // 2))
    angles = cache_lengths.astype(jnp.float32)[:, None] * frequency
    cosine, sine = jnp.cos(angles), jnp.sin(angles)

    left = right = activations
    near = [activations]
    for step in range(1, n // 2):
        arrived = near[1:][-2:]
        left, right = ring.step(left, right)
        if step > 1:
            sums = row_sums(arrived, [sums])
        start = (step - 1) * piece
        weight = load(piece, [(query_weight, start, piece, 0)], arrived)
        if step == 1:
            weight, (own,) = before(weight, activations)
            sums = row_sums([own])
            far_sums = lax.ppermute(sums, "gx", ring.across)
            weight, (left, right, sums) = before(weight, left, right, sums)
        else:
            weight, (left, right) = before(weight, left, right)
        weights.append(weight)
        near += [left, right]
    half = width // 2
    far = ring.step(left[:, :half], right[:, half:])
    sums = row_sums([left, right], [sums])
    jobs = [(query_weight, 3 * piece, piece, 0), (keyval_weight, 0, new_cols, None)]
    weight = load(piece + 2 * new_cols, jobs, [sums])
    sums = jnp.concatenate([sums, far_sums], axis=0)
    other_sums = swap_pair(sums)
    weight, (other_sums, *far) = before(weight, other_sums, *far)
    weights.append(weight)
    sums = (sums, other_sums)
    gain = norm_gain.astype(jnp.float32)[None, :]
    keep, give = project(n, sums, gain, near, far, weights)
    blocks = split(keep, swap_pair(give))
    arrived = [blocks[0]]
    for d in range(1, n):
        arrived.append(lax.ppermute(blocks[d], "gx", [(i, i ^ d) for i in range(n)]))
    keys, values = load_caches(cache_keys, cache_values, [blocks[1]])
    unit = output_weight.shape[0] // 12
    sizes = [3 * unit, 3 * unit, 2 * unit, 2 * unit, 2 * unit]
    weight = load(sizes[0], [(output_weight, 0, sizes[0], 0)], [blocks[1]])
    keys, arrived = before(keys, *arrived)
    weight, arrived = before(weight, *arrived)
    weights = [weight]
    mine, other = attend(cache_lengths, arrived, cosine, sine, keys, values)
    shard = jnp.concatenate([mine, swap_pair(other)], axis=0)

    left = right = shard
    near = [shard]
    for step in range(1, n // 2):
        arrived = near[-2:]
        left, right = ring.step(left, right)
        weight = load(sizes[step], [(output_weight, sum(sizes[:step]), sizes[step], 0)], arrived)
        weight, (left, right) = before(weight, left, right)
        weights.append(weight)
        near += [left, right]
    half = shard.shape[1] // 2
    far = ring.step(left[:, :half], right[:, half:])
    weight = load(sizes[-1], [(output_weight, sum(sizes[:-1]), sizes[-1], 0)], [left, right])
    weight, far = before(weight, *far)
    weights.append(weight)
    keep, give = output_project(n, near, far, weights)
    out = (keep + swap_pair(give)).astype(jnp.bfloat16)
    return out.reshape(-1, out.shape[-1])


def solution(mesh):
    return jax.shard_map(
        on_device if mesh.shape["gx"] == 8 else on_any_grid,
        mesh=mesh,
        in_specs=(
            P(("groups", "gx"), "gy"),
            P("gy"),
            P("gx", "gy"),
            P("gx", "gy"),
            P("gy", "gx"),
            P(("groups", "gx", "gy"), None, None),
            P(("groups", "gx", "gy"), None, None),
            P(("groups", "gx", "gy")),
        ),
        out_specs=P(("groups", "gy"), "gx"),
        check_vma=False,
    )
```

```python
import math

import jax
import jax.numpy as jnp
from jax import lax
from jax.experimental import pallas as pl
from jax.experimental.pallas import tpu as pltpu
from jax.sharding import PartitionSpec as P

D = 18432
HEADS = 48
DH = 256


epsilon = 1e-06
contract = (((1,), (1,)), ((), ()))
MIB = 1 << 20
ANY = pl.BlockSpec(memory_space=pl.ANY)
IN_HBM = pl.BlockSpec(memory_space=pltpu.HBM)
IN_VMEM = pl.BlockSpec(memory_space=pltpu.VMEM)
IN_SMEM = pl.BlockSpec(memory_space=pltpu.SMEM)


def rotate(vectors, places):
    half_width = vectors.shape[-1] // 2
    indices = jnp.arange(half_width, dtype=jnp.float32)
    frequency = jnp.exp(-math.log(10000.0) * indices / half_width)
    angles = places * frequency
    cosine = jnp.cos(angles)
    sine = jnp.sin(angles)
    first_half = vectors[..., :half_width]
    second_half = vectors[..., half_width:]
    return jnp.concatenate(
        [first_half * cosine - second_half * sine, second_half * cosine + first_half * sine],
        axis=-1,
    )


def ring_order(n):
    return list(range(0, n, 2)) + list(range(n - 1, 0, -2))


def swap_pair(x):
    return lax.ppermute(x, "gy", [(0, 1), (1, 0)])


class Ring:
    def __init__(self, n):
        order = ring_order(n)
        self.onward = [(order[p], order[(p + 1) % n]) for p in range(n)]
        self.back = [(order[p], order[(p - 1) % n]) for p in range(n)]
        self.across = [(order[p], order[(p + n // 2) % n]) for p in range(n)]

    def step(self, left, right):
        return lax.ppermute(left, "gx", self.onward), lax.ppermute(right, "gx", self.back)

    def send_across(self, shard, part):
        half = shard.shape[1] // 2
        return lax.ppermute(shard[:, part * half : (part + 1) * half], "gx", self.across)


def owners(n):
    offsets = [0]
    for step in range(1, n // 2):
        offsets += [-step, step]
    offsets.append(n // 2)
    me = lax.axis_index("gx")
    half = lax.div(me, 2)
    place = jnp.where(lax.rem(me, 2) == 0, half, n - 1 - half)
    result = []
    for offset in offsets:
        at = lax.rem(place + (offset + n), n)
        result.append(jnp.where(at < n // 2, 2 * at, 2 * (n - 1 - at) + 1))
    return result


def start_copies(source, target, sems, count):
    rows = source.shape[0]
    size = -(-rows // (16 * count)) * 16
    copies = []
    for i, first in enumerate(range(0, rows, size)):
        at = pl.ds(first, min(size, rows - first))
        copy = pltpu.make_async_copy(source.at[at], target.at[at], sems.at[i])
        copy.start()
        copies.append(copy)
    return copies


def load_kernel(jobs, *refs):
    sources, target, sems = refs[: len(jobs)], refs[-2], refs[-1]
    copies = []
    for i, (first, size, at) in enumerate(jobs):
        if at is None:
            at = target.shape[0] - 2 * size
            odd = lax.rem(lax.axis_index("gx"), 2)
            unused = pl.ds(pl.multiple_of(at + (1 - odd) * size, size), size)
            at = pl.multiple_of(at + odd * size, size)
            target[unused, :] = jnp.zeros((size, target.shape[1]), target.dtype)
        part = sources[i].at[pl.ds(first, size)]
        copies += start_copies(part, target.at[pl.ds(at, size)], sems.at[i], 4)
    for copy in copies:
        copy.wait()


def load(rows, jobs, after=()):
    array = jobs[0][0]
    return pl.pallas_call(
        lambda *refs: load_kernel([job[1:] for job in jobs], *refs),
        out_shape=pltpu.VMEM((rows, array.shape[1]), array.dtype),
        in_specs=[IN_HBM] * len(jobs) + [ANY] * len(after),
        out_specs=IN_VMEM,
        scratch_shapes=[pltpu.SemaphoreType.DMA((len(jobs), 4))],
        compiler_params=pltpu.CompilerParams(vmem_limit_bytes=MIB),
        name="load",
    )(*[in_hbm(job[0]) for job in jobs], *after)


def in_hbm(array):
    return pltpu.with_memory_space_constraint(array, pltpu.HBM)


def in_vmem(array):
    return pltpu.with_memory_space_constraint(array, pltpu.VMEM)


def before(done, *rest):
    held = lax.optimization_barrier((done,) + rest)
    return held[0], held[1:]


def sums_kernel(ready, count, *refs):
    out = refs[-1]
    start = 0
    for ref in refs[:ready]:
        out[start : start + ref.shape[0], :] = ref[...]
        start += ref.shape[0]
    rows = refs[ready].shape[0]
    lane = lax.broadcasted_iota(jnp.int32, (rows, 128), 1)
    for ref in refs[ready : ready + count]:
        x = ref[...].astype(jnp.float32)
        total = jnp.sum(x, axis=1, keepdims=True)
        square = jnp.sum(x * x, axis=1, keepdims=True)
        both = jnp.where(lane == 0, total, jnp.where(lane == 1, square, 0.0))
        out[start : start + rows, :] = both
        start += rows


def row_sums(shards, ready=(), after=()):
    rows = shards[0].shape[0] * len(shards) + sum(r.shape[0] for r in ready)
    return pl.pallas_call(
        lambda *refs: sums_kernel(len(ready), len(shards), *refs),
        out_shape=jax.ShapeDtypeStruct((rows, 128), jnp.float32),
        in_specs=[IN_VMEM] * (len(ready) + len(shards)) + [ANY] * len(after),
        out_specs=IN_VMEM,
        compiler_params=pltpu.CompilerParams(vmem_limit_bytes=8 * MIB),
        name="row_sums",
    )(*ready, *shards, *after)


def project_kernel(n, parts, *refs):
    sums_a, sums_b, gain = refs[:3]
    shards = refs[3 : 3 + n]
    weights = refs[3 + n : 3 + n + parts]
    caches = refs[3 + n + parts : 5 + n + parts]
    keep, give, *copied, normed, total, sems = refs[5 + n + parts :]
    copies = []
    for i, (source, target) in enumerate(zip(caches, copied)):
        for row in range(source.shape[0]):
            copies.append(pltpu.make_async_copy(source.at[row], target.at[row], sems.at[i, row]))
            copies[-1].start()
    rows, width = shards[0].shape
    sums = sums_a[...] + sums_b[...]
    row_mean = sums[:, :1] / D
    row_square = sums[:, 1:2] / D
    scale = lax.rsqrt(row_square - row_mean * row_mean + epsilon)
    for part in range(2):
        cols = slice(part * width // 2, (part + 1) * width // 2)
        for i, shard in enumerate(shards):
            at = slice(i * rows, (i + 1) * rows)
            x = shard[:, cols].astype(jnp.float32)
            normed[at, cols] = (x - row_mean[at]) * scale[at] * gain[:, cols]
        x = normed[:, cols].astype(jnp.bfloat16)
        start = 0
        for weight in weights:
            term = lax.dot_general(
                x, weight[:, cols], contract, preferred_element_type=jnp.float32
            )
            stripe = slice(start, start + weight.shape[0])
            if part == 0:
                total[:, stripe] = term
            else:
                total[:, stripe] += term
            start = stripe.stop
    side = lax.axis_index("gy")
    local = rows // 2
    for i, owner in enumerate(owners(n)):
        block = total[i * rows : (i + 1) * rows, :]
        low, high = block[:local], block[local:]
        keep[owner] = jnp.where(side == 0, low, high)
        give[owner] = jnp.where(side == 0, high, low)
    for copy in copies:
        copy.wait()


def project(sums, gain, shards, weights, caches):
    n = len(shards)
    rows, width = shards[0].shape
    stripe = sum(w.shape[0] for w in weights)
    shape = jax.ShapeDtypeStruct((n, rows // 2, stripe), jnp.float32)
    return pl.pallas_call(
        lambda *refs: project_kernel(n, len(weights), *refs),
        out_shape=[shape, shape] + [pltpu.VMEM(a.shape, a.dtype) for a in caches],
        in_specs=[IN_VMEM] * (3 + n + len(weights)) + [IN_HBM] * 2,
        out_specs=[IN_VMEM] * 4,
        scratch_shapes=[
            pltpu.VMEM((n * rows, width), jnp.float32),
            pltpu.VMEM((n * rows, stripe), jnp.float32),
            pltpu.SemaphoreType.DMA((2, caches[0].shape[0])),
        ],
        compiler_params=pltpu.CompilerParams(vmem_limit_bytes=8 * MIB),
        name="project",
    )(*sums, gain, *shards, *[in_vmem(w) for w in weights], *[in_hbm(a) for a in caches])


def split_kernel(keep, got, here, there):
    me = lax.axis_index("gx")
    for d in range(keep.shape[0]):
        at = jnp.bitwise_xor(me, d)
        out = there if d % 2 else here
        out[d // 2] = (keep[at] + got[at]).astype(jnp.bfloat16)


def split(keep, got):
    shape = jax.ShapeDtypeStruct((keep.shape[0] // 2,) + keep.shape[1:], jnp.bfloat16)
    return pl.pallas_call(
        split_kernel,
        out_shape=[shape] * 2,
        in_specs=[IN_VMEM] * 2,
        out_specs=[IN_VMEM] * 2,
        compiler_params=pltpu.CompilerParams(vmem_limit_bytes=8 * MIB),
        name="split",
    )(keep, got)


def pair_kernel(here, came, *outs):
    for d, out in enumerate(outs):
        out[0] = here[d]
        out[1] = came[d]


def pair(here, came):
    shape = jax.ShapeDtypeStruct((2,) + here.shape[1:], here.dtype)
    return pl.pallas_call(
        pair_kernel,
        out_shape=[shape] * here.shape[0],
        in_specs=[IN_VMEM] * 2,
        out_specs=[IN_VMEM] * here.shape[0],
        compiler_params=pltpu.CompilerParams(vmem_limit_bytes=8 * MIB),
        name="pair",
    )(here, came)


def attend_kernel(n, lengths, *refs):
    arrived = refs[: n // 2]
    cosine, sine, keys, values, mine, other, spread, held = refs[n // 2 :]
    _, rows, stripe = arrived[0].shape
    me = lax.axis_index("gx")
    query_cols = stripe - 128
    side = lax.axis_index("gy")
    score_scale = 1.0 / math.sqrt(DH)
    for d in range(n):
        block = arrived[d // 2][d % 2].astype(jnp.float32)
        for r in range(rows):
            spread[r, pl.ds(jnp.bitwise_xor(me, d), 1), :] = block[r : r + 1, :]
    for r in range(rows):
        given = spread[r]
        cos, sin = cosine[r : r + 1, :], sine[r : r + 1, :]

        def turn(a, b):
            turned = jnp.concatenate([a * cos - b * sin, b * cos + a * sin], axis=1)
            return turned.astype(jnp.bfloat16)

        starts = range(0, query_cols, DH)
        q = turn(
            jnp.concatenate([given[:, c : c + DH // 2] for c in starts], axis=0),
            jnp.concatenate([given[:, c + DH // 2 : c + DH] for c in starts], axis=0),
        )
        new = [
            given[i : i + 1, query_cols:] + given[i + 1 : i + 2, query_cols:]
            for i in range(0, n, 2)
        ]
        new_key = turn(new[0], new[1]).astype(jnp.float32)
        new_value = jnp.concatenate(new[2:], axis=1)
        scores = lax.dot_general(q, keys[r], contract, preferred_element_type=jnp.float32)
        scores = scores * score_scale
        place = lax.broadcasted_iota(jnp.int32, scores.shape, 1)
        scores = jnp.where(place < lengths[r], scores, -1e30)
        own_score = jnp.sum(q.astype(jnp.float32) * new_key, axis=1, keepdims=True) * score_scale
        highest = jnp.maximum(jnp.max(scores, axis=1, keepdims=True), own_score)
        weights = jnp.exp(scores - highest)
        own_weight = jnp.exp(own_score - highest)
        totals = jnp.sum(weights, axis=1, keepdims=True) + own_weight
        blended = jnp.dot(
            weights.astype(jnp.bfloat16), values[r], preferred_element_type=jnp.float32
        )
        blended = (blended + own_weight * new_value) / totals
        for j in range(len(starts)):
            block = blended[j * n : (j + 1) * n]
            swapped = pltpu.roll(block, n // 2, 0)
            parts = [jnp.where(side == 0, block, swapped), jnp.where(side == 0, swapped, block)]
            for i in range(n // 2):
                at = (i * len(starts) + j) * DH
                for k, part in enumerate(parts):
                    held[k, r : r + 1, at : at + DH] = part[i : i + 1]
    mine[...] = held[0].astype(jnp.bfloat16)
    other[...] = held[1].astype(jnp.bfloat16)


def attend(lengths, arrived, cosine, sine, keys, values):
    n = 2 * len(arrived)
    _, rows, stripe = arrived[0].shape
    shape = jax.ShapeDtypeStruct((rows, HEADS * DH // 2), jnp.bfloat16)
    return pl.pallas_call(
        lambda *refs: attend_kernel(n, *refs),
        out_shape=[shape, shape],
        in_specs=[IN_SMEM] + [IN_VMEM] * (n // 2 + 4),
        out_specs=[IN_VMEM] * 2,
        scratch_shapes=[
            pltpu.VMEM((rows, n, stripe), jnp.float32),
            pltpu.VMEM((2, rows, HEADS * DH // 2), jnp.float32),
        ],
        compiler_params=pltpu.CompilerParams(vmem_limit_bytes=8 * MIB),
        name="attend",
    )(lengths, *arrived, cosine, sine, in_vmem(keys), in_vmem(values))


def output_kernel(n, *refs):
    shards = refs[:n]
    weights = refs[n:-4]
    keep, give, total, placed = refs[-4:]
    rows = shards[0].shape[0]
    start = 0
    for weight in weights:
        cols = slice(start, start + weight.shape[0])
        x = jnp.concatenate([ref[:, cols].astype(jnp.float32) for ref in shards], axis=0)
        term = jnp.dot(x.astype(jnp.bfloat16), weight[...], preferred_element_type=jnp.float32)
        if start == 0:
            total[...] = term
        else:
            total[...] += term
        start = cols.stop
    side = lax.axis_index("gy")
    for i, owner in enumerate(owners(n)):
        block = total[i * rows : (i + 1) * rows, :]
        placed[owner] = jnp.where(side == 0, block, pltpu.roll(block, rows // 2, 0))
    keep[...] = placed[pl.ds(side * (n // 2), n // 2)]
    give[...] = placed[pl.ds((1 - side) * (n // 2), n // 2)]


def output_project(shards, weights):
    n = len(shards)
    rows = shards[0].shape[0]
    cols = weights[0].shape[1]
    shape = jax.ShapeDtypeStruct((n // 2, rows, cols), jnp.float32)
    return pl.pallas_call(
        lambda *refs: output_kernel(n, *refs),
        out_shape=[shape, shape],
        in_specs=[IN_VMEM] * (n + len(weights)),
        out_specs=[IN_VMEM] * 2,
        scratch_shapes=[
            pltpu.VMEM((n * rows, cols), jnp.float32),
            pltpu.VMEM((n, rows, cols), jnp.float32),
        ],
        compiler_params=pltpu.CompilerParams(vmem_limit_bytes=8 * MIB),
        name="output_project",
    )(*shards, *[in_vmem(w) for w in weights])


def on_any_grid(
    activations,
    norm_gain,
    query_weight,
    keyval_weight,
    output_weight,
    cache_keys,
    cache_values,
    cache_lengths,
):
    inputs = activations.astype(jnp.float32)
    row_sums, square_sums = lax.psum(
        (jnp.sum(inputs, axis=1), jnp.sum(inputs * inputs, axis=1)), "gy"
    )
    row_mean = row_sums[:, None] / D
    row_square = square_sums[:, None] / D
    variance = row_square - row_mean * row_mean
    normed = (
        (inputs - row_mean) * lax.rsqrt(variance + epsilon) * norm_gain.astype(jnp.float32)
    ).astype(jnp.bfloat16)
    shard_rows = lax.all_gather(normed, "gx", axis=0, tiled=True)
    query_part = lax.dot_general(
        shard_rows, query_weight, contract, preferred_element_type=jnp.float32
    )
    keyval_part = lax.dot_general(
        shard_rows, keyval_weight, contract, preferred_element_type=jnp.float32
    )
    partial_sums = jnp.concatenate([query_part, keyval_part], axis=1)
    wide_count = lax.axis_size("gx")
    pair_count = lax.axis_size("gy")
    local_rows = cache_lengths.shape[0]
    stripe = partial_sums.shape[1]
    arrived = lax.all_to_all(partial_sums, ("gx", "gy"), split_axis=0, concat_axis=1, tiled=True)
    gathered = jnp.sum(arrived.reshape(local_rows, wide_count, pair_count, stripe), axis=2).astype(
        jnp.bfloat16
    )
    query_cols = query_weight.shape[0]
    queries = gathered[:, :, :query_cols].reshape(local_rows, HEADS, DH)
    keyvals = gathered[:, :, query_cols:].reshape(local_rows, 2 * DH)
    places = cache_lengths.astype(jnp.float32)
    queries = rotate(queries.astype(jnp.float32), places[:, None, None]).astype(jnp.bfloat16)
    new_keys = rotate(keyvals[:, :DH].astype(jnp.float32), places[:, None]).astype(jnp.bfloat16)
    new_values = keyvals[:, DH:].astype(jnp.float32)
    score_scale = 1.0 / math.sqrt(DH)
    scores = (
        jnp.einsum("rhd,rtd->rht", queries, cache_keys, preferred_element_type=jnp.float32)
        * score_scale
    )
    visible = jnp.arange(cache_keys.shape[1])[None, :] < cache_lengths[:, None]
    scores = jnp.where(visible[:, None, :], scores, -1e30)
    own_score = (
        jnp.einsum("rhd,rd->rh", queries, new_keys, preferred_element_type=jnp.float32)
        * score_scale
    )
    highest = jnp.maximum(jnp.max(scores, axis=2), own_score)
    weights = jnp.exp(scores - highest[:, :, None])
    own_weight = jnp.exp(own_score - highest)
    totals = jnp.sum(weights, axis=2) + own_weight
    blended = jnp.einsum(
        "rht,rtd->rhd",
        weights.astype(jnp.bfloat16),
        cache_values,
        preferred_element_type=jnp.float32,
    )
    blended = blended + own_weight[:, :, None] * new_values[:, None, :]
    attended = (blended / totals[:, :, None]).astype(jnp.bfloat16).reshape(local_rows, HEADS * DH)
    swapped = lax.all_to_all(attended, "gy", split_axis=1, concat_axis=0, tiled=True)
    partial_out = jnp.dot(
        lax.all_gather(swapped, "gx", axis=0, tiled=True),
        output_weight,
        preferred_element_type=jnp.float32,
    )
    return lax.psum_scatter(partial_out, "gy", scatter_dimension=0, tiled=True).astype(jnp.bfloat16)


def on_device(
    activations,
    norm_gain,
    query_weight,
    keyval_weight,
    output_weight,
    cache_keys,
    cache_values,
    cache_lengths,
):
    n = lax.axis_size("gx")
    ring = Ring(n)
    query_cols, width = query_weight.shape
    new_cols = keyval_weight.shape[0]
    piece = query_cols // 4
    weights = []

    indices = jnp.arange(DH // 2, dtype=jnp.float32)
    frequency = jnp.exp(-math.log(10000.0) * indices / (DH // 2))
    angles = cache_lengths.astype(jnp.float32)[:, None] * frequency
    cosine, sine = jnp.cos(angles), jnp.sin(angles)

    def piece_of(array, start, size, after):
        return load(size, [(array, start, size, 0)], after)

    left = right = activations
    shards = [activations]
    far = []
    sums = ()
    for step in range(1, n // 2):
        arrived = shards[-2:] if step > 1 else shards
        left, right = ring.step(left, right)
        weight = piece_of(query_weight, (step - 1) * piece, piece, arrived if step > 1 else [])
        if step <= 2:
            half = ring.send_across(activations, step - 1)
            weight, (half,) = before(weight, half)
            far.append(half)
        weight, (left, right, *arrived) = before(weight, left, right, *arrived)
        sums = (row_sums(arrived, sums),)
        weights.append(weight)
        shards += [left, right]
    shards.append(jnp.concatenate(far, axis=1))
    sums = row_sums([left, right, shards[-1]], sums)
    jobs = [(query_weight, 3 * piece, piece, 0), (keyval_weight, 0, new_cols, None)]
    weight = load(piece + 2 * new_cols, jobs, [sums])
    other_sums = swap_pair(sums)
    weight, (other_sums,) = before(weight, other_sums)
    weights.append(weight)
    gain = norm_gain.astype(jnp.float32)[None, :]
    keep, give, keys, values = project(
        (sums, other_sums), gain, shards, weights, [cache_keys, cache_values]
    )

    here, there = split(keep, swap_pair(give))
    came = lax.ppermute(there, "gx", [(i, i ^ 1) for i in range(n)])
    blocks = pair(here, came)
    arrived = [blocks[0]]
    for d in range(1, n // 2):
        arrived.append(lax.ppermute(blocks[d], "gx", [(i, i ^ (2 * d)) for i in range(n)]))
    piece = output_weight.shape[0] // 4
    weight = piece_of(output_weight, 0, piece, [blocks[1]])
    weight, arrived = before(weight, *arrived)
    weights = [weight]
    mine, other = attend(cache_lengths, arrived, cosine, sine, keys, values)
    shard = jnp.concatenate([mine, swap_pair(other)], axis=0)

    left = right = shard
    shards = [shard]
    far = []
    for step in range(1, n // 2):
        arrived = shards[-2:]
        left, right = ring.step(left, right)
        weight = piece_of(output_weight, step * piece, piece, arrived)
        if step <= 2:
            half = ring.send_across(shard, step - 1)
            weight, (half,) = before(weight, half)
            far.append(half)
        weight, (left, right) = before(weight, left, right)
        weights.append(weight)
        shards += [left, right]
    shards.append(jnp.concatenate(far, axis=1))
    keep, give = output_project(shards, weights)
    out = (keep + swap_pair(give)).astype(jnp.bfloat16)
    return out.reshape(-1, out.shape[-1])


def solution(mesh):
    return jax.shard_map(
        on_device if mesh.shape["gx"] == 8 else on_any_grid,
        mesh=mesh,
        in_specs=(
            P(("groups", "gx"), "gy"),
            P("gy"),
            P("gx", "gy"),
            P("gx", "gy"),
            P("gy", "gx"),
            P(("groups", "gx", "gy"), None, None),
            P(("groups", "gx", "gy"), None, None),
            P(("groups", "gx", "gy")),
        ),
        out_specs=P(("groups", "gy"), "gx"),
        check_vma=False,
    )
```

```python
import math

import jax
import jax.numpy as jnp
from jax import lax
from jax.experimental import pallas as pl
from jax.experimental.pallas import tpu as pltpu
from jax.sharding import PartitionSpec as P

D = 18432
HEADS = 48
DH = 256


epsilon = 1e-06
contract = (((1,), (1,)), ((), ()))
MIB = 1 << 20
ANY = pl.BlockSpec(memory_space=pl.ANY)
IN_HBM = pl.BlockSpec(memory_space=pltpu.HBM)
IN_VMEM = pl.BlockSpec(memory_space=pltpu.VMEM)
IN_SMEM = pl.BlockSpec(memory_space=pltpu.SMEM)


def rotate(vectors, places):
    half_width = vectors.shape[-1] // 2
    indices = jnp.arange(half_width, dtype=jnp.float32)
    frequency = jnp.exp(-math.log(10000.0) * indices / half_width)
    angles = places * frequency
    cosine = jnp.cos(angles)
    sine = jnp.sin(angles)
    first_half = vectors[..., :half_width]
    second_half = vectors[..., half_width:]
    return jnp.concatenate(
        [first_half * cosine - second_half * sine, second_half * cosine + first_half * sine],
        axis=-1,
    )


def ring_order(n):
    return list(range(0, n, 2)) + list(range(n - 1, 0, -2))


def swap_pair(x):
    return lax.ppermute(x, "gy", [(0, 1), (1, 0)])


class Ring:
    def __init__(self, n):
        order = ring_order(n)
        self.onward = [(order[p], order[(p + 1) % n]) for p in range(n)]
        self.back = [(order[p], order[(p - 1) % n]) for p in range(n)]
        self.across = [(order[p], order[(p + n // 2) % n]) for p in range(n)]

    def step(self, left, right):
        return lax.ppermute(left, "gx", self.onward), lax.ppermute(right, "gx", self.back)


def owners(n):
    offsets = [0]
    for step in range(1, n // 2):
        offsets += [-step, step]
    offsets.append(n // 2)
    me = lax.axis_index("gx")
    half = lax.div(me, 2)
    place = jnp.where(lax.rem(me, 2) == 0, half, n - 1 - half)
    result = []
    for offset in offsets:
        at = lax.rem(place + (offset + n), n)
        result.append(jnp.where(at < n // 2, 2 * at, 2 * (n - 1 - at) + 1))
    return result


def start_copies(source, target, sems, count):
    rows = source.shape[0]
    size = -(-rows // (16 * count)) * 16
    copies = []
    for i, first in enumerate(range(0, rows, size)):
        at = pl.ds(first, min(size, rows - first))
        copy = pltpu.make_async_copy(source.at[at], target.at[at], sems.at[i])
        copy.start()
        copies.append(copy)
    return copies


def load_kernel(jobs, *refs):
    sources, target, sems = refs[: len(jobs)], refs[-2], refs[-1]
    copies = []
    for i, (first, size, at) in enumerate(jobs):
        if at is None:
            at = target.shape[0] - 2 * size
            odd = lax.rem(lax.axis_index("gx"), 2)
            unused = pl.ds(pl.multiple_of(at + (1 - odd) * size, size), size)
            at = pl.multiple_of(at + odd * size, size)
            target[unused, :] = jnp.zeros((size, target.shape[1]), target.dtype)
        part = sources[i].at[pl.ds(first, size)]
        copies += start_copies(part, target.at[pl.ds(at, size)], sems.at[i], 4)
    for copy in copies:
        copy.wait()


def load(rows, jobs, after=()):
    array = jobs[0][0]
    return pl.pallas_call(
        lambda *refs: load_kernel([job[1:] for job in jobs], *refs),
        out_shape=pltpu.VMEM((rows, array.shape[1]), array.dtype),
        in_specs=[IN_HBM] * len(jobs) + [ANY] * len(after),
        out_specs=IN_VMEM,
        scratch_shapes=[pltpu.SemaphoreType.DMA((len(jobs), 4))],
        compiler_params=pltpu.CompilerParams(vmem_limit_bytes=MIB),
        name="load",
    )(*[in_hbm(job[0]) for job in jobs], *after)


def load_caches_kernel(*refs):
    sources, targets, sems = refs[:2], refs[-3:-1], refs[-1]
    copies = []
    for i, (source, target) in enumerate(zip(sources, targets)):
        for row in range(source.shape[0]):
            copies.append(pltpu.make_async_copy(source.at[row], target.at[row], sems.at[i, row]))
            copies[-1].start()
    for copy in copies:
        copy.wait()


def load_caches(keys, values, after):
    return pl.pallas_call(
        load_caches_kernel,
        out_shape=[pltpu.VMEM(a.shape, a.dtype) for a in (keys, values)],
        in_specs=[IN_HBM] * 2 + [ANY] * len(after),
        out_specs=[IN_VMEM] * 2,
        scratch_shapes=[pltpu.SemaphoreType.DMA((2, keys.shape[0]))],
        compiler_params=pltpu.CompilerParams(vmem_limit_bytes=MIB),
        name="load_caches",
    )(in_hbm(keys), in_hbm(values), *after)


def in_hbm(array):
    return pltpu.with_memory_space_constraint(array, pltpu.HBM)


def in_vmem(array):
    return pltpu.with_memory_space_constraint(array, pltpu.VMEM)


def before(done, *rest):
    held = lax.optimization_barrier((done,) + rest)
    return held[0], held[1:]


def sums_kernel(ready, count, *refs):
    out = refs[-1]
    start = 0
    for ref in refs[:ready]:
        out[start : start + ref.shape[0], :] = ref[...]
        start += ref.shape[0]
    rows = refs[ready].shape[0]
    lane = lax.broadcasted_iota(jnp.int32, (rows, 128), 1)
    for ref in refs[ready : ready + count]:
        x = ref[...].astype(jnp.float32)
        total = jnp.sum(x, axis=1, keepdims=True)
        square = jnp.sum(x * x, axis=1, keepdims=True)
        both = jnp.where(lane == 0, total, jnp.where(lane == 1, square, 0.0))
        out[start : start + rows, :] = both
        start += rows


def row_sums(shards, ready=(), after=()):
    rows = shards[0].shape[0] * len(shards) + sum(r.shape[0] for r in ready)
    return pl.pallas_call(
        lambda *refs: sums_kernel(len(ready), len(shards), *refs),
        out_shape=jax.ShapeDtypeStruct((rows, 128), jnp.float32),
        in_specs=[IN_VMEM] * (len(ready) + len(shards)) + [ANY] * len(after),
        out_specs=IN_VMEM,
        compiler_params=pltpu.CompilerParams(vmem_limit_bytes=8 * MIB),
        name="row_sums",
    )(*ready, *shards, *after)


def project_kernel(n, parts, *refs):
    sums_a, sums_b, gain = refs[:3]
    shards = refs[3 : 3 + n - 1]
    far = refs[3 + n - 1 : 3 + n + 1]
    weights = refs[4 + n : 4 + n + parts]
    later, keep, give, early, normed, total, sems = refs[4 + n + parts :]
    copies = start_copies(later.at[pl.ds(0, early.shape[0])], early, sems, 4)
    rows, width = shards[0].shape
    sums = sums_a[...] + sums_b[...]
    row_mean = sums[:, :1] / D
    row_square = sums[:, 1:2] / D
    scale = lax.rsqrt(row_square - row_mean * row_mean + epsilon)
    for part in range(2):
        cols = slice(part * width // 2, (part + 1) * width // 2)
        for i in range(n):
            at = slice(i * rows, (i + 1) * rows)
            x = shards[i][:, cols] if i < n - 1 else far[part][...]
            x = x.astype(jnp.float32)
            normed[at, cols] = (x - row_mean[at]) * scale[at] * gain[:, cols]
        x = normed[:, cols].astype(jnp.bfloat16)
        start = 0
        for weight in weights:
            term = lax.dot_general(
                x, weight[:, cols], contract, preferred_element_type=jnp.float32
            )
            stripe = slice(start, start + weight.shape[0])
            if part == 0:
                total[:, stripe] = term
            else:
                total[:, stripe] += term
            start = stripe.stop
    side = lax.axis_index("gy")
    local = rows // 2
    for i, owner in enumerate(owners(n)):
        block = total[i * rows : (i + 1) * rows, :]
        low, high = block[:local], block[local:]
        keep[owner] = jnp.where(side == 0, low, high)
        give[owner] = jnp.where(side == 0, high, low)
    for copy in copies:
        copy.wait()


def project(sums, gain, shards, far, weights, later, size):
    n = len(shards) + 1
    rows, width = shards[0].shape
    stripe = sum(w.shape[0] for w in weights)
    shape = jax.ShapeDtypeStruct((n, rows // 2, stripe), jnp.float32)
    return pl.pallas_call(
        lambda *refs: project_kernel(n, len(weights), *refs),
        out_shape=[shape, shape, pltpu.VMEM((size, later.shape[1]), later.dtype)],
        in_specs=[IN_VMEM] * (4 + n + len(weights)) + [IN_HBM],
        out_specs=[IN_VMEM] * 3,
        scratch_shapes=[
            pltpu.VMEM((n * rows, width), jnp.float32),
            pltpu.VMEM((n * rows, stripe), jnp.float32),
            pltpu.SemaphoreType.DMA((4,)),
        ],
        compiler_params=pltpu.CompilerParams(vmem_limit_bytes=6 * MIB),
        name="project",
    )(
        *sums,
        gain,
        *shards,
        *far,
        *[in_vmem(w) for w in weights],
        in_hbm(later),
    )


def split_kernel(keep, got, here, there):
    me = lax.axis_index("gx")
    for d in range(keep.shape[0]):
        at = jnp.bitwise_xor(me, d)
        out = there if d % 2 else here
        out[d // 2] = (keep[at] + got[at]).astype(jnp.bfloat16)


def split(keep, got):
    shape = jax.ShapeDtypeStruct((keep.shape[0] // 2,) + keep.shape[1:], jnp.bfloat16)
    return pl.pallas_call(
        split_kernel,
        out_shape=[shape] * 2,
        in_specs=[IN_VMEM] * 2,
        out_specs=[IN_VMEM] * 2,
        compiler_params=pltpu.CompilerParams(vmem_limit_bytes=8 * MIB),
        name="split",
    )(keep, got)


def pair_kernel(here, came, *outs):
    for d, out in enumerate(outs):
        out[0] = here[d]
        out[1] = came[d]


def pair(here, came):
    shape = jax.ShapeDtypeStruct((2,) + here.shape[1:], here.dtype)
    return pl.pallas_call(
        pair_kernel,
        out_shape=[shape] * here.shape[0],
        in_specs=[IN_VMEM] * 2,
        out_specs=[IN_VMEM] * here.shape[0],
        compiler_params=pltpu.CompilerParams(vmem_limit_bytes=8 * MIB),
        name="pair",
    )(here, came)


def attend_kernel(n, lengths, *refs):
    arrived = refs[: n // 2]
    cosine, sine, keys, values, mine, other, spread, held = refs[n // 2 :]
    _, rows, stripe = arrived[0].shape
    me = lax.axis_index("gx")
    query_cols = stripe - 128
    side = lax.axis_index("gy")
    score_scale = 1.0 / math.sqrt(DH)
    for d in range(n):
        block = arrived[d // 2][d % 2].astype(jnp.float32)
        for r in range(rows):
            spread[r, pl.ds(jnp.bitwise_xor(me, d), 1), :] = block[r : r + 1, :]
    for r in range(rows):
        given = spread[r]
        cos, sin = cosine[r : r + 1, :], sine[r : r + 1, :]

        def turn(a, b):
            turned = jnp.concatenate([a * cos - b * sin, b * cos + a * sin], axis=1)
            return turned.astype(jnp.bfloat16)

        starts = range(0, query_cols, DH)
        q = turn(
            jnp.concatenate([given[:, c : c + DH // 2] for c in starts], axis=0),
            jnp.concatenate([given[:, c + DH // 2 : c + DH] for c in starts], axis=0),
        )
        new = [
            given[i : i + 1, query_cols:] + given[i + 1 : i + 2, query_cols:]
            for i in range(0, n, 2)
        ]
        new_key = turn(new[0], new[1]).astype(jnp.float32)
        new_value = jnp.concatenate(new[2:], axis=1)
        scores = lax.dot_general(q, keys[r], contract, preferred_element_type=jnp.float32)
        scores = scores * score_scale
        place = lax.broadcasted_iota(jnp.int32, scores.shape, 1)
        scores = jnp.where(place < lengths[r], scores, -1e30)
        own_score = jnp.sum(q.astype(jnp.float32) * new_key, axis=1, keepdims=True) * score_scale
        highest = jnp.maximum(jnp.max(scores, axis=1, keepdims=True), own_score)
        weights = jnp.exp(scores - highest)
        own_weight = jnp.exp(own_score - highest)
        totals = jnp.sum(weights, axis=1, keepdims=True) + own_weight
        blended = jnp.dot(
            weights.astype(jnp.bfloat16), values[r], preferred_element_type=jnp.float32
        )
        blended = (blended + own_weight * new_value) / totals
        for j in range(len(starts)):
            block = blended[j * n : (j + 1) * n]
            swapped = pltpu.roll(block, n // 2, 0)
            parts = [jnp.where(side == 0, block, swapped), jnp.where(side == 0, swapped, block)]
            for i in range(n // 2):
                at = (i * len(starts) + j) * DH
                for k, part in enumerate(parts):
                    held[k, r : r + 1, at : at + DH] = part[i : i + 1]
    mine[...] = held[0].astype(jnp.bfloat16)
    other[...] = held[1].astype(jnp.bfloat16)


def attend(lengths, arrived, cosine, sine, keys, values):
    n = 2 * len(arrived)
    _, rows, stripe = arrived[0].shape
    shape = jax.ShapeDtypeStruct((rows, HEADS * DH // 2), jnp.bfloat16)
    return pl.pallas_call(
        lambda *refs: attend_kernel(n, *refs),
        out_shape=[shape, shape],
        in_specs=[IN_SMEM] + [IN_VMEM] * (n // 2 + 4),
        out_specs=[IN_VMEM] * 2,
        scratch_shapes=[
            pltpu.VMEM((rows, n, stripe), jnp.float32),
            pltpu.VMEM((2, rows, HEADS * DH // 2), jnp.float32),
        ],
        compiler_params=pltpu.CompilerParams(vmem_limit_bytes=8 * MIB),
        name="attend",
    )(lengths, *arrived, cosine, sine, in_vmem(keys), in_vmem(values))


def output_kernel(n, *refs):
    shards = refs[: n - 1]
    far = refs[n - 1 : n + 1]
    weights = refs[n + 1 : -4]
    keep, give, total, placed = refs[-4:]
    rows = shards[0].shape[0]
    half = far[0].shape[1]
    for part in range(2):
        start = part * half
        cols = slice(start, start + half)
        x = [ref[:, cols] for ref in shards] + [far[part][...]]
        x = jnp.concatenate([piece.astype(jnp.float32) for piece in x], axis=0)
        x = x.astype(jnp.bfloat16)
        first = 0
        for weight in weights:
            last = first + weight.shape[0]
            if start <= first and last <= start + half:
                term = jnp.dot(
                    x[:, first - start : last - start],
                    weight[...],
                    preferred_element_type=jnp.float32,
                )
                if first == 0:
                    total[...] = term
                else:
                    total[...] += term
            first = last
    side = lax.axis_index("gy")
    for i, owner in enumerate(owners(n)):
        block = total[i * rows : (i + 1) * rows, :]
        placed[owner] = jnp.where(side == 0, block, pltpu.roll(block, rows // 2, 0))
    keep[...] = placed[pl.ds(side * (n // 2), n // 2)]
    give[...] = placed[pl.ds((1 - side) * (n // 2), n // 2)]


def output_project(shards, far, weights):
    n = len(shards) + 1
    rows = shards[0].shape[0]
    cols = weights[0].shape[1]
    shape = jax.ShapeDtypeStruct((n // 2, rows, cols), jnp.float32)
    return pl.pallas_call(
        lambda *refs: output_kernel(n, *refs),
        out_shape=[shape, shape],
        in_specs=[IN_VMEM] * (n + 1 + len(weights)),
        out_specs=[IN_VMEM] * 2,
        scratch_shapes=[
            pltpu.VMEM((n * rows, cols), jnp.float32),
            pltpu.VMEM((n, rows, cols), jnp.float32),
        ],
        compiler_params=pltpu.CompilerParams(vmem_limit_bytes=8 * MIB),
        name="output_project",
    )(*shards, *far, *[in_vmem(w) for w in weights])


def on_any_grid(
    activations,
    norm_gain,
    query_weight,
    keyval_weight,
    output_weight,
    cache_keys,
    cache_values,
    cache_lengths,
):
    inputs = activations.astype(jnp.float32)
    row_sums, square_sums = lax.psum(
        (jnp.sum(inputs, axis=1), jnp.sum(inputs * inputs, axis=1)), "gy"
    )
    row_mean = row_sums[:, None] / D
    row_square = square_sums[:, None] / D
    variance = row_square - row_mean * row_mean
    normed = (
        (inputs - row_mean) * lax.rsqrt(variance + epsilon) * norm_gain.astype(jnp.float32)
    ).astype(jnp.bfloat16)
    shard_rows = lax.all_gather(normed, "gx", axis=0, tiled=True)
    query_part = lax.dot_general(
        shard_rows, query_weight, contract, preferred_element_type=jnp.float32
    )
    keyval_part = lax.dot_general(
        shard_rows, keyval_weight, contract, preferred_element_type=jnp.float32
    )
    partial_sums = jnp.concatenate([query_part, keyval_part], axis=1)
    wide_count = lax.axis_size("gx")
    pair_count = lax.axis_size("gy")
    local_rows = cache_lengths.shape[0]
    stripe = partial_sums.shape[1]
    arrived = lax.all_to_all(partial_sums, ("gx", "gy"), split_axis=0, concat_axis=1, tiled=True)
    gathered = jnp.sum(arrived.reshape(local_rows, wide_count, pair_count, stripe), axis=2).astype(
        jnp.bfloat16
    )
    query_cols = query_weight.shape[0]
    queries = gathered[:, :, :query_cols].reshape(local_rows, HEADS, DH)
    keyvals = gathered[:, :, query_cols:].reshape(local_rows, 2 * DH)
    places = cache_lengths.astype(jnp.float32)
    queries = rotate(queries.astype(jnp.float32), places[:, None, None]).astype(jnp.bfloat16)
    new_keys = rotate(keyvals[:, :DH].astype(jnp.float32), places[:, None]).astype(jnp.bfloat16)
    new_values = keyvals[:, DH:].astype(jnp.float32)
    score_scale = 1.0 / math.sqrt(DH)
    scores = (
        jnp.einsum("rhd,rtd->rht", queries, cache_keys, preferred_element_type=jnp.float32)
        * score_scale
    )
    visible = jnp.arange(cache_keys.shape[1])[None, :] < cache_lengths[:, None]
    scores = jnp.where(visible[:, None, :], scores, -1e30)
    own_score = (
        jnp.einsum("rhd,rd->rh", queries, new_keys, preferred_element_type=jnp.float32)
        * score_scale
    )
    highest = jnp.maximum(jnp.max(scores, axis=2), own_score)
    weights = jnp.exp(scores - highest[:, :, None])
    own_weight = jnp.exp(own_score - highest)
    totals = jnp.sum(weights, axis=2) + own_weight
    blended = jnp.einsum(
        "rht,rtd->rhd",
        weights.astype(jnp.bfloat16),
        cache_values,
        preferred_element_type=jnp.float32,
    )
    blended = blended + own_weight[:, :, None] * new_values[:, None, :]
    attended = (blended / totals[:, :, None]).astype(jnp.bfloat16).reshape(local_rows, HEADS * DH)
    swapped = lax.all_to_all(attended, "gy", split_axis=1, concat_axis=0, tiled=True)
    partial_out = jnp.dot(
        lax.all_gather(swapped, "gx", axis=0, tiled=True),
        output_weight,
        preferred_element_type=jnp.float32,
    )
    return lax.psum_scatter(partial_out, "gy", scatter_dimension=0, tiled=True).astype(jnp.bfloat16)


def on_device(
    activations,
    norm_gain,
    query_weight,
    keyval_weight,
    output_weight,
    cache_keys,
    cache_values,
    cache_lengths,
):
    n = lax.axis_size("gx")
    ring = Ring(n)
    query_cols, width = query_weight.shape
    new_cols = keyval_weight.shape[0]
    piece = query_cols // 4
    weights = []

    indices = jnp.arange(DH // 2, dtype=jnp.float32)
    frequency = jnp.exp(-math.log(10000.0) * indices / (DH // 2))
    angles = cache_lengths.astype(jnp.float32)[:, None] * frequency
    cosine, sine = jnp.cos(angles), jnp.sin(angles)

    def piece_of(array, start, size, after):
        return load(size, [(array, start, size, 0)], after)

    left = right = activations
    shards = [activations]
    for step in range(1, n // 2):
        arrived = shards[-2:] if step > 1 else []
        left, right = ring.step(left, right)
        if step > 1:
            sums = row_sums(arrived, [sums])
        weight = piece_of(query_weight, (step - 1) * piece, piece, arrived)
        if step == 1:
            weight, (own,) = before(weight, activations)
            sums = row_sums([own])
            far_sums = lax.ppermute(sums, "gx", ring.across)
            weight, (left, right, sums) = before(weight, left, right, sums)
        else:
            weight, (left, right) = before(weight, left, right)
        weights.append(weight)
        shards += [left, right]
    cut, (cut_right, left, right) = before(
        left[:, : width // 2], right[:, width // 2 :], left, right
    )
    far = ring.step(cut, cut_right)
    sums = row_sums([left, right], [sums])
    jobs = [(query_weight, 3 * piece, piece, 0), (keyval_weight, 0, new_cols, None)]
    weight = load(piece + 2 * new_cols, jobs, [sums])
    sums = jnp.concatenate([sums, far_sums], axis=0)
    other_sums = swap_pair(sums)
    weight, (other_sums, *far) = before(weight, other_sums, *far)
    weights.append(weight)
    gain = norm_gain.astype(jnp.float32)[None, :]
    piece = output_weight.shape[0] // 4
    keep, give, weight = project(
        (sums, other_sums), gain, shards, far, weights, output_weight, 2 * piece
    )
    weights = [weight]

    here, there = split(keep, swap_pair(give))
    came = lax.ppermute(there, "gx", [(i, i ^ 1) for i in range(n)])
    keys, values = load_caches(cache_keys, cache_values, [there])
    keys, (came,) = before(keys, came)
    blocks = pair(here, came)
    arrived = [blocks[0]]
    for d in range(1, n // 2):
        arrived.append(lax.ppermute(blocks[d], "gx", [(i, i ^ (2 * d)) for i in range(n)]))
    mine, other = attend(cache_lengths, arrived, cosine, sine, keys, values)
    shard = jnp.concatenate([mine, swap_pair(other)], axis=0)

    left = right = shard
    shards = [shard]
    for step in range(1, n // 2):
        arrived = shards[-2:]
        left, right = ring.step(left, right)
        if step <= 2:
            weight = piece_of(output_weight, (1 + step) * piece, piece, arrived)
            weight, (left, right) = before(weight, left, right)
            weights.append(weight)
        shards += [left, right]
    half = shard.shape[1] // 2
    far = ring.step(left[:, :half], right[:, half:])
    keep, give = output_project(shards, far, weights)
    out = (keep + swap_pair(give)).astype(jnp.bfloat16)
    return out.reshape(-1, out.shape[-1])


def solution(mesh):
    return jax.shard_map(
        on_device if mesh.shape["gx"] == 8 else on_any_grid,
        mesh=mesh,
        in_specs=(
            P(("groups", "gx"), "gy"),
            P("gy"),
            P("gx", "gy"),
            P("gx", "gy"),
            P("gy", "gx"),
            P(("groups", "gx", "gy"), None, None),
            P(("groups", "gx", "gy"), None, None),
            P(("groups", "gx", "gy")),
        ),
        out_specs=P(("groups", "gy"), "gx"),
        check_vma=False,
    )
```

```python
import math

import jax
import jax.numpy as jnp
from jax import lax
from jax.experimental import pallas as pl
from jax.experimental.pallas import tpu as pltpu
from jax.sharding import PartitionSpec as P

D = 18432
HEADS = 48
DH = 256


epsilon = 1e-06
contract = (((1,), (1,)), ((), ()))
MIB = 1 << 20
ANY = pl.BlockSpec(memory_space=pl.ANY)
IN_HBM = pl.BlockSpec(memory_space=pltpu.HBM)
IN_VMEM = pl.BlockSpec(memory_space=pltpu.VMEM)
IN_SMEM = pl.BlockSpec(memory_space=pltpu.SMEM)


def rotate(vectors, places):
    half_width = vectors.shape[-1] // 2
    indices = jnp.arange(half_width, dtype=jnp.float32)
    frequency = jnp.exp(-math.log(10000.0) * indices / half_width)
    angles = places * frequency
    cosine = jnp.cos(angles)
    sine = jnp.sin(angles)
    first_half = vectors[..., :half_width]
    second_half = vectors[..., half_width:]
    return jnp.concatenate(
        [first_half * cosine - second_half * sine, second_half * cosine + first_half * sine],
        axis=-1,
    )


def ring_order(n):
    return list(range(0, n, 2)) + list(range(n - 1, 0, -2))


def swap_pair(x):
    return lax.ppermute(x, "gy", [(0, 1), (1, 0)])


class Ring:
    def __init__(self, n):
        order = ring_order(n)
        self.onward = [(order[p], order[(p + 1) % n]) for p in range(n)]
        self.back = [(order[p], order[(p - 1) % n]) for p in range(n)]
        self.across = [(order[p], order[(p + n // 2) % n]) for p in range(n)]

    def step(self, left, right):
        return lax.ppermute(left, "gx", self.onward), lax.ppermute(right, "gx", self.back)


def owners(n):
    offsets = [0]
    for step in range(1, n // 2):
        offsets += [-step, step]
    offsets.append(n // 2)
    me = lax.axis_index("gx")
    half = lax.div(me, 2)
    place = jnp.where(lax.rem(me, 2) == 0, half, n - 1 - half)
    result = []
    for offset in offsets:
        at = lax.rem(place + (offset + n), n)
        result.append(jnp.where(at < n // 2, 2 * at, 2 * (n - 1 - at) + 1))
    return result


def start_copies(source, target, sems, count):
    rows = source.shape[0]
    size = -(-rows // (16 * count)) * 16
    copies = []
    for i, first in enumerate(range(0, rows, size)):
        at = pl.ds(first, min(size, rows - first))
        copy = pltpu.make_async_copy(source.at[at], target.at[at], sems.at[i])
        copy.start()
        copies.append(copy)
    return copies


def load_kernel(jobs, *refs):
    sources, target, sems = refs[: len(jobs)], refs[-2], refs[-1]
    copies = []
    for i, (first, size, at) in enumerate(jobs):
        if at is None:
            at = target.shape[0] - 2 * size
            odd = lax.rem(lax.axis_index("gx"), 2)
            unused = pl.ds(pl.multiple_of(at + (1 - odd) * size, size), size)
            at = pl.multiple_of(at + odd * size, size)
            target[unused, :] = jnp.zeros((size, target.shape[1]), target.dtype)
        part = sources[i].at[pl.ds(first, size)]
        copies += start_copies(part, target.at[pl.ds(at, size)], sems.at[i], 4)
    for copy in copies:
        copy.wait()


def load(rows, jobs, after=()):
    array = jobs[0][0]
    return pl.pallas_call(
        lambda *refs: load_kernel([job[1:] for job in jobs], *refs),
        out_shape=pltpu.VMEM((rows, array.shape[1]), array.dtype),
        in_specs=[IN_HBM] * len(jobs) + [ANY] * len(after),
        out_specs=IN_VMEM,
        scratch_shapes=[pltpu.SemaphoreType.DMA((len(jobs), 4))],
        compiler_params=pltpu.CompilerParams(vmem_limit_bytes=MIB),
        name="load",
    )(*[in_hbm(job[0]) for job in jobs], *after)


def load_cache_kernel(source, *refs):
    target, sems = refs[-2:]
    copies = []
    for row in range(source.shape[0]):
        copies.append(pltpu.make_async_copy(source.at[row], target.at[row], sems.at[row]))
        copies[-1].start()
    for copy in copies:
        copy.wait()


def load_cache(cache, after):
    return pl.pallas_call(
        load_cache_kernel,
        out_shape=pltpu.VMEM(cache.shape, cache.dtype),
        in_specs=[IN_HBM] + [ANY] * len(after),
        out_specs=IN_VMEM,
        scratch_shapes=[pltpu.SemaphoreType.DMA((cache.shape[0],))],
        compiler_params=pltpu.CompilerParams(vmem_limit_bytes=MIB),
        name="load_cache",
    )(in_hbm(cache), *after)


def in_hbm(array):
    return pltpu.with_memory_space_constraint(array, pltpu.HBM)


def in_vmem(array):
    return pltpu.with_memory_space_constraint(array, pltpu.VMEM)


def before(done, *rest):
    held = lax.optimization_barrier((done,) + rest)
    return held[0], held[1:]


def sums_kernel(ready, count, *refs):
    out = refs[-1]
    start = 0
    for ref in refs[:ready]:
        out[start : start + ref.shape[0], :] = ref[...]
        start += ref.shape[0]

    def both_sums(ref):
        x = ref[...].astype(jnp.float32)
        total = jnp.sum(x, axis=1, keepdims=True)
        square = jnp.sum(x * x, axis=1, keepdims=True)
        lane = lax.broadcasted_iota(jnp.int32, (x.shape[0], 128), 1)
        return jnp.where(lane == 0, total, jnp.where(lane == 1, square, 0.0))

    for ref in refs[ready : ready + count]:
        out[start : start + ref.shape[0], :] = both_sums(ref)
        start += ref.shape[0]
    halves = refs[ready + count : -1]
    if halves:
        out[start:, :] = both_sums(halves[0]) + both_sums(halves[1])


def row_sums(shards, ready=(), halves=()):
    rows = sum(a.shape[0] for a in (*ready, *shards, *halves[:1]))
    return pl.pallas_call(
        lambda *refs: sums_kernel(len(ready), len(shards), *refs),
        out_shape=jax.ShapeDtypeStruct((rows, 128), jnp.float32),
        in_specs=[IN_VMEM] * (len(ready) + len(shards) + len(halves)),
        out_specs=IN_VMEM,
        compiler_params=pltpu.CompilerParams(vmem_limit_bytes=8 * MIB),
        name="row_sums",
    )(*ready, *shards, *halves)


def project_kernel(n, parts, *refs):
    sums_a, sums_b, gain = refs[:3]
    shards = refs[3 : 3 + n - 1]
    far = refs[3 + n - 1 : 3 + n + 1]
    weights = refs[4 + n : 4 + n + parts]
    later, keep, give, early, normed, total, sems = refs[4 + n + parts :]
    copies = start_copies(later.at[pl.ds(0, early.shape[0])], early, sems, 4)
    rows, width = shards[0].shape
    sums = sums_a[...] + sums_b[...]
    row_mean = sums[:, :1] / D
    row_square = sums[:, 1:2] / D
    scale = lax.rsqrt(row_square - row_mean * row_mean + epsilon)
    for part in range(2):
        cols = slice(part * width // 2, (part + 1) * width // 2)
        for i in range(0, n, 2):
            x = [ref[:, cols] if ref is not far[part] else ref[...] for ref in (*shards, far[part])]
            x = jnp.concatenate([piece.astype(jnp.float32) for piece in x[i : i + 2]], axis=0)
            at = slice(i * rows, (i + 2) * rows)
            x = (x - row_mean[at]) * scale[at] * gain[:, cols]
            normed[at, cols] = x.astype(jnp.bfloat16)
        x = normed[:, cols]
        start = 0
        for weight in weights:
            term = lax.dot_general(
                x, weight[:, cols], contract, preferred_element_type=jnp.float32
            )
            stripe = slice(start, start + weight.shape[0])
            if part == 0:
                total[:, stripe] = term
            else:
                total[:, stripe] += term
            start = stripe.stop
    side = lax.axis_index("gy")
    local = rows // 2
    for i, owner in enumerate(owners(n)):
        block = total[i * rows : (i + 1) * rows, :]
        low, high = block[:local], block[local:]
        keep[owner] = jnp.where(side == 0, low, high)
        give[owner] = jnp.where(side == 0, high, low)
    for copy in copies:
        copy.wait()


def project(sums, gain, shards, far, weights, later, size):
    n = len(shards) + 1
    rows, width = shards[0].shape
    stripe = sum(w.shape[0] for w in weights)
    shape = jax.ShapeDtypeStruct((n, rows // 2, stripe), jnp.float32)
    return pl.pallas_call(
        lambda *refs: project_kernel(n, len(weights), *refs),
        out_shape=[shape, shape, pltpu.VMEM((size, later.shape[1]), later.dtype)],
        in_specs=[IN_VMEM] * (4 + n + len(weights)) + [IN_HBM],
        out_specs=[IN_VMEM] * 3,
        scratch_shapes=[
            pltpu.VMEM((n * rows, width), jnp.bfloat16),
            pltpu.VMEM((n * rows, stripe), jnp.float32),
            pltpu.SemaphoreType.DMA((4,)),
        ],
        compiler_params=pltpu.CompilerParams(vmem_limit_bytes=6 * MIB),
        name="project",
    )(
        *sums,
        gain,
        *shards,
        *far,
        *[in_vmem(w) for w in weights],
        in_hbm(later),
    )


def split_kernel(keep, got, here, there):
    me = lax.axis_index("gx")
    for d in range(keep.shape[0]):
        at = jnp.bitwise_xor(me, d)
        out = there if d % 2 else here
        out[d // 2] = (keep[at] + got[at]).astype(jnp.bfloat16)


def split(keep, got):
    shape = jax.ShapeDtypeStruct((keep.shape[0] // 2,) + keep.shape[1:], jnp.bfloat16)
    return pl.pallas_call(
        split_kernel,
        out_shape=[shape] * 2,
        in_specs=[IN_VMEM] * 2,
        out_specs=[IN_VMEM] * 2,
        compiler_params=pltpu.CompilerParams(vmem_limit_bytes=8 * MIB),
        name="split",
    )(keep, got)


def pack(picks, *sources):
    def pack_kernel(*refs):
        for k, (i, j) in enumerate(picks):
            refs[-1][k] = refs[i][j]

    return pl.pallas_call(
        pack_kernel,
        out_shape=jax.ShapeDtypeStruct((len(picks),) + sources[0].shape[1:], sources[0].dtype),
        in_specs=[IN_VMEM] * len(sources),
        out_specs=IN_VMEM,
        compiler_params=pltpu.CompilerParams(vmem_limit_bytes=8 * MIB),
        name="pack",
    )(*sources)


ARRIVED = [(0, 0), (1, 0), (2, 0), (2, 1), (3, 0), (3, 1), (3, 2), (3, 3)]


def attend_kernel(lengths, *refs):
    arrived = refs[:4]
    cosine, sine, keys, values, mine, other, spread, held = refs[4:]
    n, rows, stripe = spread.shape[1], spread.shape[0], spread.shape[2]
    me = lax.axis_index("gx")
    query_cols = stripe - 128
    side = lax.axis_index("gy")
    score_scale = 1.0 / math.sqrt(DH)
    for d, (i, j) in enumerate(ARRIVED):
        block = arrived[i][j].astype(jnp.float32)
        for r in range(rows):
            spread[r, pl.ds(jnp.bitwise_xor(me, d), 1), :] = block[r : r + 1, :]
    for r in range(rows):
        given = spread[r]
        cos, sin = cosine[r : r + 1, :], sine[r : r + 1, :]

        def turn(a, b):
            turned = jnp.concatenate([a * cos - b * sin, b * cos + a * sin], axis=1)
            return turned.astype(jnp.bfloat16)

        starts = range(0, query_cols, DH)
        q = turn(
            jnp.concatenate([given[:, c : c + DH // 2] for c in starts], axis=0),
            jnp.concatenate([given[:, c + DH // 2 : c + DH] for c in starts], axis=0),
        )
        new = [
            given[i : i + 1, query_cols:] + given[i + 1 : i + 2, query_cols:]
            for i in range(0, n, 2)
        ]
        new_key = turn(new[0], new[1]).astype(jnp.float32)
        new_value = jnp.concatenate(new[2:], axis=1)
        scores = lax.dot_general(q, keys[r], contract, preferred_element_type=jnp.float32)
        scores = scores * score_scale
        place = lax.broadcasted_iota(jnp.int32, scores.shape, 1)
        scores = jnp.where(place < lengths[r], scores, -1e30)
        own_score = jnp.sum(q.astype(jnp.float32) * new_key, axis=1, keepdims=True) * score_scale
        highest = jnp.maximum(jnp.max(scores, axis=1, keepdims=True), own_score)
        weights = jnp.exp(scores - highest)
        own_weight = jnp.exp(own_score - highest)
        totals = jnp.sum(weights, axis=1, keepdims=True) + own_weight
        blended = jnp.dot(
            weights.astype(jnp.bfloat16), values[r], preferred_element_type=jnp.float32
        )
        blended = (blended + own_weight * new_value) / totals
        for j in range(len(starts)):
            block = blended[j * n : (j + 1) * n]
            swapped = pltpu.roll(block, n // 2, 0)
            parts = [jnp.where(side == 0, block, swapped), jnp.where(side == 0, swapped, block)]
            for i in range(n // 2):
                at = (i * len(starts) + j) * DH
                for k, part in enumerate(parts):
                    held[k, r : r + 1, at : at + DH] = part[i : i + 1]
    mine[...] = held[0].astype(jnp.bfloat16)
    other[...] = held[1].astype(jnp.bfloat16)


def attend(lengths, arrived, cosine, sine, keys, values):
    n = len(ARRIVED)
    _, rows, stripe = arrived[0].shape
    shape = jax.ShapeDtypeStruct((rows, HEADS * DH // 2), jnp.bfloat16)
    return pl.pallas_call(
        attend_kernel,
        out_shape=[shape, shape],
        in_specs=[IN_SMEM] + [IN_VMEM] * 8,
        out_specs=[IN_VMEM] * 2,
        scratch_shapes=[
            pltpu.VMEM((rows, n, stripe), jnp.float32),
            pltpu.VMEM((2, rows, HEADS * DH // 2), jnp.float32),
        ],
        compiler_params=pltpu.CompilerParams(vmem_limit_bytes=8 * MIB),
        name="attend",
    )(lengths, *arrived, cosine, sine, in_vmem(keys), in_vmem(values))


def output_kernel(n, *refs):
    shards = refs[: n - 1]
    far = refs[n - 1 : n + 1]
    weights = refs[n + 1 : -4]
    keep, give, total, placed = refs[-4:]
    rows = shards[0].shape[0]
    half = far[0].shape[1]
    for part in range(2):
        start = part * half
        cols = slice(start, start + half)
        x = [ref[:, cols] for ref in shards] + [far[part][...]]
        x = jnp.concatenate([piece.astype(jnp.float32) for piece in x], axis=0)
        x = x.astype(jnp.bfloat16)
        first = 0
        for weight in weights:
            last = first + weight.shape[0]
            if start <= first and last <= start + half:
                term = jnp.dot(
                    x[:, first - start : last - start],
                    weight[...],
                    preferred_element_type=jnp.float32,
                )
                if first == 0:
                    total[...] = term
                else:
                    total[...] += term
            first = last
    side = lax.axis_index("gy")
    for i, owner in enumerate(owners(n)):
        block = total[i * rows : (i + 1) * rows, :]
        placed[owner] = jnp.where(side == 0, block, pltpu.roll(block, rows // 2, 0))
    keep[...] = placed[pl.ds(side * (n // 2), n // 2)]
    give[...] = placed[pl.ds((1 - side) * (n // 2), n // 2)]


def output_project(shards, far, weights):
    n = len(shards) + 1
    rows = shards[0].shape[0]
    cols = weights[0].shape[1]
    shape = jax.ShapeDtypeStruct((n // 2, rows, cols), jnp.float32)
    return pl.pallas_call(
        lambda *refs: output_kernel(n, *refs),
        out_shape=[shape, shape],
        in_specs=[IN_VMEM] * (n + 1 + len(weights)),
        out_specs=[IN_VMEM] * 2,
        scratch_shapes=[
            pltpu.VMEM((n * rows, cols), jnp.float32),
            pltpu.VMEM((n, rows, cols), jnp.float32),
        ],
        compiler_params=pltpu.CompilerParams(vmem_limit_bytes=8 * MIB),
        name="output_project",
    )(*shards, *far, *[in_vmem(w) for w in weights])


def on_any_grid(
    activations,
    norm_gain,
    query_weight,
    keyval_weight,
    output_weight,
    cache_keys,
    cache_values,
    cache_lengths,
):
    inputs = activations.astype(jnp.float32)
    row_sums, square_sums = lax.psum(
        (jnp.sum(inputs, axis=1), jnp.sum(inputs * inputs, axis=1)), "gy"
    )
    row_mean = row_sums[:, None] / D
    row_square = square_sums[:, None] / D
    variance = row_square - row_mean * row_mean
    normed = (
        (inputs - row_mean) * lax.rsqrt(variance + epsilon) * norm_gain.astype(jnp.float32)
    ).astype(jnp.bfloat16)
    shard_rows = lax.all_gather(normed, "gx", axis=0, tiled=True)
    query_part = lax.dot_general(
        shard_rows, query_weight, contract, preferred_element_type=jnp.float32
    )
    keyval_part = lax.dot_general(
        shard_rows, keyval_weight, contract, preferred_element_type=jnp.float32
    )
    partial_sums = jnp.concatenate([query_part, keyval_part], axis=1)
    wide_count = lax.axis_size("gx")
    pair_count = lax.axis_size("gy")
    local_rows = cache_lengths.shape[0]
    stripe = partial_sums.shape[1]
    arrived = lax.all_to_all(partial_sums, ("gx", "gy"), split_axis=0, concat_axis=1, tiled=True)
    gathered = jnp.sum(arrived.reshape(local_rows, wide_count, pair_count, stripe), axis=2).astype(
        jnp.bfloat16
    )
    query_cols = query_weight.shape[0]
    queries = gathered[:, :, :query_cols].reshape(local_rows, HEADS, DH)
    keyvals = gathered[:, :, query_cols:].reshape(local_rows, 2 * DH)
    places = cache_lengths.astype(jnp.float32)
    queries = rotate(queries.astype(jnp.float32), places[:, None, None]).astype(jnp.bfloat16)
    new_keys = rotate(keyvals[:, :DH].astype(jnp.float32), places[:, None]).astype(jnp.bfloat16)
    new_values = keyvals[:, DH:].astype(jnp.float32)
    score_scale = 1.0 / math.sqrt(DH)
    scores = (
        jnp.einsum("rhd,rtd->rht", queries, cache_keys, preferred_element_type=jnp.float32)
        * score_scale
    )
    visible = jnp.arange(cache_keys.shape[1])[None, :] < cache_lengths[:, None]
    scores = jnp.where(visible[:, None, :], scores, -1e30)
    own_score = (
        jnp.einsum("rhd,rd->rh", queries, new_keys, preferred_element_type=jnp.float32)
        * score_scale
    )
    highest = jnp.maximum(jnp.max(scores, axis=2), own_score)
    weights = jnp.exp(scores - highest[:, :, None])
    own_weight = jnp.exp(own_score - highest)
    totals = jnp.sum(weights, axis=2) + own_weight
    blended = jnp.einsum(
        "rht,rtd->rhd",
        weights.astype(jnp.bfloat16),
        cache_values,
        preferred_element_type=jnp.float32,
    )
    blended = blended + own_weight[:, :, None] * new_values[:, None, :]
    attended = (blended / totals[:, :, None]).astype(jnp.bfloat16).reshape(local_rows, HEADS * DH)
    swapped = lax.all_to_all(attended, "gy", split_axis=1, concat_axis=0, tiled=True)
    partial_out = jnp.dot(
        lax.all_gather(swapped, "gx", axis=0, tiled=True),
        output_weight,
        preferred_element_type=jnp.float32,
    )
    return lax.psum_scatter(partial_out, "gy", scatter_dimension=0, tiled=True).astype(jnp.bfloat16)


def on_device(
    activations,
    norm_gain,
    query_weight,
    keyval_weight,
    output_weight,
    cache_keys,
    cache_values,
    cache_lengths,
):
    n = lax.axis_size("gx")
    ring = Ring(n)
    query_cols, width = query_weight.shape
    new_cols = keyval_weight.shape[0]
    piece = query_cols // 4
    weights = []

    indices = jnp.arange(DH // 2, dtype=jnp.float32)
    frequency = jnp.exp(-math.log(10000.0) * indices / (DH // 2))
    angles = cache_lengths.astype(jnp.float32)[:, None] * frequency
    cosine, sine = jnp.cos(angles), jnp.sin(angles)

    def piece_of(array, start, size, after):
        return load(size, [(array, start, size, 0)], after)

    left = right = activations
    shards = [activations]
    sums = []
    for step in range(1, n // 2):
        arrived = shards[-2:] if step > 1 else []
        left, right = ring.step(left, right)
        if step > 1:
            sums = [row_sums([activations, *arrived] if step == 2 else arrived, sums)]
        weight = piece_of(query_weight, (step - 1) * piece, piece, arrived)
        weight, (left, right, *sums) = before(weight, left, right, *sums)
        weights.append(weight)
        shards += [left, right]
    far = ring.step(left[:, : width // 2], right[:, width // 2 :])
    sums = row_sums([left, right], sums)
    jobs = [(query_weight, 3 * piece, piece, 0), (keyval_weight, 0, new_cols, None)]
    weight = load(piece + 2 * new_cols, jobs, [left, right])
    weight, far = before(weight, *far)
    sums = row_sums([], [sums], far)
    other_sums = swap_pair(sums)
    weights.append(weight)
    gain = norm_gain.astype(jnp.float32)[None, :]
    piece = output_weight.shape[0] // 4
    keep, give, weight = project(
        (sums, other_sums), gain, shards, far, weights, output_weight, 2 * piece
    )
    weights = [weight]

    here, there = split(keep, swap_pair(give))
    def exchange(blocks, bit):
        return lax.ppermute(blocks, "gx", [(i, i ^ bit) for i in range(n)])

    second = exchange(there, 1)
    keys = load_cache(cache_keys, [there])
    keys, (second,) = before(keys, second)
    across = pack([(0, 1), (1, 1), (0, 3), (1, 3)], here, second)
    third = exchange(across, 2)
    values = load_cache(cache_values, [across])
    values, (third,) = before(values, third)
    across = pack([(0, 2), (1, 2), (2, 2), (2, 3)], here, second, third)
    fourth = exchange(across, 4)
    arrived = [here, second, third, fourth]
    mine, other = attend(cache_lengths, arrived, cosine, sine, keys, values)
    shard = jnp.concatenate([mine, swap_pair(other)], axis=0)

    left = right = shard
    shards = [shard]
    done = 2 * piece
    piece = piece // 2

    for step in range(1, n // 2):
        arrived = shards[-2:]
        left, right = ring.step(left, right)
        weight = piece_of(output_weight, done + (step - 1) * piece, piece, arrived)
        weight, (left, right) = before(weight, left, right)
        weights.append(weight)
        shards += [left, right]
    half = shard.shape[1] // 2
    far = ring.step(left[:, :half], right[:, half:])
    weight = piece_of(output_weight, done + 3 * piece, piece, [left, right])
    weight, far = before(weight, *far)
    weights.append(weight)
    keep, give = output_project(shards, far, weights)
    out = (keep + swap_pair(give)).astype(jnp.bfloat16)
    return out.reshape(-1, out.shape[-1])


def solution(mesh):
    return jax.shard_map(
        on_device if mesh.shape["gx"] == 8 else on_any_grid,
        mesh=mesh,
        in_specs=(
            P(("groups", "gx"), "gy"),
            P("gy"),
            P("gx", "gy"),
            P("gx", "gy"),
            P("gy", "gx"),
            P(("groups", "gx", "gy"), None, None),
            P(("groups", "gx", "gy"), None, None),
            P(("groups", "gx", "gy")),
        ),
        out_specs=P(("groups", "gy"), "gx"),
        check_vma=False,
    )
```

```python
import math

import jax
import jax.numpy as jnp
from jax import lax
from jax.experimental import pallas as pl
from jax.experimental.pallas import tpu as pltpu
from jax.sharding import PartitionSpec as P

D = 18432
HEADS = 48
DH = 256


epsilon = 1e-06
contract = (((1,), (1,)), ((), ()))
MIB = 1 << 20
ANY = pl.BlockSpec(memory_space=pl.ANY)
IN_HBM = pl.BlockSpec(memory_space=pltpu.HBM)
IN_VMEM = pl.BlockSpec(memory_space=pltpu.VMEM)
IN_SMEM = pl.BlockSpec(memory_space=pltpu.SMEM)


def rotate(vectors, places):
    half_width = vectors.shape[-1] // 2
    indices = jnp.arange(half_width, dtype=jnp.float32)
    frequency = jnp.exp(-math.log(10000.0) * indices / half_width)
    angles = places * frequency
    cosine = jnp.cos(angles)
    sine = jnp.sin(angles)
    first_half = vectors[..., :half_width]
    second_half = vectors[..., half_width:]
    return jnp.concatenate(
        [first_half * cosine - second_half * sine, second_half * cosine + first_half * sine],
        axis=-1,
    )


def ring_order(n):
    return list(range(0, n, 2)) + list(range(n - 1, 0, -2))


def swap_pair(x):
    return lax.ppermute(x, "gy", [(0, 1), (1, 0)])


class Ring:
    def __init__(self, n):
        order = ring_order(n)
        self.onward = [(order[p], order[(p + 1) % n]) for p in range(n)]
        self.back = [(order[p], order[(p - 1) % n]) for p in range(n)]
        self.across = [(order[p], order[(p + n // 2) % n]) for p in range(n)]

    def step(self, left, right):
        return lax.ppermute(left, "gx", self.onward), lax.ppermute(right, "gx", self.back)


def owners(n):
    offsets = [0]
    for step in range(1, n // 2):
        offsets += [-step, step]
    offsets.append(n // 2)
    me = lax.axis_index("gx")
    half = lax.div(me, 2)
    place = jnp.where(lax.rem(me, 2) == 0, half, n - 1 - half)
    result = []
    for offset in offsets:
        at = lax.rem(place + (offset + n), n)
        result.append(jnp.where(at < n // 2, 2 * at, 2 * (n - 1 - at) + 1))
    return result


def start_copies(source, target, sems, count):
    rows = source.shape[0]
    size = -(-rows // (16 * count)) * 16
    copies = []
    for i, first in enumerate(range(0, rows, size)):
        at = pl.ds(first, min(size, rows - first))
        copy = pltpu.make_async_copy(source.at[at], target.at[at], sems.at[i])
        copy.start()
        copies.append(copy)
    return copies


def load_kernel(jobs, *refs):
    sources, target, sems = refs[: len(jobs)], refs[-2], refs[-1]
    copies = []
    for i, (first, size, at) in enumerate(jobs):
        if at is None:
            at = target.shape[0] - 2 * size
            odd = lax.rem(lax.axis_index("gx"), 2)
            unused = pl.ds(pl.multiple_of(at + (1 - odd) * size, size), size)
            at = pl.multiple_of(at + odd * size, size)
            target[unused, :] = jnp.zeros((size, target.shape[1]), target.dtype)
        part = sources[i].at[pl.ds(first, size)]
        copies += start_copies(part, target.at[pl.ds(at, size)], sems.at[i], 4)
    for copy in copies:
        copy.wait()


def load(rows, jobs, after=()):
    array = jobs[0][0]
    return pl.pallas_call(
        lambda *refs: load_kernel([job[1:] for job in jobs], *refs),
        out_shape=pltpu.VMEM((rows, array.shape[1]), array.dtype),
        in_specs=[IN_HBM] * len(jobs) + [ANY] * len(after),
        out_specs=IN_VMEM,
        scratch_shapes=[pltpu.SemaphoreType.DMA((len(jobs), 4))],
        compiler_params=pltpu.CompilerParams(vmem_limit_bytes=MIB),
        name="load",
    )(*[in_hbm(job[0]) for job in jobs], *after)


def load_cache_kernel(source, *refs):
    target, sems = refs[-2:]
    copies = []
    for row in range(source.shape[0]):
        copies.append(pltpu.make_async_copy(source.at[row], target.at[row], sems.at[row]))
        copies[-1].start()
    for copy in copies:
        copy.wait()


def load_cache(cache, after):
    return pl.pallas_call(
        load_cache_kernel,
        out_shape=pltpu.VMEM(cache.shape, cache.dtype),
        in_specs=[IN_HBM] + [ANY] * len(after),
        out_specs=IN_VMEM,
        scratch_shapes=[pltpu.SemaphoreType.DMA((cache.shape[0],))],
        compiler_params=pltpu.CompilerParams(vmem_limit_bytes=MIB),
        name="load_cache",
    )(in_hbm(cache), *after)


def in_hbm(array):
    return pltpu.with_memory_space_constraint(array, pltpu.HBM)


def in_vmem(array):
    return pltpu.with_memory_space_constraint(array, pltpu.VMEM)


def before(done, *rest):
    held = lax.optimization_barrier((done,) + rest)
    return held[0], held[1:]


def sums_kernel(ready, count, *refs):
    out = refs[-1]
    start = 0
    for ref in refs[:ready]:
        out[start : start + ref.shape[0], :] = ref[...]
        start += ref.shape[0]

    def both_sums(ref):
        x = ref[...].astype(jnp.float32)
        total = jnp.sum(x, axis=1, keepdims=True)
        square = jnp.sum(x * x, axis=1, keepdims=True)
        lane = lax.broadcasted_iota(jnp.int32, (x.shape[0], 128), 1)
        return jnp.where(lane == 0, total, jnp.where(lane == 1, square, 0.0))

    for ref in refs[ready : ready + count]:
        out[start : start + ref.shape[0], :] = both_sums(ref)
        start += ref.shape[0]
    halves = refs[ready + count : -1]
    if halves:
        out[start:, :] = both_sums(halves[0]) + both_sums(halves[1])


def row_sums(shards, ready=(), halves=()):
    rows = sum(a.shape[0] for a in (*ready, *shards, *halves[:1]))
    return pl.pallas_call(
        lambda *refs: sums_kernel(len(ready), len(shards), *refs),
        out_shape=jax.ShapeDtypeStruct((rows, 128), jnp.float32),
        in_specs=[IN_VMEM] * (len(ready) + len(shards) + len(halves)),
        out_specs=IN_VMEM,
        compiler_params=pltpu.CompilerParams(vmem_limit_bytes=8 * MIB),
        name="row_sums",
    )(*ready, *shards, *halves)


def project_kernel(n, parts, *refs):
    sums_a, sums_b, gain = refs[:3]
    shards = refs[3 : 3 + n - 1]
    far = refs[3 + n - 1 : 3 + n + 1]
    weights = refs[4 + n : 4 + n + parts]
    later, keep, give, early, normed, total, sems = refs[4 + n + parts :]
    copies = start_copies(later.at[pl.ds(0, early.shape[0])], early, sems, 4)
    rows, width = shards[0].shape
    sums = sums_a[...] + sums_b[...]
    row_mean = sums[:, :1] / D
    row_square = sums[:, 1:2] / D
    scale = lax.rsqrt(row_square - row_mean * row_mean + epsilon)
    for part in range(2):
        cols = slice(part * width // 2, (part + 1) * width // 2)
        for i in range(0, n, 2):
            x = [ref[:, cols] if ref is not far[part] else ref[...] for ref in (*shards, far[part])]
            x = jnp.concatenate([piece.astype(jnp.float32) for piece in x[i : i + 2]], axis=0)
            at = slice(i * rows, (i + 2) * rows)
            x = (x - row_mean[at]) * scale[at] * gain[:, cols]
            normed[at, cols] = x.astype(jnp.bfloat16)
        x = normed[:, cols]
        start = 0
        for weight in weights:
            term = lax.dot_general(
                x, weight[:, cols], contract, preferred_element_type=jnp.float32
            )
            stripe = slice(start, start + weight.shape[0])
            if part == 0:
                total[:, stripe] = term
            else:
                total[:, stripe] += term
            start = stripe.stop
    side = lax.axis_index("gy")
    local = rows // 2
    for i, owner in enumerate(owners(n)):
        block = total[i * rows : (i + 1) * rows, :]
        low, high = block[:local], block[local:]
        keep[owner] = jnp.where(side == 0, low, high)
        give[owner] = jnp.where(side == 0, high, low)
    for copy in copies:
        copy.wait()


def project(sums, gain, shards, far, weights, later, size):
    n = len(shards) + 1
    rows, width = shards[0].shape
    stripe = sum(w.shape[0] for w in weights)
    shape = jax.ShapeDtypeStruct((n, rows // 2, stripe), jnp.float32)
    return pl.pallas_call(
        lambda *refs: project_kernel(n, len(weights), *refs),
        out_shape=[shape, shape, pltpu.VMEM((size, later.shape[1]), later.dtype)],
        in_specs=[IN_VMEM] * (4 + n + len(weights)) + [IN_HBM],
        out_specs=[IN_VMEM] * 3,
        scratch_shapes=[
            pltpu.VMEM((n * rows, width), jnp.bfloat16),
            pltpu.VMEM((n * rows, stripe), jnp.float32),
            pltpu.SemaphoreType.DMA((4,)),
        ],
        compiler_params=pltpu.CompilerParams(vmem_limit_bytes=6 * MIB),
        name="project",
    )(
        *sums,
        gain,
        *shards,
        *far,
        *[in_vmem(w) for w in weights],
        in_hbm(later),
    )


def split_kernel(keep, got, *outs):
    me = lax.axis_index("gx")
    for d in range(keep.shape[0]):
        at = jnp.bitwise_xor(me, d)
        outs[d % 4][d // 4] = (keep[at] + got[at]).astype(jnp.bfloat16)


def split(keep, got):
    shape = jax.ShapeDtypeStruct((2,) + keep.shape[1:], jnp.bfloat16)
    return pl.pallas_call(
        split_kernel,
        out_shape=[shape] * 4,
        in_specs=[IN_VMEM] * 2,
        out_specs=[IN_VMEM] * 4,
        compiler_params=pltpu.CompilerParams(vmem_limit_bytes=8 * MIB),
        name="split",
    )(keep, got)


def pack(picks, *sources):
    def pack_kernel(*refs):
        for k, (i, j) in enumerate(picks):
            refs[-1][k] = refs[i][j]

    return pl.pallas_call(
        pack_kernel,
        out_shape=jax.ShapeDtypeStruct((len(picks),) + sources[0].shape[1:], sources[0].dtype),
        in_specs=[IN_VMEM] * len(sources),
        out_specs=IN_VMEM,
        compiler_params=pltpu.CompilerParams(vmem_limit_bytes=8 * MIB),
        name="pack",
    )(*sources)


ARRIVED = [(0, 0), (1, 0), (2, 0), (3, 0), (4, 0), (4, 1), (4, 2), (4, 3)]


def attend_kernel(lengths, *refs):
    arrived = refs[:5]
    cosine, sine, keys, values, mine, other, spread, held = refs[5:]
    n, rows, stripe = spread.shape[1], spread.shape[0], spread.shape[2]
    me = lax.axis_index("gx")
    query_cols = stripe - 128
    side = lax.axis_index("gy")
    score_scale = 1.0 / math.sqrt(DH)
    for d, (i, j) in enumerate(ARRIVED):
        block = arrived[i][j].astype(jnp.float32)
        for r in range(rows):
            spread[r, pl.ds(jnp.bitwise_xor(me, d), 1), :] = block[r : r + 1, :]
    for r in range(rows):
        given = spread[r]
        cos, sin = cosine[r : r + 1, :], sine[r : r + 1, :]

        def turn(a, b):
            turned = jnp.concatenate([a * cos - b * sin, b * cos + a * sin], axis=1)
            return turned.astype(jnp.bfloat16)

        starts = range(0, query_cols, DH)
        q = turn(
            jnp.concatenate([given[:, c : c + DH // 2] for c in starts], axis=0),
            jnp.concatenate([given[:, c + DH // 2 : c + DH] for c in starts], axis=0),
        )
        new = [
            given[i : i + 1, query_cols:] + given[i + 1 : i + 2, query_cols:]
            for i in range(0, n, 2)
        ]
        new_key = turn(new[0], new[1]).astype(jnp.float32)
        new_value = jnp.concatenate(new[2:], axis=1)
        scores = lax.dot_general(q, keys[r], contract, preferred_element_type=jnp.float32)
        scores = scores * score_scale
        place = lax.broadcasted_iota(jnp.int32, scores.shape, 1)
        scores = jnp.where(place < lengths[r], scores, -1e30)
        own_score = jnp.sum(q.astype(jnp.float32) * new_key, axis=1, keepdims=True) * score_scale
        highest = jnp.maximum(jnp.max(scores, axis=1, keepdims=True), own_score)
        weights = jnp.exp(scores - highest)
        own_weight = jnp.exp(own_score - highest)
        totals = jnp.sum(weights, axis=1, keepdims=True) + own_weight
        blended = jnp.dot(
            weights.astype(jnp.bfloat16), values[r], preferred_element_type=jnp.float32
        )
        blended = (blended + own_weight * new_value) / totals
        for j in range(len(starts)):
            block = blended[j * n : (j + 1) * n]
            swapped = pltpu.roll(block, n // 2, 0)
            parts = [jnp.where(side == 0, block, swapped), jnp.where(side == 0, swapped, block)]
            for i in range(n // 2):
                at = (i * len(starts) + j) * DH
                for k, part in enumerate(parts):
                    held[k, r : r + 1, at : at + DH] = part[i : i + 1]
    mine[...] = held[0].astype(jnp.bfloat16)
    other[...] = held[1].astype(jnp.bfloat16)


def attend(lengths, arrived, cosine, sine, keys, values):
    n = len(ARRIVED)
    _, rows, stripe = arrived[0].shape
    shape = jax.ShapeDtypeStruct((rows, HEADS * DH // 2), jnp.bfloat16)
    return pl.pallas_call(
        attend_kernel,
        out_shape=[shape, shape],
        in_specs=[IN_SMEM] + [IN_VMEM] * 9,
        out_specs=[IN_VMEM] * 2,
        scratch_shapes=[
            pltpu.VMEM((rows, n, stripe), jnp.float32),
            pltpu.VMEM((2, rows, HEADS * DH // 2), jnp.float32),
        ],
        compiler_params=pltpu.CompilerParams(vmem_limit_bytes=8 * MIB),
        name="attend",
    )(lengths, *arrived, cosine, sine, in_vmem(keys), in_vmem(values))


def output_kernel(n, *refs):
    shards = refs[: n - 1]
    far = refs[n - 1 : n + 1]
    weights = refs[n + 1 : -4]
    keep, give, total, placed = refs[-4:]
    rows = shards[0].shape[0]
    half = far[0].shape[1]
    for part in range(2):
        start = part * half
        cols = slice(start, start + half)
        x = [ref[:, cols] for ref in shards] + [far[part][...]]
        x = jnp.concatenate([piece.astype(jnp.float32) for piece in x], axis=0)
        x = x.astype(jnp.bfloat16)
        first = 0
        for weight in weights:
            last = first + weight.shape[0]
            if start <= first and last <= start + half:
                term = jnp.dot(
                    x[:, first - start : last - start],
                    weight[...],
                    preferred_element_type=jnp.float32,
                )
                if first == 0:
                    total[...] = term
                else:
                    total[...] += term
            first = last
    side = lax.axis_index("gy")
    for i, owner in enumerate(owners(n)):
        block = total[i * rows : (i + 1) * rows, :]
        placed[owner] = jnp.where(side == 0, block, pltpu.roll(block, rows // 2, 0))
    keep[...] = placed[pl.ds(side * (n // 2), n // 2)]
    give[...] = placed[pl.ds((1 - side) * (n // 2), n // 2)]


def output_project(shards, far, weights):
    n = len(shards) + 1
    rows = shards[0].shape[0]
    cols = weights[0].shape[1]
    shape = jax.ShapeDtypeStruct((n // 2, rows, cols), jnp.float32)
    return pl.pallas_call(
        lambda *refs: output_kernel(n, *refs),
        out_shape=[shape, shape],
        in_specs=[IN_VMEM] * (n + 1 + len(weights)),
        out_specs=[IN_VMEM] * 2,
        scratch_shapes=[
            pltpu.VMEM((n * rows, cols), jnp.float32),
            pltpu.VMEM((n, rows, cols), jnp.float32),
        ],
        compiler_params=pltpu.CompilerParams(vmem_limit_bytes=8 * MIB),
        name="output_project",
    )(*shards, *far, *[in_vmem(w) for w in weights])


def on_any_grid(
    activations,
    norm_gain,
    query_weight,
    keyval_weight,
    output_weight,
    cache_keys,
    cache_values,
    cache_lengths,
):
    inputs = activations.astype(jnp.float32)
    row_sums, square_sums = lax.psum(
        (jnp.sum(inputs, axis=1), jnp.sum(inputs * inputs, axis=1)), "gy"
    )
    row_mean = row_sums[:, None] / D
    row_square = square_sums[:, None] / D
    variance = row_square - row_mean * row_mean
    normed = (
        (inputs - row_mean) * lax.rsqrt(variance + epsilon) * norm_gain.astype(jnp.float32)
    ).astype(jnp.bfloat16)
    shard_rows = lax.all_gather(normed, "gx", axis=0, tiled=True)
    query_part = lax.dot_general(
        shard_rows, query_weight, contract, preferred_element_type=jnp.float32
    )
    keyval_part = lax.dot_general(
        shard_rows, keyval_weight, contract, preferred_element_type=jnp.float32
    )
    partial_sums = jnp.concatenate([query_part, keyval_part], axis=1)
    wide_count = lax.axis_size("gx")
    pair_count = lax.axis_size("gy")
    local_rows = cache_lengths.shape[0]
    stripe = partial_sums.shape[1]
    arrived = lax.all_to_all(partial_sums, ("gx", "gy"), split_axis=0, concat_axis=1, tiled=True)
    gathered = jnp.sum(arrived.reshape(local_rows, wide_count, pair_count, stripe), axis=2).astype(
        jnp.bfloat16
    )
    query_cols = query_weight.shape[0]
    queries = gathered[:, :, :query_cols].reshape(local_rows, HEADS, DH)
    keyvals = gathered[:, :, query_cols:].reshape(local_rows, 2 * DH)
    places = cache_lengths.astype(jnp.float32)
    queries = rotate(queries.astype(jnp.float32), places[:, None, None]).astype(jnp.bfloat16)
    new_keys = rotate(keyvals[:, :DH].astype(jnp.float32), places[:, None]).astype(jnp.bfloat16)
    new_values = keyvals[:, DH:].astype(jnp.float32)
    score_scale = 1.0 / math.sqrt(DH)
    scores = (
        jnp.einsum("rhd,rtd->rht", queries, cache_keys, preferred_element_type=jnp.float32)
        * score_scale
    )
    visible = jnp.arange(cache_keys.shape[1])[None, :] < cache_lengths[:, None]
    scores = jnp.where(visible[:, None, :], scores, -1e30)
    own_score = (
        jnp.einsum("rhd,rd->rh", queries, new_keys, preferred_element_type=jnp.float32)
        * score_scale
    )
    highest = jnp.maximum(jnp.max(scores, axis=2), own_score)
    weights = jnp.exp(scores - highest[:, :, None])
    own_weight = jnp.exp(own_score - highest)
    totals = jnp.sum(weights, axis=2) + own_weight
    blended = jnp.einsum(
        "rht,rtd->rhd",
        weights.astype(jnp.bfloat16),
        cache_values,
        preferred_element_type=jnp.float32,
    )
    blended = blended + own_weight[:, :, None] * new_values[:, None, :]
    attended = (blended / totals[:, :, None]).astype(jnp.bfloat16).reshape(local_rows, HEADS * DH)
    swapped = lax.all_to_all(attended, "gy", split_axis=1, concat_axis=0, tiled=True)
    partial_out = jnp.dot(
        lax.all_gather(swapped, "gx", axis=0, tiled=True),
        output_weight,
        preferred_element_type=jnp.float32,
    )
    return lax.psum_scatter(partial_out, "gy", scatter_dimension=0, tiled=True).astype(jnp.bfloat16)


def on_device(
    activations,
    norm_gain,
    query_weight,
    keyval_weight,
    output_weight,
    cache_keys,
    cache_values,
    cache_lengths,
):
    n = lax.axis_size("gx")
    ring = Ring(n)
    query_cols, width = query_weight.shape
    new_cols = keyval_weight.shape[0]
    piece = query_cols // 4
    weights = []

    indices = jnp.arange(DH // 2, dtype=jnp.float32)
    frequency = jnp.exp(-math.log(10000.0) * indices / (DH // 2))
    angles = cache_lengths.astype(jnp.float32)[:, None] * frequency
    cosine, sine = jnp.cos(angles), jnp.sin(angles)

    def piece_of(array, start, size, after):
        return load(size, [(array, start, size, 0)], after)

    left = right = activations
    shards = [activations]
    sums = []
    for step in range(1, n // 2):
        arrived = shards[-2:] if step > 1 else []
        left, right = ring.step(left, right)
        if step > 1:
            sums = [row_sums([activations, *arrived] if step == 2 else arrived, sums)]
        weight = piece_of(query_weight, (step - 1) * piece, piece, arrived)
        weight, (left, right, *sums) = before(weight, left, right, *sums)
        weights.append(weight)
        shards += [left, right]
    far = ring.step(left[:, : width // 2], right[:, width // 2 :])
    sums = row_sums([left, right], sums)
    jobs = [(query_weight, 3 * piece, piece, 0), (keyval_weight, 0, new_cols, None)]
    weight = load(piece + 2 * new_cols, jobs, [left, right])
    weight, far = before(weight, *far)
    sums = row_sums([], [sums], far)
    other_sums = swap_pair(sums)
    weights.append(weight)
    gain = norm_gain.astype(jnp.float32)[None, :]
    piece = output_weight.shape[0] // 4
    keep, give, weight = project(
        (sums, other_sums), gain, shards, far, weights, output_weight, 2 * piece
    )
    weights = [weight]

    def exchange(blocks, d):
        return lax.ppermute(blocks, "gx", [(i, i ^ d) for i in range(n)])

    blocks = split(keep, swap_pair(give))
    arrived = [blocks[0]] + [exchange(blocks[d], d) for d in range(1, 4)]
    keys = load_cache(cache_keys, [blocks[1]])
    keys, arrived = before(keys, *arrived)
    across = pack([(0, 1), (1, 1), (2, 1), (3, 1)], *arrived)
    last = exchange(across, 4)
    values = load_cache(cache_values, [across])
    values, (last,) = before(values, last)
    arrived = [*arrived, last]
    mine, other = attend(cache_lengths, arrived, cosine, sine, keys, values)
    shard = jnp.concatenate([mine, swap_pair(other)], axis=0)

    left = right = shard
    shards = [shard]
    done = 2 * piece
    piece = piece // 2

    for step in range(1, n // 2):
        arrived = shards[-2:]
        left, right = ring.step(left, right)
        weight = piece_of(output_weight, done + (step - 1) * piece, piece, arrived)
        weight, (left, right) = before(weight, left, right)
        weights.append(weight)
        shards += [left, right]
    half = shard.shape[1] // 2
    far = ring.step(left[:, :half], right[:, half:])
    weight = piece_of(output_weight, done + 3 * piece, piece, [left, right])
    weight, far = before(weight, *far)
    weights.append(weight)
    keep, give = output_project(shards, far, weights)
    out = (keep + swap_pair(give)).astype(jnp.bfloat16)
    return out.reshape(-1, out.shape[-1])


def solution(mesh):
    return jax.shard_map(
        on_device if mesh.shape["gx"] == 8 else on_any_grid,
        mesh=mesh,
        in_specs=(
            P(("groups", "gx"), "gy"),
            P("gy"),
            P("gx", "gy"),
            P("gx", "gy"),
            P("gy", "gx"),
            P(("groups", "gx", "gy"), None, None),
            P(("groups", "gx", "gy"), None, None),
            P(("groups", "gx", "gy")),
        ),
        out_specs=P(("groups", "gy"), "gx"),
        check_vma=False,
    )
```

```python
import math

import jax
import jax.numpy as jnp
from jax import lax
from jax.experimental import pallas as pl
from jax.experimental.pallas import tpu as pltpu
from jax.sharding import PartitionSpec as P

D = 18432
HEADS = 48
DH = 256


epsilon = 1e-06
contract = (((1,), (1,)), ((), ()))
MIB = 1 << 20
ANY = pl.BlockSpec(memory_space=pl.ANY)
IN_HBM = pl.BlockSpec(memory_space=pltpu.HBM)
IN_VMEM = pl.BlockSpec(memory_space=pltpu.VMEM)
IN_SMEM = pl.BlockSpec(memory_space=pltpu.SMEM)


def rotate(vectors, places):
    half_width = vectors.shape[-1] // 2
    indices = jnp.arange(half_width, dtype=jnp.float32)
    frequency = jnp.exp(-math.log(10000.0) * indices / half_width)
    angles = places * frequency
    cosine = jnp.cos(angles)
    sine = jnp.sin(angles)
    first_half = vectors[..., :half_width]
    second_half = vectors[..., half_width:]
    return jnp.concatenate(
        [first_half * cosine - second_half * sine, second_half * cosine + first_half * sine],
        axis=-1,
    )


def ring_order(n):
    return list(range(0, n, 2)) + list(range(n - 1, 0, -2))


def swap_pair(x):
    return lax.ppermute(x, "gy", [(0, 1), (1, 0)])


class Ring:
    def __init__(self, n):
        order = ring_order(n)
        self.onward = [(order[p], order[(p + 1) % n]) for p in range(n)]
        self.back = [(order[p], order[(p - 1) % n]) for p in range(n)]
        self.across = [(order[p], order[(p + n // 2) % n]) for p in range(n)]

    def step(self, left, right):
        return lax.ppermute(left, "gx", self.onward), lax.ppermute(right, "gx", self.back)


def owners(n):
    offsets = [0]
    for step in range(1, n // 2):
        offsets += [-step, step]
    offsets.append(n // 2)
    me = lax.axis_index("gx")
    half = lax.div(me, 2)
    place = jnp.where(lax.rem(me, 2) == 0, half, n - 1 - half)
    result = []
    for offset in offsets:
        at = lax.rem(place + (offset + n), n)
        result.append(jnp.where(at < n // 2, 2 * at, 2 * (n - 1 - at) + 1))
    return result


def start_copies(source, target, sems, count):
    rows = source.shape[0]
    size = -(-rows // (16 * count)) * 16
    copies = []
    for i, first in enumerate(range(0, rows, size)):
        at = pl.ds(first, min(size, rows - first))
        copy = pltpu.make_async_copy(source.at[at], target.at[at], sems.at[i])
        copy.start()
        copies.append(copy)
    return copies


def load_kernel(start, source, *refs):
    target, sems = refs[-2:]
    part = source.at[pl.ds(start, target.shape[0])]
    for copy in start_copies(part, target, sems, 4):
        copy.wait()


def load(array, start, size, after):
    return pl.pallas_call(
        lambda *refs: load_kernel(start, *refs),
        out_shape=pltpu.VMEM((size, array.shape[1]), array.dtype),
        in_specs=[IN_HBM] + [ANY] * len(after),
        out_specs=IN_VMEM,
        scratch_shapes=[pltpu.SemaphoreType.DMA((4,))],
        compiler_params=pltpu.CompilerParams(vmem_limit_bytes=MIB),
        name="load",
    )(in_hbm(array), *after)


def load_cache_kernel(source, *refs):
    target, sems = refs[-2:]
    copies = []
    for row in range(source.shape[0]):
        copies.append(pltpu.make_async_copy(source.at[row], target.at[row], sems.at[row]))
        copies[-1].start()
    for copy in copies:
        copy.wait()


def load_cache(cache, after):
    return pl.pallas_call(
        load_cache_kernel,
        out_shape=pltpu.VMEM(cache.shape, cache.dtype),
        in_specs=[IN_HBM] + [ANY] * len(after),
        out_specs=IN_VMEM,
        scratch_shapes=[pltpu.SemaphoreType.DMA((cache.shape[0],))],
        compiler_params=pltpu.CompilerParams(vmem_limit_bytes=MIB),
        name="load_cache",
    )(in_hbm(cache), *after)


def in_hbm(array):
    return pltpu.with_memory_space_constraint(array, pltpu.HBM)


def in_vmem(array):
    return pltpu.with_memory_space_constraint(array, pltpu.VMEM)


def before(done, *rest):
    held = lax.optimization_barrier((done,) + rest)
    return held[0], held[1:]


def sums_kernel(ready, count, *refs):
    out = refs[-1]
    start = 0
    for ref in refs[:ready]:
        out[start : start + ref.shape[0], :] = ref[...]
        start += ref.shape[0]

    def both_sums(ref):
        x = ref[...].astype(jnp.float32)
        total = jnp.sum(x, axis=1, keepdims=True)
        square = jnp.sum(x * x, axis=1, keepdims=True)
        lane = lax.broadcasted_iota(jnp.int32, (x.shape[0], 128), 1)
        return jnp.where(lane == 0, total, jnp.where(lane == 1, square, 0.0))

    for ref in refs[ready : ready + count]:
        out[start : start + ref.shape[0], :] = both_sums(ref)
        start += ref.shape[0]
    halves = refs[ready + count : -1]
    if halves:
        out[start:, :] = both_sums(halves[0]) + both_sums(halves[1])


def row_sums(shards, ready=(), halves=()):
    rows = sum(a.shape[0] for a in (*ready, *shards, *halves[:1]))
    return pl.pallas_call(
        lambda *refs: sums_kernel(len(ready), len(shards), *refs),
        out_shape=jax.ShapeDtypeStruct((rows, 128), jnp.float32),
        in_specs=[IN_VMEM] * (len(ready) + len(shards) + len(halves)),
        out_specs=IN_VMEM,
        compiler_params=pltpu.CompilerParams(vmem_limit_bytes=8 * MIB),
        name="row_sums",
    )(*ready, *shards, *halves)


def project_kernel(n, parts, *refs):
    sums_a, sums_b, gain = refs[:3]
    shards = refs[3 : 3 + n - 1]
    far = refs[3 + n - 1 : 3 + n + 1]
    early = refs[4 + n : 4 + n + parts]
    query_weight, keyval_weight, keep, give, late, normed, total, sems = refs[4 + n + parts :]
    first = sum(w.shape[0] for w in early)
    rest = query_weight.shape[0] - first
    size = keyval_weight.shape[0]
    odd = lax.rem(lax.axis_index("gx"), 2)
    at = pl.multiple_of(rest + odd * size, size)
    copies = start_copies(query_weight.at[pl.ds(first, rest)], late.at[pl.ds(0, rest)], sems.at[0], 4)
    copies += start_copies(keyval_weight, late.at[pl.ds(at, size)], sems.at[1], 1)
    unused = pl.ds(pl.multiple_of(rest + (1 - odd) * size, size), size)
    late[unused, :] = jnp.zeros((size, late.shape[1]), late.dtype)
    rows, width = shards[0].shape
    sums = sums_a[...] + sums_b[...]
    row_mean = sums[:, :1] / D
    row_square = sums[:, 1:2] / D
    scale = lax.rsqrt(row_square - row_mean * row_mean + epsilon)

    def multiply(weight, part, start):
        cols = slice(part * width // 2, (part + 1) * width // 2)
        term = lax.dot_general(
            normed[:, cols], weight[:, cols], contract, preferred_element_type=jnp.float32
        )
        stripe = slice(start, start + weight.shape[0])
        if part == 0:
            total[:, stripe] = term
        else:
            total[:, stripe] += term
        return stripe.stop

    for part in range(2):
        cols = slice(part * width // 2, (part + 1) * width // 2)
        for i in range(0, n, 2):
            x = [ref[:, cols] if ref is not far[part] else ref[...] for ref in (*shards, far[part])]
            x = jnp.concatenate([piece.astype(jnp.float32) for piece in x[i : i + 2]], axis=0)
            at = slice(i * rows, (i + 2) * rows)
            x = (x - row_mean[at]) * scale[at] * gain[:, cols]
            normed[at, cols] = x.astype(jnp.bfloat16)
        start = 0
        for weight in early:
            start = multiply(weight, part, start)
    for copy in copies:
        copy.wait()
    for part in range(2):
        multiply(late, part, first)
    side = lax.axis_index("gy")
    local = rows // 2
    for i, owner in enumerate(owners(n)):
        block = total[i * rows : (i + 1) * rows, :]
        low, high = block[:local], block[local:]
        keep[owner] = jnp.where(side == 0, low, high)
        give[owner] = jnp.where(side == 0, high, low)


def project(sums, gain, shards, far, early, query_weight, keyval_weight):
    n = len(shards) + 1
    rows, width = shards[0].shape
    stripe = query_weight.shape[0] + 2 * keyval_weight.shape[0]
    late = stripe - sum(w.shape[0] for w in early)
    shape = jax.ShapeDtypeStruct((n, rows // 2, stripe), jnp.float32)
    return pl.pallas_call(
        lambda *refs: project_kernel(n, len(early), *refs),
        out_shape=[shape, shape],
        in_specs=[IN_VMEM] * (4 + n + len(early)) + [IN_HBM] * 2,
        out_specs=[IN_VMEM] * 2,
        scratch_shapes=[
            pltpu.VMEM((late, width), jnp.bfloat16),
            pltpu.VMEM((n * rows, width), jnp.bfloat16),
            pltpu.VMEM((n * rows, stripe), jnp.float32),
            pltpu.SemaphoreType.DMA((2, 4)),
        ],
        compiler_params=pltpu.CompilerParams(vmem_limit_bytes=20 * MIB),
        name="project",
    )(
        *sums,
        gain,
        *shards,
        *far,
        *[in_vmem(w) for w in early],
        in_hbm(query_weight),
        in_hbm(keyval_weight),
    )


def split_kernel(keep, got, *outs):
    me = lax.axis_index("gx")
    for d in range(keep.shape[0]):
        at = jnp.bitwise_xor(me, d)
        outs[d % 4][d // 4] = (keep[at] + got[at]).astype(jnp.bfloat16)


def split(keep, got):
    shape = jax.ShapeDtypeStruct((2,) + keep.shape[1:], jnp.bfloat16)
    return pl.pallas_call(
        split_kernel,
        out_shape=[shape] * 4,
        in_specs=[IN_VMEM] * 2,
        out_specs=[IN_VMEM] * 4,
        compiler_params=pltpu.CompilerParams(vmem_limit_bytes=8 * MIB),
        name="split",
    )(keep, got)


def pack(picks, *sources):
    def pack_kernel(*refs):
        for k, (i, j) in enumerate(picks):
            refs[-1][k] = refs[i][j]

    return pl.pallas_call(
        pack_kernel,
        out_shape=jax.ShapeDtypeStruct((len(picks),) + sources[0].shape[1:], sources[0].dtype),
        in_specs=[IN_VMEM] * len(sources),
        out_specs=IN_VMEM,
        compiler_params=pltpu.CompilerParams(vmem_limit_bytes=8 * MIB),
        name="pack",
    )(*sources)


ARRIVED = [(0, 0), (1, 0), (2, 0), (3, 0), (4, 0), (4, 1), (4, 2), (4, 3)]


def attend_kernel(first, lengths, *refs):
    arrived = refs[:5]
    cosine, sine, keys, values, later, mine, other, copied, spread, held, sems = refs[5:]
    copies = start_copies(later.at[pl.ds(first, copied.shape[0])], copied, sems, 4)
    n, rows, stripe = spread.shape[1], spread.shape[0], spread.shape[2]
    me = lax.axis_index("gx")
    query_cols = stripe - 128
    side = lax.axis_index("gy")
    score_scale = 1.0 / math.sqrt(DH)
    for d, (i, j) in enumerate(ARRIVED):
        block = arrived[i][j].astype(jnp.float32)
        for r in range(rows):
            spread[r, pl.ds(jnp.bitwise_xor(me, d), 1), :] = block[r : r + 1, :]
    for r in range(rows):
        given = spread[r]
        cos, sin = cosine[r : r + 1, :], sine[r : r + 1, :]

        def turn(a, b):
            turned = jnp.concatenate([a * cos - b * sin, b * cos + a * sin], axis=1)
            return turned.astype(jnp.bfloat16)

        starts = range(0, query_cols, DH)
        q = turn(
            jnp.concatenate([given[:, c : c + DH // 2] for c in starts], axis=0),
            jnp.concatenate([given[:, c + DH // 2 : c + DH] for c in starts], axis=0),
        )
        new = [
            given[i : i + 1, query_cols:] + given[i + 1 : i + 2, query_cols:]
            for i in range(0, n, 2)
        ]
        new_key = turn(new[0], new[1]).astype(jnp.float32)
        new_value = jnp.concatenate(new[2:], axis=1)
        scores = lax.dot_general(q, keys[r], contract, preferred_element_type=jnp.float32)
        scores = scores * score_scale
        place = lax.broadcasted_iota(jnp.int32, scores.shape, 1)
        scores = jnp.where(place < lengths[r], scores, -1e30)
        own_score = jnp.sum(q.astype(jnp.float32) * new_key, axis=1, keepdims=True) * score_scale
        highest = jnp.maximum(jnp.max(scores, axis=1, keepdims=True), own_score)
        weights = jnp.exp(scores - highest)
        own_weight = jnp.exp(own_score - highest)
        totals = jnp.sum(weights, axis=1, keepdims=True) + own_weight
        blended = jnp.dot(
            weights.astype(jnp.bfloat16), values[r], preferred_element_type=jnp.float32
        )
        blended = (blended + own_weight * new_value) / totals
        for j in range(len(starts)):
            block = blended[j * n : (j + 1) * n]
            swapped = pltpu.roll(block, n // 2, 0)
            parts = [jnp.where(side == 0, block, swapped), jnp.where(side == 0, swapped, block)]
            for i in range(n // 2):
                at = (i * len(starts) + j) * DH
                for k, part in enumerate(parts):
                    held[k, r : r + 1, at : at + DH] = part[i : i + 1]
    mine[...] = held[0].astype(jnp.bfloat16)
    other[...] = held[1].astype(jnp.bfloat16)
    for copy in copies:
        copy.wait()


def attend(lengths, arrived, cosine, sine, keys, values, later, first, size):
    n = len(ARRIVED)
    _, rows, stripe = arrived[0].shape
    shape = jax.ShapeDtypeStruct((rows, HEADS * DH // 2), jnp.bfloat16)
    return pl.pallas_call(
        lambda *refs: attend_kernel(first, *refs),
        out_shape=[shape, shape, pltpu.VMEM((size, later.shape[1]), later.dtype)],
        in_specs=[IN_SMEM] + [IN_VMEM] * 9 + [IN_HBM],
        out_specs=[IN_VMEM] * 3,
        scratch_shapes=[
            pltpu.VMEM((rows, n, stripe), jnp.float32),
            pltpu.VMEM((2, rows, HEADS * DH // 2), jnp.float32),
            pltpu.SemaphoreType.DMA((4,)),
        ],
        compiler_params=pltpu.CompilerParams(vmem_limit_bytes=8 * MIB),
        name="attend",
    )(lengths, *arrived, cosine, sine, in_vmem(keys), in_vmem(values), in_hbm(later))


def output_kernel(n, *refs):
    shards = refs[: n - 1]
    far = refs[n - 1 : n + 1]
    weights = refs[n + 1 : -4]
    keep, give, total, placed = refs[-4:]
    rows = shards[0].shape[0]
    half = far[0].shape[1]
    for part in range(2):
        start = part * half
        cols = slice(start, start + half)
        x = [ref[:, cols] for ref in shards] + [far[part][...]]
        x = jnp.concatenate([piece.astype(jnp.float32) for piece in x], axis=0)
        x = x.astype(jnp.bfloat16)
        first = 0
        for weight in weights:
            last = first + weight.shape[0]
            low, high = max(first, start), min(last, start + half)
            if low < high:
                term = jnp.dot(
                    x[:, low - start : high - start],
                    weight[low - first : high - first, :],
                    preferred_element_type=jnp.float32,
                )
                if low == 0:
                    total[...] = term
                else:
                    total[...] += term
            first = last
    side = lax.axis_index("gy")
    for i, owner in enumerate(owners(n)):
        block = total[i * rows : (i + 1) * rows, :]
        placed[owner] = jnp.where(side == 0, block, pltpu.roll(block, rows // 2, 0))
    keep[...] = placed[pl.ds(side * (n // 2), n // 2)]
    give[...] = placed[pl.ds((1 - side) * (n // 2), n // 2)]


def output_project(shards, far, weights):
    n = len(shards) + 1
    rows = shards[0].shape[0]
    cols = weights[0].shape[1]
    shape = jax.ShapeDtypeStruct((n // 2, rows, cols), jnp.float32)
    return pl.pallas_call(
        lambda *refs: output_kernel(n, *refs),
        out_shape=[shape, shape],
        in_specs=[IN_VMEM] * (n + 1 + len(weights)),
        out_specs=[IN_VMEM] * 2,
        scratch_shapes=[
            pltpu.VMEM((n * rows, cols), jnp.float32),
            pltpu.VMEM((n, rows, cols), jnp.float32),
        ],
        compiler_params=pltpu.CompilerParams(vmem_limit_bytes=8 * MIB),
        name="output_project",
    )(*shards, *far, *[in_vmem(w) for w in weights])


def on_any_grid(
    activations,
    norm_gain,
    query_weight,
    keyval_weight,
    output_weight,
    cache_keys,
    cache_values,
    cache_lengths,
):
    inputs = activations.astype(jnp.float32)
    row_sums, square_sums = lax.psum(
        (jnp.sum(inputs, axis=1), jnp.sum(inputs * inputs, axis=1)), "gy"
    )
    row_mean = row_sums[:, None] / D
    row_square = square_sums[:, None] / D
    variance = row_square - row_mean * row_mean
    normed = (
        (inputs - row_mean) * lax.rsqrt(variance + epsilon) * norm_gain.astype(jnp.float32)
    ).astype(jnp.bfloat16)
    shard_rows = lax.all_gather(normed, "gx", axis=0, tiled=True)
    query_part = lax.dot_general(
        shard_rows, query_weight, contract, preferred_element_type=jnp.float32
    )
    keyval_part = lax.dot_general(
        shard_rows, keyval_weight, contract, preferred_element_type=jnp.float32
    )
    partial_sums = jnp.concatenate([query_part, keyval_part], axis=1)
    wide_count = lax.axis_size("gx")
    pair_count = lax.axis_size("gy")
    local_rows = cache_lengths.shape[0]
    stripe = partial_sums.shape[1]
    arrived = lax.all_to_all(partial_sums, ("gx", "gy"), split_axis=0, concat_axis=1, tiled=True)
    gathered = jnp.sum(arrived.reshape(local_rows, wide_count, pair_count, stripe), axis=2).astype(
        jnp.bfloat16
    )
    query_cols = query_weight.shape[0]
    queries = gathered[:, :, :query_cols].reshape(local_rows, HEADS, DH)
    keyvals = gathered[:, :, query_cols:].reshape(local_rows, 2 * DH)
    places = cache_lengths.astype(jnp.float32)
    queries = rotate(queries.astype(jnp.float32), places[:, None, None]).astype(jnp.bfloat16)
    new_keys = rotate(keyvals[:, :DH].astype(jnp.float32), places[:, None]).astype(jnp.bfloat16)
    new_values = keyvals[:, DH:].astype(jnp.float32)
    score_scale = 1.0 / math.sqrt(DH)
    scores = (
        jnp.einsum("rhd,rtd->rht", queries, cache_keys, preferred_element_type=jnp.float32)
        * score_scale
    )
    visible = jnp.arange(cache_keys.shape[1])[None, :] < cache_lengths[:, None]
    scores = jnp.where(visible[:, None, :], scores, -1e30)
    own_score = (
        jnp.einsum("rhd,rd->rh", queries, new_keys, preferred_element_type=jnp.float32)
        * score_scale
    )
    highest = jnp.maximum(jnp.max(scores, axis=2), own_score)
    weights = jnp.exp(scores - highest[:, :, None])
    own_weight = jnp.exp(own_score - highest)
    totals = jnp.sum(weights, axis=2) + own_weight
    blended = jnp.einsum(
        "rht,rtd->rhd",
        weights.astype(jnp.bfloat16),
        cache_values,
        preferred_element_type=jnp.float32,
    )
    blended = blended + own_weight[:, :, None] * new_values[:, None, :]
    attended = (blended / totals[:, :, None]).astype(jnp.bfloat16).reshape(local_rows, HEADS * DH)
    swapped = lax.all_to_all(attended, "gy", split_axis=1, concat_axis=0, tiled=True)
    partial_out = jnp.dot(
        lax.all_gather(swapped, "gx", axis=0, tiled=True),
        output_weight,
        preferred_element_type=jnp.float32,
    )
    return lax.psum_scatter(partial_out, "gy", scatter_dimension=0, tiled=True).astype(jnp.bfloat16)


def on_device(
    activations,
    norm_gain,
    query_weight,
    keyval_weight,
    output_weight,
    cache_keys,
    cache_values,
    cache_lengths,
):
    n = lax.axis_size("gx")
    ring = Ring(n)
    query_cols, width = query_weight.shape
    piece = query_cols // 6
    weights = []

    indices = jnp.arange(DH // 2, dtype=jnp.float32)
    frequency = jnp.exp(-math.log(10000.0) * indices / (DH // 2))
    angles = cache_lengths.astype(jnp.float32)[:, None] * frequency
    cosine, sine = jnp.cos(angles), jnp.sin(angles)

    left = right = activations
    shards = [activations]
    sums = []
    for step in range(1, n // 2):
        arrived = shards[-2:] if step > 1 else []
        left, right = ring.step(left, right)
        if step > 1:
            sums = [row_sums([activations, *arrived] if step == 2 else arrived, sums)]
        weight = load(query_weight, (step - 1) * piece, piece, arrived)
        weight, (left, right, *sums) = before(weight, left, right, *sums)
        weights.append(weight)
        shards += [left, right]
    far = ring.step(left[:, : width // 2], right[:, width // 2 :])
    sums = row_sums([left, right], sums)
    weight = load(query_weight, 3 * piece, piece, [left, right])
    weight, far = before(weight, *far)
    sums = row_sums([], [sums], far)
    other_sums = swap_pair(sums)
    weights.append(weight)
    gain = norm_gain.astype(jnp.float32)[None, :]
    keep, give = project(
        (sums, other_sums), gain, shards, far, weights, query_weight, keyval_weight
    )

    def exchange(blocks, d):
        return lax.ppermute(blocks, "gx", [(i, i ^ d) for i in range(n)])

    blocks = split(keep, swap_pair(give))
    arrived = [blocks[0]] + [exchange(blocks[d], d) for d in range(1, 4)]
    keys = load_cache(cache_keys, [blocks[1]])
    keys, arrived = before(keys, *arrived)
    across = pack([(0, 1), (1, 1), (2, 1), (3, 1)], *arrived)
    last = exchange(across, 4)
    values = load_cache(cache_values, [across])
    unit = output_weight.shape[0] // 48
    sizes = [8 * unit, 12 * unit] + [7 * unit] * 4
    starts = [sum(sizes[:i]) for i in range(len(sizes))]
    weight = load(output_weight, starts[0], sizes[0], [across])
    values, (last,) = before(values, last)
    weight, (last,) = before(weight, last)
    arrived = [*arrived, last]
    mine, other, copied = attend(
        cache_lengths, arrived, cosine, sine, keys, values, output_weight, starts[1], sizes[1]
    )
    weights = [weight, copied]
    shard = jnp.concatenate([mine, swap_pair(other)], axis=0)

    left = right = shard
    shards = [shard]
    for step in range(1, n // 2):
        arrived = shards[-2:]
        left, right = ring.step(left, right)
        weight = load(output_weight, starts[1 + step], sizes[1 + step], arrived)
        weight, (left, right) = before(weight, left, right)
        weights.append(weight)
        shards += [left, right]
    half = shard.shape[1] // 2
    far = ring.step(left[:, :half], right[:, half:])
    weight = load(output_weight, starts[-1], sizes[-1], [left, right])
    weight, far = before(weight, *far)
    weights.append(weight)
    keep, give = output_project(shards, far, weights)
    out = (keep + swap_pair(give)).astype(jnp.bfloat16)
    return out.reshape(-1, out.shape[-1])


def solution(mesh):
    return jax.shard_map(
        on_device if mesh.shape["gx"] == 8 else on_any_grid,
        mesh=mesh,
        in_specs=(
            P(("groups", "gx"), "gy"),
            P("gy"),
            P("gx", "gy"),
            P("gx", "gy"),
            P("gy", "gx"),
            P(("groups", "gx", "gy"), None, None),
            P(("groups", "gx", "gy"), None, None),
            P(("groups", "gx", "gy")),
        ),
        out_specs=P(("groups", "gy"), "gx"),
        check_vma=False,
    )
```

```python
import math

import jax
import jax.numpy as jnp
from jax import lax
from jax.experimental import pallas as pl
from jax.experimental.pallas import tpu as pltpu
from jax.sharding import PartitionSpec as P

D = 18432
HEADS = 48
DH = 256


epsilon = 1e-06
contract = (((1,), (1,)), ((), ()))
MIB = 1 << 20
ANY = pl.BlockSpec(memory_space=pl.ANY)
IN_HBM = pl.BlockSpec(memory_space=pltpu.HBM)
IN_VMEM = pl.BlockSpec(memory_space=pltpu.VMEM)
IN_SMEM = pl.BlockSpec(memory_space=pltpu.SMEM)


def rotate(vectors, places):
    half_width = vectors.shape[-1] // 2
    indices = jnp.arange(half_width, dtype=jnp.float32)
    frequency = jnp.exp(-math.log(10000.0) * indices / half_width)
    angles = places * frequency
    cosine = jnp.cos(angles)
    sine = jnp.sin(angles)
    first_half = vectors[..., :half_width]
    second_half = vectors[..., half_width:]
    return jnp.concatenate(
        [first_half * cosine - second_half * sine, second_half * cosine + first_half * sine],
        axis=-1,
    )


def ring_order(n):
    return list(range(0, n, 2)) + list(range(n - 1, 0, -2))


def swap_pair(x):
    return lax.ppermute(x, "gy", [(0, 1), (1, 0)])


def ring_move(x):
    n = lax.axis_size("gx")
    order = ring_order(n)
    onward = [(2 * order[p], 2 * order[(p + 1) % n]) for p in range(n)]
    back = [(2 * order[p] + 1, 2 * order[(p - 1) % n] + 1) for p in range(n)]
    return lax.ppermute(x, ("gx", "gy"), onward + back)


def owners(n):
    steps = n // 2 - 1
    me, side = lax.axis_index("gx"), lax.axis_index("gy")
    half = lax.div(me, 2)
    place = jnp.where(lax.rem(me, 2) == 0, half, n - 1 - half)
    ahead = 2 * side - 1
    offsets = [0 * ahead]
    offsets += [ahead * step for step in range(1, steps + 1)]
    offsets += [-ahead * step for step in range(1, steps + 1)]
    offsets.append(0 * ahead + n // 2)
    result = []
    for offset in offsets:
        at = lax.rem(place + offset + n, n)
        result.append(jnp.where(at < n // 2, 2 * at, 2 * (n - 1 - at) + 1))
    return result


def start_copies(source, target, sems, count):
    rows = source.shape[0]
    size = -(-rows // (16 * count)) * 16
    copies = []
    for i, first in enumerate(range(0, rows, size)):
        at = pl.ds(first, min(size, rows - first))
        copy = pltpu.make_async_copy(source.at[at], target.at[at], sems.at[i])
        copy.start()
        copies.append(copy)
    return copies


def load_kernel(jobs, *refs):
    sources, target, sems = refs[: len(jobs)], refs[-2], refs[-1]
    copies = []
    for i, (first, size, at) in enumerate(jobs):
        if at is None:
            at = target.shape[0] - 2 * size
            odd = lax.rem(lax.axis_index("gx"), 2)
            unused = pl.ds(pl.multiple_of(at + (1 - odd) * size, size), size)
            at = pl.multiple_of(at + odd * size, size)
            target[unused, :] = jnp.zeros((size, target.shape[1]), target.dtype)
        part = sources[i].at[pl.ds(first, size)]
        copies += start_copies(part, target.at[pl.ds(at, size)], sems.at[i], 4)
    for copy in copies:
        copy.wait()


def load(rows, jobs, after=()):
    array = jobs[0][0]
    return pl.pallas_call(
        lambda *refs: load_kernel([job[1:] for job in jobs], *refs),
        out_shape=pltpu.VMEM((rows, array.shape[1]), array.dtype),
        in_specs=[IN_HBM] * len(jobs) + [ANY] * len(after),
        out_specs=IN_VMEM,
        scratch_shapes=[pltpu.SemaphoreType.DMA((len(jobs), 4))],
        compiler_params=pltpu.CompilerParams(vmem_limit_bytes=MIB),
        name="load",
    )(*[in_hbm(job[0]) for job in jobs], *after)


def load_cache_kernel(source, *refs):
    target, sems = refs[-2:]
    copies = []
    for row in range(source.shape[0]):
        copies.append(pltpu.make_async_copy(source.at[row], target.at[row], sems.at[row]))
        copies[-1].start()
    for copy in copies:
        copy.wait()


def load_cache(cache, after):
    return pl.pallas_call(
        load_cache_kernel,
        out_shape=pltpu.VMEM(cache.shape, cache.dtype),
        in_specs=[IN_HBM] + [ANY] * len(after),
        out_specs=IN_VMEM,
        scratch_shapes=[pltpu.SemaphoreType.DMA((cache.shape[0],))],
        compiler_params=pltpu.CompilerParams(vmem_limit_bytes=MIB),
        name="load_cache",
    )(in_hbm(cache), *after)


def in_hbm(array):
    return pltpu.with_memory_space_constraint(array, pltpu.HBM)


def in_vmem(array):
    return pltpu.with_memory_space_constraint(array, pltpu.VMEM)


def before(done, *rest):
    held = lax.optimization_barrier((done,) + rest)
    return held[0], held[1:]


def both_sums(x):
    rows = x.shape[0] // 2
    total = jnp.sum(x, axis=1, keepdims=True)
    square = jnp.sum(x * x, axis=1, keepdims=True)
    total = total[:rows] + total[rows:]
    square = square[:rows] + square[rows:]
    lane = lax.broadcasted_iota(jnp.int32, (rows, 128), 1)
    return jnp.where(lane == 0, total, jnp.where(lane == 1, square, 0.0))


def sums_kernel(shard, *refs):
    out = refs[-1]
    start = 0
    for ref in refs[:-1]:
        out[start : start + ref.shape[0], :] = ref[...]
        start += ref.shape[0]
    out[start:, :] = both_sums(shard[...].astype(jnp.float32))


def row_sums(shard, ready):
    rows = shard.shape[0] // 2 + sum(a.shape[0] for a in ready)
    return pl.pallas_call(
        sums_kernel,
        out_shape=jax.ShapeDtypeStruct((rows, 128), jnp.float32),
        in_specs=[IN_VMEM] * (1 + len(ready)),
        out_specs=IN_VMEM,
        compiler_params=pltpu.CompilerParams(vmem_limit_bytes=8 * MIB),
        name="row_sums",
    )(shard, *ready)


def last_kernel(shard, ready, payload, sums):
    rows, width = shard.shape[0] // 2, shard.shape[1]
    x = shard[...].astype(jnp.float32)
    new = both_sums(x)
    first = ready.shape[0]
    sums[:first, :] = ready[...]
    sums[first:, :] = new
    payload[:, :width] = x[:rows].astype(jnp.bfloat16)
    lane = lax.broadcasted_iota(jnp.int32, (rows, 128), 1)
    value = jnp.where(lane < 3, new[:, :1], new[:, 1:2])
    high = value.astype(jnp.bfloat16).astype(jnp.float32)
    middle = (value - high).astype(jnp.bfloat16).astype(jnp.float32)
    low = value - high - middle
    part = jnp.where(lane % 3 == 0, high, jnp.where(lane % 3 == 1, middle, low))
    payload[:, width:] = part.astype(jnp.bfloat16)


def last_payload(shard, ready):
    rows, width = shard.shape[0] // 2, shard.shape[1]
    return pl.pallas_call(
        last_kernel,
        out_shape=[
            jax.ShapeDtypeStruct((rows, width + 128), jnp.bfloat16),
            jax.ShapeDtypeStruct((ready.shape[0] + rows, 128), jnp.float32),
        ],
        in_specs=[IN_VMEM] * 2,
        out_specs=[IN_VMEM] * 2,
        compiler_params=pltpu.CompilerParams(vmem_limit_bytes=8 * MIB),
        name="last_payload",
    )(shard, ready)


def project_kernel(n, parts, *refs):
    sums_here, sums_there, gain = refs[:3]
    shards = refs[3 : 3 + n]
    weights = refs[3 + n : 3 + n + parts]
    later, keep, give, early, normed, total, sems = refs[3 + n + parts :]
    copies = start_copies(later.at[pl.ds(0, early.shape[0])], early, sems, 4)
    rows, width = shards[0].shape
    beside = shards[-1][:, width:].astype(jnp.float32)
    far_total = beside[:, 0:1] + beside[:, 1:2] + beside[:, 2:3]
    far_square = beside[:, 3:4] + beside[:, 4:5] + beside[:, 5:6]
    here, there = sums_here[...], sums_there[...]
    row_mean = jnp.concatenate([here[:, :1], there[rows:, :1], far_total], axis=0) / D
    row_square = jnp.concatenate([here[:, 1:2], there[rows:, 1:2], far_square], axis=0) / D
    scale = lax.rsqrt(row_square - row_mean * row_mean + epsilon)
    for part in range(2):
        cols = slice(part * width // 2, (part + 1) * width // 2)
        for i in range(0, n, 2):
            x = [ref[:, cols].astype(jnp.float32)[:rows] for ref in shards[i : i + 2]]
            x = jnp.concatenate(x, axis=0)
            at = slice(i * rows, (i + 2) * rows)
            x = (x - row_mean[at]) * scale[at] * gain[:, cols]
            normed[at, cols] = x.astype(jnp.bfloat16)
        x = normed[:, cols]
        start = 0
        for weight in weights:
            term = lax.dot_general(
                x, weight[:, cols], contract, preferred_element_type=jnp.float32
            )
            stripe = slice(start, start + weight.shape[0])
            if part == 0:
                total[:, stripe] = term
            else:
                total[:, stripe] += term
            start = stripe.stop
    side = lax.axis_index("gy")
    local = rows // 2
    for i, owner in enumerate(owners(n)):
        block = total[i * rows : (i + 1) * rows, :]
        low, high = block[:local], block[local:]
        keep[owner] = jnp.where(side == 0, low, high)
        give[owner] = jnp.where(side == 0, high, low)
    for copy in copies:
        copy.wait()


def project(sums, gain, shards, weights, later, size):
    n = len(shards)
    rows, width = shards[0].shape
    stripe = sum(w.shape[0] for w in weights)
    shape = jax.ShapeDtypeStruct((n, rows // 2, stripe), jnp.float32)
    return pl.pallas_call(
        lambda *refs: project_kernel(n, len(weights), *refs),
        out_shape=[shape, shape, pltpu.VMEM((size, later.shape[1]), later.dtype)],
        in_specs=[IN_VMEM] * (3 + n + len(weights)) + [IN_HBM],
        out_specs=[IN_VMEM] * 3,
        scratch_shapes=[
            pltpu.VMEM((n * rows, width), jnp.bfloat16),
            pltpu.VMEM((n * rows, stripe), jnp.float32),
            pltpu.SemaphoreType.DMA((4,)),
        ],
        compiler_params=pltpu.CompilerParams(vmem_limit_bytes=6 * MIB),
        name="project",
    )(
        *sums,
        gain,
        *shards,
        *[in_vmem(w) for w in weights],
        in_hbm(later),
    )


def split_kernel(keep, got, *outs):
    me = lax.axis_index("gx")
    for d in range(keep.shape[0]):
        at = jnp.bitwise_xor(me, d)
        outs[d % 4][d // 4] = (keep[at] + got[at]).astype(jnp.bfloat16)


def split(keep, got):
    shape = jax.ShapeDtypeStruct((2,) + keep.shape[1:], jnp.bfloat16)
    return pl.pallas_call(
        split_kernel,
        out_shape=[shape] * 4,
        in_specs=[IN_VMEM] * 2,
        out_specs=[IN_VMEM] * 4,
        compiler_params=pltpu.CompilerParams(vmem_limit_bytes=8 * MIB),
        name="split",
    )(keep, got)


def pack(picks, *sources):
    def pack_kernel(*refs):
        for k, (i, j) in enumerate(picks):
            refs[-1][k] = refs[i][j]

    return pl.pallas_call(
        pack_kernel,
        out_shape=jax.ShapeDtypeStruct((len(picks),) + sources[0].shape[1:], sources[0].dtype),
        in_specs=[IN_VMEM] * len(sources),
        out_specs=IN_VMEM,
        compiler_params=pltpu.CompilerParams(vmem_limit_bytes=8 * MIB),
        name="pack",
    )(*sources)


ARRIVED = [(0, 0), (1, 0), (2, 0), (3, 0), (4, 0), (4, 1), (4, 2), (4, 3)]


def attend_kernel(lengths, *refs):
    arrived = refs[:5]
    cosine, sine, keys, values, out, spread, held = refs[5:]
    n, rows, stripe = spread.shape[1], spread.shape[0], spread.shape[2]
    me = lax.axis_index("gx")
    query_cols = stripe - 128
    side = lax.axis_index("gy")
    score_scale = 1.0 / math.sqrt(DH)
    for d, (i, j) in enumerate(ARRIVED):
        block = arrived[i][j].astype(jnp.float32)
        for r in range(rows):
            spread[r, pl.ds(jnp.bitwise_xor(me, d), 1), :] = block[r : r + 1, :]
    for r in range(rows):
        given = spread[r]
        cos, sin = cosine[r : r + 1, :], sine[r : r + 1, :]

        def turn(a, b):
            turned = jnp.concatenate([a * cos - b * sin, b * cos + a * sin], axis=1)
            return turned.astype(jnp.bfloat16)

        starts = range(0, query_cols, DH)
        q = turn(
            jnp.concatenate([given[:, c : c + DH // 2] for c in starts], axis=0),
            jnp.concatenate([given[:, c + DH // 2 : c + DH] for c in starts], axis=0),
        )
        new = [
            given[i : i + 1, query_cols:] + given[i + 1 : i + 2, query_cols:]
            for i in range(0, n, 2)
        ]
        new_key = turn(new[0], new[1]).astype(jnp.float32)
        new_value = jnp.concatenate(new[2:], axis=1)
        scores = lax.dot_general(q, keys[r], contract, preferred_element_type=jnp.float32)
        scores = scores * score_scale
        place = lax.broadcasted_iota(jnp.int32, scores.shape, 1)
        scores = jnp.where(place < lengths[r], scores, -1e30)
        own_score = jnp.sum(q.astype(jnp.float32) * new_key, axis=1, keepdims=True) * score_scale
        highest = jnp.maximum(jnp.max(scores, axis=1, keepdims=True), own_score)
        weights = jnp.exp(scores - highest)
        own_weight = jnp.exp(own_score - highest)
        totals = jnp.sum(weights, axis=1, keepdims=True) + own_weight
        blended = jnp.dot(
            weights.astype(jnp.bfloat16), values[r], preferred_element_type=jnp.float32
        )
        blended = (blended + own_weight * new_value) / totals
        for j in range(len(starts)):
            block = blended[j * n : (j + 1) * n]
            swapped = pltpu.roll(block, n // 2, 0)
            parts = [jnp.where(side == 0, block, swapped), jnp.where(side == 0, swapped, block)]
            for i in range(n // 2):
                at = (i * len(starts) + j) * DH
                for k, part in enumerate(parts):
                    held[k, r : r + 1, at : at + DH] = part[i : i + 1]
    out[...] = jnp.concatenate([held[1], held[0]], axis=0).astype(jnp.bfloat16)


def attend(lengths, arrived, cosine, sine, keys, values):
    n = len(ARRIVED)
    _, rows, stripe = arrived[0].shape
    shape = jax.ShapeDtypeStruct((2 * rows, HEADS * DH // 2), jnp.bfloat16)
    return pl.pallas_call(
        attend_kernel,
        out_shape=shape,
        in_specs=[IN_SMEM] + [IN_VMEM] * 9,
        out_specs=IN_VMEM,
        scratch_shapes=[
            pltpu.VMEM((rows, n, stripe), jnp.float32),
            pltpu.VMEM((2, rows, HEADS * DH // 2), jnp.float32),
        ],
        compiler_params=pltpu.CompilerParams(vmem_limit_bytes=8 * MIB),
        name="attend",
    )(lengths, *arrived, cosine, sine, in_vmem(keys), in_vmem(values))


def output_kernel(n, *refs):
    shards = refs[:n]
    weights = refs[n:-4]
    keep, give, total, placed = refs[-4:]
    rows, width = shards[-1].shape
    half = width // 2
    for part in range(2):
        start = part * half
        cols = slice(start, start + half)
        x = [ref[:, cols].astype(jnp.float32)[:rows] for ref in shards]
        x = jnp.concatenate(x, axis=0).astype(jnp.bfloat16)
        first = 0
        for weight in weights:
            last = first + weight.shape[0]
            if start <= first and last <= start + half:
                term = jnp.dot(
                    x[:, first - start : last - start],
                    weight[...],
                    preferred_element_type=jnp.float32,
                )
                if first == 0:
                    total[...] = term
                else:
                    total[...] += term
            first = last
    side = lax.axis_index("gy")
    for i, owner in enumerate(owners(n)):
        block = total[i * rows : (i + 1) * rows, :]
        sender = 1 - side if n // 2 <= i < n - 1 else side
        placed[owner] = jnp.where(sender == 0, block, pltpu.roll(block, rows // 2, 0))
    keep[...] = placed[pl.ds(side * (n // 2), n // 2)]
    give[...] = placed[pl.ds((1 - side) * (n // 2), n // 2)]


def output_project(shards, weights):
    n = len(shards)
    rows = shards[-1].shape[0]
    cols = weights[0].shape[1]
    shape = jax.ShapeDtypeStruct((n // 2, rows, cols), jnp.float32)
    return pl.pallas_call(
        lambda *refs: output_kernel(n, *refs),
        out_shape=[shape, shape],
        in_specs=[IN_VMEM] * (n + len(weights)),
        out_specs=[IN_VMEM] * 2,
        scratch_shapes=[
            pltpu.VMEM((n * rows, cols), jnp.float32),
            pltpu.VMEM((n, rows, cols), jnp.float32),
        ],
        compiler_params=pltpu.CompilerParams(vmem_limit_bytes=8 * MIB),
        name="output_project",
    )(*shards, *[in_vmem(w) for w in weights])


def on_any_grid(
    activations,
    norm_gain,
    query_weight,
    keyval_weight,
    output_weight,
    cache_keys,
    cache_values,
    cache_lengths,
):
    inputs = activations.astype(jnp.float32)
    row_sums, square_sums = lax.psum(
        (jnp.sum(inputs, axis=1), jnp.sum(inputs * inputs, axis=1)), "gy"
    )
    row_mean = row_sums[:, None] / D
    row_square = square_sums[:, None] / D
    variance = row_square - row_mean * row_mean
    normed = (
        (inputs - row_mean) * lax.rsqrt(variance + epsilon) * norm_gain.astype(jnp.float32)
    ).astype(jnp.bfloat16)
    shard_rows = lax.all_gather(normed, "gx", axis=0, tiled=True)
    query_part = lax.dot_general(
        shard_rows, query_weight, contract, preferred_element_type=jnp.float32
    )
    keyval_part = lax.dot_general(
        shard_rows, keyval_weight, contract, preferred_element_type=jnp.float32
    )
    partial_sums = jnp.concatenate([query_part, keyval_part], axis=1)
    wide_count = lax.axis_size("gx")
    pair_count = lax.axis_size("gy")
    local_rows = cache_lengths.shape[0]
    stripe = partial_sums.shape[1]
    arrived = lax.all_to_all(partial_sums, ("gx", "gy"), split_axis=0, concat_axis=1, tiled=True)
    gathered = jnp.sum(arrived.reshape(local_rows, wide_count, pair_count, stripe), axis=2).astype(
        jnp.bfloat16
    )
    query_cols = query_weight.shape[0]
    queries = gathered[:, :, :query_cols].reshape(local_rows, HEADS, DH)
    keyvals = gathered[:, :, query_cols:].reshape(local_rows, 2 * DH)
    places = cache_lengths.astype(jnp.float32)
    queries = rotate(queries.astype(jnp.float32), places[:, None, None]).astype(jnp.bfloat16)
    new_keys = rotate(keyvals[:, :DH].astype(jnp.float32), places[:, None]).astype(jnp.bfloat16)
    new_values = keyvals[:, DH:].astype(jnp.float32)
    score_scale = 1.0 / math.sqrt(DH)
    scores = (
        jnp.einsum("rhd,rtd->rht", queries, cache_keys, preferred_element_type=jnp.float32)
        * score_scale
    )
    visible = jnp.arange(cache_keys.shape[1])[None, :] < cache_lengths[:, None]
    scores = jnp.where(visible[:, None, :], scores, -1e30)
    own_score = (
        jnp.einsum("rhd,rd->rh", queries, new_keys, preferred_element_type=jnp.float32)
        * score_scale
    )
    highest = jnp.maximum(jnp.max(scores, axis=2), own_score)
    weights = jnp.exp(scores - highest[:, :, None])
    own_weight = jnp.exp(own_score - highest)
    totals = jnp.sum(weights, axis=2) + own_weight
    blended = jnp.einsum(
        "rht,rtd->rhd",
        weights.astype(jnp.bfloat16),
        cache_values,
        preferred_element_type=jnp.float32,
    )
    blended = blended + own_weight[:, :, None] * new_values[:, None, :]
    attended = (blended / totals[:, :, None]).astype(jnp.bfloat16).reshape(local_rows, HEADS * DH)
    swapped = lax.all_to_all(attended, "gy", split_axis=1, concat_axis=0, tiled=True)
    partial_out = jnp.dot(
        lax.all_gather(swapped, "gx", axis=0, tiled=True),
        output_weight,
        preferred_element_type=jnp.float32,
    )
    return lax.psum_scatter(partial_out, "gy", scatter_dimension=0, tiled=True).astype(jnp.bfloat16)


def on_device(
    activations,
    norm_gain,
    query_weight,
    keyval_weight,
    output_weight,
    cache_keys,
    cache_values,
    cache_lengths,
):
    n = lax.axis_size("gx")
    query_cols, width = query_weight.shape
    new_cols = keyval_weight.shape[0]
    piece = query_cols // 4
    weights = []

    indices = jnp.arange(DH // 2, dtype=jnp.float32)
    frequency = jnp.exp(-math.log(10000.0) * indices / (DH // 2))
    angles = cache_lengths.astype(jnp.float32)[:, None] * frequency
    cosine, sine = jnp.cos(angles), jnp.sin(angles)

    def piece_of(array, start, size, after):
        return load(size, [(array, start, size, 0)], after)

    rows = activations.shape[0]
    shard = jnp.concatenate([activations, swap_pair(activations)], axis=0)
    came, swapped, sums = [], [], []
    for step in range(1, n // 2):
        moved = ring_move(shard)
        if step > 1:
            swapped.append(swap_pair(shard[rows:]))
        sums = [row_sums(shard, sums)]
        weight = load(piece, [(query_weight, (step - 1) * piece, piece, 0)], [shard])
        weight, (moved, *held) = before(weight, moved, *sums, *swapped)
        sums, swapped = held[:1], held[1:]
        weights.append(weight)
        came.append(moved)
        shard = moved
    payload, sums = last_payload(shard, sums[0])
    far = ring_move(payload)
    swapped.append(swap_pair(shard[rows:]))
    other_sums = swap_pair(sums)
    jobs = [(query_weight, 3 * piece, piece, 0), (keyval_weight, 0, new_cols, None)]
    weight = load(piece + 2 * new_cols, jobs, [payload])
    weight, (far, other_sums, *swapped) = before(weight, far, other_sums, *swapped)
    weights.append(weight)
    shards = [activations, *came, *swapped, far]
    sums = (sums, other_sums)
    gain = norm_gain.astype(jnp.float32)[None, :]
    piece = output_weight.shape[0] // 4
    keep, give, weight = project(
        sums, gain, shards, weights, output_weight, 2 * piece
    )
    weights = [weight]

    def exchange(blocks, d):
        return lax.ppermute(blocks, "gx", [(i, i ^ d) for i in range(n)])

    blocks = split(keep, swap_pair(give))
    arrived = [blocks[0]] + [exchange(blocks[d], d) for d in range(1, 4)]
    keys = load_cache(cache_keys, [blocks[1]])
    keys, arrived = before(keys, *arrived)
    across = pack([(0, 1), (1, 1), (2, 1), (3, 1)], *arrived)
    last = exchange(across, 4)
    values = load_cache(cache_values, [across])
    values, (last,) = before(values, last)
    arrived = [*arrived, last]
    halves = attend(cache_lengths, arrived, cosine, sine, keys, values)
    got = swap_pair(halves)
    rows = halves.shape[0]
    local = rows // 2
    shard = jnp.concatenate([halves[local:], got[:local], halves[:local], got[local:]], axis=0)

    done = 2 * piece
    piece = piece // 2
    shards, swapped = [shard], []
    for step in range(1, n // 2):
        moved = ring_move(shard)
        if step > 1:
            swapped.append(swap_pair(shard[rows:]))
        weight = load(piece, [(output_weight, done + (step - 1) * piece, piece, 0)], [shard])
        weight, (moved, *swapped) = before(weight, moved, *swapped)
        weights.append(weight)
        shards.append(moved)
        shard = moved
    far = ring_move(shard[:rows])
    swapped.append(swap_pair(shard[rows:]))
    weight = load(piece, [(output_weight, done + 3 * piece, piece, 0)], [shard])
    weight, (far, *swapped) = before(weight, far, *swapped)
    weights.append(weight)
    keep, give = output_project([*shards, *swapped, far], weights)
    out = (keep + swap_pair(give)).astype(jnp.bfloat16)
    return out.reshape(-1, out.shape[-1])


def solution(mesh):
    return jax.shard_map(
        on_device if mesh.shape["gx"] == 8 else on_any_grid,
        mesh=mesh,
        in_specs=(
            P(("groups", "gx"), "gy"),
            P("gy"),
            P("gx", "gy"),
            P("gx", "gy"),
            P("gy", "gx"),
            P(("groups", "gx", "gy"), None, None),
            P(("groups", "gx", "gy"), None, None),
            P(("groups", "gx", "gy")),
        ),
        out_specs=P(("groups", "gy"), "gx"),
        check_vma=False,
    )
```

```python
import math

import jax
import jax.numpy as jnp
from jax import lax
from jax.experimental import pallas as pl
from jax.experimental.pallas import tpu as pltpu
from jax.sharding import PartitionSpec as P

D = 18432
HEADS = 48
DH = 256


epsilon = 1e-06
contract = (((1,), (1,)), ((), ()))
MIB = 1 << 20
ANY = pl.BlockSpec(memory_space=pl.ANY)
IN_HBM = pl.BlockSpec(memory_space=pltpu.HBM)
IN_VMEM = pl.BlockSpec(memory_space=pltpu.VMEM)
IN_SMEM = pl.BlockSpec(memory_space=pltpu.SMEM)


def rotate(vectors, places):
    half_width = vectors.shape[-1] // 2
    indices = jnp.arange(half_width, dtype=jnp.float32)
    frequency = jnp.exp(-math.log(10000.0) * indices / half_width)
    angles = places * frequency
    cosine = jnp.cos(angles)
    sine = jnp.sin(angles)
    first_half = vectors[..., :half_width]
    second_half = vectors[..., half_width:]
    return jnp.concatenate(
        [first_half * cosine - second_half * sine, second_half * cosine + first_half * sine],
        axis=-1,
    )


def ring_order(n):
    return list(range(0, n, 2)) + list(range(n - 1, 0, -2))


def swap_pair(x):
    return lax.ppermute(x, "gy", [(0, 1), (1, 0)])


class Ring:
    def __init__(self, n):
        order = ring_order(n)
        self.onward = [(order[p], order[(p + 1) % n]) for p in range(n)]
        self.back = [(order[p], order[(p - 1) % n]) for p in range(n)]
        self.across = [(order[p], order[(p + n // 2) % n]) for p in range(n)]

    def step(self, left, right):
        return lax.ppermute(left, "gx", self.onward), lax.ppermute(right, "gx", self.back)


def owners(n):
    offsets = [0]
    for step in range(1, n // 2):
        offsets += [-step, step]
    offsets.append(n // 2)
    me = lax.axis_index("gx")
    half = lax.div(me, 2)
    place = jnp.where(lax.rem(me, 2) == 0, half, n - 1 - half)
    result = []
    for offset in offsets:
        at = lax.rem(place + (offset + n), n)
        result.append(jnp.where(at < n // 2, 2 * at, 2 * (n - 1 - at) + 1))
    return result


def start_copies(source, target, sems, count):
    rows = source.shape[0]
    size = -(-rows // (16 * count)) * 16
    copies = []
    for i, first in enumerate(range(0, rows, size)):
        at = pl.ds(first, min(size, rows - first))
        copy = pltpu.make_async_copy(source.at[at], target.at[at], sems.at[i])
        copy.start()
        copies.append(copy)
    return copies


def load_kernel(jobs, *refs):
    sources, target, sems = refs[: len(jobs)], refs[-2], refs[-1]
    copies = []
    for i, (first, size, at) in enumerate(jobs):
        if at is None:
            at = target.shape[0] - 2 * size
            odd = lax.rem(lax.axis_index("gx"), 2)
            unused = pl.ds(pl.multiple_of(at + (1 - odd) * size, size), size)
            at = pl.multiple_of(at + odd * size, size)
            target[unused, :] = jnp.zeros((size, target.shape[1]), target.dtype)
        part = sources[i].at[pl.ds(first, size)]
        copies += start_copies(part, target.at[pl.ds(at, size)], sems.at[i], 4)
    for copy in copies:
        copy.wait()


def load(rows, jobs, after=()):
    array = jobs[0][0]
    return pl.pallas_call(
        lambda *refs: load_kernel([job[1:] for job in jobs], *refs),
        out_shape=pltpu.VMEM((rows, array.shape[1]), array.dtype),
        in_specs=[IN_HBM] * len(jobs) + [ANY] * len(after),
        out_specs=IN_VMEM,
        scratch_shapes=[pltpu.SemaphoreType.DMA((len(jobs), 4))],
        compiler_params=pltpu.CompilerParams(vmem_limit_bytes=MIB),
        name="load",
    )(*[in_hbm(job[0]) for job in jobs], *after)


def load_cache_kernel(source, *refs):
    target, sems = refs[-2:]
    copies = []
    for row in range(source.shape[0]):
        copies.append(pltpu.make_async_copy(source.at[row], target.at[row], sems.at[row]))
        copies[-1].start()
    for copy in copies:
        copy.wait()


def load_cache(cache, after):
    return pl.pallas_call(
        load_cache_kernel,
        out_shape=pltpu.VMEM(cache.shape, cache.dtype),
        in_specs=[IN_HBM] + [ANY] * len(after),
        out_specs=IN_VMEM,
        scratch_shapes=[pltpu.SemaphoreType.DMA((cache.shape[0],))],
        compiler_params=pltpu.CompilerParams(vmem_limit_bytes=MIB),
        name="load_cache",
    )(in_hbm(cache), *after)


def in_hbm(array):
    return pltpu.with_memory_space_constraint(array, pltpu.HBM)


def in_vmem(array):
    return pltpu.with_memory_space_constraint(array, pltpu.VMEM)


def before(done, *rest):
    held = lax.optimization_barrier((done,) + rest)
    return held[0], held[1:]


def sums_kernel(ready, count, *refs):
    out = refs[-1]
    start = 0
    for ref in refs[:ready]:
        out[start : start + ref.shape[0], :] = ref[...]
        start += ref.shape[0]

    def both_sums(ref):
        x = ref[...].astype(jnp.float32)
        total = jnp.sum(x, axis=1, keepdims=True)
        square = jnp.sum(x * x, axis=1, keepdims=True)
        lane = lax.broadcasted_iota(jnp.int32, (x.shape[0], 128), 1)
        return jnp.where(lane == 0, total, jnp.where(lane == 1, square, 0.0))

    for ref in refs[ready : ready + count]:
        out[start : start + ref.shape[0], :] = both_sums(ref)
        start += ref.shape[0]
    halves = refs[ready + count : -1]
    if halves:
        out[start:, :] = both_sums(halves[0]) + both_sums(halves[1])


def row_sums(shards, ready=(), halves=()):
    rows = sum(a.shape[0] for a in (*ready, *shards, *halves[:1]))
    return pl.pallas_call(
        lambda *refs: sums_kernel(len(ready), len(shards), *refs),
        out_shape=jax.ShapeDtypeStruct((rows, 128), jnp.float32),
        in_specs=[IN_VMEM] * (len(ready) + len(shards) + len(halves)),
        out_specs=IN_VMEM,
        compiler_params=pltpu.CompilerParams(vmem_limit_bytes=8 * MIB),
        name="row_sums",
    )(*ready, *shards, *halves)


def project_kernel(n, parts, *refs):
    sums_a, sums_b, gain = refs[:3]
    shards = refs[3 : 3 + n - 1]
    far = refs[3 + n - 1 : 3 + n + 1]
    weights = refs[4 + n : 4 + n + parts]
    keep, give, normed, total = refs[4 + n + parts :]
    rows, width = shards[0].shape
    sums = sums_a[...] + sums_b[...]
    row_mean = sums[:, :1] / D
    row_square = sums[:, 1:2] / D
    scale = lax.rsqrt(row_square - row_mean * row_mean + epsilon)
    for part in range(2):
        cols = slice(part * width // 2, (part + 1) * width // 2)
        for i in range(0, n, 2):
            x = [ref[:, cols] if ref is not far[part] else ref[...] for ref in (*shards, far[part])]
            x = jnp.concatenate([piece.astype(jnp.float32) for piece in x[i : i + 2]], axis=0)
            at = slice(i * rows, (i + 2) * rows)
            x = (x - row_mean[at]) * scale[at] * gain[:, cols]
            normed[at, cols] = x.astype(jnp.bfloat16)
        x = normed[:, cols]
        start = 0
        for weight in weights:
            term = lax.dot_general(
                x, weight[:, cols], contract, preferred_element_type=jnp.float32
            )
            stripe = slice(start, start + weight.shape[0])
            if part == 0:
                total[:, stripe] = term
            else:
                total[:, stripe] += term
            start = stripe.stop
    side = lax.axis_index("gy")
    local = rows // 2
    for i, owner in enumerate(owners(n)):
        block = total[i * rows : (i + 1) * rows, :]
        low, high = block[:local], block[local:]
        keep[owner] = jnp.where(side == 0, low, high)
        give[owner] = jnp.where(side == 0, high, low)


def project(sums, gain, shards, far, weights):
    n = len(shards) + 1
    rows, width = shards[0].shape
    stripe = sum(w.shape[0] for w in weights)
    shape = jax.ShapeDtypeStruct((n, rows // 2, stripe), jnp.float32)
    return pl.pallas_call(
        lambda *refs: project_kernel(n, len(weights), *refs),
        out_shape=[shape, shape],
        in_specs=[IN_VMEM] * (4 + n + len(weights)),
        out_specs=[IN_VMEM] * 2,
        scratch_shapes=[
            pltpu.VMEM((n * rows, width), jnp.bfloat16),
            pltpu.VMEM((n * rows, stripe), jnp.float32),
        ],
        compiler_params=pltpu.CompilerParams(vmem_limit_bytes=6 * MIB),
        name="project",
    )(
        *sums,
        gain,
        *shards,
        *far,
        *[in_vmem(w) for w in weights],
    )


def split_kernel(keep, got, *outs):
    me = lax.axis_index("gx")
    for d in range(keep.shape[0]):
        at = jnp.bitwise_xor(me, d)
        outs[d % 4][d // 4] = (keep[at] + got[at]).astype(jnp.bfloat16)


def split(keep, got):
    shape = jax.ShapeDtypeStruct((2,) + keep.shape[1:], jnp.bfloat16)
    return pl.pallas_call(
        split_kernel,
        out_shape=[shape] * 4,
        in_specs=[IN_VMEM] * 2,
        out_specs=[IN_VMEM] * 4,
        compiler_params=pltpu.CompilerParams(vmem_limit_bytes=8 * MIB),
        name="split",
    )(keep, got)


def pack(picks, *sources):
    def pack_kernel(*refs):
        for k, (i, j) in enumerate(picks):
            refs[-1][k] = refs[i][j]

    return pl.pallas_call(
        pack_kernel,
        out_shape=jax.ShapeDtypeStruct((len(picks),) + sources[0].shape[1:], sources[0].dtype),
        in_specs=[IN_VMEM] * len(sources),
        out_specs=IN_VMEM,
        compiler_params=pltpu.CompilerParams(vmem_limit_bytes=8 * MIB),
        name="pack",
    )(*sources)


ARRIVED = [(0, 0), (1, 0), (2, 0), (3, 0), (4, 0), (4, 1), (4, 2), (4, 3)]


def attend_kernel(lengths, *refs):
    arrived = refs[:5]
    cosine, sine, keys, values, mine, other, spread, held = refs[5:]
    n, rows, stripe = spread.shape[1], spread.shape[0], spread.shape[2]
    me = lax.axis_index("gx")
    query_cols = stripe - 128
    side = lax.axis_index("gy")
    score_scale = 1.0 / math.sqrt(DH)
    for d, (i, j) in enumerate(ARRIVED):
        block = arrived[i][j].astype(jnp.float32)
        for r in range(rows):
            spread[r, pl.ds(jnp.bitwise_xor(me, d), 1), :] = block[r : r + 1, :]
    for r in range(rows):
        given = spread[r]
        cos, sin = cosine[r : r + 1, :], sine[r : r + 1, :]

        def turn(a, b):
            turned = jnp.concatenate([a * cos - b * sin, b * cos + a * sin], axis=1)
            return turned.astype(jnp.bfloat16)

        starts = range(0, query_cols, DH)
        q = turn(
            jnp.concatenate([given[:, c : c + DH // 2] for c in starts], axis=0),
            jnp.concatenate([given[:, c + DH // 2 : c + DH] for c in starts], axis=0),
        )
        new = [
            given[i : i + 1, query_cols:] + given[i + 1 : i + 2, query_cols:]
            for i in range(0, n, 2)
        ]
        new_key = turn(new[0], new[1]).astype(jnp.float32)
        new_value = jnp.concatenate(new[2:], axis=1)
        scores = lax.dot_general(q, keys[r], contract, preferred_element_type=jnp.float32)
        scores = scores * score_scale
        place = lax.broadcasted_iota(jnp.int32, scores.shape, 1)
        scores = jnp.where(place < lengths[r], scores, -1e30)
        own_score = jnp.sum(q.astype(jnp.float32) * new_key, axis=1, keepdims=True) * score_scale
        highest = jnp.maximum(jnp.max(scores, axis=1, keepdims=True), own_score)
        weights = jnp.exp(scores - highest)
        own_weight = jnp.exp(own_score - highest)
        totals = jnp.sum(weights, axis=1, keepdims=True) + own_weight
        blended = jnp.dot(
            weights.astype(jnp.bfloat16), values[r], preferred_element_type=jnp.float32
        )
        blended = (blended + own_weight * new_value) / totals
        for j in range(len(starts)):
            block = blended[j * n : (j + 1) * n]
            swapped = pltpu.roll(block, n // 2, 0)
            parts = [jnp.where(side == 0, block, swapped), jnp.where(side == 0, swapped, block)]
            for i in range(n // 2):
                at = (i * len(starts) + j) * DH
                for k, part in enumerate(parts):
                    held[k, r : r + 1, at : at + DH] = part[i : i + 1]
    mine[...] = held[0].astype(jnp.bfloat16)
    other[...] = held[1].astype(jnp.bfloat16)


def attend(lengths, arrived, cosine, sine, keys, values):
    n = len(ARRIVED)
    _, rows, stripe = arrived[0].shape
    shape = jax.ShapeDtypeStruct((rows, HEADS * DH // 2), jnp.bfloat16)
    return pl.pallas_call(
        attend_kernel,
        out_shape=[shape, shape],
        in_specs=[IN_SMEM] + [IN_VMEM] * 9,
        out_specs=[IN_VMEM] * 2,
        scratch_shapes=[
            pltpu.VMEM((rows, n, stripe), jnp.float32),
            pltpu.VMEM((2, rows, HEADS * DH // 2), jnp.float32),
        ],
        compiler_params=pltpu.CompilerParams(vmem_limit_bytes=8 * MIB),
        name="attend",
    )(lengths, *arrived, cosine, sine, in_vmem(keys), in_vmem(values))


def output_kernel(n, *refs):
    shards = refs[: n - 1]
    far = refs[n - 1 : n + 1]
    weights = refs[n + 1 : -4]
    keep, give, total, placed = refs[-4:]
    rows = shards[0].shape[0]
    half = far[0].shape[1]
    for part in range(2):
        start = part * half
        cols = slice(start, start + half)
        x = [ref[:, cols] for ref in shards] + [far[part][...]]
        x = jnp.concatenate([piece.astype(jnp.float32) for piece in x], axis=0)
        x = x.astype(jnp.bfloat16)
        first = 0
        for weight in weights:
            last = first + weight.shape[0]
            low, high = max(first, start), min(last, start + half)
            if low < high:
                term = jnp.dot(
                    x[:, low - start : high - start],
                    weight[low - first : high - first, :],
                    preferred_element_type=jnp.float32,
                )
                if low == 0:
                    total[...] = term
                else:
                    total[...] += term
            first = last
    side = lax.axis_index("gy")
    for i, owner in enumerate(owners(n)):
        block = total[i * rows : (i + 1) * rows, :]
        placed[owner] = jnp.where(side == 0, block, pltpu.roll(block, rows // 2, 0))
    keep[...] = placed[pl.ds(side * (n // 2), n // 2)]
    give[...] = placed[pl.ds((1 - side) * (n // 2), n // 2)]


def output_project(shards, far, weights):
    n = len(shards) + 1
    rows = shards[0].shape[0]
    cols = weights[0].shape[1]
    shape = jax.ShapeDtypeStruct((n // 2, rows, cols), jnp.float32)
    return pl.pallas_call(
        lambda *refs: output_kernel(n, *refs),
        out_shape=[shape, shape],
        in_specs=[IN_VMEM] * (n + 1 + len(weights)),
        out_specs=[IN_VMEM] * 2,
        scratch_shapes=[
            pltpu.VMEM((n * rows, cols), jnp.float32),
            pltpu.VMEM((n, rows, cols), jnp.float32),
        ],
        compiler_params=pltpu.CompilerParams(vmem_limit_bytes=8 * MIB),
        name="output_project",
    )(*shards, *far, *[in_vmem(w) for w in weights])


def on_any_grid(
    activations,
    norm_gain,
    query_weight,
    keyval_weight,
    output_weight,
    cache_keys,
    cache_values,
    cache_lengths,
):
    inputs = activations.astype(jnp.float32)
    row_sums, square_sums = lax.psum(
        (jnp.sum(inputs, axis=1), jnp.sum(inputs * inputs, axis=1)), "gy"
    )
    row_mean = row_sums[:, None] / D
    row_square = square_sums[:, None] / D
    variance = row_square - row_mean * row_mean
    normed = (
        (inputs - row_mean) * lax.rsqrt(variance + epsilon) * norm_gain.astype(jnp.float32)
    ).astype(jnp.bfloat16)
    shard_rows = lax.all_gather(normed, "gx", axis=0, tiled=True)
    query_part = lax.dot_general(
        shard_rows, query_weight, contract, preferred_element_type=jnp.float32
    )
    keyval_part = lax.dot_general(
        shard_rows, keyval_weight, contract, preferred_element_type=jnp.float32
    )
    partial_sums = jnp.concatenate([query_part, keyval_part], axis=1)
    wide_count = lax.axis_size("gx")
    pair_count = lax.axis_size("gy")
    local_rows = cache_lengths.shape[0]
    stripe = partial_sums.shape[1]
    arrived = lax.all_to_all(partial_sums, ("gx", "gy"), split_axis=0, concat_axis=1, tiled=True)
    gathered = jnp.sum(arrived.reshape(local_rows, wide_count, pair_count, stripe), axis=2).astype(
        jnp.bfloat16
    )
    query_cols = query_weight.shape[0]
    queries = gathered[:, :, :query_cols].reshape(local_rows, HEADS, DH)
    keyvals = gathered[:, :, query_cols:].reshape(local_rows, 2 * DH)
    places = cache_lengths.astype(jnp.float32)
    queries = rotate(queries.astype(jnp.float32), places[:, None, None]).astype(jnp.bfloat16)
    new_keys = rotate(keyvals[:, :DH].astype(jnp.float32), places[:, None]).astype(jnp.bfloat16)
    new_values = keyvals[:, DH:].astype(jnp.float32)
    score_scale = 1.0 / math.sqrt(DH)
    scores = (
        jnp.einsum("rhd,rtd->rht", queries, cache_keys, preferred_element_type=jnp.float32)
        * score_scale
    )
    visible = jnp.arange(cache_keys.shape[1])[None, :] < cache_lengths[:, None]
    scores = jnp.where(visible[:, None, :], scores, -1e30)
    own_score = (
        jnp.einsum("rhd,rd->rh", queries, new_keys, preferred_element_type=jnp.float32)
        * score_scale
    )
    highest = jnp.maximum(jnp.max(scores, axis=2), own_score)
    weights = jnp.exp(scores - highest[:, :, None])
    own_weight = jnp.exp(own_score - highest)
    totals = jnp.sum(weights, axis=2) + own_weight
    blended = jnp.einsum(
        "rht,rtd->rhd",
        weights.astype(jnp.bfloat16),
        cache_values,
        preferred_element_type=jnp.float32,
    )
    blended = blended + own_weight[:, :, None] * new_values[:, None, :]
    attended = (blended / totals[:, :, None]).astype(jnp.bfloat16).reshape(local_rows, HEADS * DH)
    swapped = lax.all_to_all(attended, "gy", split_axis=1, concat_axis=0, tiled=True)
    partial_out = jnp.dot(
        lax.all_gather(swapped, "gx", axis=0, tiled=True),
        output_weight,
        preferred_element_type=jnp.float32,
    )
    return lax.psum_scatter(partial_out, "gy", scatter_dimension=0, tiled=True).astype(jnp.bfloat16)


def on_device(
    activations,
    norm_gain,
    query_weight,
    keyval_weight,
    output_weight,
    cache_keys,
    cache_values,
    cache_lengths,
):
    n = lax.axis_size("gx")
    ring = Ring(n)
    query_cols, width = query_weight.shape
    new_cols = keyval_weight.shape[0]
    piece = query_cols // 4
    weights = []

    indices = jnp.arange(DH // 2, dtype=jnp.float32)
    frequency = jnp.exp(-math.log(10000.0) * indices / (DH // 2))
    angles = cache_lengths.astype(jnp.float32)[:, None] * frequency
    cosine, sine = jnp.cos(angles), jnp.sin(angles)

    def piece_of(array, start, size, after):
        return load(size, [(array, start, size, 0)], after)

    left = right = activations
    shards = [activations]
    sums = []
    for step in range(1, n // 2):
        arrived = shards[-2:] if step > 1 else []
        left, right = ring.step(left, right)
        if step > 1:
            sums = [row_sums([activations, *arrived] if step == 2 else arrived, sums)]
        weight = piece_of(query_weight, (step - 1) * piece, piece, arrived)
        weight, (left, right, *sums) = before(weight, left, right, *sums)
        weights.append(weight)
        shards += [left, right]
    far = ring.step(left[:, : width // 2], right[:, width // 2 :])
    sums = row_sums([left, right], sums)
    jobs = [(query_weight, 3 * piece, piece, 0), (keyval_weight, 0, new_cols, None)]
    weight = load(piece + 2 * new_cols, jobs, [left, right])
    weight, far = before(weight, *far)
    sums = row_sums([], [sums], far)
    other_sums = swap_pair(sums)
    weights.append(weight)
    gain = norm_gain.astype(jnp.float32)[None, :]
    keep, give = project((sums, other_sums), gain, shards, far, weights)

    def exchange(blocks, d):
        return lax.ppermute(blocks, "gx", [(i, i ^ d) for i in range(n)])

    blocks = split(keep, swap_pair(give))
    arrived = [blocks[0]] + [exchange(blocks[d], d) for d in range(1, 4)]
    keys = load_cache(cache_keys, [blocks[1]])
    keys, arrived = before(keys, *arrived)
    across = pack([(0, 1), (1, 1), (2, 1), (3, 1)], *arrived)
    last = exchange(across, 4)
    values = load_cache(cache_values, [across])
    done = output_weight.shape[0] // 6
    weight = load(done, [(output_weight, 0, done, 0)], [across])
    values, (last,) = before(values, last)
    weight, (last,) = before(weight, last)
    weights = [weight]
    arrived = [*arrived, last]
    mine, other = attend(cache_lengths, arrived, cosine, sine, keys, values)
    shard = jnp.concatenate([mine, swap_pair(other)], axis=0)

    left = right = shard
    shards = [shard]
    piece = (output_weight.shape[0] - done) // 4

    for step in range(1, n // 2):
        arrived = shards[-2:]
        left, right = ring.step(left, right)
        weight = piece_of(output_weight, done + (step - 1) * piece, piece, arrived)
        weight, (left, right) = before(weight, left, right)
        weights.append(weight)
        shards += [left, right]
    half = shard.shape[1] // 2
    far = ring.step(left[:, :half], right[:, half:])
    weight = piece_of(output_weight, done + 3 * piece, piece, [left, right])
    weight, far = before(weight, *far)
    weights.append(weight)
    keep, give = output_project(shards, far, weights)
    out = (keep + swap_pair(give)).astype(jnp.bfloat16)
    return out.reshape(-1, out.shape[-1])


def solution(mesh):
    return jax.shard_map(
        on_device if mesh.shape["gx"] == 8 else on_any_grid,
        mesh=mesh,
        in_specs=(
            P(("groups", "gx"), "gy"),
            P("gy"),
            P("gx", "gy"),
            P("gx", "gy"),
            P("gy", "gx"),
            P(("groups", "gx", "gy"), None, None),
            P(("groups", "gx", "gy"), None, None),
            P(("groups", "gx", "gy")),
        ),
        out_specs=P(("groups", "gy"), "gx"),
        check_vma=False,
    )
```

```python
import math

import jax
import jax.numpy as jnp
from jax import lax
from jax.experimental import pallas as pl
from jax.experimental.pallas import tpu as pltpu
from jax.sharding import PartitionSpec as P

D = 18432
HEADS = 48
DH = 256


epsilon = 1e-06
contract = (((1,), (1,)), ((), ()))
MIB = 1 << 20
ANY = pl.BlockSpec(memory_space=pl.ANY)
IN_HBM = pl.BlockSpec(memory_space=pltpu.HBM)
IN_VMEM = pl.BlockSpec(memory_space=pltpu.VMEM)
IN_SMEM = pl.BlockSpec(memory_space=pltpu.SMEM)


def rotate(vectors, places):
    half_width = vectors.shape[-1] // 2
    indices = jnp.arange(half_width, dtype=jnp.float32)
    frequency = jnp.exp(-math.log(10000.0) * indices / half_width)
    angles = places * frequency
    cosine = jnp.cos(angles)
    sine = jnp.sin(angles)
    first_half = vectors[..., :half_width]
    second_half = vectors[..., half_width:]
    return jnp.concatenate(
        [first_half * cosine - second_half * sine, second_half * cosine + first_half * sine],
        axis=-1,
    )


def ring_order(n):
    return list(range(0, n, 2)) + list(range(n - 1, 0, -2))


def swap_pair(x):
    return lax.ppermute(x, "gy", [(0, 1), (1, 0)])


class Ring:
    def __init__(self, n):
        order = ring_order(n)
        self.onward = [(order[p], order[(p + 1) % n]) for p in range(n)]
        self.back = [(order[p], order[(p - 1) % n]) for p in range(n)]
        self.across = [(order[p], order[(p + n // 2) % n]) for p in range(n)]

    def step(self, left, right):
        return lax.ppermute(left, "gx", self.onward), lax.ppermute(right, "gx", self.back)


def owners(n):
    offsets = [0]
    for step in range(1, n // 2):
        offsets += [-step, step]
    offsets.append(n // 2)
    me = lax.axis_index("gx")
    half = lax.div(me, 2)
    place = jnp.where(lax.rem(me, 2) == 0, half, n - 1 - half)
    result = []
    for offset in offsets:
        at = lax.rem(place + (offset + n), n)
        result.append(jnp.where(at < n // 2, 2 * at, 2 * (n - 1 - at) + 1))
    return result


def start_copies(source, target, sems, count):
    rows = source.shape[0]
    size = -(-rows // (16 * count)) * 16
    copies = []
    for i, first in enumerate(range(0, rows, size)):
        at = pl.ds(first, min(size, rows - first))
        copy = pltpu.make_async_copy(source.at[at], target.at[at], sems.at[i])
        copy.start()
        copies.append(copy)
    return copies


def load_kernel(jobs, *refs):
    sources, target, sems = refs[: len(jobs)], refs[-2], refs[-1]
    copies = []
    for i, (first, size, at) in enumerate(jobs):
        if at is None:
            at = target.shape[0] - 2 * size
            odd = lax.rem(lax.axis_index("gx"), 2)
            unused = pl.ds(pl.multiple_of(at + (1 - odd) * size, size), size)
            at = pl.multiple_of(at + odd * size, size)
            target[unused, :] = jnp.zeros((size, target.shape[1]), target.dtype)
        part = sources[i].at[pl.ds(first, size)]
        copies += start_copies(part, target.at[pl.ds(at, size)], sems.at[i], 4)
    for copy in copies:
        copy.wait()


def load(rows, jobs, after=()):
    array = jobs[0][0]
    return pl.pallas_call(
        lambda *refs: load_kernel([job[1:] for job in jobs], *refs),
        out_shape=pltpu.VMEM((rows, array.shape[1]), array.dtype),
        in_specs=[IN_HBM] * len(jobs) + [ANY] * len(after),
        out_specs=IN_VMEM,
        scratch_shapes=[pltpu.SemaphoreType.DMA((len(jobs), 4))],
        compiler_params=pltpu.CompilerParams(vmem_limit_bytes=MIB),
        name="load",
    )(*[in_hbm(job[0]) for job in jobs], *after)


def load_cache_kernel(source, *refs):
    target, sems = refs[-2:]
    copies = []
    for row in range(source.shape[0]):
        copies.append(pltpu.make_async_copy(source.at[row], target.at[row], sems.at[row]))
        copies[-1].start()
    for copy in copies:
        copy.wait()


def load_cache(cache, after):
    return pl.pallas_call(
        load_cache_kernel,
        out_shape=pltpu.VMEM(cache.shape, cache.dtype),
        in_specs=[IN_HBM] + [ANY] * len(after),
        out_specs=IN_VMEM,
        scratch_shapes=[pltpu.SemaphoreType.DMA((cache.shape[0],))],
        compiler_params=pltpu.CompilerParams(vmem_limit_bytes=MIB),
        name="load_cache",
    )(in_hbm(cache), *after)


def in_hbm(array):
    return pltpu.with_memory_space_constraint(array, pltpu.HBM)


def in_vmem(array):
    return pltpu.with_memory_space_constraint(array, pltpu.VMEM)


def before(done, *rest):
    held = lax.optimization_barrier((done,) + rest)
    return held[0], held[1:]


def sums_kernel(ready, count, *refs):
    out = refs[-1]
    start = 0
    for ref in refs[:ready]:
        out[start : start + ref.shape[0], :] = ref[...]
        start += ref.shape[0]

    def both_sums(ref):
        x = ref[...].astype(jnp.float32)
        total = jnp.sum(x, axis=1, keepdims=True)
        square = jnp.sum(x * x, axis=1, keepdims=True)
        lane = lax.broadcasted_iota(jnp.int32, (x.shape[0], 128), 1)
        return jnp.where(lane == 0, total, jnp.where(lane == 1, square, 0.0))

    for ref in refs[ready : ready + count]:
        out[start : start + ref.shape[0], :] = both_sums(ref)
        start += ref.shape[0]
    halves = refs[ready + count : -1]
    if halves:
        out[start:, :] = both_sums(halves[0]) + both_sums(halves[1])


def row_sums(shards, ready=(), halves=()):
    rows = sum(a.shape[0] for a in (*ready, *shards, *halves[:1]))
    return pl.pallas_call(
        lambda *refs: sums_kernel(len(ready), len(shards), *refs),
        out_shape=jax.ShapeDtypeStruct((rows, 128), jnp.float32),
        in_specs=[IN_VMEM] * (len(ready) + len(shards) + len(halves)),
        out_specs=IN_VMEM,
        compiler_params=pltpu.CompilerParams(vmem_limit_bytes=8 * MIB),
        name="row_sums",
    )(*ready, *shards, *halves)


def project_kernel(n, parts, *refs):
    sums_a, sums_b, gain = refs[:3]
    shards = refs[3 : 3 + n - 1]
    far = refs[3 + n - 1 : 3 + n + 1]
    weights = refs[4 + n : 4 + n + parts]
    later, keep, give, early, normed, total, sems = refs[4 + n + parts :]
    copies = start_copies(later.at[pl.ds(0, early.shape[0])], early, sems, 4)
    rows, width = shards[0].shape
    sums = sums_a[...] + sums_b[...]
    row_mean = sums[:, :1] / D
    row_square = sums[:, 1:2] / D
    scale = lax.rsqrt(row_square - row_mean * row_mean + epsilon)
    for part in range(2):
        cols = slice(part * width // 2, (part + 1) * width // 2)
        for i in range(0, n, 2):
            x = [ref[:, cols] if ref is not far[part] else ref[...] for ref in (*shards, far[part])]
            x = jnp.concatenate([piece.astype(jnp.float32) for piece in x[i : i + 2]], axis=0)
            at = slice(i * rows, (i + 2) * rows)
            x = (x - row_mean[at]) * scale[at] * gain[:, cols]
            normed[at, cols] = x.astype(jnp.bfloat16)
        x = normed[:, cols]
        start = 0
        for weight in weights:
            term = lax.dot_general(
                x, weight[:, cols], contract, preferred_element_type=jnp.float32
            )
            stripe = slice(start, start + weight.shape[0])
            if part == 0:
                total[:, stripe] = term
            else:
                total[:, stripe] += term
            start = stripe.stop
    side = lax.axis_index("gy")
    local = rows // 2
    for i, owner in enumerate(owners(n)):
        block = total[i * rows : (i + 1) * rows, :]
        low, high = block[:local], block[local:]
        keep[owner] = jnp.where(side == 0, low, high)
        give[owner] = jnp.where(side == 0, high, low)
    for copy in copies:
        copy.wait()


def project(sums, gain, shards, far, weights, later, size):
    n = len(shards) + 1
    rows, width = shards[0].shape
    stripe = sum(w.shape[0] for w in weights)
    shape = jax.ShapeDtypeStruct((n, rows // 2, stripe), jnp.float32)
    return pl.pallas_call(
        lambda *refs: project_kernel(n, len(weights), *refs),
        out_shape=[shape, shape, pltpu.VMEM((size, later.shape[1]), later.dtype)],
        in_specs=[IN_VMEM] * (4 + n + len(weights)) + [IN_HBM],
        out_specs=[IN_VMEM] * 3,
        scratch_shapes=[
            pltpu.VMEM((n * rows, width), jnp.bfloat16),
            pltpu.VMEM((n * rows, stripe), jnp.float32),
            pltpu.SemaphoreType.DMA((4,)),
        ],
        compiler_params=pltpu.CompilerParams(vmem_limit_bytes=6 * MIB),
        name="project",
    )(
        *sums,
        gain,
        *shards,
        *far,
        *[in_vmem(w) for w in weights],
        in_hbm(later),
    )


def split_kernel(keep, got, *outs):
    me = lax.axis_index("gx")
    for d in range(keep.shape[0]):
        at = jnp.bitwise_xor(me, d)
        outs[d % 4][d // 4] = (keep[at] + got[at]).astype(jnp.bfloat16)


def split(keep, got):
    shape = jax.ShapeDtypeStruct((2,) + keep.shape[1:], jnp.bfloat16)
    return pl.pallas_call(
        split_kernel,
        out_shape=[shape] * 4,
        in_specs=[IN_VMEM] * 2,
        out_specs=[IN_VMEM] * 4,
        compiler_params=pltpu.CompilerParams(vmem_limit_bytes=8 * MIB),
        name="split",
    )(keep, got)


def pack(picks, *sources):
    def pack_kernel(*refs):
        for k, (i, j) in enumerate(picks):
            refs[-1][k] = refs[i][j]

    return pl.pallas_call(
        pack_kernel,
        out_shape=jax.ShapeDtypeStruct((len(picks),) + sources[0].shape[1:], sources[0].dtype),
        in_specs=[IN_VMEM] * len(sources),
        out_specs=IN_VMEM,
        compiler_params=pltpu.CompilerParams(vmem_limit_bytes=8 * MIB),
        name="pack",
    )(*sources)


ARRIVED = [(0, 0), (1, 0), (2, 0), (3, 0), (4, 0), (4, 1), (4, 2), (4, 3)]


def attend_kernel(lengths, *refs):
    arrived = refs[:5]
    cosine, sine, keys, values, mine, other, spread, held = refs[5:]
    n, rows, stripe = spread.shape[1], spread.shape[0], spread.shape[2]
    me = lax.axis_index("gx")
    query_cols = stripe - 128
    side = lax.axis_index("gy")
    score_scale = 1.0 / math.sqrt(DH)
    for d, (i, j) in enumerate(ARRIVED):
        block = arrived[i][j].astype(jnp.float32)
        for r in range(rows):
            spread[r, pl.ds(jnp.bitwise_xor(me, d), 1), :] = block[r : r + 1, :]
    starts = range(0, query_cols, DH)
    ready = []
    for r in range(rows):
        given = spread[r]
        cos, sin = cosine[r : r + 1, :], sine[r : r + 1, :]

        def turn(a, b):
            turned = jnp.concatenate([a * cos - b * sin, b * cos + a * sin], axis=1)
            return turned.astype(jnp.bfloat16)

        q = turn(
            jnp.concatenate([given[:, c : c + DH // 2] for c in starts], axis=0),
            jnp.concatenate([given[:, c + DH // 2 : c + DH] for c in starts], axis=0),
        )
        q = (q.astype(jnp.float32) * score_scale).astype(jnp.bfloat16)
        new = [
            given[i : i + 1, query_cols:] + given[i + 1 : i + 2, query_cols:]
            for i in range(0, n, 2)
        ]
        new_key = turn(new[0], new[1]).astype(jnp.float32)
        new_value = jnp.concatenate(new[2:], axis=1)
        scores = lax.dot_general(q, keys[r], contract, preferred_element_type=jnp.float32)
        own_score = jnp.sum(q.astype(jnp.float32) * new_key, axis=1, keepdims=True)
        ready.append((scores, own_score, new_value))
    for r, (scores, own_score, new_value) in enumerate(ready):
        place = lax.broadcasted_iota(jnp.int32, scores.shape, 1)
        scores = jnp.where(place < lengths[r], scores, -1e30)
        highest = jnp.maximum(jnp.max(scores, axis=1, keepdims=True), own_score)
        weights = jnp.exp(scores - highest)
        own_weight = jnp.exp(own_score - highest)
        totals = jnp.sum(weights, axis=1, keepdims=True) + own_weight
        blended = jnp.dot(
            weights.astype(jnp.bfloat16), values[r], preferred_element_type=jnp.float32
        )
        blended = (blended + own_weight * new_value) / totals
        for j in range(len(starts)):
            block = blended[j * n : (j + 1) * n]
            swapped = pltpu.roll(block, n // 2, 0)
            parts = [jnp.where(side == 0, block, swapped), jnp.where(side == 0, swapped, block)]
            for i in range(n // 2):
                at = (i * len(starts) + j) * DH
                for k, part in enumerate(parts):
                    held[k, r : r + 1, at : at + DH] = part[i : i + 1]
    mine[...] = held[0].astype(jnp.bfloat16)
    other[...] = held[1].astype(jnp.bfloat16)


def attend(lengths, arrived, cosine, sine, keys, values):
    n = len(ARRIVED)
    _, rows, stripe = arrived[0].shape
    shape = jax.ShapeDtypeStruct((rows, HEADS * DH // 2), jnp.bfloat16)
    return pl.pallas_call(
        attend_kernel,
        out_shape=[shape, shape],
        in_specs=[IN_SMEM] + [IN_VMEM] * 9,
        out_specs=[IN_VMEM] * 2,
        scratch_shapes=[
            pltpu.VMEM((rows, n, stripe), jnp.float32),
            pltpu.VMEM((2, rows, HEADS * DH // 2), jnp.float32),
        ],
        compiler_params=pltpu.CompilerParams(vmem_limit_bytes=8 * MIB),
        name="attend",
    )(lengths, *arrived, cosine, sine, in_vmem(keys), in_vmem(values))


def output_kernel(n, *refs):
    shards = refs[: n - 1]
    far = refs[n - 1 : n + 1]
    weights = refs[n + 1 : -4]
    keep, give, total, placed = refs[-4:]
    rows = shards[0].shape[0]
    half = far[0].shape[1]
    for part in range(2):
        start = part * half
        cols = slice(start, start + half)
        x = [ref[:, cols] for ref in shards] + [far[part][...]]
        x = jnp.concatenate([piece.astype(jnp.float32) for piece in x], axis=0)
        x = x.astype(jnp.bfloat16)
        first = 0
        for weight in weights:
            last = first + weight.shape[0]
            low, high = max(first, start), min(last, start + half)
            if low < high:
                term = jnp.dot(
                    x[:, low - start : high - start],
                    weight[low - first : high - first, :],
                    preferred_element_type=jnp.float32,
                )
                if low == 0:
                    total[...] = term
                else:
                    total[...] += term
            first = last
    side = lax.axis_index("gy")
    for i, owner in enumerate(owners(n)):
        block = total[i * rows : (i + 1) * rows, :]
        placed[owner] = jnp.where(side == 0, block, pltpu.roll(block, rows // 2, 0))
    keep[...] = placed[pl.ds(side * (n // 2), n // 2)]
    give[...] = placed[pl.ds((1 - side) * (n // 2), n // 2)]


def output_project(shards, far, weights):
    n = len(shards) + 1
    rows = shards[0].shape[0]
    cols = weights[0].shape[1]
    shape = jax.ShapeDtypeStruct((n // 2, rows, cols), jnp.float32)
    return pl.pallas_call(
        lambda *refs: output_kernel(n, *refs),
        out_shape=[shape, shape],
        in_specs=[IN_VMEM] * (n + 1 + len(weights)),
        out_specs=[IN_VMEM] * 2,
        scratch_shapes=[
            pltpu.VMEM((n * rows, cols), jnp.float32),
            pltpu.VMEM((n, rows, cols), jnp.float32),
        ],
        compiler_params=pltpu.CompilerParams(vmem_limit_bytes=8 * MIB),
        name="output_project",
    )(*shards, *far, *[in_vmem(w) for w in weights])


def on_any_grid(
    activations,
    norm_gain,
    query_weight,
    keyval_weight,
    output_weight,
    cache_keys,
    cache_values,
    cache_lengths,
):
    inputs = activations.astype(jnp.float32)
    row_sums, square_sums = lax.psum(
        (jnp.sum(inputs, axis=1), jnp.sum(inputs * inputs, axis=1)), "gy"
    )
    row_mean = row_sums[:, None] / D
    row_square = square_sums[:, None] / D
    variance = row_square - row_mean * row_mean
    normed = (
        (inputs - row_mean) * lax.rsqrt(variance + epsilon) * norm_gain.astype(jnp.float32)
    ).astype(jnp.bfloat16)
    shard_rows = lax.all_gather(normed, "gx", axis=0, tiled=True)
    query_part = lax.dot_general(
        shard_rows, query_weight, contract, preferred_element_type=jnp.float32
    )
    keyval_part = lax.dot_general(
        shard_rows, keyval_weight, contract, preferred_element_type=jnp.float32
    )
    partial_sums = jnp.concatenate([query_part, keyval_part], axis=1)
    wide_count = lax.axis_size("gx")
    pair_count = lax.axis_size("gy")
    local_rows = cache_lengths.shape[0]
    stripe = partial_sums.shape[1]
    arrived = lax.all_to_all(partial_sums, ("gx", "gy"), split_axis=0, concat_axis=1, tiled=True)
    gathered = jnp.sum(arrived.reshape(local_rows, wide_count, pair_count, stripe), axis=2).astype(
        jnp.bfloat16
    )
    query_cols = query_weight.shape[0]
    queries = gathered[:, :, :query_cols].reshape(local_rows, HEADS, DH)
    keyvals = gathered[:, :, query_cols:].reshape(local_rows, 2 * DH)
    places = cache_lengths.astype(jnp.float32)
    queries = rotate(queries.astype(jnp.float32), places[:, None, None]).astype(jnp.bfloat16)
    new_keys = rotate(keyvals[:, :DH].astype(jnp.float32), places[:, None]).astype(jnp.bfloat16)
    new_values = keyvals[:, DH:].astype(jnp.float32)
    score_scale = 1.0 / math.sqrt(DH)
    scores = (
        jnp.einsum("rhd,rtd->rht", queries, cache_keys, preferred_element_type=jnp.float32)
        * score_scale
    )
    visible = jnp.arange(cache_keys.shape[1])[None, :] < cache_lengths[:, None]
    scores = jnp.where(visible[:, None, :], scores, -1e30)
    own_score = (
        jnp.einsum("rhd,rd->rh", queries, new_keys, preferred_element_type=jnp.float32)
        * score_scale
    )
    highest = jnp.maximum(jnp.max(scores, axis=2), own_score)
    weights = jnp.exp(scores - highest[:, :, None])
    own_weight = jnp.exp(own_score - highest)
    totals = jnp.sum(weights, axis=2) + own_weight
    blended = jnp.einsum(
        "rht,rtd->rhd",
        weights.astype(jnp.bfloat16),
        cache_values,
        preferred_element_type=jnp.float32,
    )
    blended = blended + own_weight[:, :, None] * new_values[:, None, :]
    attended = (blended / totals[:, :, None]).astype(jnp.bfloat16).reshape(local_rows, HEADS * DH)
    swapped = lax.all_to_all(attended, "gy", split_axis=1, concat_axis=0, tiled=True)
    partial_out = jnp.dot(
        lax.all_gather(swapped, "gx", axis=0, tiled=True),
        output_weight,
        preferred_element_type=jnp.float32,
    )
    return lax.psum_scatter(partial_out, "gy", scatter_dimension=0, tiled=True).astype(jnp.bfloat16)


def on_device(
    activations,
    norm_gain,
    query_weight,
    keyval_weight,
    output_weight,
    cache_keys,
    cache_values,
    cache_lengths,
):
    n = lax.axis_size("gx")
    ring = Ring(n)
    query_cols, width = query_weight.shape
    new_cols = keyval_weight.shape[0]
    piece = query_cols // 4
    weights = []

    indices = jnp.arange(DH // 2, dtype=jnp.float32)
    frequency = jnp.exp(-math.log(10000.0) * indices / (DH // 2))
    angles = cache_lengths.astype(jnp.float32)[:, None] * frequency
    cosine, sine = jnp.cos(angles), jnp.sin(angles)

    def piece_of(array, start, size, after):
        return load(size, [(array, start, size, 0)], after)

    left = right = activations
    shards = [activations]
    sums = []
    for step in range(1, n // 2):
        arrived = shards[-2:] if step > 1 else []
        left, right = ring.step(left, right)
        if step > 1:
            sums = [row_sums([activations, *arrived] if step == 2 else arrived, sums)]
        weight = piece_of(query_weight, (step - 1) * piece, piece, arrived)
        weight, (left, right, *sums) = before(weight, left, right, *sums)
        weights.append(weight)
        shards += [left, right]
    far = ring.step(left[:, : width // 2], right[:, width // 2 :])
    sums = row_sums([left, right], sums)
    jobs = [(query_weight, 3 * piece, piece, 0), (keyval_weight, 0, new_cols, None)]
    weight = load(piece + 2 * new_cols, jobs, [left, right])
    weight, far = before(weight, *far)
    sums = row_sums([], [sums], far)
    other_sums = swap_pair(sums)
    weights.append(weight)
    gain = norm_gain.astype(jnp.float32)[None, :]
    unit = output_weight.shape[0] // 24
    keep, give, weight = project(
        (sums, other_sums), gain, shards, far, weights, output_weight, 8 * unit
    )
    weights = [weight]

    def exchange(blocks, d):
        return lax.ppermute(blocks, "gx", [(i, i ^ d) for i in range(n)])

    blocks = split(keep, swap_pair(give))
    arrived = [blocks[0]] + [exchange(blocks[d], d) for d in range(1, 4)]
    keys = load_cache(cache_keys, [blocks[1]])
    keys, arrived = before(keys, *arrived)
    across = pack([(0, 1), (1, 1), (2, 1), (3, 1)], *arrived)
    last = exchange(across, 4)
    values = load_cache(cache_values, [across])
    weight = load(4 * unit, [(output_weight, 8 * unit, 4 * unit, 0)], [across])
    values, (last,) = before(values, last)
    weight, (last,) = before(weight, last)
    weights.append(weight)
    arrived = [*arrived, last]
    mine, other = attend(cache_lengths, arrived, cosine, sine, keys, values)
    shard = jnp.concatenate([mine, swap_pair(other)], axis=0)

    left = right = shard
    shards = [shard]
    done, piece = 12 * unit, 3 * unit

    for step in range(1, n // 2):
        arrived = shards[-2:]
        left, right = ring.step(left, right)
        weight = piece_of(output_weight, done + (step - 1) * piece, piece, arrived)
        weight, (left, right) = before(weight, left, right)
        weights.append(weight)
        shards += [left, right]
    half = shard.shape[1] // 2
    far = ring.step(left[:, :half], right[:, half:])
    weight = piece_of(output_weight, done + 3 * piece, piece, [left, right])
    weight, far = before(weight, *far)
    weights.append(weight)
    keep, give = output_project(shards, far, weights)
    out = (keep + swap_pair(give)).astype(jnp.bfloat16)
    return out.reshape(-1, out.shape[-1])


def solution(mesh):
    return jax.shard_map(
        on_device if mesh.shape["gx"] == 8 else on_any_grid,
        mesh=mesh,
        in_specs=(
            P(("groups", "gx"), "gy"),
            P("gy"),
            P("gx", "gy"),
            P("gx", "gy"),
            P("gy", "gx"),
            P(("groups", "gx", "gy"), None, None),
            P(("groups", "gx", "gy"), None, None),
            P(("groups", "gx", "gy")),
        ),
        out_specs=P(("groups", "gy"), "gx"),
        check_vma=False,
    )
```

```python
import math

import jax
import jax.numpy as jnp
from jax import lax
from jax.experimental import pallas as pl
from jax.experimental.pallas import tpu as pltpu
from jax.sharding import PartitionSpec as P

D = 18432
HEADS = 48
DH = 256


epsilon = 1e-06
contract = (((1,), (1,)), ((), ()))
MIB = 1 << 20
ANY = pl.BlockSpec(memory_space=pl.ANY)
IN_HBM = pl.BlockSpec(memory_space=pltpu.HBM)
IN_VMEM = pl.BlockSpec(memory_space=pltpu.VMEM)
IN_SMEM = pl.BlockSpec(memory_space=pltpu.SMEM)


def rotate(vectors, places):
    half_width = vectors.shape[-1] // 2
    indices = jnp.arange(half_width, dtype=jnp.float32)
    frequency = jnp.exp(-math.log(10000.0) * indices / half_width)
    angles = places * frequency
    cosine = jnp.cos(angles)
    sine = jnp.sin(angles)
    first_half = vectors[..., :half_width]
    second_half = vectors[..., half_width:]
    return jnp.concatenate(
        [first_half * cosine - second_half * sine, second_half * cosine + first_half * sine],
        axis=-1,
    )


def ring_order(n):
    return list(range(0, n, 2)) + list(range(n - 1, 0, -2))


def swap_pair(x):
    return lax.ppermute(x, "gy", [(0, 1), (1, 0)])


class Ring:
    def __init__(self, n):
        order = ring_order(n)
        self.onward = [(order[p], order[(p + 1) % n]) for p in range(n)]
        self.back = [(order[p], order[(p - 1) % n]) for p in range(n)]
        self.across = [(order[p], order[(p + n // 2) % n]) for p in range(n)]

    def step(self, left, right):
        return lax.ppermute(left, "gx", self.onward), lax.ppermute(right, "gx", self.back)


def owners(n):
    offsets = [0]
    for step in range(1, n // 2):
        offsets += [-step, step]
    offsets.append(n // 2)
    me = lax.axis_index("gx")
    half = lax.div(me, 2)
    place = jnp.where(lax.rem(me, 2) == 0, half, n - 1 - half)
    result = []
    for offset in offsets:
        at = lax.rem(place + (offset + n), n)
        result.append(jnp.where(at < n // 2, 2 * at, 2 * (n - 1 - at) + 1))
    return result


def start_copies(source, target, sems, count):
    rows = source.shape[0]
    size = -(-rows // (16 * count)) * 16
    copies = []
    for i, first in enumerate(range(0, rows, size)):
        at = pl.ds(first, min(size, rows - first))
        copy = pltpu.make_async_copy(source.at[at], target.at[at], sems.at[i])
        copy.start()
        copies.append(copy)
    return copies


def load_kernel(jobs, *refs):
    sources, target, sems = refs[: len(jobs)], refs[-2], refs[-1]
    copies = []
    for i, (first, size, at) in enumerate(jobs):
        part = sources[i].at[pl.ds(first, size)]
        copies += start_copies(part, target.at[pl.ds(at, size)], sems.at[i], 4)
    for copy in copies:
        copy.wait()


def load(rows, jobs, after=()):
    array = jobs[0][0]
    return pl.pallas_call(
        lambda *refs: load_kernel([job[1:] for job in jobs], *refs),
        out_shape=pltpu.VMEM((rows, array.shape[1]), array.dtype),
        in_specs=[IN_HBM] * len(jobs) + [ANY] * len(after),
        out_specs=IN_VMEM,
        scratch_shapes=[pltpu.SemaphoreType.DMA((len(jobs), 4))],
        compiler_params=pltpu.CompilerParams(vmem_limit_bytes=MIB),
        name="load",
    )(*[in_hbm(job[0]) for job in jobs], *after)


def load_cache_kernel(source, *refs):
    target, sems = refs[-2:]
    copies = []
    for row in range(source.shape[0]):
        copies.append(pltpu.make_async_copy(source.at[row], target.at[row], sems.at[row]))
        copies[-1].start()
    for copy in copies:
        copy.wait()


def load_cache(cache, after):
    return pl.pallas_call(
        load_cache_kernel,
        out_shape=pltpu.VMEM(cache.shape, cache.dtype),
        in_specs=[IN_HBM] + [ANY] * len(after),
        out_specs=IN_VMEM,
        scratch_shapes=[pltpu.SemaphoreType.DMA((cache.shape[0],))],
        compiler_params=pltpu.CompilerParams(vmem_limit_bytes=MIB),
        name="load_cache",
    )(in_hbm(cache), *after)


def in_hbm(array):
    return pltpu.with_memory_space_constraint(array, pltpu.HBM)


def in_vmem(array):
    return pltpu.with_memory_space_constraint(array, pltpu.VMEM)


def before(done, *rest):
    held = lax.optimization_barrier((done,) + rest)
    return held[0], held[1:]


def sums_kernel(ready, count, *refs):
    out = refs[-1]
    start = 0
    for ref in refs[:ready]:
        out[start : start + ref.shape[0], :] = ref[...]
        start += ref.shape[0]
    rows = refs[ready].shape[0]
    lane = lax.broadcasted_iota(jnp.int32, (rows, 128), 1)
    for ref in refs[ready : ready + count]:
        x = ref[...].astype(jnp.float32)
        total = jnp.sum(x, axis=1, keepdims=True)
        square = jnp.sum(x * x, axis=1, keepdims=True)
        both = jnp.where(lane == 0, total, jnp.where(lane == 1, square, 0.0))
        out[start : start + rows, :] = both
        start += rows


def row_sums(shards, ready=(), after=()):
    rows = shards[0].shape[0] * len(shards) + sum(r.shape[0] for r in ready)
    return pl.pallas_call(
        lambda *refs: sums_kernel(len(ready), len(shards), *refs),
        out_shape=jax.ShapeDtypeStruct((rows, 128), jnp.float32),
        in_specs=[IN_VMEM] * (len(ready) + len(shards)) + [ANY] * len(after),
        out_specs=IN_VMEM,
        compiler_params=pltpu.CompilerParams(vmem_limit_bytes=8 * MIB),
        name="row_sums",
    )(*ready, *shards, *after)


def project_kernel(n, parts, *refs):
    sums_a, sums_b, gain = refs[:3]
    shards = refs[3 : 3 + n - 1]
    far = refs[3 + n - 1 : 3 + n + 1]
    weights = refs[4 + n : 4 + n + parts]
    keep, give, normed, total = refs[4 + n + parts :]
    rows, width = shards[0].shape
    sums = sums_a[...] + sums_b[...]
    row_mean = sums[:, :1] / D
    row_square = sums[:, 1:2] / D
    scale = lax.rsqrt(row_square - row_mean * row_mean + epsilon)
    for part in range(2):
        cols = slice(part * width // 2, (part + 1) * width // 2)
        for i in range(0, n, 2):
            x = [ref[:, cols] if ref is not far[part] else ref[...] for ref in (*shards, far[part])]
            x = jnp.concatenate([piece.astype(jnp.float32) for piece in x[i : i + 2]], axis=0)
            at = slice(i * rows, (i + 2) * rows)
            x = (x - row_mean[at]) * scale[at] * gain[:, cols]
            normed[at, cols] = x.astype(jnp.bfloat16)
        x = normed[:, cols]
        start = 0
        for weight in weights:
            term = lax.dot_general(
                x, weight[:, cols], contract, preferred_element_type=jnp.float32
            )
            stripe = slice(start, start + weight.shape[0])
            if part == 0:
                total[:, stripe] = term
            else:
                total[:, stripe] += term
            start = stripe.stop
    last = slice(total.shape[1] - 128, total.shape[1])
    lane = lax.broadcasted_iota(jnp.int32, (total.shape[0], 128), 1)
    new = jnp.where(lane < 64, total[:, last], 0.0)
    odd = lax.rem(lax.axis_index("gx"), 2)
    total[:, last] = jnp.where(odd == 0, new, pltpu.roll(new, 64, 1))
    side = lax.axis_index("gy")
    local = rows // 2
    for i, owner in enumerate(owners(n)):
        block = total[i * rows : (i + 1) * rows, :]
        low, high = block[:local], block[local:]
        keep[owner] = jnp.where(side == 0, low, high)
        give[owner] = jnp.where(side == 0, high, low)


def project(sums, gain, shards, far, weights):
    n = len(shards) + 1
    rows, width = shards[0].shape
    stripe = sum(w.shape[0] for w in weights) + 64
    shape = jax.ShapeDtypeStruct((n, rows // 2, stripe), jnp.float32)
    return pl.pallas_call(
        lambda *refs: project_kernel(n, len(weights), *refs),
        out_shape=[shape, shape],
        in_specs=[IN_VMEM] * (4 + n + len(weights)),
        out_specs=[IN_VMEM] * 2,
        scratch_shapes=[
            pltpu.VMEM((n * rows, width), jnp.bfloat16),
            pltpu.VMEM((n * rows, stripe), jnp.float32),
        ],
        compiler_params=pltpu.CompilerParams(vmem_limit_bytes=6 * MIB),
        name="project",
    )(
        *sums,
        gain,
        *shards,
        *far,
        *[in_vmem(w) for w in weights],
    )


def split_kernel(keep, got, *outs):
    me = lax.axis_index("gx")
    for d in range(keep.shape[0]):
        at = jnp.bitwise_xor(me, d)
        outs[d % 4][d // 4] = (keep[at] + got[at]).astype(jnp.bfloat16)


def split(keep, got):
    shape = jax.ShapeDtypeStruct((2,) + keep.shape[1:], jnp.bfloat16)
    return pl.pallas_call(
        split_kernel,
        out_shape=[shape] * 4,
        in_specs=[IN_VMEM] * 2,
        out_specs=[IN_VMEM] * 4,
        compiler_params=pltpu.CompilerParams(vmem_limit_bytes=8 * MIB),
        name="split",
    )(keep, got)


def pack(picks, *sources):
    def pack_kernel(*refs):
        for k, (i, j) in enumerate(picks):
            refs[-1][k] = refs[i][j]

    return pl.pallas_call(
        pack_kernel,
        out_shape=jax.ShapeDtypeStruct((len(picks),) + sources[0].shape[1:], sources[0].dtype),
        in_specs=[IN_VMEM] * len(sources),
        out_specs=IN_VMEM,
        compiler_params=pltpu.CompilerParams(vmem_limit_bytes=8 * MIB),
        name="pack",
    )(*sources)


ARRIVED = [(0, 0), (1, 0), (2, 0), (3, 0), (4, 0), (4, 1), (4, 2), (4, 3)]


def attend_kernel(lengths, *refs):
    arrived = refs[:5]
    cosine, sine, keys, values, mine, other, spread, held = refs[5:]
    n, rows, stripe = spread.shape[1], spread.shape[0], spread.shape[2]
    me = lax.axis_index("gx")
    query_cols = stripe - 128
    side = lax.axis_index("gy")
    score_scale = 1.0 / math.sqrt(DH)
    for d, (i, j) in enumerate(ARRIVED):
        block = arrived[i][j].astype(jnp.float32)
        for r in range(rows):
            spread[r, pl.ds(jnp.bitwise_xor(me, d), 1), :] = block[r : r + 1, :]
    starts = range(0, query_cols, DH)
    ready = []
    for r in range(rows):
        given = spread[r]
        cos, sin = cosine[r : r + 1, :], sine[r : r + 1, :]

        def turn(a, b):
            turned = jnp.concatenate([a * cos - b * sin, b * cos + a * sin], axis=1)
            return turned.astype(jnp.bfloat16)

        q = turn(
            jnp.concatenate([given[:, c : c + DH // 2] for c in starts], axis=0),
            jnp.concatenate([given[:, c + DH // 2 : c + DH] for c in starts], axis=0),
        )
        q = (q.astype(jnp.float32) * score_scale).astype(jnp.bfloat16)
        new = [
            given[i : i + 1, query_cols:] + given[i + 1 : i + 2, query_cols:]
            for i in range(0, n, 2)
        ]
        new_key = turn(new[0], new[1]).astype(jnp.float32)
        new_value = jnp.concatenate(new[2:], axis=1)
        scores = lax.dot_general(q, keys[r], contract, preferred_element_type=jnp.float32)
        own_score = jnp.sum(q.astype(jnp.float32) * new_key, axis=1, keepdims=True)
        ready.append((scores, own_score, new_value))
    for r, (scores, own_score, new_value) in enumerate(ready):
        place = lax.broadcasted_iota(jnp.int32, scores.shape, 1)
        scores = jnp.where(place < lengths[r], scores, -1e30)
        highest = jnp.maximum(jnp.max(scores, axis=1, keepdims=True), own_score)
        weights = jnp.exp(scores - highest)
        own_weight = jnp.exp(own_score - highest)
        totals = jnp.sum(weights, axis=1, keepdims=True) + own_weight
        blended = jnp.dot(
            weights.astype(jnp.bfloat16), values[r], preferred_element_type=jnp.float32
        )
        blended = (blended + own_weight * new_value) / totals
        for j in range(len(starts)):
            block = blended[j * n : (j + 1) * n]
            swapped = pltpu.roll(block, n // 2, 0)
            parts = [jnp.where(side == 0, block, swapped), jnp.where(side == 0, swapped, block)]
            for i in range(n // 2):
                at = (i * len(starts) + j) * DH
                for k, part in enumerate(parts):
                    held[k, r : r + 1, at : at + DH] = part[i : i + 1]
    mine[...] = held[0].astype(jnp.bfloat16)
    other[...] = held[1].astype(jnp.bfloat16)


def attend(lengths, arrived, cosine, sine, keys, values):
    n = len(ARRIVED)
    _, rows, stripe = arrived[0].shape
    shape = jax.ShapeDtypeStruct((rows, HEADS * DH // 2), jnp.bfloat16)
    return pl.pallas_call(
        attend_kernel,
        out_shape=[shape, shape],
        in_specs=[IN_SMEM] + [IN_VMEM] * 9,
        out_specs=[IN_VMEM] * 2,
        scratch_shapes=[
            pltpu.VMEM((rows, n, stripe), jnp.float32),
            pltpu.VMEM((2, rows, HEADS * DH // 2), jnp.float32),
        ],
        compiler_params=pltpu.CompilerParams(vmem_limit_bytes=8 * MIB),
        name="attend",
    )(lengths, *arrived, cosine, sine, in_vmem(keys), in_vmem(values))


def output_kernel(n, *refs):
    shards = refs[: n - 1]
    far = refs[n - 1 : n + 1]
    weights = refs[n + 1 : -4]
    keep, give, total, placed = refs[-4:]
    rows = shards[0].shape[0]
    half = far[0].shape[1]
    for part in range(2):
        start = part * half
        cols = slice(start, start + half)
        x = [ref[:, cols] for ref in shards] + [far[part][...]]
        x = jnp.concatenate([piece.astype(jnp.float32) for piece in x], axis=0)
        x = x.astype(jnp.bfloat16)
        first = 0
        for weight in weights:
            last = first + weight.shape[0]
            low, high = max(first, start), min(last, start + half)
            if low < high:
                term = jnp.dot(
                    x[:, low - start : high - start],
                    weight[low - first : high - first, :],
                    preferred_element_type=jnp.float32,
                )
                if low == 0:
                    total[...] = term
                else:
                    total[...] += term
            first = last
    side = lax.axis_index("gy")
    for i, owner in enumerate(owners(n)):
        block = total[i * rows : (i + 1) * rows, :]
        placed[owner] = jnp.where(side == 0, block, pltpu.roll(block, rows // 2, 0))
    keep[...] = placed[pl.ds(side * (n // 2), n // 2)]
    give[...] = placed[pl.ds((1 - side) * (n // 2), n // 2)]


def output_project(shards, far, weights):
    n = len(shards) + 1
    rows = shards[0].shape[0]
    cols = weights[0].shape[1]
    shape = jax.ShapeDtypeStruct((n // 2, rows, cols), jnp.float32)
    return pl.pallas_call(
        lambda *refs: output_kernel(n, *refs),
        out_shape=[shape, shape],
        in_specs=[IN_VMEM] * (n + 1 + len(weights)),
        out_specs=[IN_VMEM] * 2,
        scratch_shapes=[
            pltpu.VMEM((n * rows, cols), jnp.float32),
            pltpu.VMEM((n, rows, cols), jnp.float32),
        ],
        compiler_params=pltpu.CompilerParams(vmem_limit_bytes=8 * MIB),
        name="output_project",
    )(*shards, *far, *[in_vmem(w) for w in weights])


def on_any_grid(
    activations,
    norm_gain,
    query_weight,
    keyval_weight,
    output_weight,
    cache_keys,
    cache_values,
    cache_lengths,
):
    inputs = activations.astype(jnp.float32)
    row_sums, square_sums = lax.psum(
        (jnp.sum(inputs, axis=1), jnp.sum(inputs * inputs, axis=1)), "gy"
    )
    row_mean = row_sums[:, None] / D
    row_square = square_sums[:, None] / D
    variance = row_square - row_mean * row_mean
    normed = (
        (inputs - row_mean) * lax.rsqrt(variance + epsilon) * norm_gain.astype(jnp.float32)
    ).astype(jnp.bfloat16)
    shard_rows = lax.all_gather(normed, "gx", axis=0, tiled=True)
    query_part = lax.dot_general(
        shard_rows, query_weight, contract, preferred_element_type=jnp.float32
    )
    keyval_part = lax.dot_general(
        shard_rows, keyval_weight, contract, preferred_element_type=jnp.float32
    )
    partial_sums = jnp.concatenate([query_part, keyval_part], axis=1)
    wide_count = lax.axis_size("gx")
    pair_count = lax.axis_size("gy")
    local_rows = cache_lengths.shape[0]
    stripe = partial_sums.shape[1]
    arrived = lax.all_to_all(partial_sums, ("gx", "gy"), split_axis=0, concat_axis=1, tiled=True)
    gathered = jnp.sum(arrived.reshape(local_rows, wide_count, pair_count, stripe), axis=2).astype(
        jnp.bfloat16
    )
    query_cols = query_weight.shape[0]
    queries = gathered[:, :, :query_cols].reshape(local_rows, HEADS, DH)
    keyvals = gathered[:, :, query_cols:].reshape(local_rows, 2 * DH)
    places = cache_lengths.astype(jnp.float32)
    queries = rotate(queries.astype(jnp.float32), places[:, None, None]).astype(jnp.bfloat16)
    new_keys = rotate(keyvals[:, :DH].astype(jnp.float32), places[:, None]).astype(jnp.bfloat16)
    new_values = keyvals[:, DH:].astype(jnp.float32)
    score_scale = 1.0 / math.sqrt(DH)
    scores = (
        jnp.einsum("rhd,rtd->rht", queries, cache_keys, preferred_element_type=jnp.float32)
        * score_scale
    )
    visible = jnp.arange(cache_keys.shape[1])[None, :] < cache_lengths[:, None]
    scores = jnp.where(visible[:, None, :], scores, -1e30)
    own_score = (
        jnp.einsum("rhd,rd->rh", queries, new_keys, preferred_element_type=jnp.float32)
        * score_scale
    )
    highest = jnp.maximum(jnp.max(scores, axis=2), own_score)
    weights = jnp.exp(scores - highest[:, :, None])
    own_weight = jnp.exp(own_score - highest)
    totals = jnp.sum(weights, axis=2) + own_weight
    blended = jnp.einsum(
        "rht,rtd->rhd",
        weights.astype(jnp.bfloat16),
        cache_values,
        preferred_element_type=jnp.float32,
    )
    blended = blended + own_weight[:, :, None] * new_values[:, None, :]
    attended = (blended / totals[:, :, None]).astype(jnp.bfloat16).reshape(local_rows, HEADS * DH)
    swapped = lax.all_to_all(attended, "gy", split_axis=1, concat_axis=0, tiled=True)
    partial_out = jnp.dot(
        lax.all_gather(swapped, "gx", axis=0, tiled=True),
        output_weight,
        preferred_element_type=jnp.float32,
    )
    return lax.psum_scatter(partial_out, "gy", scatter_dimension=0, tiled=True).astype(jnp.bfloat16)


def on_device(
    activations,
    norm_gain,
    query_weight,
    keyval_weight,
    output_weight,
    cache_keys,
    cache_values,
    cache_lengths,
):
    n = lax.axis_size("gx")
    ring = Ring(n)
    query_cols, width = query_weight.shape
    new_cols = keyval_weight.shape[0]
    piece = query_cols // 4
    weights = []

    indices = jnp.arange(DH // 2, dtype=jnp.float32)
    frequency = jnp.exp(-math.log(10000.0) * indices / (DH // 2))
    angles = cache_lengths.astype(jnp.float32)[:, None] * frequency
    cosine, sine = jnp.cos(angles), jnp.sin(angles)

    def piece_of(array, start, size, after):
        return load(size, [(array, start, size, 0)], after)

    left = right = activations
    shards = [activations]
    sums = []
    for step in range(1, n // 2):
        arrived = shards[-2:] if step > 1 else []
        left, right = ring.step(left, right)
        if step > 1:
            sums = [row_sums([activations, *arrived] if step == 2 else arrived, sums)]
        if step == 3:
            far_sums = lax.ppermute(sums[0][: activations.shape[0]], "gx", ring.across)
        weight = piece_of(query_weight, (step - 1) * piece, piece, arrived)
        weight, (left, right, *sums) = before(weight, left, right, *sums)
        weights.append(weight)
        shards += [left, right]
    cut, (cut_right, left, right) = before(
        left[:, : width // 2], right[:, width // 2 :], left, right
    )
    far = ring.step(cut, cut_right)
    sums = row_sums([left, right], sums)
    jobs = [(query_weight, 3 * piece, piece, 0), (keyval_weight, 0, new_cols, piece)]
    weight = load(piece + new_cols, jobs, [sums])
    sums = jnp.concatenate([sums, far_sums], axis=0)
    other_sums = swap_pair(sums)
    weight, (other_sums, *far) = before(weight, other_sums, *far)
    weights.append(weight)
    gain = norm_gain.astype(jnp.float32)[None, :]
    keep, give = project((sums, other_sums), gain, shards, far, weights)

    def exchange(blocks, d):
        return lax.ppermute(blocks, "gx", [(i, i ^ d) for i in range(n)])

    blocks = split(keep, swap_pair(give))
    arrived = [blocks[0]] + [exchange(blocks[d], d) for d in range(1, 4)]
    keys = load_cache(cache_keys, [blocks[1]])
    keys, arrived = before(keys, *arrived)
    across = pack([(0, 1), (1, 1), (2, 1), (3, 1)], *arrived)
    last = exchange(across, 4)
    values = load_cache(cache_values, [across])
    done = output_weight.shape[0] // 6
    weight = load(done, [(output_weight, 0, done, 0)], [across])
    values, (last,) = before(values, last)
    weight, (last,) = before(weight, last)
    weights = [weight]
    arrived = [*arrived, last]
    mine, other = attend(cache_lengths, arrived, cosine, sine, keys, values)
    shard = jnp.concatenate([mine, swap_pair(other)], axis=0)

    left = right = shard
    shards = [shard]
    piece = (output_weight.shape[0] - done) // 4

    for step in range(1, n // 2):
        arrived = shards[-2:]
        left, right = ring.step(left, right)
        weight = piece_of(output_weight, done + (step - 1) * piece, piece, arrived)
        weight, (left, right) = before(weight, left, right)
        weights.append(weight)
        shards += [left, right]
    half = shard.shape[1] // 2
    far = ring.step(left[:, :half], right[:, half:])
    weight = piece_of(output_weight, done + 3 * piece, piece, [left, right])
    weight, far = before(weight, *far)
    weights.append(weight)
    keep, give = output_project(shards, far, weights)
    out = (keep + swap_pair(give)).astype(jnp.bfloat16)
    return out.reshape(-1, out.shape[-1])


def solution(mesh):
    return jax.shard_map(
        on_device if mesh.shape["gx"] == 8 else on_any_grid,
        mesh=mesh,
        in_specs=(
            P(("groups", "gx"), "gy"),
            P("gy"),
            P("gx", "gy"),
            P("gx", "gy"),
            P("gy", "gx"),
            P(("groups", "gx", "gy"), None, None),
            P(("groups", "gx", "gy"), None, None),
            P(("groups", "gx", "gy")),
        ),
        out_specs=P(("groups", "gy"), "gx"),
        check_vma=False,
    )
```

```python
import math

import jax
import jax.numpy as jnp
from jax import lax
from jax.experimental import pallas as pl
from jax.experimental.pallas import tpu as pltpu
from jax.sharding import PartitionSpec as P

D = 18432
HEADS = 48
DH = 256


epsilon = 1e-06
contract = (((1,), (1,)), ((), ()))
MIB = 1 << 20
ANY = pl.BlockSpec(memory_space=pl.ANY)
IN_HBM = pl.BlockSpec(memory_space=pltpu.HBM)
IN_VMEM = pl.BlockSpec(memory_space=pltpu.VMEM)
IN_SMEM = pl.BlockSpec(memory_space=pltpu.SMEM)


def rotate(vectors, places):
    half_width = vectors.shape[-1] // 2
    indices = jnp.arange(half_width, dtype=jnp.float32)
    frequency = jnp.exp(-math.log(10000.0) * indices / half_width)
    angles = places * frequency
    cosine = jnp.cos(angles)
    sine = jnp.sin(angles)
    first_half = vectors[..., :half_width]
    second_half = vectors[..., half_width:]
    return jnp.concatenate(
        [first_half * cosine - second_half * sine, second_half * cosine + first_half * sine],
        axis=-1,
    )


def ring_order(n):
    return list(range(0, n, 2)) + list(range(n - 1, 0, -2))


def swap_pair(x):
    return lax.ppermute(x, "gy", [(0, 1), (1, 0)])


class Ring:
    def __init__(self, n):
        order = ring_order(n)
        self.onward = [(order[p], order[(p + 1) % n]) for p in range(n)]
        self.back = [(order[p], order[(p - 1) % n]) for p in range(n)]
        self.across = [(order[p], order[(p + n // 2) % n]) for p in range(n)]

    def step(self, left, right):
        return lax.ppermute(left, "gx", self.onward), lax.ppermute(right, "gx", self.back)


def owners(n):
    offsets = [0]
    for step in range(1, n // 2):
        offsets += [-step, step]
    offsets.append(n // 2)
    me = lax.axis_index("gx")
    half = lax.div(me, 2)
    place = jnp.where(lax.rem(me, 2) == 0, half, n - 1 - half)
    result = []
    for offset in offsets:
        at = lax.rem(place + (offset + n), n)
        result.append(jnp.where(at < n // 2, 2 * at, 2 * (n - 1 - at) + 1))
    return result


def start_copies(source, target, sems, count):
    rows = source.shape[0]
    size = -(-rows // (16 * count)) * 16
    copies = []
    for i, first in enumerate(range(0, rows, size)):
        at = pl.ds(first, min(size, rows - first))
        copy = pltpu.make_async_copy(source.at[at], target.at[at], sems.at[i])
        copy.start()
        copies.append(copy)
    return copies


def load_kernel(jobs, *refs):
    sources, target, sems = refs[: len(jobs)], refs[-2], refs[-1]
    copies = []
    for i, (first, size, at) in enumerate(jobs):
        part = sources[i].at[pl.ds(first, size)]
        copies += start_copies(part, target.at[pl.ds(at, size)], sems.at[i], 4)
    for copy in copies:
        copy.wait()


def load(rows, jobs, after=()):
    array = jobs[0][0]
    return pl.pallas_call(
        lambda *refs: load_kernel([job[1:] for job in jobs], *refs),
        out_shape=pltpu.VMEM((rows, array.shape[1]), array.dtype),
        in_specs=[IN_HBM] * len(jobs) + [ANY] * len(after),
        out_specs=IN_VMEM,
        scratch_shapes=[pltpu.SemaphoreType.DMA((len(jobs), 4))],
        compiler_params=pltpu.CompilerParams(vmem_limit_bytes=MIB),
        name="load",
    )(*[in_hbm(job[0]) for job in jobs], *after)


def load_cache_kernel(source, *refs):
    target, sems = refs[-2:]
    copies = []
    for row in range(source.shape[0]):
        copies.append(pltpu.make_async_copy(source.at[row], target.at[row], sems.at[row]))
        copies[-1].start()
    for copy in copies:
        copy.wait()


def load_cache(cache, after):
    return pl.pallas_call(
        load_cache_kernel,
        out_shape=pltpu.VMEM(cache.shape, cache.dtype),
        in_specs=[IN_HBM] + [ANY] * len(after),
        out_specs=IN_VMEM,
        scratch_shapes=[pltpu.SemaphoreType.DMA((cache.shape[0],))],
        compiler_params=pltpu.CompilerParams(vmem_limit_bytes=MIB),
        name="load_cache",
    )(in_hbm(cache), *after)


def in_hbm(array):
    return pltpu.with_memory_space_constraint(array, pltpu.HBM)


def in_vmem(array):
    return pltpu.with_memory_space_constraint(array, pltpu.VMEM)


def before(done, *rest):
    held = lax.optimization_barrier((done,) + rest)
    return held[0], held[1:]


def sums_kernel(ready, count, *refs):
    out = refs[-1]
    start = 0
    for ref in refs[:ready]:
        out[start : start + ref.shape[0], :] = ref[...]
        start += ref.shape[0]
    rows = refs[ready].shape[0]
    lane = lax.broadcasted_iota(jnp.int32, (rows, 128), 1)
    for ref in refs[ready : ready + count]:
        x = ref[...].astype(jnp.float32)
        total = jnp.sum(x, axis=1, keepdims=True)
        square = jnp.sum(x * x, axis=1, keepdims=True)
        both = jnp.where(lane == 0, total, jnp.where(lane == 1, square, 0.0))
        out[start : start + rows, :] = both
        start += rows


def row_sums(shards, ready=(), after=()):
    rows = shards[0].shape[0] * len(shards) + sum(r.shape[0] for r in ready)
    return pl.pallas_call(
        lambda *refs: sums_kernel(len(ready), len(shards), *refs),
        out_shape=jax.ShapeDtypeStruct((rows, 128), jnp.float32),
        in_specs=[IN_VMEM] * (len(ready) + len(shards)) + [ANY] * len(after),
        out_specs=IN_VMEM,
        compiler_params=pltpu.CompilerParams(vmem_limit_bytes=8 * MIB),
        name="row_sums",
    )(*ready, *shards, *after)


def project_kernel(n, parts, *refs):
    sums_a, sums_b, gain = refs[:3]
    shards = refs[3 : 3 + n - 1]
    far = refs[3 + n - 1 : 3 + n + 1]
    weights = refs[4 + n : 4 + n + parts]
    keep, give, normed, total = refs[4 + n + parts :]
    rows, width = shards[0].shape
    sums = sums_a[...] + sums_b[...]
    row_mean = sums[:, :1] / D
    row_square = sums[:, 1:2] / D
    scale = lax.rsqrt(row_square - row_mean * row_mean + epsilon)
    for part in range(2):
        cols = slice(part * width // 2, (part + 1) * width // 2)
        for i in range(0, n, 2):
            x = [ref[:, cols] if ref is not far[part] else ref[...] for ref in (*shards, far[part])]
            x = jnp.concatenate([piece.astype(jnp.float32) for piece in x[i : i + 2]], axis=0)
            at = slice(i * rows, (i + 2) * rows)
            x = (x - row_mean[at]) * scale[at] * gain[:, cols]
            normed[at, cols] = x.astype(jnp.bfloat16)
        x = normed[:, cols]
        start = 0
        for weight in weights:
            term = lax.dot_general(
                x, weight[:, cols], contract, preferred_element_type=jnp.float32
            )
            stripe = slice(start, start + weight.shape[0])
            if part == 0:
                total[:, stripe] = term
            else:
                total[:, stripe] += term
            start = stripe.stop
    last = slice(total.shape[1] - 128, total.shape[1])
    lane = lax.broadcasted_iota(jnp.int32, (total.shape[0], 128), 1)
    new = jnp.where(lane < 64, total[:, last], 0.0)
    odd = lax.rem(lax.axis_index("gx"), 2)
    total[:, last] = jnp.where(odd == 0, new, pltpu.roll(new, 64, 1))
    side = lax.axis_index("gy")
    local = rows // 2
    for i, owner in enumerate(owners(n)):
        block = total[i * rows : (i + 1) * rows, :]
        low, high = block[:local], block[local:]
        keep[owner] = jnp.where(side == 0, low, high)
        give[owner] = jnp.where(side == 0, high, low)


def project(sums, gain, shards, far, weights):
    n = len(shards) + 1
    rows, width = shards[0].shape
    stripe = sum(w.shape[0] for w in weights) + 64
    shape = jax.ShapeDtypeStruct((n, rows // 2, stripe), jnp.float32)
    return pl.pallas_call(
        lambda *refs: project_kernel(n, len(weights), *refs),
        out_shape=[shape, shape],
        in_specs=[IN_VMEM] * (4 + n + len(weights)),
        out_specs=[IN_VMEM] * 2,
        scratch_shapes=[
            pltpu.VMEM((n * rows, width), jnp.bfloat16),
            pltpu.VMEM((n * rows, stripe), jnp.float32),
        ],
        compiler_params=pltpu.CompilerParams(vmem_limit_bytes=6 * MIB),
        name="project",
    )(
        *sums,
        gain,
        *shards,
        *far,
        *[in_vmem(w) for w in weights],
    )


def split_kernel(keep, got, *outs):
    me = lax.axis_index("gx")
    for d in range(keep.shape[0]):
        at = jnp.bitwise_xor(me, d)
        outs[d % 4][d // 4] = (keep[at] + got[at]).astype(jnp.bfloat16)


def split(keep, got):
    shape = jax.ShapeDtypeStruct((2,) + keep.shape[1:], jnp.bfloat16)
    return pl.pallas_call(
        split_kernel,
        out_shape=[shape] * 4,
        in_specs=[IN_VMEM] * 2,
        out_specs=[IN_VMEM] * 4,
        compiler_params=pltpu.CompilerParams(vmem_limit_bytes=8 * MIB),
        name="split",
    )(keep, got)


def pack(picks, *sources):
    def pack_kernel(*refs):
        for k, (i, j) in enumerate(picks):
            refs[-1][k] = refs[i][j]

    return pl.pallas_call(
        pack_kernel,
        out_shape=jax.ShapeDtypeStruct((len(picks),) + sources[0].shape[1:], sources[0].dtype),
        in_specs=[IN_VMEM] * len(sources),
        out_specs=IN_VMEM,
        compiler_params=pltpu.CompilerParams(vmem_limit_bytes=8 * MIB),
        name="pack",
    )(*sources)


ARRIVED = [(0, 0), (1, 0), (2, 0), (3, 0), (4, 0), (4, 1), (4, 2), (4, 3)]


def attend_kernel(lengths, *refs):
    arrived = refs[:5]
    cosine, sine, keys, values, mine, other, spread, held = refs[5:]
    n, rows, stripe = spread.shape[1], spread.shape[0], spread.shape[2]
    me = lax.axis_index("gx")
    query_cols = stripe - 128
    side = lax.axis_index("gy")
    score_scale = 1.0 / math.sqrt(DH)
    for d, (i, j) in enumerate(ARRIVED):
        block = arrived[i][j].astype(jnp.float32)
        for r in range(rows):
            spread[r, pl.ds(jnp.bitwise_xor(me, d), 1), :] = block[r : r + 1, :]
    starts = range(0, query_cols, DH)
    ready = []
    for r in range(rows):
        given = spread[r]
        cos, sin = cosine[r : r + 1, :], sine[r : r + 1, :]

        def turn(a, b):
            turned = jnp.concatenate([a * cos - b * sin, b * cos + a * sin], axis=1)
            return turned.astype(jnp.bfloat16)

        q = turn(
            jnp.concatenate([given[:, c : c + DH // 2] for c in starts], axis=0),
            jnp.concatenate([given[:, c + DH // 2 : c + DH] for c in starts], axis=0),
        )
        q = (q.astype(jnp.float32) * score_scale).astype(jnp.bfloat16)
        new = [
            given[i : i + 1, query_cols:] + given[i + 1 : i + 2, query_cols:]
            for i in range(0, n, 2)
        ]
        new_key = turn(new[0], new[1]).astype(jnp.float32)
        new_value = jnp.concatenate(new[2:], axis=1)
        scores = lax.dot_general(q, keys[r], contract, preferred_element_type=jnp.float32)
        own_score = jnp.sum(q.astype(jnp.float32) * new_key, axis=1, keepdims=True)
        ready.append((scores, own_score, new_value))
    for r, (scores, own_score, new_value) in enumerate(ready):
        place = lax.broadcasted_iota(jnp.int32, scores.shape, 1)
        scores = jnp.where(place < lengths[r], scores, -1e30)
        highest = jnp.maximum(jnp.max(scores, axis=1, keepdims=True), own_score)
        weights = jnp.exp(scores - highest)
        own_weight = jnp.exp(own_score - highest)
        totals = jnp.sum(weights, axis=1, keepdims=True) + own_weight
        blended = jnp.dot(
            weights.astype(jnp.bfloat16), values[r], preferred_element_type=jnp.float32
        )
        blended = (blended + own_weight * new_value) / totals
        for j in range(len(starts)):
            block = blended[j * n : (j + 1) * n]
            swapped = pltpu.roll(block, n // 2, 0)
            parts = [jnp.where(side == 0, block, swapped), jnp.where(side == 0, swapped, block)]
            for i in range(n // 2):
                at = (i * len(starts) + j) * DH
                for k, part in enumerate(parts):
                    held[k, r : r + 1, at : at + DH] = part[i : i + 1]
    mine[...] = held[0].astype(jnp.bfloat16)
    other[...] = held[1].astype(jnp.bfloat16)


def attend(lengths, arrived, cosine, sine, keys, values):
    n = len(ARRIVED)
    _, rows, stripe = arrived[0].shape
    shape = jax.ShapeDtypeStruct((rows, HEADS * DH // 2), jnp.bfloat16)
    return pl.pallas_call(
        attend_kernel,
        out_shape=[shape, shape],
        in_specs=[IN_SMEM] + [IN_VMEM] * 9,
        out_specs=[IN_VMEM] * 2,
        scratch_shapes=[
            pltpu.VMEM((rows, n, stripe), jnp.float32),
            pltpu.VMEM((2, rows, HEADS * DH // 2), jnp.float32),
        ],
        compiler_params=pltpu.CompilerParams(vmem_limit_bytes=8 * MIB),
        name="attend",
    )(lengths, *arrived, cosine, sine, in_vmem(keys), in_vmem(values))


def output_kernel(n, *refs):
    shards = refs[: n - 1]
    far = refs[n - 1 : n + 1]
    weights = refs[n + 1 : -4]
    keep, give, total, placed = refs[-4:]
    rows = shards[0].shape[0]
    half = far[0].shape[1]
    for part in range(2):
        start = part * half
        cols = slice(start, start + half)
        x = [ref[:, cols] for ref in shards] + [far[part][...]]
        x = jnp.concatenate([piece.astype(jnp.float32) for piece in x], axis=0)
        x = x.astype(jnp.bfloat16)
        first = 0
        for weight in weights:
            last = first + weight.shape[0]
            low, high = max(first, start), min(last, start + half)
            if low < high:
                term = jnp.dot(
                    x[:, low - start : high - start],
                    weight[low - first : high - first, :],
                    preferred_element_type=jnp.float32,
                )
                if low == 0:
                    total[...] = term
                else:
                    total[...] += term
            first = last
    side = lax.axis_index("gy")
    for i, owner in enumerate(owners(n)):
        block = total[i * rows : (i + 1) * rows, :]
        placed[owner] = jnp.where(side == 0, block, pltpu.roll(block, rows // 2, 0))
    keep[...] = placed[pl.ds(side * (n // 2), n // 2)]
    give[...] = placed[pl.ds((1 - side) * (n // 2), n // 2)]


def output_project(shards, far, weights):
    n = len(shards) + 1
    rows = shards[0].shape[0]
    cols = weights[0].shape[1]
    shape = jax.ShapeDtypeStruct((n // 2, rows, cols), jnp.float32)
    return pl.pallas_call(
        lambda *refs: output_kernel(n, *refs),
        out_shape=[shape, shape],
        in_specs=[IN_VMEM] * (n + 1 + len(weights)),
        out_specs=[IN_VMEM] * 2,
        scratch_shapes=[
            pltpu.VMEM((n * rows, cols), jnp.float32),
            pltpu.VMEM((n, rows, cols), jnp.float32),
        ],
        compiler_params=pltpu.CompilerParams(vmem_limit_bytes=8 * MIB),
        name="output_project",
    )(*shards, *far, *[in_vmem(w) for w in weights])


def on_any_grid(
    activations,
    norm_gain,
    query_weight,
    keyval_weight,
    output_weight,
    cache_keys,
    cache_values,
    cache_lengths,
):
    inputs = activations.astype(jnp.float32)
    row_sums, square_sums = lax.psum(
        (jnp.sum(inputs, axis=1), jnp.sum(inputs * inputs, axis=1)), "gy"
    )
    row_mean = row_sums[:, None] / D
    row_square = square_sums[:, None] / D
    variance = row_square - row_mean * row_mean
    normed = (
        (inputs - row_mean) * lax.rsqrt(variance + epsilon) * norm_gain.astype(jnp.float32)
    ).astype(jnp.bfloat16)
    shard_rows = lax.all_gather(normed, "gx", axis=0, tiled=True)
    query_part = lax.dot_general(
        shard_rows, query_weight, contract, preferred_element_type=jnp.float32
    )
    keyval_part = lax.dot_general(
        shard_rows, keyval_weight, contract, preferred_element_type=jnp.float32
    )
    partial_sums = jnp.concatenate([query_part, keyval_part], axis=1)
    wide_count = lax.axis_size("gx")
    pair_count = lax.axis_size("gy")
    local_rows = cache_lengths.shape[0]
    stripe = partial_sums.shape[1]
    arrived = lax.all_to_all(partial_sums, ("gx", "gy"), split_axis=0, concat_axis=1, tiled=True)
    gathered = jnp.sum(arrived.reshape(local_rows, wide_count, pair_count, stripe), axis=2).astype(
        jnp.bfloat16
    )
    query_cols = query_weight.shape[0]
    queries = gathered[:, :, :query_cols].reshape(local_rows, HEADS, DH)
    keyvals = gathered[:, :, query_cols:].reshape(local_rows, 2 * DH)
    places = cache_lengths.astype(jnp.float32)
    queries = rotate(queries.astype(jnp.float32), places[:, None, None]).astype(jnp.bfloat16)
    new_keys = rotate(keyvals[:, :DH].astype(jnp.float32), places[:, None]).astype(jnp.bfloat16)
    new_values = keyvals[:, DH:].astype(jnp.float32)
    score_scale = 1.0 / math.sqrt(DH)
    scores = (
        jnp.einsum("rhd,rtd->rht", queries, cache_keys, preferred_element_type=jnp.float32)
        * score_scale
    )
    visible = jnp.arange(cache_keys.shape[1])[None, :] < cache_lengths[:, None]
    scores = jnp.where(visible[:, None, :], scores, -1e30)
    own_score = (
        jnp.einsum("rhd,rd->rh", queries, new_keys, preferred_element_type=jnp.float32)
        * score_scale
    )
    highest = jnp.maximum(jnp.max(scores, axis=2), own_score)
    weights = jnp.exp(scores - highest[:, :, None])
    own_weight = jnp.exp(own_score - highest)
    totals = jnp.sum(weights, axis=2) + own_weight
    blended = jnp.einsum(
        "rht,rtd->rhd",
        weights.astype(jnp.bfloat16),
        cache_values,
        preferred_element_type=jnp.float32,
    )
    blended = blended + own_weight[:, :, None] * new_values[:, None, :]
    attended = (blended / totals[:, :, None]).astype(jnp.bfloat16).reshape(local_rows, HEADS * DH)
    swapped = lax.all_to_all(attended, "gy", split_axis=1, concat_axis=0, tiled=True)
    partial_out = jnp.dot(
        lax.all_gather(swapped, "gx", axis=0, tiled=True),
        output_weight,
        preferred_element_type=jnp.float32,
    )
    return lax.psum_scatter(partial_out, "gy", scatter_dimension=0, tiled=True).astype(jnp.bfloat16)


def on_device(
    activations,
    norm_gain,
    query_weight,
    keyval_weight,
    output_weight,
    cache_keys,
    cache_values,
    cache_lengths,
):
    n = lax.axis_size("gx")
    ring = Ring(n)
    query_cols, width = query_weight.shape
    new_cols = keyval_weight.shape[0]
    unit = query_cols // 6
    sizes = [2 * unit, 2 * unit, unit, unit]
    weights = []

    indices = jnp.arange(DH // 2, dtype=jnp.float32)
    frequency = jnp.exp(-math.log(10000.0) * indices / (DH // 2))
    angles = cache_lengths.astype(jnp.float32)[:, None] * frequency
    cosine, sine = jnp.cos(angles), jnp.sin(angles)

    def piece_of(array, start, size, after):
        return load(size, [(array, start, size, 0)], after)

    left = right = activations
    shards = [activations]
    sums = []
    for step in range(1, n // 2):
        arrived = shards[-2:] if step > 1 else []
        left, right = ring.step(left, right)
        if step > 1:
            sums = [row_sums([activations, *arrived] if step == 2 else arrived, sums)]
        if step == 3:
            far_sums = lax.ppermute(sums[0][: activations.shape[0]], "gx", ring.across)
        weight = piece_of(query_weight, sum(sizes[: step - 1]), sizes[step - 1], arrived)
        weight, (left, right, *sums) = before(weight, left, right, *sums)
        weights.append(weight)
        shards += [left, right]
    cut, (cut_right, left, right) = before(
        left[:, : width // 2], right[:, width // 2 :], left, right
    )
    far = ring.step(cut, cut_right)
    sums = row_sums([left, right], sums)
    jobs = [(query_weight, 5 * unit, unit, 0), (keyval_weight, 0, new_cols, unit)]
    weight = load(unit + new_cols, jobs, [sums])
    sums = jnp.concatenate([sums, far_sums], axis=0)
    other_sums = swap_pair(sums)
    weight, (other_sums, *far) = before(weight, other_sums, *far)
    weights.append(weight)
    gain = norm_gain.astype(jnp.float32)[None, :]
    keep, give = project((sums, other_sums), gain, shards, far, weights)

    def exchange(blocks, d):
        return lax.ppermute(blocks, "gx", [(i, i ^ d) for i in range(n)])

    blocks = split(keep, swap_pair(give))
    arrived = [blocks[0]] + [exchange(blocks[d], d) for d in range(1, 4)]
    keys = load_cache(cache_keys, [blocks[1]])
    keys, arrived = before(keys, *arrived)
    across = pack([(0, 1), (1, 1), (2, 1), (3, 1)], *arrived)
    last = exchange(across, 4)
    values = load_cache(cache_values, [across])
    unit = output_weight.shape[0] // 12
    sizes = [unit, 3 * unit, 3 * unit, 3 * unit, 2 * unit]
    weight = load(unit, [(output_weight, 0, unit, 0)], [across])
    values, (last,) = before(values, last)
    weight, (last,) = before(weight, last)
    weights = [weight]
    arrived = [*arrived, last]
    mine, other = attend(cache_lengths, arrived, cosine, sine, keys, values)
    shard = jnp.concatenate([mine, swap_pair(other)], axis=0)

    left = right = shard
    shards = [shard]

    for step in range(1, n // 2):
        arrived = shards[-2:]
        left, right = ring.step(left, right)
        weight = piece_of(output_weight, sum(sizes[:step]), sizes[step], arrived)
        weight, (left, right) = before(weight, left, right)
        weights.append(weight)
        shards += [left, right]
    half = shard.shape[1] // 2
    far = ring.step(left[:, :half], right[:, half:])
    weight = piece_of(output_weight, sum(sizes[:4]), sizes[4], [left, right])
    weight, far = before(weight, *far)
    weights.append(weight)
    keep, give = output_project(shards, far, weights)
    out = (keep + swap_pair(give)).astype(jnp.bfloat16)
    return out.reshape(-1, out.shape[-1])


def solution(mesh):
    return jax.shard_map(
        on_device if mesh.shape["gx"] == 8 else on_any_grid,
        mesh=mesh,
        in_specs=(
            P(("groups", "gx"), "gy"),
            P("gy"),
            P("gx", "gy"),
            P("gx", "gy"),
            P("gy", "gx"),
            P(("groups", "gx", "gy"), None, None),
            P(("groups", "gx", "gy"), None, None),
            P(("groups", "gx", "gy")),
        ),
        out_specs=P(("groups", "gy"), "gx"),
        check_vma=False,
    )
```

```python
import math

import jax
import jax.numpy as jnp
from jax import lax
from jax.experimental import pallas as pl
from jax.experimental.pallas import tpu as pltpu
from jax.sharding import PartitionSpec as P

D = 18432
HEADS = 48
DH = 256


epsilon = 1e-06
contract = (((1,), (1,)), ((), ()))
MIB = 1 << 20
ANY = pl.BlockSpec(memory_space=pl.ANY)
IN_HBM = pl.BlockSpec(memory_space=pltpu.HBM)
IN_VMEM = pl.BlockSpec(memory_space=pltpu.VMEM)
IN_SMEM = pl.BlockSpec(memory_space=pltpu.SMEM)


def rotate(vectors, places):
    half_width = vectors.shape[-1] // 2
    indices = jnp.arange(half_width, dtype=jnp.float32)
    frequency = jnp.exp(-math.log(10000.0) * indices / half_width)
    angles = places * frequency
    cosine = jnp.cos(angles)
    sine = jnp.sin(angles)
    first_half = vectors[..., :half_width]
    second_half = vectors[..., half_width:]
    return jnp.concatenate(
        [first_half * cosine - second_half * sine, second_half * cosine + first_half * sine],
        axis=-1,
    )


def ring_order(n):
    return list(range(0, n, 2)) + list(range(n - 1, 0, -2))


def swap_pair(x):
    return lax.ppermute(x, "gy", [(0, 1), (1, 0)])


class Ring:
    def __init__(self, n):
        order = ring_order(n)
        self.onward = [(order[p], order[(p + 1) % n]) for p in range(n)]
        self.back = [(order[p], order[(p - 1) % n]) for p in range(n)]
        self.across = [(order[p], order[(p + n // 2) % n]) for p in range(n)]

    def step(self, left, right):
        return lax.ppermute(left, "gx", self.onward), lax.ppermute(right, "gx", self.back)


def owners(n):
    offsets = [0]
    for step in range(1, n // 2):
        offsets += [-step, step]
    offsets.append(n // 2)
    me = lax.axis_index("gx")
    half = lax.div(me, 2)
    place = jnp.where(lax.rem(me, 2) == 0, half, n - 1 - half)
    result = []
    for offset in offsets:
        at = lax.rem(place + (offset + n), n)
        result.append(jnp.where(at < n // 2, 2 * at, 2 * (n - 1 - at) + 1))
    return result


def start_copies(source, target, sems, count):
    rows = source.shape[0]
    size = -(-rows // (16 * count)) * 16
    copies = []
    for i, first in enumerate(range(0, rows, size)):
        at = pl.ds(first, min(size, rows - first))
        copy = pltpu.make_async_copy(source.at[at], target.at[at], sems.at[i])
        copy.start()
        copies.append(copy)
    return copies


def load_kernel(jobs, *refs):
    sources, target, sems = refs[: len(jobs)], refs[-2], refs[-1]
    copies = []
    for i, (first, size, at) in enumerate(jobs):
        part = sources[i].at[pl.ds(first, size)]
        copies += start_copies(part, target.at[pl.ds(at, size)], sems.at[i], 4)
    for copy in copies:
        copy.wait()


def load(rows, jobs, after=()):
    array = jobs[0][0]
    return pl.pallas_call(
        lambda *refs: load_kernel([job[1:] for job in jobs], *refs),
        out_shape=pltpu.VMEM((rows, array.shape[1]), array.dtype),
        in_specs=[IN_HBM] * len(jobs) + [ANY] * len(after),
        out_specs=IN_VMEM,
        scratch_shapes=[pltpu.SemaphoreType.DMA((len(jobs), 4))],
        compiler_params=pltpu.CompilerParams(vmem_limit_bytes=MIB),
        name="load",
    )(*[in_hbm(job[0]) for job in jobs], *after)


def load_cache_kernel(source, *refs):
    target, sems = refs[-2:]
    copies = []
    for row in range(source.shape[0]):
        copies.append(pltpu.make_async_copy(source.at[row], target.at[row], sems.at[row]))
        copies[-1].start()
    for copy in copies:
        copy.wait()


def load_cache(cache, after):
    return pl.pallas_call(
        load_cache_kernel,
        out_shape=pltpu.VMEM(cache.shape, cache.dtype),
        in_specs=[IN_HBM] + [ANY] * len(after),
        out_specs=IN_VMEM,
        scratch_shapes=[pltpu.SemaphoreType.DMA((cache.shape[0],))],
        compiler_params=pltpu.CompilerParams(vmem_limit_bytes=MIB),
        name="load_cache",
    )(in_hbm(cache), *after)


def in_hbm(array):
    return pltpu.with_memory_space_constraint(array, pltpu.HBM)


def in_vmem(array):
    return pltpu.with_memory_space_constraint(array, pltpu.VMEM)


def before(done, *rest):
    held = lax.optimization_barrier((done,) + rest)
    return held[0], held[1:]


def sums_kernel(ready, count, *refs):
    out = refs[-1]
    start = 0
    for ref in refs[:ready]:
        out[start : start + ref.shape[0], :] = ref[...]
        start += ref.shape[0]
    rows = refs[ready].shape[0]
    lane = lax.broadcasted_iota(jnp.int32, (rows, 128), 1)
    for ref in refs[ready : ready + count]:
        x = ref[...].astype(jnp.float32)
        total = jnp.sum(x, axis=1, keepdims=True)
        square = jnp.sum(x * x, axis=1, keepdims=True)
        both = jnp.where(lane == 0, total, jnp.where(lane == 1, square, 0.0))
        out[start : start + rows, :] = both
        start += rows


def row_sums(shards, ready=(), after=()):
    rows = shards[0].shape[0] * len(shards) + sum(r.shape[0] for r in ready)
    return pl.pallas_call(
        lambda *refs: sums_kernel(len(ready), len(shards), *refs),
        out_shape=jax.ShapeDtypeStruct((rows, 128), jnp.float32),
        in_specs=[IN_VMEM] * (len(ready) + len(shards)) + [ANY] * len(after),
        out_specs=IN_VMEM,
        compiler_params=pltpu.CompilerParams(vmem_limit_bytes=8 * MIB),
        name="row_sums",
    )(*ready, *shards, *after)


def project_kernel(n, parts, *refs):
    sums_a, sums_b, gain = refs[:3]
    shards = refs[3 : 3 + n - 1]
    far = refs[3 + n - 1 : 3 + n + 1]
    weights = refs[4 + n : 4 + n + parts]
    keep, give, normed, total = refs[4 + n + parts :]
    rows, width = shards[0].shape
    sums = sums_a[...] + sums_b[...]
    row_mean = sums[:, :1] / D
    row_square = sums[:, 1:2] / D
    scale = lax.rsqrt(row_square - row_mean * row_mean + epsilon)
    for part in range(2):
        cols = slice(part * width // 2, (part + 1) * width // 2)
        for i in range(0, n, 2):
            x = [ref[:, cols] if ref is not far[part] else ref[...] for ref in (*shards, far[part])]
            x = jnp.concatenate([piece.astype(jnp.float32) for piece in x[i : i + 2]], axis=0)
            at = slice(i * rows, (i + 2) * rows)
            x = (x - row_mean[at]) * scale[at] * gain[:, cols]
            normed[at, cols] = x.astype(jnp.bfloat16)
        x = normed[:, cols]
        start = 0
        for weight in weights:
            term = lax.dot_general(
                x, weight[:, cols], contract, preferred_element_type=jnp.float32
            )
            stripe = slice(start, start + weight.shape[0])
            if part == 0:
                total[:, stripe] = term
            else:
                total[:, stripe] += term
            start = stripe.stop
    last = slice(total.shape[1] - 128, total.shape[1])
    lane = lax.broadcasted_iota(jnp.int32, (total.shape[0], 128), 1)
    new = jnp.where(lane < 64, total[:, last], 0.0)
    odd = lax.rem(lax.axis_index("gx"), 2)
    total[:, last] = jnp.where(odd == 0, new, pltpu.roll(new, 64, 1))
    side = lax.axis_index("gy")
    local = rows // 2
    for i, owner in enumerate(owners(n)):
        block = total[i * rows : (i + 1) * rows, :]
        low, high = block[:local], block[local:]
        keep[owner] = jnp.where(side == 0, low, high)
        give[owner] = jnp.where(side == 0, high, low)


def project(sums, gain, shards, far, weights):
    n = len(shards) + 1
    rows, width = shards[0].shape
    stripe = sum(w.shape[0] for w in weights) + 64
    shape = jax.ShapeDtypeStruct((n, rows // 2, stripe), jnp.float32)
    return pl.pallas_call(
        lambda *refs: project_kernel(n, len(weights), *refs),
        out_shape=[shape, shape],
        in_specs=[IN_VMEM] * (4 + n + len(weights)),
        out_specs=[IN_VMEM] * 2,
        scratch_shapes=[
            pltpu.VMEM((n * rows, width), jnp.bfloat16),
            pltpu.VMEM((n * rows, stripe), jnp.float32),
        ],
        compiler_params=pltpu.CompilerParams(vmem_limit_bytes=6 * MIB),
        name="project",
    )(
        *sums,
        gain,
        *shards,
        *far,
        *[in_vmem(w) for w in weights],
    )


def split_kernel(keep, got, *outs):
    me = lax.axis_index("gx")
    for d in range(keep.shape[0]):
        at = jnp.bitwise_xor(me, d)
        outs[d % 4][d // 4] = (keep[at] + got[at]).astype(jnp.bfloat16)


def split(keep, got):
    shape = jax.ShapeDtypeStruct((2,) + keep.shape[1:], jnp.bfloat16)
    return pl.pallas_call(
        split_kernel,
        out_shape=[shape] * 4,
        in_specs=[IN_VMEM] * 2,
        out_specs=[IN_VMEM] * 4,
        compiler_params=pltpu.CompilerParams(vmem_limit_bytes=8 * MIB),
        name="split",
    )(keep, got)


def pack(picks, *sources):
    def pack_kernel(*refs):
        for k, (i, j) in enumerate(picks):
            refs[-1][k] = refs[i][j]

    return pl.pallas_call(
        pack_kernel,
        out_shape=jax.ShapeDtypeStruct((len(picks),) + sources[0].shape[1:], sources[0].dtype),
        in_specs=[IN_VMEM] * len(sources),
        out_specs=IN_VMEM,
        compiler_params=pltpu.CompilerParams(vmem_limit_bytes=8 * MIB),
        name="pack",
    )(*sources)


ARRIVED = [(0, 0), (1, 0), (2, 0), (3, 0), (4, 0), (4, 1), (4, 2), (4, 3)]


def attend_kernel(lengths, *refs):
    arrived = refs[:5]
    cosine, sine, keys, values, mine, other, spread, held = refs[5:]
    n, rows, stripe = spread.shape[1], spread.shape[0], spread.shape[2]
    me = lax.axis_index("gx")
    query_cols = stripe - 128
    side = lax.axis_index("gy")
    score_scale = 1.0 / math.sqrt(DH)
    for d, (i, j) in enumerate(ARRIVED):
        block = arrived[i][j].astype(jnp.float32)
        for r in range(rows):
            spread[r, pl.ds(jnp.bitwise_xor(me, d), 1), :] = block[r : r + 1, :]
    starts = range(0, query_cols, DH)
    ready = []
    for r in range(rows):
        given = spread[r]
        cos, sin = cosine[r : r + 1, :], sine[r : r + 1, :]

        def turn(a, b):
            turned = jnp.concatenate([a * cos - b * sin, b * cos + a * sin], axis=1)
            return turned.astype(jnp.bfloat16)

        q = turn(
            jnp.concatenate([given[:, c : c + DH // 2] for c in starts], axis=0),
            jnp.concatenate([given[:, c + DH // 2 : c + DH] for c in starts], axis=0),
        )
        q = (q.astype(jnp.float32) * score_scale).astype(jnp.bfloat16)
        new = [
            given[i : i + 1, query_cols:] + given[i + 1 : i + 2, query_cols:]
            for i in range(0, n, 2)
        ]
        new_key = turn(new[0], new[1]).astype(jnp.float32)
        new_value = jnp.concatenate(new[2:], axis=1)
        scores = lax.dot_general(q, keys[r], contract, preferred_element_type=jnp.float32)
        own_score = jnp.sum(q.astype(jnp.float32) * new_key, axis=1, keepdims=True)
        ready.append((scores, own_score, new_value))
    for r, (scores, own_score, new_value) in enumerate(ready):
        place = lax.broadcasted_iota(jnp.int32, scores.shape, 1)
        scores = jnp.where(place < lengths[r], scores, -1e30)
        highest = jnp.maximum(jnp.max(scores, axis=1, keepdims=True), own_score)
        weights = jnp.exp(scores - highest)
        own_weight = jnp.exp(own_score - highest)
        totals = jnp.sum(weights, axis=1, keepdims=True) + own_weight
        blended = jnp.dot(
            weights.astype(jnp.bfloat16), values[r], preferred_element_type=jnp.float32
        )
        blended = (blended + own_weight * new_value) / totals
        for j in range(len(starts)):
            block = blended[j * n : (j + 1) * n]
            swapped = pltpu.roll(block, n // 2, 0)
            parts = [jnp.where(side == 0, block, swapped), jnp.where(side == 0, swapped, block)]
            for i in range(n // 2):
                at = (i * len(starts) + j) * DH
                for k, part in enumerate(parts):
                    held[k, r : r + 1, at : at + DH] = part[i : i + 1]
    mine[...] = held[0].astype(jnp.bfloat16)
    other[...] = held[1].astype(jnp.bfloat16)


def attend(lengths, arrived, cosine, sine, keys, values):
    n = len(ARRIVED)
    _, rows, stripe = arrived[0].shape
    shape = jax.ShapeDtypeStruct((rows, HEADS * DH // 2), jnp.bfloat16)
    return pl.pallas_call(
        attend_kernel,
        out_shape=[shape, shape],
        in_specs=[IN_SMEM] + [IN_VMEM] * 9,
        out_specs=[IN_VMEM] * 2,
        scratch_shapes=[
            pltpu.VMEM((rows, n, stripe), jnp.float32),
            pltpu.VMEM((2, rows, HEADS * DH // 2), jnp.float32),
        ],
        compiler_params=pltpu.CompilerParams(vmem_limit_bytes=8 * MIB),
        name="attend",
    )(lengths, *arrived, cosine, sine, in_vmem(keys), in_vmem(values))


def output_kernel(n, *refs):
    shards = refs[: n - 1]
    far = refs[n - 1 : n + 1]
    weights = refs[n + 1 : -5]
    keep, give, rounded, total, placed = refs[-5:]
    rows = shards[0].shape[0]
    half = far[0].shape[1]
    for part in range(2):
        cols = slice(part * half, (part + 1) * half)
        x = [ref[:, cols] for ref in shards] + [far[part][...]]
        x = jnp.concatenate([piece.astype(jnp.float32) for piece in x], axis=0)
        rounded[:, cols] = x.astype(jnp.bfloat16)
    width = total.shape[1] // 3
    for start in range(0, total.shape[1], width):
        cols = slice(start, start + width)
        first = 0
        terms = []
        for weight in weights:
            last = first + weight.shape[0]
            terms.append(
                jnp.dot(
                    rounded[:, first:last], weight[:, cols], preferred_element_type=jnp.float32
                )
            )
            first = last
        total[:, cols] = sum(terms[1:], terms[0])
    side = lax.axis_index("gy")
    for i, owner in enumerate(owners(n)):
        block = total[i * rows : (i + 1) * rows, :]
        placed[owner] = jnp.where(side == 0, block, pltpu.roll(block, rows // 2, 0))
    keep[...] = placed[pl.ds(side * (n // 2), n // 2)]
    give[...] = placed[pl.ds((1 - side) * (n // 2), n // 2)]


def output_project(shards, far, weights):
    n = len(shards) + 1
    rows = shards[0].shape[0]
    cols = weights[0].shape[1]
    shape = jax.ShapeDtypeStruct((n // 2, rows, cols), jnp.float32)
    return pl.pallas_call(
        lambda *refs: output_kernel(n, *refs),
        out_shape=[shape, shape],
        in_specs=[IN_VMEM] * (n + 1 + len(weights)),
        out_specs=[IN_VMEM] * 2,
        scratch_shapes=[
            pltpu.VMEM((n * rows, 2 * far[0].shape[1]), jnp.bfloat16),
            pltpu.VMEM((n * rows, cols), jnp.float32),
            pltpu.VMEM((n, rows, cols), jnp.float32),
        ],
        compiler_params=pltpu.CompilerParams(vmem_limit_bytes=8 * MIB),
        name="output_project",
    )(*shards, *far, *[in_vmem(w) for w in weights])


def on_any_grid(
    activations,
    norm_gain,
    query_weight,
    keyval_weight,
    output_weight,
    cache_keys,
    cache_values,
    cache_lengths,
):
    inputs = activations.astype(jnp.float32)
    row_sums, square_sums = lax.psum(
        (jnp.sum(inputs, axis=1), jnp.sum(inputs * inputs, axis=1)), "gy"
    )
    row_mean = row_sums[:, None] / D
    row_square = square_sums[:, None] / D
    variance = row_square - row_mean * row_mean
    normed = (
        (inputs - row_mean) * lax.rsqrt(variance + epsilon) * norm_gain.astype(jnp.float32)
    ).astype(jnp.bfloat16)
    shard_rows = lax.all_gather(normed, "gx", axis=0, tiled=True)
    query_part = lax.dot_general(
        shard_rows, query_weight, contract, preferred_element_type=jnp.float32
    )
    keyval_part = lax.dot_general(
        shard_rows, keyval_weight, contract, preferred_element_type=jnp.float32
    )
    partial_sums = jnp.concatenate([query_part, keyval_part], axis=1)
    wide_count = lax.axis_size("gx")
    pair_count = lax.axis_size("gy")
    local_rows = cache_lengths.shape[0]
    stripe = partial_sums.shape[1]
    arrived = lax.all_to_all(partial_sums, ("gx", "gy"), split_axis=0, concat_axis=1, tiled=True)
    gathered = jnp.sum(arrived.reshape(local_rows, wide_count, pair_count, stripe), axis=2).astype(
        jnp.bfloat16
    )
    query_cols = query_weight.shape[0]
    queries = gathered[:, :, :query_cols].reshape(local_rows, HEADS, DH)
    keyvals = gathered[:, :, query_cols:].reshape(local_rows, 2 * DH)
    places = cache_lengths.astype(jnp.float32)
    queries = rotate(queries.astype(jnp.float32), places[:, None, None]).astype(jnp.bfloat16)
    new_keys = rotate(keyvals[:, :DH].astype(jnp.float32), places[:, None]).astype(jnp.bfloat16)
    new_values = keyvals[:, DH:].astype(jnp.float32)
    score_scale = 1.0 / math.sqrt(DH)
    scores = (
        jnp.einsum("rhd,rtd->rht", queries, cache_keys, preferred_element_type=jnp.float32)
        * score_scale
    )
    visible = jnp.arange(cache_keys.shape[1])[None, :] < cache_lengths[:, None]
    scores = jnp.where(visible[:, None, :], scores, -1e30)
    own_score = (
        jnp.einsum("rhd,rd->rh", queries, new_keys, preferred_element_type=jnp.float32)
        * score_scale
    )
    highest = jnp.maximum(jnp.max(scores, axis=2), own_score)
    weights = jnp.exp(scores - highest[:, :, None])
    own_weight = jnp.exp(own_score - highest)
    totals = jnp.sum(weights, axis=2) + own_weight
    blended = jnp.einsum(
        "rht,rtd->rhd",
        weights.astype(jnp.bfloat16),
        cache_values,
        preferred_element_type=jnp.float32,
    )
    blended = blended + own_weight[:, :, None] * new_values[:, None, :]
    attended = (blended / totals[:, :, None]).astype(jnp.bfloat16).reshape(local_rows, HEADS * DH)
    swapped = lax.all_to_all(attended, "gy", split_axis=1, concat_axis=0, tiled=True)
    partial_out = jnp.dot(
        lax.all_gather(swapped, "gx", axis=0, tiled=True),
        output_weight,
        preferred_element_type=jnp.float32,
    )
    return lax.psum_scatter(partial_out, "gy", scatter_dimension=0, tiled=True).astype(jnp.bfloat16)


def on_device(
    activations,
    norm_gain,
    query_weight,
    keyval_weight,
    output_weight,
    cache_keys,
    cache_values,
    cache_lengths,
):
    n = lax.axis_size("gx")
    ring = Ring(n)
    query_cols, width = query_weight.shape
    new_cols = keyval_weight.shape[0]
    unit = query_cols // 6
    sizes = [5 * unit // 2, 2 * unit, unit // 2, unit]
    weights = []

    indices = jnp.arange(DH // 2, dtype=jnp.float32)
    frequency = jnp.exp(-math.log(10000.0) * indices / (DH // 2))
    angles = cache_lengths.astype(jnp.float32)[:, None] * frequency
    cosine, sine = jnp.cos(angles), jnp.sin(angles)

    def piece_of(array, start, size, after):
        return load(size, [(array, start, size, 0)], after)

    left = right = activations
    shards = [activations]
    sums = []
    for step in range(1, n // 2):
        arrived = shards[-2:] if step > 1 else []
        left, right = ring.step(left, right)
        if step > 1:
            sums = [row_sums([activations, *arrived] if step == 2 else arrived, sums)]
        if step == 3:
            far_sums = lax.ppermute(sums[0][: activations.shape[0]], "gx", ring.across)
        weight = piece_of(query_weight, sum(sizes[: step - 1]), sizes[step - 1], arrived)
        weight, (left, right, *sums) = before(weight, left, right, *sums)
        weights.append(weight)
        shards += [left, right]
    cut, (cut_right, left, right) = before(
        left[:, : width // 2], right[:, width // 2 :], left, right
    )
    far = ring.step(cut, cut_right)
    sums = row_sums([left, right], sums)
    jobs = [(query_weight, 5 * unit, unit, 0), (keyval_weight, 0, new_cols, unit)]
    weight = load(unit + new_cols, jobs, [sums])
    sums = jnp.concatenate([sums, far_sums], axis=0)
    other_sums = swap_pair(sums)
    weight, (other_sums, *far) = before(weight, other_sums, *far)
    weights.append(weight)
    gain = norm_gain.astype(jnp.float32)[None, :]
    keep, give = project((sums, other_sums), gain, shards, far, weights)

    def exchange(blocks, d):
        return lax.ppermute(blocks, "gx", [(i, i ^ d) for i in range(n)])

    blocks = split(keep, swap_pair(give))
    arrived = [blocks[0]] + [exchange(blocks[d], d) for d in range(1, 4)]
    keys = load_cache(cache_keys, [blocks[1]])
    keys, arrived = before(keys, *arrived)
    across = pack([(0, 1), (1, 1), (2, 1), (3, 1)], *arrived)
    last = exchange(across, 4)
    values = load_cache(cache_values, [across])
    unit = output_weight.shape[0] // 12
    sizes = [unit, 3 * unit, 3 * unit, 3 * unit, 2 * unit]
    weight = load(unit, [(output_weight, 0, unit, 0)], [across])
    values, (last,) = before(values, last)
    weight, (last,) = before(weight, last)
    weights = [weight]
    arrived = [*arrived, last]
    mine, other = attend(cache_lengths, arrived, cosine, sine, keys, values)
    shard = jnp.concatenate([mine, swap_pair(other)], axis=0)

    left = right = shard
    shards = [shard]

    for step in range(1, n // 2):
        arrived = shards[-2:]
        left, right = ring.step(left, right)
        weight = piece_of(output_weight, sum(sizes[:step]), sizes[step], arrived)
        weight, (left, right) = before(weight, left, right)
        weights.append(weight)
        shards += [left, right]
    half = shard.shape[1] // 2
    far = ring.step(left[:, :half], right[:, half:])
    weight = piece_of(output_weight, sum(sizes[:4]), sizes[4], [left, right])
    weight, far = before(weight, *far)
    weights.append(weight)
    keep, give = output_project(shards, far, weights)
    out = (keep + swap_pair(give)).astype(jnp.bfloat16)
    return out.reshape(-1, out.shape[-1])


def solution(mesh):
    return jax.shard_map(
        on_device if mesh.shape["gx"] == 8 else on_any_grid,
        mesh=mesh,
        in_specs=(
            P(("groups", "gx"), "gy"),
            P("gy"),
            P("gx", "gy"),
            P("gx", "gy"),
            P("gy", "gx"),
            P(("groups", "gx", "gy"), None, None),
            P(("groups", "gx", "gy"), None, None),
            P(("groups", "gx", "gy")),
        ),
        out_specs=P(("groups", "gy"), "gx"),
        check_vma=False,
    )
```

```python
import math

import jax
import jax.numpy as jnp
from jax import lax
from jax.experimental import pallas as pl
from jax.experimental.pallas import tpu as pltpu
from jax.sharding import PartitionSpec as P

D = 18432
HEADS = 48
DH = 256


epsilon = 1e-06
contract = (((1,), (1,)), ((), ()))
MIB = 1 << 20
ANY = pl.BlockSpec(memory_space=pl.ANY)
IN_HBM = pl.BlockSpec(memory_space=pltpu.HBM)
IN_VMEM = pl.BlockSpec(memory_space=pltpu.VMEM)
IN_SMEM = pl.BlockSpec(memory_space=pltpu.SMEM)


def rotate(vectors, places):
    half_width = vectors.shape[-1] // 2
    indices = jnp.arange(half_width, dtype=jnp.float32)
    frequency = jnp.exp(-math.log(10000.0) * indices / half_width)
    angles = places * frequency
    cosine = jnp.cos(angles)
    sine = jnp.sin(angles)
    first_half = vectors[..., :half_width]
    second_half = vectors[..., half_width:]
    return jnp.concatenate(
        [first_half * cosine - second_half * sine, second_half * cosine + first_half * sine],
        axis=-1,
    )


def ring_order(n):
    return list(range(0, n, 2)) + list(range(n - 1, 0, -2))


def swap_pair(x):
    return lax.ppermute(x, "gy", [(0, 1), (1, 0)])


class Ring:
    def __init__(self, n):
        order = ring_order(n)
        self.onward = [(order[p], order[(p + 1) % n]) for p in range(n)]
        self.back = [(order[p], order[(p - 1) % n]) for p in range(n)]
        self.across = [(order[p], order[(p + n // 2) % n]) for p in range(n)]

    def step(self, left, right):
        return lax.ppermute(left, "gx", self.onward), lax.ppermute(right, "gx", self.back)


def owners(n):
    offsets = [0]
    for step in range(1, n // 2):
        offsets += [-step, step]
    offsets.append(n // 2)
    me = lax.axis_index("gx")
    half = lax.div(me, 2)
    place = jnp.where(lax.rem(me, 2) == 0, half, n - 1 - half)
    result = []
    for offset in offsets:
        at = lax.rem(place + (offset + n), n)
        result.append(jnp.where(at < n // 2, 2 * at, 2 * (n - 1 - at) + 1))
    return result


def start_copies(source, target, sems, count):
    rows = source.shape[0]
    size = -(-rows // (16 * count)) * 16
    copies = []
    for i, first in enumerate(range(0, rows, size)):
        at = pl.ds(first, min(size, rows - first))
        copy = pltpu.make_async_copy(source.at[at], target.at[at], sems.at[i])
        copy.start()
        copies.append(copy)
    return copies


def load_kernel(jobs, *refs):
    sources, target, sems = refs[: len(jobs)], refs[-2], refs[-1]
    copies = []
    for i, (first, size, at) in enumerate(jobs):
        part = sources[i].at[pl.ds(first, size)]
        copies += start_copies(part, target.at[pl.ds(at, size)], sems.at[i], 4)
    for copy in copies:
        copy.wait()


def load(rows, jobs, after=()):
    array = jobs[0][0]
    return pl.pallas_call(
        lambda *refs: load_kernel([job[1:] for job in jobs], *refs),
        out_shape=pltpu.VMEM((rows, array.shape[1]), array.dtype),
        in_specs=[IN_HBM] * len(jobs) + [ANY] * len(after),
        out_specs=IN_VMEM,
        scratch_shapes=[pltpu.SemaphoreType.DMA((len(jobs), 4))],
        compiler_params=pltpu.CompilerParams(vmem_limit_bytes=MIB),
        name="load",
    )(*[in_hbm(job[0]) for job in jobs], *after)


def load_cache_kernel(source, *refs):
    target, sems = refs[-2:]
    copies = []
    for row in range(source.shape[0]):
        copies.append(pltpu.make_async_copy(source.at[row], target.at[row], sems.at[row]))
        copies[-1].start()
    for copy in copies:
        copy.wait()


def load_cache(cache, after):
    return pl.pallas_call(
        load_cache_kernel,
        out_shape=pltpu.VMEM(cache.shape, cache.dtype),
        in_specs=[IN_HBM] + [ANY] * len(after),
        out_specs=IN_VMEM,
        scratch_shapes=[pltpu.SemaphoreType.DMA((cache.shape[0],))],
        compiler_params=pltpu.CompilerParams(vmem_limit_bytes=MIB),
        name="load_cache",
    )(in_hbm(cache), *after)


def in_hbm(array):
    return pltpu.with_memory_space_constraint(array, pltpu.HBM)


def in_vmem(array):
    return pltpu.with_memory_space_constraint(array, pltpu.VMEM)


def before(done, *rest):
    held = lax.optimization_barrier((done,) + rest)
    return held[0], held[1:]


def sums_kernel(ready, count, *refs):
    out = refs[-1]
    start = 0
    for ref in refs[:ready]:
        out[start : start + ref.shape[0], :] = ref[...]
        start += ref.shape[0]
    rows = refs[ready].shape[0]
    lane = lax.broadcasted_iota(jnp.int32, (rows, 128), 1)
    for ref in refs[ready : ready + count]:
        x = ref[...].astype(jnp.float32)
        total = jnp.sum(x, axis=1, keepdims=True)
        square = jnp.sum(x * x, axis=1, keepdims=True)
        both = jnp.where(lane == 0, total, jnp.where(lane == 1, square, 0.0))
        out[start : start + rows, :] = both
        start += rows


def row_sums(shards, ready=(), after=()):
    rows = shards[0].shape[0] * len(shards) + sum(r.shape[0] for r in ready)
    return pl.pallas_call(
        lambda *refs: sums_kernel(len(ready), len(shards), *refs),
        out_shape=jax.ShapeDtypeStruct((rows, 128), jnp.float32),
        in_specs=[IN_VMEM] * (len(ready) + len(shards)) + [ANY] * len(after),
        out_specs=IN_VMEM,
        compiler_params=pltpu.CompilerParams(vmem_limit_bytes=8 * MIB),
        name="row_sums",
    )(*ready, *shards, *after)


def project_kernel(n, parts, *refs):
    sums_a, sums_b, gain = refs[:3]
    shards = refs[3 : 3 + n - 1]
    far = refs[3 + n - 1 : 3 + n + 1]
    weights = refs[4 + n : 4 + n + parts]
    keep, give, normed, total = refs[4 + n + parts :]
    rows, width = shards[0].shape
    sums = sums_a[...] + sums_b[...]
    row_mean = sums[:, :1] / D
    row_square = sums[:, 1:2] / D
    scale = lax.rsqrt(row_square - row_mean * row_mean + epsilon)
    for part in range(2):
        cols = slice(part * width // 2, (part + 1) * width // 2)
        for i in range(0, n, 2):
            x = [ref[:, cols] if ref is not far[part] else ref[...] for ref in (*shards, far[part])]
            x = jnp.concatenate([piece.astype(jnp.float32) for piece in x[i : i + 2]], axis=0)
            at = slice(i * rows, (i + 2) * rows)
            x = (x - row_mean[at]) * scale[at] * gain[:, cols]
            normed[at, cols] = x.astype(jnp.bfloat16)
    start = 0
    for weight in weights:
        stripe = slice(start, start + weight.shape[0])
        total[:, stripe] = lax.dot_general(
            normed[...], weight[...], contract, preferred_element_type=jnp.float32
        )
        start = stripe.stop
    last = slice(total.shape[1] - 128, total.shape[1])
    lane = lax.broadcasted_iota(jnp.int32, (total.shape[0], 128), 1)
    new = jnp.where(lane < 64, total[:, last], 0.0)
    odd = lax.rem(lax.axis_index("gx"), 2)
    total[:, last] = jnp.where(odd == 0, new, pltpu.roll(new, 64, 1))
    side = lax.axis_index("gy")
    local = rows // 2
    for i, owner in enumerate(owners(n)):
        block = total[i * rows : (i + 1) * rows, :]
        low, high = block[:local], block[local:]
        keep[owner] = jnp.where(side == 0, low, high)
        give[owner] = jnp.where(side == 0, high, low)


def project(sums, gain, shards, far, weights):
    n = len(shards) + 1
    rows, width = shards[0].shape
    stripe = sum(w.shape[0] for w in weights) + 64
    shape = jax.ShapeDtypeStruct((n, rows // 2, stripe), jnp.float32)
    return pl.pallas_call(
        lambda *refs: project_kernel(n, len(weights), *refs),
        out_shape=[shape, shape],
        in_specs=[IN_VMEM] * (4 + n + len(weights)),
        out_specs=[IN_VMEM] * 2,
        scratch_shapes=[
            pltpu.VMEM((n * rows, width), jnp.bfloat16),
            pltpu.VMEM((n * rows, stripe), jnp.float32),
        ],
        compiler_params=pltpu.CompilerParams(vmem_limit_bytes=6 * MIB),
        name="project",
    )(
        *sums,
        gain,
        *shards,
        *far,
        *[in_vmem(w) for w in weights],
    )


def split_kernel(keep, got, *outs):
    me = lax.axis_index("gx")
    for d in range(keep.shape[0]):
        at = jnp.bitwise_xor(me, d)
        outs[d % 4][d // 4] = (keep[at] + got[at]).astype(jnp.bfloat16)


def split(keep, got):
    shape = jax.ShapeDtypeStruct((2,) + keep.shape[1:], jnp.bfloat16)
    return pl.pallas_call(
        split_kernel,
        out_shape=[shape] * 4,
        in_specs=[IN_VMEM] * 2,
        out_specs=[IN_VMEM] * 4,
        compiler_params=pltpu.CompilerParams(vmem_limit_bytes=8 * MIB),
        name="split",
    )(keep, got)


def pack(picks, *sources):
    def pack_kernel(*refs):
        for k, (i, j) in enumerate(picks):
            refs[-1][k] = refs[i][j]

    return pl.pallas_call(
        pack_kernel,
        out_shape=jax.ShapeDtypeStruct((len(picks),) + sources[0].shape[1:], sources[0].dtype),
        in_specs=[IN_VMEM] * len(sources),
        out_specs=IN_VMEM,
        compiler_params=pltpu.CompilerParams(vmem_limit_bytes=8 * MIB),
        name="pack",
    )(*sources)


ARRIVED = [(0, 0), (1, 0), (2, 0), (3, 0), (4, 0), (4, 1), (4, 2), (4, 3)]


def attend_kernel(lengths, *refs):
    arrived = refs[:5]
    cosine, sine, keys, values, mine, other, spread, held = refs[5:]
    n, rows, stripe = spread.shape[1], spread.shape[0], spread.shape[2]
    me = lax.axis_index("gx")
    query_cols = stripe - 128
    side = lax.axis_index("gy")
    score_scale = 1.0 / math.sqrt(DH)
    for d, (i, j) in enumerate(ARRIVED):
        block = arrived[i][j].astype(jnp.float32)
        for r in range(rows):
            spread[r, pl.ds(jnp.bitwise_xor(me, d), 1), :] = block[r : r + 1, :]
    starts = range(0, query_cols, DH)
    ready = []
    for r in range(rows):
        given = spread[r]
        cos, sin = cosine[r : r + 1, :], sine[r : r + 1, :]

        def turn(a, b):
            turned = jnp.concatenate([a * cos - b * sin, b * cos + a * sin], axis=1)
            return turned.astype(jnp.bfloat16)

        q = turn(
            jnp.concatenate([given[:, c : c + DH // 2] for c in starts], axis=0),
            jnp.concatenate([given[:, c + DH // 2 : c + DH] for c in starts], axis=0),
        )
        q = (q.astype(jnp.float32) * score_scale).astype(jnp.bfloat16)
        new = [
            given[i : i + 1, query_cols:] + given[i + 1 : i + 2, query_cols:]
            for i in range(0, n, 2)
        ]
        new_key = turn(new[0], new[1]).astype(jnp.float32)
        new_value = jnp.concatenate(new[2:], axis=1)
        scores = lax.dot_general(q, keys[r], contract, preferred_element_type=jnp.float32)
        own_score = jnp.sum(q.astype(jnp.float32) * new_key, axis=1, keepdims=True)
        ready.append((scores, own_score, new_value))
    for r, (scores, own_score, new_value) in enumerate(ready):
        place = lax.broadcasted_iota(jnp.int32, scores.shape, 1)
        scores = jnp.where(place < lengths[r], scores, -1e30)
        highest = jnp.maximum(jnp.max(scores, axis=1, keepdims=True), own_score)
        weights = jnp.exp(scores - highest)
        own_weight = jnp.exp(own_score - highest)
        totals = jnp.sum(weights, axis=1, keepdims=True) + own_weight
        blended = jnp.dot(
            weights.astype(jnp.bfloat16), values[r], preferred_element_type=jnp.float32
        )
        blended = (blended + own_weight * new_value) / totals
        for j in range(len(starts)):
            block = blended[j * n : (j + 1) * n]
            swapped = pltpu.roll(block, n // 2, 0)
            parts = [jnp.where(side == 0, block, swapped), jnp.where(side == 0, swapped, block)]
            for i in range(n // 2):
                at = (i * len(starts) + j) * DH
                for k, part in enumerate(parts):
                    held[k, r : r + 1, at : at + DH] = part[i : i + 1]
    mine[...] = held[0].astype(jnp.bfloat16)
    other[...] = held[1].astype(jnp.bfloat16)


def attend(lengths, arrived, cosine, sine, keys, values):
    n = len(ARRIVED)
    _, rows, stripe = arrived[0].shape
    shape = jax.ShapeDtypeStruct((rows, HEADS * DH // 2), jnp.bfloat16)
    return pl.pallas_call(
        attend_kernel,
        out_shape=[shape, shape],
        in_specs=[IN_SMEM] + [IN_VMEM] * 9,
        out_specs=[IN_VMEM] * 2,
        scratch_shapes=[
            pltpu.VMEM((rows, n, stripe), jnp.float32),
            pltpu.VMEM((2, rows, HEADS * DH // 2), jnp.float32),
        ],
        compiler_params=pltpu.CompilerParams(vmem_limit_bytes=8 * MIB),
        name="attend",
    )(lengths, *arrived, cosine, sine, in_vmem(keys), in_vmem(values))


def output_kernel(n, *refs):
    shards = refs[: n - 1]
    far = refs[n - 1 : n + 1]
    weights = refs[n + 1 : -4]
    keep, give, total, placed = refs[-4:]
    rows = shards[0].shape[0]
    half = far[0].shape[1]
    for part in range(2):
        start = part * half
        cols = slice(start, start + half)
        x = [ref[:, cols] for ref in shards] + [far[part][...]]
        x = jnp.concatenate([piece.astype(jnp.float32) for piece in x], axis=0)
        x = x.astype(jnp.bfloat16)
        first = 0
        for weight in weights:
            last = first + weight.shape[0]
            low, high = max(first, start), min(last, start + half)
            if low < high:
                term = jnp.dot(
                    x[:, low - start : high - start],
                    weight[low - first : high - first, :],
                    preferred_element_type=jnp.float32,
                )
                if low == 0:
                    total[...] = term
                else:
                    total[...] += term
            first = last
    side = lax.axis_index("gy")
    for i, owner in enumerate(owners(n)):
        block = total[i * rows : (i + 1) * rows, :]
        placed[owner] = jnp.where(side == 0, block, pltpu.roll(block, rows // 2, 0))
    keep[...] = placed[pl.ds(side * (n // 2), n // 2)]
    give[...] = placed[pl.ds((1 - side) * (n // 2), n // 2)]


def output_project(shards, far, weights):
    n = len(shards) + 1
    rows = shards[0].shape[0]
    cols = weights[0].shape[1]
    shape = jax.ShapeDtypeStruct((n // 2, rows, cols), jnp.float32)
    return pl.pallas_call(
        lambda *refs: output_kernel(n, *refs),
        out_shape=[shape, shape],
        in_specs=[IN_VMEM] * (n + 1 + len(weights)),
        out_specs=[IN_VMEM] * 2,
        scratch_shapes=[
            pltpu.VMEM((n * rows, cols), jnp.float32),
            pltpu.VMEM((n, rows, cols), jnp.float32),
        ],
        compiler_params=pltpu.CompilerParams(vmem_limit_bytes=8 * MIB),
        name="output_project",
    )(*shards, *far, *[in_vmem(w) for w in weights])


def on_any_grid(
    activations,
    norm_gain,
    query_weight,
    keyval_weight,
    output_weight,
    cache_keys,
    cache_values,
    cache_lengths,
):
    inputs = activations.astype(jnp.float32)
    row_sums, square_sums = lax.psum(
        (jnp.sum(inputs, axis=1), jnp.sum(inputs * inputs, axis=1)), "gy"
    )
    row_mean = row_sums[:, None] / D
    row_square = square_sums[:, None] / D
    variance = row_square - row_mean * row_mean
    normed = (
        (inputs - row_mean) * lax.rsqrt(variance + epsilon) * norm_gain.astype(jnp.float32)
    ).astype(jnp.bfloat16)
    shard_rows = lax.all_gather(normed, "gx", axis=0, tiled=True)
    query_part = lax.dot_general(
        shard_rows, query_weight, contract, preferred_element_type=jnp.float32
    )
    keyval_part = lax.dot_general(
        shard_rows, keyval_weight, contract, preferred_element_type=jnp.float32
    )
    partial_sums = jnp.concatenate([query_part, keyval_part], axis=1)
    wide_count = lax.axis_size("gx")
    pair_count = lax.axis_size("gy")
    local_rows = cache_lengths.shape[0]
    stripe = partial_sums.shape[1]
    arrived = lax.all_to_all(partial_sums, ("gx", "gy"), split_axis=0, concat_axis=1, tiled=True)
    gathered = jnp.sum(arrived.reshape(local_rows, wide_count, pair_count, stripe), axis=2).astype(
        jnp.bfloat16
    )
    query_cols = query_weight.shape[0]
    queries = gathered[:, :, :query_cols].reshape(local_rows, HEADS, DH)
    keyvals = gathered[:, :, query_cols:].reshape(local_rows, 2 * DH)
    places = cache_lengths.astype(jnp.float32)
    queries = rotate(queries.astype(jnp.float32), places[:, None, None]).astype(jnp.bfloat16)
    new_keys = rotate(keyvals[:, :DH].astype(jnp.float32), places[:, None]).astype(jnp.bfloat16)
    new_values = keyvals[:, DH:].astype(jnp.float32)
    score_scale = 1.0 / math.sqrt(DH)
    scores = (
        jnp.einsum("rhd,rtd->rht", queries, cache_keys, preferred_element_type=jnp.float32)
        * score_scale
    )
    visible = jnp.arange(cache_keys.shape[1])[None, :] < cache_lengths[:, None]
    scores = jnp.where(visible[:, None, :], scores, -1e30)
    own_score = (
        jnp.einsum("rhd,rd->rh", queries, new_keys, preferred_element_type=jnp.float32)
        * score_scale
    )
    highest = jnp.maximum(jnp.max(scores, axis=2), own_score)
    weights = jnp.exp(scores - highest[:, :, None])
    own_weight = jnp.exp(own_score - highest)
    totals = jnp.sum(weights, axis=2) + own_weight
    blended = jnp.einsum(
        "rht,rtd->rhd",
        weights.astype(jnp.bfloat16),
        cache_values,
        preferred_element_type=jnp.float32,
    )
    blended = blended + own_weight[:, :, None] * new_values[:, None, :]
    attended = (blended / totals[:, :, None]).astype(jnp.bfloat16).reshape(local_rows, HEADS * DH)
    swapped = lax.all_to_all(attended, "gy", split_axis=1, concat_axis=0, tiled=True)
    partial_out = jnp.dot(
        lax.all_gather(swapped, "gx", axis=0, tiled=True),
        output_weight,
        preferred_element_type=jnp.float32,
    )
    return lax.psum_scatter(partial_out, "gy", scatter_dimension=0, tiled=True).astype(jnp.bfloat16)


def on_device(
    activations,
    norm_gain,
    query_weight,
    keyval_weight,
    output_weight,
    cache_keys,
    cache_values,
    cache_lengths,
):
    n = lax.axis_size("gx")
    ring = Ring(n)
    query_cols, width = query_weight.shape
    new_cols = keyval_weight.shape[0]
    unit = query_cols // 6
    sizes = [2 * unit, 2 * unit, unit, unit]
    weights = []

    indices = jnp.arange(DH // 2, dtype=jnp.float32)
    frequency = jnp.exp(-math.log(10000.0) * indices / (DH // 2))
    angles = cache_lengths.astype(jnp.float32)[:, None] * frequency
    cosine, sine = jnp.cos(angles), jnp.sin(angles)

    def piece_of(array, start, size, after):
        return load(size, [(array, start, size, 0)], after)

    left = right = activations
    shards = [activations]
    sums = []
    for step in range(1, n // 2):
        arrived = shards[-2:] if step > 1 else []
        left, right = ring.step(left, right)
        if step > 1:
            sums = [row_sums([activations, *arrived] if step == 2 else arrived, sums)]
        if step == 3:
            far_sums = lax.ppermute(sums[0][: activations.shape[0]], "gx", ring.across)
        weight = piece_of(query_weight, sum(sizes[: step - 1]), sizes[step - 1], arrived)
        weight, (left, right, *sums) = before(weight, left, right, *sums)
        weights.append(weight)
        shards += [left, right]
    cut, (cut_right, left, right) = before(
        left[:, : width // 2], right[:, width // 2 :], left, right
    )
    far = ring.step(cut, cut_right)
    sums = row_sums([left, right], sums)
    jobs = [(query_weight, 5 * unit, unit, 0), (keyval_weight, 0, new_cols, unit)]
    weight = load(unit + new_cols, jobs, [sums])
    sums = jnp.concatenate([sums, far_sums], axis=0)
    other_sums = swap_pair(sums)
    weight, (other_sums, *far) = before(weight, other_sums, *far)
    weights.append(weight)
    gain = norm_gain.astype(jnp.float32)[None, :]
    keep, give = project((sums, other_sums), gain, shards, far, weights)

    def exchange(blocks, d):
        return lax.ppermute(blocks, "gx", [(i, i ^ d) for i in range(n)])

    blocks = split(keep, swap_pair(give))
    arrived = [blocks[0]] + [exchange(blocks[d], d) for d in range(1, 4)]
    keys = load_cache(cache_keys, [blocks[1]])
    keys, arrived = before(keys, *arrived)
    across = pack([(0, 1), (1, 1), (2, 1), (3, 1)], *arrived)
    last = exchange(across, 4)
    values = load_cache(cache_values, [across])
    unit = output_weight.shape[0] // 12
    sizes = [unit, 3 * unit, 3 * unit, 3 * unit, 2 * unit]
    weight = load(unit, [(output_weight, 0, unit, 0)], [across])
    values, (last,) = before(values, last)
    weight, (last,) = before(weight, last)
    weights = [weight]
    arrived = [*arrived, last]
    mine, other = attend(cache_lengths, arrived, cosine, sine, keys, values)
    shard = jnp.concatenate([mine, swap_pair(other)], axis=0)

    left = right = shard
    shards = [shard]

    for step in range(1, n // 2):
        arrived = shards[-2:]
        left, right = ring.step(left, right)
        weight = piece_of(output_weight, sum(sizes[:step]), sizes[step], arrived)
        weight, (left, right) = before(weight, left, right)
        weights.append(weight)
        shards += [left, right]
    half = shard.shape[1] // 2
    far = ring.step(left[:, :half], right[:, half:])
    weight = piece_of(output_weight, sum(sizes[:4]), sizes[4], [left, right])
    weight, far = before(weight, *far)
    weights.append(weight)
    keep, give = output_project(shards, far, weights)
    out = (keep + swap_pair(give)).astype(jnp.bfloat16)
    return out.reshape(-1, out.shape[-1])


def solution(mesh):
    return jax.shard_map(
        on_device if mesh.shape["gx"] == 8 else on_any_grid,
        mesh=mesh,
        in_specs=(
            P(("groups", "gx"), "gy"),
            P("gy"),
            P("gx", "gy"),
            P("gx", "gy"),
            P("gy", "gx"),
            P(("groups", "gx", "gy"), None, None),
            P(("groups", "gx", "gy"), None, None),
            P(("groups", "gx", "gy")),
        ),
        out_specs=P(("groups", "gy"), "gx"),
        check_vma=False,
    )
```

```python
import math

import jax
import jax.numpy as jnp
from jax import lax
from jax.experimental import pallas as pl
from jax.experimental.pallas import tpu as pltpu
from jax.sharding import PartitionSpec as P

D = 18432
HEADS = 48
DH = 256


epsilon = 1e-06
contract = (((1,), (1,)), ((), ()))
MIB = 1 << 20
ANY = pl.BlockSpec(memory_space=pl.ANY)
IN_HBM = pl.BlockSpec(memory_space=pltpu.HBM)
IN_VMEM = pl.BlockSpec(memory_space=pltpu.VMEM)
IN_SMEM = pl.BlockSpec(memory_space=pltpu.SMEM)


def rotate(vectors, places):
    half_width = vectors.shape[-1] // 2
    indices = jnp.arange(half_width, dtype=jnp.float32)
    frequency = jnp.exp(-math.log(10000.0) * indices / half_width)
    angles = places * frequency
    cosine = jnp.cos(angles)
    sine = jnp.sin(angles)
    first_half = vectors[..., :half_width]
    second_half = vectors[..., half_width:]
    return jnp.concatenate(
        [first_half * cosine - second_half * sine, second_half * cosine + first_half * sine],
        axis=-1,
    )


def ring_order(n):
    return list(range(0, n, 2)) + list(range(n - 1, 0, -2))


def swap_pair(x):
    return lax.ppermute(x, "gy", [(0, 1), (1, 0)])


class Ring:
    def __init__(self, n):
        order = ring_order(n)
        self.onward = [(order[p], order[(p + 1) % n]) for p in range(n)]
        self.back = [(order[p], order[(p - 1) % n]) for p in range(n)]
        self.across = [(order[p], order[(p + n // 2) % n]) for p in range(n)]

    def step(self, left, right):
        return lax.ppermute(left, "gx", self.onward), lax.ppermute(right, "gx", self.back)


def owners(n):
    offsets = [0]
    for step in range(1, n // 2):
        offsets += [-step, step]
    offsets.append(n // 2)
    me = lax.axis_index("gx")
    half = lax.div(me, 2)
    place = jnp.where(lax.rem(me, 2) == 0, half, n - 1 - half)
    result = []
    for offset in offsets:
        at = lax.rem(place + (offset + n), n)
        result.append(jnp.where(at < n // 2, 2 * at, 2 * (n - 1 - at) + 1))
    return result


def start_copies(source, target, sems, count):
    rows = source.shape[0]
    size = -(-rows // (16 * count)) * 16
    copies = []
    for i, first in enumerate(range(0, rows, size)):
        at = pl.ds(first, min(size, rows - first))
        copy = pltpu.make_async_copy(source.at[at], target.at[at], sems.at[i])
        copy.start()
        copies.append(copy)
    return copies


def load_kernel(jobs, *refs):
    sources, target, sems = refs[: len(jobs)], refs[-2], refs[-1]
    copies = []
    for i, (first, size, at) in enumerate(jobs):
        part = sources[i].at[pl.ds(first, size)]
        copies += start_copies(part, target.at[pl.ds(at, size)], sems.at[i], 4)
    for copy in copies:
        copy.wait()


def load(rows, jobs, after=()):
    array = jobs[0][0]
    return pl.pallas_call(
        lambda *refs: load_kernel([job[1:] for job in jobs], *refs),
        out_shape=pltpu.VMEM((rows, array.shape[1]), array.dtype),
        in_specs=[IN_HBM] * len(jobs) + [ANY] * len(after),
        out_specs=IN_VMEM,
        scratch_shapes=[pltpu.SemaphoreType.DMA((len(jobs), 4))],
        compiler_params=pltpu.CompilerParams(vmem_limit_bytes=MIB),
        name="load",
    )(*[in_hbm(job[0]) for job in jobs], *after)


def load_cache_kernel(source, *refs):
    target, sems = refs[-2:]
    copies = []
    for row in range(source.shape[0]):
        copies.append(pltpu.make_async_copy(source.at[row], target.at[row], sems.at[row]))
        copies[-1].start()
    for copy in copies:
        copy.wait()


def load_cache(cache, after):
    return pl.pallas_call(
        load_cache_kernel,
        out_shape=pltpu.VMEM(cache.shape, cache.dtype),
        in_specs=[IN_HBM] + [ANY] * len(after),
        out_specs=IN_VMEM,
        scratch_shapes=[pltpu.SemaphoreType.DMA((cache.shape[0],))],
        compiler_params=pltpu.CompilerParams(vmem_limit_bytes=MIB),
        name="load_cache",
    )(in_hbm(cache), *after)


def in_hbm(array):
    return pltpu.with_memory_space_constraint(array, pltpu.HBM)


def in_vmem(array):
    return pltpu.with_memory_space_constraint(array, pltpu.VMEM)


def before(done, *rest):
    held = lax.optimization_barrier((done,) + rest)
    return held[0], held[1:]


def sums_kernel(ready, count, *refs):
    out = refs[-1]
    start = 0
    for ref in refs[:ready]:
        out[start : start + ref.shape[0], :] = ref[...]
        start += ref.shape[0]
    rows = refs[ready].shape[0]
    lane = lax.broadcasted_iota(jnp.int32, (rows, 128), 1)
    for ref in refs[ready : ready + count]:
        x = ref[...].astype(jnp.float32)
        total = jnp.sum(x, axis=1, keepdims=True)
        square = jnp.sum(x * x, axis=1, keepdims=True)
        both = jnp.where(lane == 0, total, jnp.where(lane == 1, square, 0.0))
        out[start : start + rows, :] = both
        start += rows


def row_sums(shards, ready=(), after=()):
    rows = shards[0].shape[0] * len(shards) + sum(r.shape[0] for r in ready)
    return pl.pallas_call(
        lambda *refs: sums_kernel(len(ready), len(shards), *refs),
        out_shape=jax.ShapeDtypeStruct((rows, 128), jnp.float32),
        in_specs=[IN_VMEM] * (len(ready) + len(shards)) + [ANY] * len(after),
        out_specs=IN_VMEM,
        compiler_params=pltpu.CompilerParams(vmem_limit_bytes=8 * MIB),
        name="row_sums",
    )(*ready, *shards, *after)


def project_kernel(n, parts, *refs):
    sums_a, sums_b, gain = refs[:3]
    shards = refs[3 : 3 + n - 1]
    far = refs[3 + n - 1 : 3 + n + 1]
    weights = refs[4 + n : 4 + n + parts]
    keep, give, normed, total = refs[4 + n + parts :]
    rows, width = shards[0].shape
    sums = sums_a[...] + sums_b[...]
    row_mean = sums[:, :1] / D
    row_square = sums[:, 1:2] / D
    scale = lax.rsqrt(row_square - row_mean * row_mean + epsilon)
    for part in range(4):
        cols = slice(part * width // 4, (part + 1) * width // 4)
        end = slice(part % 2 * width // 4, (part % 2 + 1) * width // 4)
        for i in range(0, n, 2):
            x = [ref[:, cols] for ref in shards] + [far[part // 2][:, end]]
            x = jnp.concatenate([piece.astype(jnp.float32) for piece in x[i : i + 2]], axis=0)
            at = slice(i * rows, (i + 2) * rows)
            x = (x - row_mean[at]) * scale[at] * gain[:, cols]
            normed[at, cols] = x.astype(jnp.bfloat16)
        x = normed[:, cols]
        start = 0
        for weight in weights:
            term = lax.dot_general(
                x, weight[:, cols], contract, preferred_element_type=jnp.float32
            )
            stripe = slice(start, start + weight.shape[0])
            if part == 0:
                total[:, stripe] = term
            else:
                total[:, stripe] += term
            start = stripe.stop
    last = slice(total.shape[1] - 128, total.shape[1])
    lane = lax.broadcasted_iota(jnp.int32, (total.shape[0], 128), 1)
    new = jnp.where(lane < 64, total[:, last], 0.0)
    odd = lax.rem(lax.axis_index("gx"), 2)
    total[:, last] = jnp.where(odd == 0, new, pltpu.roll(new, 64, 1))
    side = lax.axis_index("gy")
    local = rows // 2
    for i, owner in enumerate(owners(n)):
        block = total[i * rows : (i + 1) * rows, :]
        low, high = block[:local], block[local:]
        keep[owner] = jnp.where(side == 0, low, high)
        give[owner] = jnp.where(side == 0, high, low)


def project(sums, gain, shards, far, weights):
    n = len(shards) + 1
    rows, width = shards[0].shape
    stripe = sum(w.shape[0] for w in weights) + 64
    shape = jax.ShapeDtypeStruct((n, rows // 2, stripe), jnp.float32)
    return pl.pallas_call(
        lambda *refs: project_kernel(n, len(weights), *refs),
        out_shape=[shape, shape],
        in_specs=[IN_VMEM] * (4 + n + len(weights)),
        out_specs=[IN_VMEM] * 2,
        scratch_shapes=[
            pltpu.VMEM((n * rows, width), jnp.bfloat16),
            pltpu.VMEM((n * rows, stripe), jnp.float32),
        ],
        compiler_params=pltpu.CompilerParams(vmem_limit_bytes=6 * MIB),
        name="project",
    )(
        *sums,
        gain,
        *shards,
        *far,
        *[in_vmem(w) for w in weights],
    )


def split_kernel(keep, got, *outs):
    me = lax.axis_index("gx")
    for d in range(keep.shape[0]):
        at = jnp.bitwise_xor(me, d)
        outs[d % 4][d // 4] = (keep[at] + got[at]).astype(jnp.bfloat16)


def split(keep, got):
    shape = jax.ShapeDtypeStruct((2,) + keep.shape[1:], jnp.bfloat16)
    return pl.pallas_call(
        split_kernel,
        out_shape=[shape] * 4,
        in_specs=[IN_VMEM] * 2,
        out_specs=[IN_VMEM] * 4,
        compiler_params=pltpu.CompilerParams(vmem_limit_bytes=8 * MIB),
        name="split",
    )(keep, got)


def pack(picks, *sources):
    def pack_kernel(*refs):
        for k, (i, j) in enumerate(picks):
            refs[-1][k] = refs[i][j]

    return pl.pallas_call(
        pack_kernel,
        out_shape=jax.ShapeDtypeStruct((len(picks),) + sources[0].shape[1:], sources[0].dtype),
        in_specs=[IN_VMEM] * len(sources),
        out_specs=IN_VMEM,
        compiler_params=pltpu.CompilerParams(vmem_limit_bytes=8 * MIB),
        name="pack",
    )(*sources)


ARRIVED = [(0, 0), (1, 0), (2, 0), (3, 0), (4, 0), (4, 1), (4, 2), (4, 3)]


def attend_kernel(lengths, *refs):
    arrived = refs[:5]
    cosine, sine, keys, values, mine, other, spread, held = refs[5:]
    n, rows, stripe = spread.shape[1], spread.shape[0], spread.shape[2]
    me = lax.axis_index("gx")
    query_cols = stripe - 128
    side = lax.axis_index("gy")
    score_scale = 1.0 / math.sqrt(DH)
    for d, (i, j) in enumerate(ARRIVED):
        block = arrived[i][j].astype(jnp.float32)
        for r in range(rows):
            spread[r, pl.ds(jnp.bitwise_xor(me, d), 1), :] = block[r : r + 1, :]
    starts = range(0, query_cols, DH)
    ready = []
    for r in range(rows):
        given = spread[r]
        cos, sin = cosine[r : r + 1, :], sine[r : r + 1, :]

        def turn(a, b):
            turned = jnp.concatenate([a * cos - b * sin, b * cos + a * sin], axis=1)
            return turned.astype(jnp.bfloat16)

        q = turn(
            jnp.concatenate([given[:, c : c + DH // 2] for c in starts], axis=0),
            jnp.concatenate([given[:, c + DH // 2 : c + DH] for c in starts], axis=0),
        )
        q = (q.astype(jnp.float32) * score_scale).astype(jnp.bfloat16)
        new = [
            given[i : i + 1, query_cols:] + given[i + 1 : i + 2, query_cols:]
            for i in range(0, n, 2)
        ]
        new_key = turn(new[0], new[1]).astype(jnp.float32)
        new_value = jnp.concatenate(new[2:], axis=1)
        scores = lax.dot_general(q, keys[r], contract, preferred_element_type=jnp.float32)
        own_score = jnp.sum(q.astype(jnp.float32) * new_key, axis=1, keepdims=True)
        ready.append((scores, own_score, new_value))
    for r, (scores, own_score, new_value) in enumerate(ready):
        place = lax.broadcasted_iota(jnp.int32, scores.shape, 1)
        scores = jnp.where(place < lengths[r], scores, -1e30)
        highest = jnp.maximum(jnp.max(scores, axis=1, keepdims=True), own_score)
        weights = jnp.exp(scores - highest)
        own_weight = jnp.exp(own_score - highest)
        totals = jnp.sum(weights, axis=1, keepdims=True) + own_weight
        blended = jnp.dot(
            weights.astype(jnp.bfloat16), values[r], preferred_element_type=jnp.float32
        )
        blended = (blended + own_weight * new_value) / totals
        for j in range(len(starts)):
            block = blended[j * n : (j + 1) * n]
            swapped = pltpu.roll(block, n // 2, 0)
            parts = [jnp.where(side == 0, block, swapped), jnp.where(side == 0, swapped, block)]
            for i in range(n // 2):
                at = (i * len(starts) + j) * DH
                for k, part in enumerate(parts):
                    held[k, r : r + 1, at : at + DH] = part[i : i + 1]
    mine[...] = held[0].astype(jnp.bfloat16)
    other[...] = held[1].astype(jnp.bfloat16)


def attend(lengths, arrived, cosine, sine, keys, values):
    n = len(ARRIVED)
    _, rows, stripe = arrived[0].shape
    shape = jax.ShapeDtypeStruct((rows, HEADS * DH // 2), jnp.bfloat16)
    return pl.pallas_call(
        attend_kernel,
        out_shape=[shape, shape],
        in_specs=[IN_SMEM] + [IN_VMEM] * 9,
        out_specs=[IN_VMEM] * 2,
        scratch_shapes=[
            pltpu.VMEM((rows, n, stripe), jnp.float32),
            pltpu.VMEM((2, rows, HEADS * DH // 2), jnp.float32),
        ],
        compiler_params=pltpu.CompilerParams(vmem_limit_bytes=8 * MIB),
        name="attend",
    )(lengths, *arrived, cosine, sine, in_vmem(keys), in_vmem(values))


def output_kernel(n, *refs):
    shards = refs[: n - 1]
    far = refs[n - 1 : n + 1]
    weights = refs[n + 1 : -4]
    keep, give, total, placed = refs[-4:]
    rows = shards[0].shape[0]
    half = far[0].shape[1]
    for part in range(2):
        start = part * half
        cols = slice(start, start + half)
        x = [ref[:, cols] for ref in shards] + [far[part][...]]
        x = jnp.concatenate([piece.astype(jnp.float32) for piece in x], axis=0)
        x = x.astype(jnp.bfloat16)
        first = 0
        for weight in weights:
            last = first + weight.shape[0]
            low, high = max(first, start), min(last, start + half)
            if low < high:
                term = jnp.dot(
                    x[:, low - start : high - start],
                    weight[low - first : high - first, :],
                    preferred_element_type=jnp.float32,
                )
                if low == 0:
                    total[...] = term
                else:
                    total[...] += term
            first = last
    side = lax.axis_index("gy")
    for i, owner in enumerate(owners(n)):
        block = total[i * rows : (i + 1) * rows, :]
        placed[owner] = jnp.where(side == 0, block, pltpu.roll(block, rows // 2, 0))
    keep[...] = placed[pl.ds(side * (n // 2), n // 2)]
    give[...] = placed[pl.ds((1 - side) * (n // 2), n // 2)]


def output_project(shards, far, weights):
    n = len(shards) + 1
    rows = shards[0].shape[0]
    cols = weights[0].shape[1]
    shape = jax.ShapeDtypeStruct((n // 2, rows, cols), jnp.float32)
    return pl.pallas_call(
        lambda *refs: output_kernel(n, *refs),
        out_shape=[shape, shape],
        in_specs=[IN_VMEM] * (n + 1 + len(weights)),
        out_specs=[IN_VMEM] * 2,
        scratch_shapes=[
            pltpu.VMEM((n * rows, cols), jnp.float32),
            pltpu.VMEM((n, rows, cols), jnp.float32),
        ],
        compiler_params=pltpu.CompilerParams(vmem_limit_bytes=8 * MIB),
        name="output_project",
    )(*shards, *far, *[in_vmem(w) for w in weights])


def on_any_grid(
    activations,
    norm_gain,
    query_weight,
    keyval_weight,
    output_weight,
    cache_keys,
    cache_values,
    cache_lengths,
):
    inputs = activations.astype(jnp.float32)
    row_sums, square_sums = lax.psum(
        (jnp.sum(inputs, axis=1), jnp.sum(inputs * inputs, axis=1)), "gy"
    )
    row_mean = row_sums[:, None] / D
    row_square = square_sums[:, None] / D
    variance = row_square - row_mean * row_mean
    normed = (
        (inputs - row_mean) * lax.rsqrt(variance + epsilon) * norm_gain.astype(jnp.float32)
    ).astype(jnp.bfloat16)
    shard_rows = lax.all_gather(normed, "gx", axis=0, tiled=True)
    query_part = lax.dot_general(
        shard_rows, query_weight, contract, preferred_element_type=jnp.float32
    )
    keyval_part = lax.dot_general(
        shard_rows, keyval_weight, contract, preferred_element_type=jnp.float32
    )
    partial_sums = jnp.concatenate([query_part, keyval_part], axis=1)
    wide_count = lax.axis_size("gx")
    pair_count = lax.axis_size("gy")
    local_rows = cache_lengths.shape[0]
    stripe = partial_sums.shape[1]
    arrived = lax.all_to_all(partial_sums, ("gx", "gy"), split_axis=0, concat_axis=1, tiled=True)
    gathered = jnp.sum(arrived.reshape(local_rows, wide_count, pair_count, stripe), axis=2).astype(
        jnp.bfloat16
    )
    query_cols = query_weight.shape[0]
    queries = gathered[:, :, :query_cols].reshape(local_rows, HEADS, DH)
    keyvals = gathered[:, :, query_cols:].reshape(local_rows, 2 * DH)
    places = cache_lengths.astype(jnp.float32)
    queries = rotate(queries.astype(jnp.float32), places[:, None, None]).astype(jnp.bfloat16)
    new_keys = rotate(keyvals[:, :DH].astype(jnp.float32), places[:, None]).astype(jnp.bfloat16)
    new_values = keyvals[:, DH:].astype(jnp.float32)
    score_scale = 1.0 / math.sqrt(DH)
    scores = (
        jnp.einsum("rhd,rtd->rht", queries, cache_keys, preferred_element_type=jnp.float32)
        * score_scale
    )
    visible = jnp.arange(cache_keys.shape[1])[None, :] < cache_lengths[:, None]
    scores = jnp.where(visible[:, None, :], scores, -1e30)
    own_score = (
        jnp.einsum("rhd,rd->rh", queries, new_keys, preferred_element_type=jnp.float32)
        * score_scale
    )
    highest = jnp.maximum(jnp.max(scores, axis=2), own_score)
    weights = jnp.exp(scores - highest[:, :, None])
    own_weight = jnp.exp(own_score - highest)
    totals = jnp.sum(weights, axis=2) + own_weight
    blended = jnp.einsum(
        "rht,rtd->rhd",
        weights.astype(jnp.bfloat16),
        cache_values,
        preferred_element_type=jnp.float32,
    )
    blended = blended + own_weight[:, :, None] * new_values[:, None, :]
    attended = (blended / totals[:, :, None]).astype(jnp.bfloat16).reshape(local_rows, HEADS * DH)
    swapped = lax.all_to_all(attended, "gy", split_axis=1, concat_axis=0, tiled=True)
    partial_out = jnp.dot(
        lax.all_gather(swapped, "gx", axis=0, tiled=True),
        output_weight,
        preferred_element_type=jnp.float32,
    )
    return lax.psum_scatter(partial_out, "gy", scatter_dimension=0, tiled=True).astype(jnp.bfloat16)


def on_device(
    activations,
    norm_gain,
    query_weight,
    keyval_weight,
    output_weight,
    cache_keys,
    cache_values,
    cache_lengths,
):
    n = lax.axis_size("gx")
    ring = Ring(n)
    query_cols, width = query_weight.shape
    new_cols = keyval_weight.shape[0]
    unit = query_cols // 6
    sizes = [2 * unit, 2 * unit, unit, unit]
    weights = []

    indices = jnp.arange(DH // 2, dtype=jnp.float32)
    frequency = jnp.exp(-math.log(10000.0) * indices / (DH // 2))
    angles = cache_lengths.astype(jnp.float32)[:, None] * frequency
    cosine, sine = jnp.cos(angles), jnp.sin(angles)

    def piece_of(array, start, size, after):
        return load(size, [(array, start, size, 0)], after)

    left = right = activations
    shards = [activations]
    sums = []
    for step in range(1, n // 2):
        arrived = shards[-2:] if step > 1 else []
        left, right = ring.step(left, right)
        if step > 1:
            sums = [row_sums([activations, *arrived] if step == 2 else arrived, sums)]
        if step == 3:
            far_sums = lax.ppermute(sums[0][: activations.shape[0]], "gx", ring.across)
        weight = piece_of(query_weight, sum(sizes[: step - 1]), sizes[step - 1], arrived)
        weight, (left, right, *sums) = before(weight, left, right, *sums)
        weights.append(weight)
        shards += [left, right]
    cut, (cut_right, left, right) = before(
        left[:, : width // 2], right[:, width // 2 :], left, right
    )
    far = ring.step(cut, cut_right)
    sums = row_sums([left, right], sums)
    jobs = [(query_weight, 5 * unit, unit, 0), (keyval_weight, 0, new_cols, unit)]
    weight = load(unit + new_cols, jobs, [sums])
    sums = jnp.concatenate([sums, far_sums], axis=0)
    other_sums = swap_pair(sums)
    weight, (other_sums, *far) = before(weight, other_sums, *far)
    weights.append(weight)
    gain = norm_gain.astype(jnp.float32)[None, :]
    keep, give = project((sums, other_sums), gain, shards, far, weights)

    def exchange(blocks, d):
        return lax.ppermute(blocks, "gx", [(i, i ^ d) for i in range(n)])

    blocks = split(keep, swap_pair(give))
    arrived = [blocks[0]] + [exchange(blocks[d], d) for d in range(1, 4)]
    keys = load_cache(cache_keys, [blocks[1]])
    keys, arrived = before(keys, *arrived)
    across = pack([(0, 1), (1, 1), (2, 1), (3, 1)], *arrived)
    last = exchange(across, 4)
    values = load_cache(cache_values, [across])
    unit = output_weight.shape[0] // 12
    sizes = [unit, 3 * unit, 3 * unit, 3 * unit, 2 * unit]
    weight = load(unit, [(output_weight, 0, unit, 0)], [across])
    values, (last,) = before(values, last)
    weight, (last,) = before(weight, last)
    weights = [weight]
    arrived = [*arrived, last]
    mine, other = attend(cache_lengths, arrived, cosine, sine, keys, values)
    shard = jnp.concatenate([mine, swap_pair(other)], axis=0)

    left = right = shard
    shards = [shard]

    for step in range(1, n // 2):
        arrived = shards[-2:]
        left, right = ring.step(left, right)
        weight = piece_of(output_weight, sum(sizes[:step]), sizes[step], arrived)
        weight, (left, right) = before(weight, left, right)
        weights.append(weight)
        shards += [left, right]
    half = shard.shape[1] // 2
    far = ring.step(left[:, :half], right[:, half:])
    weight = piece_of(output_weight, sum(sizes[:4]), sizes[4], [left, right])
    weight, far = before(weight, *far)
    weights.append(weight)
    keep, give = output_project(shards, far, weights)
    out = (keep + swap_pair(give)).astype(jnp.bfloat16)
    return out.reshape(-1, out.shape[-1])


def solution(mesh):
    return jax.shard_map(
        on_device if mesh.shape["gx"] == 8 else on_any_grid,
        mesh=mesh,
        in_specs=(
            P(("groups", "gx"), "gy"),
            P("gy"),
            P("gx", "gy"),
            P("gx", "gy"),
            P("gy", "gx"),
            P(("groups", "gx", "gy"), None, None),
            P(("groups", "gx", "gy"), None, None),
            P(("groups", "gx", "gy")),
        ),
        out_specs=P(("groups", "gy"), "gx"),
        check_vma=False,
    )
```
